32 devices in a mesh: dp: 2 (over x), context: 4 (over y, core), expert: 4 (over z).
Axes of the slice: x: 2, y: 2, z: 4, core: 2. Of those that a mesh axis runs over, the one named last changes fastest.
Arguments:
- tokens: bfloat16 [8, 1024, 1536], P(('dp', 'expert'), 'context'), may hold values from -6 to 6
- lengths: int32 [8], P(('dp', 'expert')), may hold values from 769 to 1024, as said below
- routes: int32 [8, 1024, 8], P(('dp', 'expert'), 'context'), may hold values from 0 to 31, all different within a row; in each aligned block of 256 rows (0 to 255, 256 to 511, ..., all dimensions but the last counted through in order) at most 96 rows name the same one
- gain_attn: bfloat16 [1536], P(('dp', 'context', 'expert')), may hold values from 0.5 to 1.5
- w_query: bfloat16 [1536, 1536], P(('dp', 'context', 'expert')), may hold values from -0.15625 to 0.15625
- key_weight: bfloat16 [1536, 512], P(('dp', 'context', 'expert')), may hold values from -0.15625 to 0.15625
- value_weight: bfloat16 [1536, 512], P(('dp', 'context', 'expert')), may hold values from -0.15625 to 0.15625
- w_out: bfloat16 [1536, 1536], P(('dp', 'context', 'expert')), may hold values from -1.25 to 1.25
- gain_ffn: bfloat16 [1536], P(('dp', 'context', 'expert')), may hold values from 0.5 to 1.5
- w_router: bfloat16 [1536, 32], P(('dp', 'context', 'expert')), may hold values from -0.078125 to 0.078125
- w_gate: bfloat16 [32, 1536, 512], P(('context', 'expert')), may hold values from -0.15625 to 0.15625
- w_up: bfloat16 [32, 1536, 512], P(('context', 'expert')), may hold values from -0.15625 to 0.15625
- w_down: bfloat16 [32, 512, 1536], P(('context', 'expert')), may hold values from -0.75 to 0.75
- cotangent: bfloat16 [8, 1024, 1536], P(('dp', 'expert'), 'context'), may hold values from -6 to 6
Outputs:
- block_out: bfloat16 [8, 1024, 1536], P(('dp', 'expert'), 'context')
- grad_tokens: float32 [8, 1024, 1536], P(('dp', 'expert'), 'context')
- grad_gain_attn: float32 [1536], P(('dp', 'context', 'expert'))
- grad_w_query: float32 [1536, 1536], P(('dp', 'context', 'expert'))
- grad_w_key: float32 [1536, 512], P(('dp', 'context', 'expert'))
- grad_w_value: float32 [1536, 512], P(('dp', 'context', 'expert'))
- grad_w_out: float32 [1536, 1536], P(('dp', 'context', 'expert'))
- grad_gain_ffn: float32 [1536], P(('dp', 'context', 'expert'))
- grad_w_router: float32 [1536, 32], P(('dp', 'context', 'expert'))
- grad_w_gate: float32 [32, 1536, 512], P(('context', 'expert'), 'dp')
- grad_w_up: float32 [32, 1536, 512], P(('context', 'expert'), 'dp')
- grad_w_down: float32 [32, 512, 1536], P(('context', 'expert'), 'dp')
The draws below stay inside these ranges and needn't reach their ends.
Inputs may be any that keep to these rules, and one draw needn't show every extreme that they name: Within each aligned block of 256 positions of one slot, no expert is named by more than 96 of the block's routes. `lengths`: among the 1 consecutive slots that one index of dp and expert holds, one slot, drawn from the seed, is longer than 768; among the slots of one index of dp, one of these, drawn from the seed, has the full length 1024.
All inputs are finite; a program needn't handle non-finite values.
Results may differ from the reference program's by a relative error of at most 0.018.
Values may be sent and summed in bfloat16 or wider, within the bound.
A program may use at most 256 MiB of HBM per device.

```python
import math
import jax
import jax.numpy as jnp
import numpy as np
from jax import lax

MODEL_WIDTH = 1536
QUERY_HEADS = 24
KEY_VALUE_HEADS = 8
HEAD_SIZE = 64
FF = 512
TOP = 8
SEQ_DEV = 256
SEQ_GRP = 1
SLOT_LENGTH = 1024
SEQUENCE_SLOTS = 8
EXPERTS = 32
MOST = 96
N_DP = 2
N_CONTEXT = 4
N_EXPERT = 4


def draw_lengths(key, part):
    key = jax.random.fold_in(key, 7)
    first_key, second_key, third_key, fourth_key = jax.random.split(key, 4)
    shorter = jax.random.randint(first_key, (N_DP, N_EXPERT, SEQ_GRP), SLOT_LENGTH // 4, SLOT_LENGTH + 1)
    reaching = jax.random.randint(second_key, (N_DP, N_EXPERT, 1), SLOT_LENGTH - SEQ_DEV + 1, SLOT_LENGTH + 1)
    picked = jax.random.randint(third_key, (N_DP, N_EXPERT, 1), 0, SEQ_GRP)
    full_group = jax.random.randint(fourth_key, (N_DP, 1, 1), 0, N_EXPERT)
    is_picked = jnp.arange(SEQ_GRP, dtype=jnp.int32)[None, None, :] == picked
    is_full = jnp.arange(N_EXPERT, dtype=jnp.int32)[None, :, None] == full_group
    picked_length = jnp.where(is_full, SLOT_LENGTH, reaching)
    return jnp.where(is_picked, picked_length, shorter).reshape(SEQUENCE_SLOTS).astype(jnp.int32)


def steps_of(key, dims, pieces, least, top_value):
    level = 1.0
    for dim, parts in pieces:
        steps = jax.random.uniform(jax.random.fold_in(jax.random.fold_in(key, 6), dim), (parts,), jnp.float32, least / len(pieces), top_value / len(pieces))
        level = level * jnp.repeat(jnp.exp(steps), dims[dim] // parts).reshape((-1,) + (1,) * (len(dims) - 1 - dim))
    return level


def shared_out(key, own, number, rows, count, top, most, skew):
    sequence = jax.random.permutation(key, count)
    packed, common = load_shares(count, rows * top, most, skew, True), load_shares(count, rows * top, most, skew, False)
    places = jnp.arange(count)

    def named(tallies, offset_by):
        used = int((tallies > 0).sum())
        fixed = max(1, used // 4)
        moved = fixed + (places - fixed + offset_by * (used - fixed)) % max(1, count - fixed)
        return jnp.zeros((count,), jnp.int32).at[sequence[jnp.where(places < fixed, places, moved)]].set(jnp.asarray(tallies, jnp.int32))

    tallies = jnp.where(number % 4 == 0, named(packed, number // 4), named(common, number - number // 4 - 1))
    mixed = jax.random.permutation(jax.random.fold_in(own, 3), count)
    donor, receiver = mixed[0:count // 2 * 2:2], mixed[1:count // 2 * 2:2]
    room = jnp.minimum(tallies[donor] - 1, most - tallies[receiver]) // 2
    room = jnp.where((donor == sequence[0]) | (receiver == sequence[0]) | (tallies[receiver] == 0), 0, jnp.maximum(room, 0))
    moved = jax.random.randint(jax.random.fold_in(own, 4), (count // 2,), 0, 1 << 20) % (room + 1)
    tallies = tallies.at[donor].add(-moved).at[receiver].add(moved)
    labels = jnp.searchsorted(jnp.cumsum(tallies), jnp.arange(rows * top), side="right").astype(jnp.int32)
    table = labels.reshape(top, rows).T
    table = table[jax.random.permutation(jax.random.fold_in(own, 1), rows)]
    offset_by = jax.random.randint(jax.random.fold_in(own, 2), (rows, 1), 0, top)
    return jnp.take_along_axis(table, (jnp.arange(top)[None, :] + offset_by) % top, axis=1)


def load_shares(amount, total, bound, skew, full):
    portions = [(1 << 20) // math.isqrt(grade ** skew) + 1 for grade in range(1, amount + 1)]
    largest = bound if full else min(bound, max(-(-total // amount), total * portions[0] // sum(portions)))
    least = 1 if total - largest >= amount - 1 else 0
    holding, rest = [largest] + [least] * (amount - 1), total - largest - least * (amount - 1)
    while rest > 0:
        free = [i for i in range(1, amount) if holding[i] < largest] or [i for i in range(1, amount) if holding[i] < bound]
        whole, budget = sum([portions[i] for i in free]), rest
        for i in free:
            addition = min(bound - holding[i], max(1, budget * portions[i] // whole), rest)
            holding[i] = holding[i] + addition
            rest = rest - addition
    return np.array(holding)


def normal_values(key, shape, spread, limit, cuts=(), kind=jnp.bfloat16):
    loudness = steps_of(key, shape, cuts, -0.22, 0.18) if cuts else 1.0
    values = jax.random.normal(key, shape, jnp.float32) * spread * loudness
    return jnp.minimum(jnp.maximum(values, -limit), limit).astype(kind)


def setup_inputs(seed: int = 0) -> dict:
    keys = jax.random.split(jax.random.key(seed), 15)
    tokens = normal_values(keys[0], (SEQUENCE_SLOTS, SLOT_LENGTH, MODEL_WIDTH), 1.0, 6.0, ((0, 8), (1, 4)))
    lengths = draw_lengths(jax.random.fold_in(keys[14], 71), 0)
    routes_keys = jax.random.split(jax.random.fold_in(keys[2], 1), SEQUENCE_SLOTS * SLOT_LENGTH // SEQ_DEV)
    routes_turns = jax.random.permutation(jax.random.fold_in(keys[2], 3), SEQUENCE_SLOTS * SLOT_LENGTH // SEQ_DEV)
    routes = jax.vmap(lambda own, number: shared_out(jax.random.fold_in(keys[2], 2), own, number, SEQ_DEV, EXPERTS, TOP, MOST, 1))(routes_keys, routes_turns).reshape((SEQUENCE_SLOTS, SLOT_LENGTH, TOP))
    gain_attn = jnp.clip(1.0 + 0.1 * jax.random.normal(keys[3], (MODEL_WIDTH,), jnp.float32), 0.5, 1.5).astype(jnp.bfloat16)
    w_query = normal_values(keys[4], (MODEL_WIDTH, QUERY_HEADS * HEAD_SIZE), MODEL_WIDTH ** -0.5, 0.15625, ((0, 32),))
    key_weight = normal_values(keys[5], (MODEL_WIDTH, KEY_VALUE_HEADS * HEAD_SIZE), MODEL_WIDTH ** -0.5, 0.15625, ((0, 32),))
    value_weight = normal_values(keys[6], (MODEL_WIDTH, KEY_VALUE_HEADS * HEAD_SIZE), MODEL_WIDTH ** -0.5, 0.15625, ((0, 32),))
    w_out = normal_values(keys[7], (QUERY_HEADS * HEAD_SIZE, MODEL_WIDTH), (QUERY_HEADS * HEAD_SIZE // 64) ** -0.5, 1.25, ((0, 32),))
    gain_ffn = jnp.clip(1.0 + 0.1 * jax.random.normal(keys[8], (MODEL_WIDTH,), jnp.float32), 0.5, 1.5).astype(jnp.bfloat16)
    w_router = normal_values(keys[9], (MODEL_WIDTH, EXPERTS), (4 * MODEL_WIDTH) ** -0.5, 0.078125, ((0, 32),))
    w_gate = normal_values(keys[10], (EXPERTS, MODEL_WIDTH, FF), MODEL_WIDTH ** -0.5, 0.15625, ((0, 16),))
    w_up = normal_values(keys[11], (EXPERTS, MODEL_WIDTH, FF), MODEL_WIDTH ** -0.5, 0.15625, ((0, 16),))
    w_down = normal_values(keys[12], (EXPERTS, FF, MODEL_WIDTH), (FF // 8) ** -0.5, 0.75, ((0, 16),))
    cotangent = normal_values(keys[13], (SEQUENCE_SLOTS, SLOT_LENGTH, MODEL_WIDTH), 1.0, 6.0, ((0, 8), (1, 4)))
    return {"tokens": tokens, "lengths": lengths, "routes": routes, "gain_attn": gain_attn, "w_query": w_query, "key_weight": key_weight, "value_weight": value_weight, "w_out": w_out, "gain_ffn": gain_ffn, "w_router": w_router, "w_gate": w_gate, "w_up": w_up, "w_down": w_down, "cotangent": cotangent}


@jax.custom_vjp
def lower_precision(v):
    return lax.optimization_barrier(v.astype(jnp.bfloat16)).astype(jnp.float32)

@jax.custom_vjp
def lower_backward(v):
    return v

def low_keep(v):
    return (lower_precision(v), None)

def low_pass(kept, grad):
    return (grad,)

def back_keep(v):
    return (v, None)

def back_low(kept, grad):
    return (lower_precision(grad),)
lower_precision.defvjp(low_keep, low_pass)
lower_backward.defvjp(back_keep, back_low)
epsilon = 1e-05
floor_score = -1e+30

def rotation_tables(positions):
    half_size = HEAD_SIZE // 2
    exponent = jnp.arange(half_size, dtype=jnp.int32).astype(jnp.float32) * (2.0 / HEAD_SIZE)
    frequency = jnp.exp(-math.log(10000.0) * exponent)
    angles = positions.astype(jnp.float32)[:, None] * frequency[None, :]
    return (jnp.cos(angles)[:, None, :], jnp.sin(angles)[:, None, :])

def apply_rotation(values, cosine_table, sine_table):
    half_size = values.shape[-1] // 2
    first = values[..., :half_size]
    second = values[..., half_size:]
    return jnp.concatenate([first * cosine_table - second * sine_table, second * cosine_table + first * sine_table], axis=-1)

def route_tables(routes, experts, capacity):
    blocks = routes.shape[0]
    route_count = routes.shape[1] * routes.shape[2]
    flat_routes = routes.reshape(blocks, route_count).astype(jnp.int32)
    onehot = (flat_routes[..., None] == jnp.arange(experts, dtype=jnp.int32)).astype(jnp.int32)
    ranking = lax.optimization_barrier(jnp.sum((jnp.cumsum(onehot, axis=1) - 1) * onehot, axis=-1)).astype(jnp.int32)
    places = (flat_routes * capacity + ranking).astype(jnp.int32)
    block_ids = jnp.broadcast_to(jnp.arange(blocks, dtype=jnp.int32)[:, None], places.shape)
    route_ids = jnp.broadcast_to(jnp.arange(route_count, dtype=jnp.int32)[None, :], places.shape)
    slot_table = jnp.full((blocks, experts * capacity), route_count, jnp.int32).at[block_ids, places].set(route_ids)
    return (places, slot_table)

def reference(tokens, lengths, routes, gain_attn, w_query, key_weight, value_weight, w_out, gain_ffn, w_router, w_gate, w_up, w_down, cotangent):
    highest = lax.Precision.HIGHEST
    group_ratio = QUERY_HEADS // KEY_VALUE_HEADS
    places, slot_table = route_tables(routes.reshape(SEQUENCE_SLOTS * N_CONTEXT, SEQ_DEV, TOP), EXPERTS, MOST)
    places = places.reshape(SEQUENCE_SLOTS, N_CONTEXT, SEQ_DEV * TOP)
    slot_table = slot_table.reshape(SEQUENCE_SLOTS, N_CONTEXT, EXPERTS * MOST)
    positions = jnp.arange(SLOT_LENGTH, dtype=jnp.int32)
    valid = (positions[None, :] < lengths[:, None]).astype(jnp.float32)[..., None]
    cosine_table, sine_table = rotation_tables(positions)
    block_ids = jnp.arange(N_CONTEXT, dtype=jnp.int32)[:, None]

    def forward(inputs, gain_one, query_w, key_w, value_w, out_w, gain_two, router_w, gate_w, up_w, down_w):

        def attend_slot(items):
            query_scaled, key_s, value_s, length = items
            query_per_head = query_scaled.reshape(SLOT_LENGTH, KEY_VALUE_HEADS, group_ratio, HEAD_SIZE)
            scores = lower_backward(HEAD_SIZE ** (-0.5) * jnp.einsum('skrd,tkd->krst', query_per_head, key_s, precision=highest))
            allowed = (positions[None, :] <= positions[:, None]) & (positions[None, :] < length)
            scores = jnp.where(allowed, scores, floor_score)
            probs = lower_precision(jax.nn.softmax(scores, axis=-1))
            mixed_s = jnp.einsum('krst,tkd->skrd', probs, value_s, precision=highest)
            return mixed_s.reshape(SLOT_LENGTH, QUERY_HEADS * HEAD_SIZE)

        def expert_slot(items):
            rows_in, gates_in, table_in, places_in = items
            padded = jnp.concatenate([rows_in, jnp.zeros((N_CONTEXT, 1, MODEL_WIDTH), jnp.float32)], axis=1)
            sent = lower_backward(padded[block_ids, table_in // TOP]).reshape(N_CONTEXT, EXPERTS, MOST, MODEL_WIDTH)
            gate_pre = lower_backward(jnp.einsum('cemd,edf->cemf', sent, gate_w, precision=highest))
            up_pre = lower_backward(jnp.einsum('cemd,edf->cemf', sent, up_w, precision=highest))
            hidden_e = lower_backward(lower_precision(jax.nn.silu(gate_pre) * up_pre))
            expert_out = lower_backward(lower_precision(jnp.einsum('cemf,efd->cemd', hidden_e, down_w, precision=highest)))
            picked = expert_out.reshape(N_CONTEXT, EXPERTS * MOST, MODEL_WIDTH)[block_ids, places_in]
            weighted = gates_in[..., None] * picked
            return lax.optimization_barrier(jnp.sum(weighted.reshape(N_CONTEXT, SEQ_DEV, TOP, MODEL_WIDTH), axis=2))
        normed_one = inputs * lax.rsqrt(lax.optimization_barrier(jnp.mean(inputs * inputs, axis=-1, keepdims=True)) + epsilon)
        hidden_one = lower_precision(normed_one * gain_one)
        query_lin = lower_backward(jnp.einsum('abd,de->abe', hidden_one, query_w, precision=highest))
        key_linear = lower_backward(jnp.einsum('abd,de->abe', hidden_one, key_w, precision=highest))
        value_linear = jnp.einsum('abd,de->abe', hidden_one, value_w, precision=highest)
        query_rotated = lower_precision(apply_rotation(query_lin.reshape(SEQUENCE_SLOTS, SLOT_LENGTH, QUERY_HEADS, HEAD_SIZE), cosine_table, sine_table))
        key_rotated = lower_precision(apply_rotation(key_linear.reshape(SEQUENCE_SLOTS, SLOT_LENGTH, KEY_VALUE_HEADS, HEAD_SIZE), cosine_table, sine_table))
        value_lower = lower_backward(lower_precision(value_linear)).reshape(SEQUENCE_SLOTS, SLOT_LENGTH, KEY_VALUE_HEADS, HEAD_SIZE)
        mixed = lax.map(jax.checkpoint(attend_slot), (query_rotated, key_rotated, value_lower, lengths))
        mixed_low = lower_backward(lower_precision(mixed))
        attn_out = lower_backward(jnp.einsum('abe,ed->abd', mixed_low, out_w, precision=highest))
        resid = inputs + attn_out
        normed_two = resid * lax.rsqrt(lax.optimization_barrier(jnp.mean(resid * resid, axis=-1, keepdims=True)) + epsilon)
        hidden_two = lower_precision(normed_two * gain_two)
        logits = lower_backward(jnp.einsum('abd,de->abe', hidden_two, router_w, precision=highest))
        chosen = jnp.take_along_axis(logits, routes, axis=-1)
        gates = jax.nn.softmax(chosen, axis=-1)
        combined = lax.map(jax.checkpoint(expert_slot), (hidden_two.reshape(SEQUENCE_SLOTS, N_CONTEXT, SEQ_DEV, MODEL_WIDTH), gates.reshape(SEQUENCE_SLOTS, N_CONTEXT, SEQ_DEV * TOP), slot_table, places))
        combined = combined.reshape(SEQUENCE_SLOTS, SLOT_LENGTH, MODEL_WIDTH)
        return valid * (resid + combined)
    result, pullback = jax.vjp(forward, tokens.astype(jnp.float32), gain_attn.astype(jnp.float32), w_query.astype(jnp.float32), key_weight.astype(jnp.float32), value_weight.astype(jnp.float32), w_out.astype(jnp.float32), gain_ffn.astype(jnp.float32), w_router.astype(jnp.float32), w_gate.astype(jnp.float32), w_up.astype(jnp.float32), w_down.astype(jnp.float32))
    gradients = pullback(cotangent.astype(jnp.float32))
    return (result.astype(jnp.bfloat16), gradients[0], gradients[1], gradients[2], gradients[3], gradients[4], gradients[5], gradients[6], gradients[7], gradients[8], gradients[9], gradients[10])
```

```python
import math

import jax
import jax.numpy as jnp
from jax import lax
from jax.sharding import PartitionSpec as P

MODEL_WIDTH = 1536
QUERY_HEADS = 24
KEY_VALUE_HEADS = 8
HEAD_SIZE = 64
TOP = 8


epsilon = 1e-05
floor_score = -1e30


def rotation_tables(positions):
    half_size = HEAD_SIZE // 2
    exponent = jnp.arange(half_size, dtype=jnp.int32).astype(jnp.float32) * (2.0 / HEAD_SIZE)
    frequency = jnp.exp(-math.log(10000.0) * exponent)
    angles = positions.astype(jnp.float32)[:, None] * frequency[None, :]
    return (jnp.cos(angles)[:, None, :], jnp.sin(angles)[:, None, :])


def apply_rotation(values, cosine_table, sine_table):
    half_size = values.shape[-1] // 2
    first = values[..., :half_size]
    second = values[..., half_size:]
    return jnp.concatenate(
        [first * cosine_table - second * sine_table, second * cosine_table + first * sine_table],
        axis=-1,
    )


def inverse_rotation(gradient, cosine_table, sine_table):
    half_size = gradient.shape[-1] // 2
    first = gradient[..., :half_size]
    second = gradient[..., half_size:]
    return jnp.concatenate(
        [first * cosine_table + second * sine_table, second * cosine_table - first * sine_table],
        axis=-1,
    )


def norm_back(gradient, normed, inverse):
    return inverse * (gradient - normed * jnp.mean(gradient * normed, axis=-1, keepdims=True))


GROUP = ("context", "expert")
EVERY = ("dp", "context", "expert")


def experts_on_owner(hidden_all, final_all, routes_all, router_w, w_gate, w_up, w_down, capacity):
    single = jnp.float32
    bfloat = jnp.bfloat16
    local_exp = w_gate.shape[0]
    experts = router_w.shape[1]
    tokens_block = hidden_all.shape[1]
    first = (lax.axis_index("context") * lax.axis_size("expert") + lax.axis_index("expert")) * local_exp
    expert_ids = jnp.arange(experts, dtype=jnp.int32)
    routed = jnp.any(routes_all[..., None] == expert_ids, axis=2)
    logits = jnp.einsum("btd,de->bte", hidden_all, router_w, preferred_element_type=single)
    peak = jnp.max(jnp.where(routed, logits, floor_score), axis=-1, keepdims=True)
    raised = jnp.where(routed, jnp.exp(logits - peak), 0.0)
    gates = raised / jnp.sum(raised, axis=-1, keepdims=True)
    own_gates = lax.dynamic_slice_in_dim(gates, first, local_exp, axis=2)
    own_mask = lax.dynamic_slice_in_dim(routed.astype(single), first, local_exp, axis=2)
    token_ids = jnp.arange(tokens_block, dtype=jnp.int32)
    before = (token_ids[:, None] < token_ids[None, :]).astype(bfloat)
    rank = jnp.einsum("btj,ts->bjs", own_mask.astype(bfloat), before, preferred_element_type=single)
    slots = jnp.arange(capacity, dtype=jnp.int32).astype(single)
    own_mask = own_mask.swapaxes(1, 2)
    own_gates = own_gates.swapaxes(1, 2)
    picks = (rank[:, :, None, :] == slots[:, None]) & (own_mask[:, :, None, :] > 0.5)
    pick = picks.astype(bfloat)
    row_gates = jnp.sum(jnp.where(picks, own_gates[:, :, None, :], 0.0), axis=-1)
    received = jnp.einsum("bemt,btd->bemd", pick, hidden_all, preferred_element_type=single).astype(bfloat)
    row_final = jnp.einsum("bemt,btd->bemd", pick, final_all, preferred_element_type=single)
    gate_pre = jnp.einsum("bemd,edf->bemf", received, w_gate, preferred_element_type=single)
    up_pre = jnp.einsum("bemd,edf->bemf", received, w_up, preferred_element_type=single)
    sigmoid_gate = jax.nn.sigmoid(gate_pre)
    silu_gate = gate_pre * sigmoid_gate
    hidden_e = (silu_gate * up_pre).astype(bfloat)
    expert_out = jnp.einsum("bemf,efd->bemd", hidden_e, w_down, preferred_element_type=single).astype(bfloat)
    weighted = (pick.astype(single) * row_gates[..., None]).astype(bfloat)
    combined = jnp.einsum("bemt,bemd->btd", weighted, expert_out, preferred_element_type=single)
    row_score = jnp.sum(row_final * expert_out.astype(single), axis=-1)
    scores = jnp.sum(jnp.where(picks, row_score[..., None], 0.0), axis=2)
    grad_route = (row_gates[..., None] * row_final).astype(bfloat)
    grad_w_down = jnp.einsum("bemf,bemd->efd", hidden_e, grad_route, preferred_element_type=single)
    grad_hidden_e = (
        jnp.einsum("bemd,efd->bemf", grad_route, w_down, preferred_element_type=single)
        .astype(bfloat)
        .astype(single)
    )
    grad_gate_pre = (
        grad_hidden_e * up_pre * sigmoid_gate * (1.0 + gate_pre * (1.0 - sigmoid_gate))
    ).astype(bfloat)
    grad_up_pre = (grad_hidden_e * silu_gate).astype(bfloat)
    grad_w_gate = jnp.einsum("bemd,bemf->edf", received, grad_gate_pre, preferred_element_type=single)
    grad_w_up = jnp.einsum("bemd,bemf->edf", received, grad_up_pre, preferred_element_type=single)
    grad_rows = jnp.einsum("bemf,edf->bemd", grad_gate_pre, w_gate, preferred_element_type=single)
    grad_rows = (
        grad_rows + jnp.einsum("bemf,edf->bemd", grad_up_pre, w_up, preferred_element_type=single)
    ).astype(bfloat)
    grad_hidden = jnp.einsum("bemt,bemd->btd", pick, grad_rows, preferred_element_type=single)
    return combined, grad_hidden, scores, grad_w_gate, grad_w_up, grad_w_down


def on_device(
    tokens,
    lengths,
    routes,
    gain_attn,
    w_query,
    key_weight,
    value_weight,
    w_out,
    gain_ffn,
    w_router,
    w_gate,
    w_up,
    w_down,
    cotangent,
):
    query_groups = tokens.shape[0]
    sequence_per_device = tokens.shape[1]
    ctx_count = lax.axis_size("context")
    exp_count = lax.axis_size("expert")
    local_exp = w_gate.shape[0]
    experts = local_exp * ctx_count * exp_count
    capacity = sequence_per_device * TOP * 3 // (2 * experts)
    sequence_total = sequence_per_device * ctx_count
    group_ratio = QUERY_HEADS // KEY_VALUE_HEADS
    scale = HEAD_SIZE ** (-0.5)
    bfloat = jnp.bfloat16
    single = jnp.float32
    small = jnp.concatenate([w_router, gain_attn[:, None], gain_ffn[:, None]], axis=1)
    early = jnp.concatenate([w_query, key_weight, value_weight, small], axis=1)
    early = lax.all_gather(early, EVERY, axis=0, tiled=True)
    out_w = lax.all_gather(w_out, EVERY, axis=0, tiled=True)
    query_w = early[:, : w_query.shape[1]]
    key_w = early[:, w_query.shape[1] : w_query.shape[1] + key_weight.shape[1]]
    value_w = early[:, w_query.shape[1] + key_weight.shape[1] : -small.shape[1]]
    router_w = early[:, -small.shape[1] : -2]
    gain_one = early[:, -2]
    gain_two = early[:, -1]
    gain_one = gain_one.astype(single)
    gain_two = gain_two.astype(single)
    positions = lax.axis_index("context") * sequence_per_device + jnp.arange(
        sequence_per_device, dtype=jnp.int32
    )
    key_pos = jnp.arange(sequence_total, dtype=jnp.int32)
    valid = (positions[None, :] < lengths[:, None]).astype(single)[..., None]
    cosine_table, sine_table = rotation_tables(positions)
    inputs = tokens.astype(single)
    inverse_one = lax.rsqrt(jnp.mean(inputs * inputs, axis=-1, keepdims=True) + epsilon)
    normed_one = inputs * inverse_one
    hidden_one = (normed_one * gain_one).astype(bfloat)
    query_lin = jnp.einsum("gsd,de->gse", hidden_one, query_w, preferred_element_type=single)
    key_linear = jnp.einsum("gsd,de->gse", hidden_one, key_w, preferred_element_type=single)
    value_lower = jnp.einsum(
        "gsd,de->gse", hidden_one, value_w, preferred_element_type=single
    ).astype(bfloat)
    query_rotated = (
        apply_rotation(
            query_lin.reshape(query_groups, sequence_per_device, QUERY_HEADS, HEAD_SIZE),
            cosine_table,
            sine_table,
        )
        .astype(bfloat)
        .reshape(query_groups, sequence_per_device, QUERY_HEADS * HEAD_SIZE)
    )
    key_rotated = (
        apply_rotation(
            key_linear.reshape(query_groups, sequence_per_device, KEY_VALUE_HEADS, HEAD_SIZE),
            cosine_table,
            sine_table,
        )
        .astype(bfloat)
        .reshape(query_groups, sequence_per_device, KEY_VALUE_HEADS * HEAD_SIZE)
    )
    gathered_keys, gathered_values = (
        lax.all_gather(key_rotated, "context", axis=1, tiled=True),
        lax.all_gather(value_lower, "context", axis=1, tiled=True),
    )

    def attn_scores(slot_index):
        query_per_head = query_rotated[slot_index].reshape(
            sequence_per_device, KEY_VALUE_HEADS, group_ratio, HEAD_SIZE
        )
        key_per_head = gathered_keys[slot_index].reshape(sequence_total, KEY_VALUE_HEADS, HEAD_SIZE)
        scores = scale * jnp.einsum(
            "skrd,tkd->krst", query_per_head, key_per_head, preferred_element_type=single
        )
        allowed = (key_pos[None, :] <= positions[:, None]) & (
            key_pos[None, :] < lengths[slot_index]
        )
        return (jnp.where(allowed, scores, floor_score), allowed, query_per_head, key_per_head)

    slot_index = 0
    scores, allowed, query_per_head, key_per_head = attn_scores(slot_index)
    peak = jnp.max(scores, axis=-1, keepdims=True)
    raised = jnp.exp(scores - peak)
    total = jnp.sum(raised, axis=-1, keepdims=True)
    probs = raised / total
    value_per_head = gathered_values[slot_index].reshape(sequence_total, KEY_VALUE_HEADS, HEAD_SIZE)
    mixed_g = jnp.einsum(
        "krst,tkd->skrd", probs.astype(bfloat), value_per_head, preferred_element_type=single
    )
    mixed_list = [mixed_g.reshape(sequence_per_device, QUERY_HEADS * HEAD_SIZE)]
    lse_list = [peak + jnp.log(total)]
    mixed_low = jnp.stack(mixed_list).astype(bfloat)
    resid = inputs + jnp.einsum("gse,ed->gsd", mixed_low, out_w, preferred_element_type=single)
    inverse_two = lax.rsqrt(jnp.mean(resid * resid, axis=-1, keepdims=True) + epsilon)
    normed_two = resid * inverse_two
    hidden_two = (normed_two * gain_two).astype(bfloat)
    logits = jnp.einsum("gsd,de->gse", hidden_two, router_w, preferred_element_type=single)
    matches = routes[..., None] == jnp.arange(experts, dtype=jnp.int32)
    chosen = jnp.sum(jnp.where(matches, logits[:, :, None, :], 0.0), axis=-1)
    gates = jax.nn.softmax(chosen, axis=-1)
    final_low = (cotangent.astype(single) * valid).astype(bfloat)
    final_all = lax.all_gather(final_low[0], GROUP, axis=0, tiled=False)
    routes_all = lax.all_gather(routes[0], GROUP, axis=0, tiled=False)
    hidden_all = lax.all_gather(hidden_two[0], GROUP, axis=0, tiled=False)
    combined, grad_hidden, scores, grad_w_gate, grad_w_up, grad_w_down = experts_on_owner(
        hidden_all, final_all, routes_all, router_w, w_gate, w_up, w_down, capacity
    )
    combined = lax.psum_scatter(combined.astype(bfloat), GROUP, scatter_dimension=0, tiled=False)
    grad_hidden = lax.psum_scatter(grad_hidden.astype(bfloat), GROUP, scatter_dimension=0, tiled=False)
    scores = lax.all_to_all(scores, GROUP, split_axis=0, concat_axis=0, tiled=True)
    scores = scores.reshape(experts, sequence_per_device)
    block_out = (valid * (resid + combined.astype(single)[None])).astype(bfloat)
    grad_final = cotangent.astype(single) * valid
    grad_gates = jnp.sum(jnp.where(matches, scores.T[None, :, None, :], 0.0), axis=-1)
    gate_mean = jnp.sum(gates * grad_gates, axis=-1, keepdims=True)
    grad_chosen = gates * (grad_gates - gate_mean)
    grad_logits = jnp.sum(jnp.where(matches, grad_chosen[..., None], 0.0), axis=2).astype(bfloat)
    grad_w_router = jnp.einsum(
        "gsd,gse->de", hidden_two, grad_logits, preferred_element_type=single
    )
    grad_hidden_two = grad_hidden.astype(single)[None]
    grad_hidden_two = grad_hidden_two + jnp.einsum(
        "gse,de->gsd", grad_logits, router_w, preferred_element_type=single
    )
    grad_gain_ffn = jnp.sum(grad_hidden_two * normed_two, axis=(0, 1))
    grad_resid = norm_back(grad_hidden_two * gain_two, normed_two, inverse_two) + grad_final
    grad_attn = grad_resid.astype(bfloat)
    grad_w_out = jnp.einsum("gse,gsd->ed", mixed_low, grad_attn, preferred_element_type=single)
    mixed_gradient = jnp.einsum(
        "gsd,ed->gse", grad_attn, out_w, preferred_element_type=single
    ).astype(bfloat)
    slot_index = 0
    scores, allowed, query_per_head, key_per_head = attn_scores(slot_index)
    probs = jnp.where(allowed, jnp.exp(scores - lse_list[slot_index]), 0.0)
    value_per_head = gathered_values[slot_index].reshape(sequence_total, KEY_VALUE_HEADS, HEAD_SIZE)
    head_gradient = mixed_gradient[slot_index].reshape(
        sequence_per_device, KEY_VALUE_HEADS, group_ratio, HEAD_SIZE
    )
    grad_probs = jnp.einsum(
        "skrd,tkd->krst", head_gradient, value_per_head, preferred_element_type=single
    )
    row_delta = jnp.sum(probs * grad_probs, axis=-1, keepdims=True)
    grad_scores = (probs * (grad_probs - row_delta)).astype(bfloat)
    grad_queries = [
        (
            scale
            * jnp.einsum("krst,tkd->skrd", grad_scores, key_per_head, preferred_element_type=single)
        ).reshape(sequence_per_device, QUERY_HEADS, HEAD_SIZE)
    ]
    grad_keys = [
        (
            scale
            * jnp.einsum(
                "krst,skrd->tkd", grad_scores, query_per_head, preferred_element_type=single
            )
        ).reshape(sequence_total, KEY_VALUE_HEADS * HEAD_SIZE)
    ]
    grad_values = [
        jnp.einsum(
            "krst,skrd->tkd", probs.astype(bfloat), head_gradient, preferred_element_type=single
        ).reshape(sequence_total, KEY_VALUE_HEADS * HEAD_SIZE)
    ]
    key_gradient_rows, value_grad = (
        lax.psum_scatter(
            jnp.stack(grad_keys).astype(jnp.bfloat16), "context", scatter_dimension=1, tiled=True
        ).astype(jnp.float32),
        lax.psum_scatter(
            jnp.stack(grad_values).astype(jnp.bfloat16), "context", scatter_dimension=1, tiled=True
        ).astype(jnp.float32),
    )
    grad_query_lin = (
        inverse_rotation(jnp.stack(grad_queries), cosine_table, sine_table)
        .astype(bfloat)
        .reshape(query_groups, sequence_per_device, QUERY_HEADS * HEAD_SIZE)
    )
    grad_key_lin = (
        inverse_rotation(
            key_gradient_rows.reshape(
                query_groups, sequence_per_device, KEY_VALUE_HEADS, HEAD_SIZE
            ),
            cosine_table,
            sine_table,
        )
        .astype(bfloat)
        .reshape(query_groups, sequence_per_device, KEY_VALUE_HEADS * HEAD_SIZE)
    )
    grad_value_low = value_grad.astype(bfloat)
    grad_w_query = jnp.einsum(
        "gsd,gse->de", hidden_one, grad_query_lin, preferred_element_type=single
    )
    grad_w_key = jnp.einsum("gsd,gse->de", hidden_one, grad_key_lin, preferred_element_type=single)
    grad_w_value = jnp.einsum(
        "gsd,gse->de", hidden_one, grad_value_low, preferred_element_type=single
    )
    grad_hidden_one = jnp.einsum(
        "gse,de->gsd", grad_query_lin, query_w, preferred_element_type=single
    )
    grad_hidden_one = grad_hidden_one + jnp.einsum(
        "gse,de->gsd", grad_key_lin, key_w, preferred_element_type=single
    )
    grad_hidden_one = grad_hidden_one + jnp.einsum(
        "gse,de->gsd", grad_value_low, value_w, preferred_element_type=single
    )
    grad_gain_attn = jnp.sum(grad_hidden_one * normed_one, axis=(0, 1))
    grad_tokens = norm_back(grad_hidden_one * gain_one, normed_one, inverse_one) + grad_resid
    late = jnp.concatenate(
        [
            grad_w_query,
            grad_w_key,
            grad_w_value,
            grad_w_router,
            grad_gain_attn[:, None],
            grad_gain_ffn[:, None],
        ],
        axis=1,
    ).astype(bfloat)
    late = lax.psum_scatter(late, EVERY, scatter_dimension=0, tiled=True).astype(single)
    out_grad = lax.psum_scatter(
        grad_w_out.astype(bfloat), EVERY, scatter_dimension=0, tiled=True
    ).astype(single)
    width = grad_w_query.shape[1]
    narrow = grad_w_key.shape[1]
    shard_grads = (
        late[:, -2],
        late[:, :width],
        late[:, width : width + narrow],
        late[:, width + narrow : width + 2 * narrow],
        out_grad,
        late[:, -1],
        late[:, width + 2 * narrow : -2],
    )
    expert_sums = (
        lax.psum_scatter(
            grad_w_gate.astype(jnp.bfloat16), "dp", scatter_dimension=1, tiled=True
        ).astype(jnp.float32),
        lax.psum_scatter(
            grad_w_up.astype(jnp.bfloat16), "dp", scatter_dimension=1, tiled=True
        ).astype(jnp.float32),
        lax.psum_scatter(
            grad_w_down.astype(jnp.bfloat16), "dp", scatter_dimension=1, tiled=True
        ).astype(jnp.float32),
    )
    return (
        block_out,
        grad_tokens,
        shard_grads[0],
        shard_grads[1],
        shard_grads[2],
        shard_grads[3],
        shard_grads[4],
        shard_grads[5],
        shard_grads[6],
        expert_sums[0],
        expert_sums[1],
        expert_sums[2],
    )


def solution(mesh):
    in_specs = (
        P(("dp", "expert"), "context", None),
        P(("dp", "expert")),
        P(("dp", "expert"), "context", None),
        P(("dp", "context", "expert")),
        P(("dp", "context", "expert"), None),
        P(("dp", "context", "expert"), None),
        P(("dp", "context", "expert"), None),
        P(("dp", "context", "expert"), None),
        P(("dp", "context", "expert")),
        P(("dp", "context", "expert"), None),
        P(("context", "expert"), None, None),
        P(("context", "expert"), None, None),
        P(("context", "expert"), None, None),
        P(("dp", "expert"), "context", None),
    )
    out_specs = (
        P(("dp", "expert"), "context", None),
        P(("dp", "expert"), "context", None),
        P(("dp", "context", "expert")),
        P(("dp", "context", "expert"), None),
        P(("dp", "context", "expert"), None),
        P(("dp", "context", "expert"), None),
        P(("dp", "context", "expert"), None),
        P(("dp", "context", "expert")),
        P(("dp", "context", "expert"), None),
        P(("context", "expert"), "dp", None),
        P(("context", "expert"), "dp", None),
        P(("context", "expert"), "dp", None),
    )
    return jax.shard_map(
        on_device, mesh=mesh, in_specs=in_specs, out_specs=out_specs, check_vma=False
    )
```

```python
import math

import jax
import jax.numpy as jnp
from jax import lax
from jax.experimental import pallas as pl
from jax.experimental.pallas import tpu as pltpu
from jax.sharding import PartitionSpec as P

MODEL_WIDTH = 1536
QUERY_HEADS = 24
KEY_VALUE_HEADS = 8
HEAD_SIZE = 64
TOP = 8


epsilon = 1e-05
floor_score = -1e30


def rotation_tables(positions):
    half_size = HEAD_SIZE // 2
    exponent = jnp.arange(half_size, dtype=jnp.int32).astype(jnp.float32) * (2.0 / HEAD_SIZE)
    frequency = jnp.exp(-math.log(10000.0) * exponent)
    angles = positions.astype(jnp.float32)[:, None] * frequency[None, :]
    return (jnp.cos(angles)[:, None, :], jnp.sin(angles)[:, None, :])


def apply_rotation(values, cosine_table, sine_table):
    half_size = values.shape[-1] // 2
    first = values[..., :half_size]
    second = values[..., half_size:]
    return jnp.concatenate(
        [first * cosine_table - second * sine_table, second * cosine_table + first * sine_table],
        axis=-1,
    )


def inverse_rotation(gradient, cosine_table, sine_table):
    half_size = gradient.shape[-1] // 2
    first = gradient[..., :half_size]
    second = gradient[..., half_size:]
    return jnp.concatenate(
        [first * cosine_table + second * sine_table, second * cosine_table - first * sine_table],
        axis=-1,
    )


def norm_back(gradient, normed, inverse):
    return inverse * (gradient - normed * jnp.mean(gradient * normed, axis=-1, keepdims=True))


GROUP = ("context", "expert")
EVERY = ("dp", "context", "expert")


MESH_ID = pl.DeviceIdType.MESH
CHUNK = 512
HALF = 256


def contract_rows(left, right):
    return lax.dot_general(left, right, (((0,), (0,)), ((), ())), preferred_element_type=jnp.float32)


def contract_last(left, right):
    return lax.dot_general(left, right, (((1,), (1,)), ((), ())), preferred_element_type=jnp.float32)


def matmul(left, right):
    return jnp.dot(left, right, preferred_element_type=jnp.float32)


def line_order(z, step):
    half = z // 2
    inner = z + half * (3 - 2 * z)
    base = step + inner * (1 - 2 * step) * (1 - step // 2)
    return base + half * (3 - 2 * base)


def experts_kernel(
    hidden_ref,
    final_ref,
    routes_ref,
    router_ref,
    gate_hbm,
    up_hbm,
    down_hbm,
    back_ref,
    part_ref,
    score_ref,
    grad_gate_ref,
    grad_up_ref,
    grad_down_ref,
    held,
    w_gate,
    w_up,
    w_down,
    rows_in,
    rows_grad,
    slope_gate,
    slope_up,
    hidden_e,
    picks,
    row_gates,
    work,
    pool,
    before,
    gather_send,
    gather_recv,
    local_sem,
    load_sem,
    part_sem,
    sum_send,
    core_recv,
    y_recv,
    z_recv,
    ready,
):
    single = jnp.float32
    bfloat = jnp.bfloat16
    tokens_block = hidden_ref.shape[0]
    width = hidden_ref.shape[1]
    experts = router_ref.shape[0]
    local_exp = w_gate.shape[0]
    hidden_units = w_gate.shape[2]
    capacity = picks.shape[1] // local_exp
    group_rows = 4 * capacity
    ctx = lax.axis_index("context")
    z = lax.axis_index("expert")
    y = ctx // 2
    c = ctx % 2
    inner = z + (z // 2) * (3 - 2 * z)
    UP, DOWN, ACROSS, CORE = 0, 1, 2, 3

    def device(kind):
        if kind == UP:
            return {"context": ctx, "expert": z + 1}
        if kind == DOWN:
            return {"context": ctx, "expert": z - 1}
        if kind == ACROSS:
            return {"context": (1 - y) * 2 + c, "expert": z}
        return {"context": y * 2 + 1 - c, "expert": z}

    def block_id(yy, cc, zz):
        return (yy * 2 + cc) * 4 + zz

    def per_side(action):
        @pl.when(z < 3)
        def _():
            action(UP)

        @pl.when(z > 0)
        def _():
            action(DOWN)

        action(ACROSS)
        action(CORE)

    weights = (
        pltpu.make_async_copy(gate_hbm, w_gate, load_sem.at[0]),
        pltpu.make_async_copy(up_hbm, w_up, load_sem.at[1]),
        pltpu.make_async_copy(down_hbm, w_down, load_sem.at[2]),
    )
    mine = block_id(y, c, z)
    own = pltpu.make_async_copy(hidden_ref, held.at[mine], local_sem)
    own.start()
    for copy in weights:
        copy.start()

    barrier = pltpu.get_barrier_semaphore()
    per_side(
        lambda kind: pl.semaphore_signal(
            barrier, inc=1, device_id=device(kind), device_id_type=MESH_ID
        )
    )
    pl.semaphore_wait(barrier, 3 + inner)
    own.wait()

    def spread(kind, block):
        return pltpu.make_async_remote_copy(
            src_ref=held.at[block],
            dst_ref=held.at[block],
            send_sem=gather_send.at[kind, block],
            recv_sem=gather_recv.at[block],
            device_id=device(kind),
            device_id_type=MESH_ID,
        )

    def along(kind, zz):
        if kind == UP:
            return jnp.logical_and(z < 3, zz <= z)
        return jnp.logical_and(z > 0, zz >= z)

    def send_on(zz):
        block = block_id(y, c, zz)
        for kind in (UP, DOWN):

            @pl.when(along(kind, zz))
            def _():
                spread(kind, block).start()

        spread(ACROSS, block).start()
        spread(CORE, block).start()

    def forward(step):
        zz = line_order(z, step)
        spread(ACROSS, block_id(y, c, zz)).wait_recv()
        send_on(zz)

    send_on(z)
    row = lax.broadcasted_iota(jnp.int32, (tokens_block, tokens_block), 0)
    column = lax.broadcasted_iota(jnp.int32, (tokens_block, tokens_block), 1)
    before[...] = jnp.where(row < column, 1.0, 0.0).astype(bfloat)
    for copy in weights:
        copy.wait()
    first = (ctx * 4 + z) * local_exp

    def member(zz, p):
        yy = y + (p // 2) * (1 - 2 * y)
        cc = c + (p % 2) * (1 - 2 * c)
        return block_id(yy, cc, zz)

    def load_final(zz, p):
        return pltpu.make_async_copy(final_ref.at[member(zz, p)], pool.at[p], load_sem.at[p])

    def store_part(zz, p):
        return pltpu.make_async_copy(pool.at[4 + p], part_ref.at[member(zz, p)], part_sem.at[p])

    def forward_group(step, carry):
        zz = line_order(z, step)
        after = step + 1 + inner * jnp.minimum(step, 1)

        @pl.when(after < 4)
        def _():
            forward(after)

        @pl.when(jnp.logical_and(step == 0, inner == 1))
        def _():
            forward(2)

        @pl.loop(0, 4)
        def _(p):
            load_final(zz, p).start()

        spread(CORE, block_id(y, 1 - c, zz)).wait_recv()
        spread(CORE, block_id(1 - y, c, zz)).wait_recv()
        spread(CORE, block_id(1 - y, c, zz)).start()
        spread(CORE, block_id(1 - y, 1 - c, zz)).wait_recv()

        @pl.loop(0, 4)
        def _(p):
            block = member(zz, p)
            tokens_in = held[block]
            logits = contract_last(router_ref[...], tokens_in)
            expert_row = lax.broadcasted_iota(jnp.int32, (experts, tokens_block), 0)
            routed = jnp.zeros((experts, tokens_block), single)
            for k in range(routes_ref.shape[1]):
                routed = routed + jnp.where(routes_ref[block, k : k + 1, :] == expert_row, 1.0, 0.0)
            named = routed > 0.5
            peak = jnp.max(jnp.where(named, logits, floor_score), axis=0, keepdims=True)
            raised = jnp.where(named, jnp.exp(jnp.minimum(logits - peak, 0.0)), 0.0)
            gates = raised / jnp.sum(raised, axis=0, keepdims=True)
            eight = lax.broadcasted_iota(jnp.int32, (8, tokens_block), 0)
            masks = jnp.zeros((8, tokens_block), single)
            own_mask = []
            own_gate = []
            for j in range(local_exp):
                here = expert_row == first + j
                own_mask.append(jnp.sum(jnp.where(here, routed, 0.0), axis=0, keepdims=True))
                own_gate.append(jnp.sum(jnp.where(here, gates, 0.0), axis=0, keepdims=True))
                masks = masks + jnp.where(eight == j, own_mask[j], 0.0)
            rank = matmul(masks.astype(bfloat), before[...])
            slot = lax.broadcasted_iota(jnp.int32, (capacity, tokens_block), 0).astype(single)
            for j in range(local_exp):
                hit = jnp.logical_and(slot == rank[j : j + 1, :], own_mask[j] > 0.5)
                pick = jnp.where(hit, 1.0, 0.0)
                picks[step * 4 + p, pl.ds(j * capacity, capacity), :] = pick.astype(bfloat)
                gate_column = jnp.sum(pick * own_gate[j], axis=1, keepdims=True)
                row_gates[p, pl.ds(j * capacity, capacity), :] = jnp.broadcast_to(
                    gate_column, (capacity, 128)
                )
            at = pl.multiple_of(step * group_rows + p * capacity, 32)
            for n in range(width // CHUNK):
                part = pl.ds(n * CHUNK, CHUNK)
                got = matmul(picks[step * 4 + p], held[block, :, part]).astype(bfloat)
                for j in range(local_exp):
                    rows_in[j, pl.ds(at, capacity), part] = got[j * capacity : (j + 1) * capacity]

        base = pl.multiple_of(step * group_rows, 128)
        for j in range(local_exp):
            given = rows_in[j, pl.ds(base, group_rows), :]
            for n in range(hidden_units // HALF):
                part = pl.ds(n * HALF, HALF)
                gate_pre = matmul(given, w_gate[j, :, part])
                up_pre = matmul(given, w_up[j, :, part])
                sigmoid = 1.0 / (1.0 + jnp.exp(-gate_pre))
                silu = gate_pre * sigmoid
                hidden_e[j, pl.ds(base, group_rows), part] = (silu * up_pre).astype(bfloat)
                slope_gate[j, pl.ds(base, group_rows), part] = (
                    up_pre * sigmoid * (1.0 + gate_pre * (1.0 - sigmoid))
                ).astype(bfloat)
                slope_up[j, pl.ds(base, group_rows), part] = silu.astype(bfloat)
            for n in range(width // CHUNK):
                part = pl.ds(n * CHUNK, CHUNK)
                work[j, :, part] = matmul(
                    hidden_e[j, pl.ds(base, group_rows), :], w_down[j, :, part]
                ).astype(bfloat)

        @pl.loop(0, 4)
        def _(p):
            block = member(zz, p)
            at = pl.multiple_of(step * group_rows + p * capacity, 32)
            local = pl.multiple_of(p * capacity, 32)
            pick = picks[step * 4 + p]
            weight = row_gates[p][:, 0:1]
            weighted = (pick.astype(single) * weight).astype(bfloat)
            load_final(zz, p).wait()

            @pl.when(step > 0)
            def _():
                store_part(zz, p).wait()

            row_score = jnp.zeros((local_exp * capacity, 1), single)
            for n in range(width // CHUNK):
                part = pl.ds(n * CHUNK, CHUNK)
                out = jnp.concatenate(
                    [work[j, pl.ds(local, capacity), part] for j in range(local_exp)], axis=0
                )
                pool[4 + p, :, part] = contract_rows(weighted, out).astype(bfloat)
                final = matmul(pick, pool[p, :, part])
                row_score = row_score + jnp.sum(final * out.astype(single), axis=1, keepdims=True)
                graded = (final * weight).astype(bfloat)
                for j in range(local_exp):
                    rows_grad[j, pl.ds(at, capacity), part] = graded[j * capacity : (j + 1) * capacity]
            store_part(zz, p).start()
            spread_score = pick.astype(single) * row_score
            eight = lax.broadcasted_iota(jnp.int32, (8, tokens_block), 0)
            scores = jnp.zeros((8, tokens_block), single)
            for j in range(local_exp):
                total = jnp.sum(spread_score[j * capacity : (j + 1) * capacity], axis=0, keepdims=True)
                scores = scores + jnp.where(eight == j, total, 0.0)
            score_ref[block] = scores

        return carry

    lax.fori_loop(0, 4, forward_group, 0)

    @pl.loop(0, 4)
    def _(p):
        store_part(line_order(z, 3), p).wait()

    @pl.loop(0, 4)
    def _(zz):
        block = block_id(y, c, zz)
        for kind in (UP, DOWN):

            @pl.when(along(kind, zz))
            def _():
                spread(kind, block).wait_send()

        spread(ACROSS, block).wait_send()
        spread(CORE, block).wait_send()
        spread(CORE, block_id(1 - y, c, zz)).wait_send()

    opposite = {UP: DOWN, DOWN: UP, ACROSS: ACROSS, CORE: CORE}
    per_side(
        lambda kind: pl.semaphore_signal(
            ready.at[opposite[kind]], inc=1, device_id=device(kind), device_id_type=MESH_ID
        )
    )
    per_side(lambda kind: pl.semaphore_wait(ready.at[kind], 1))

    def to_core(p, zz):
        yy = y + p * (1 - 2 * y)
        return pltpu.make_async_remote_copy(
            src_ref=pool.at[p],
            dst_ref=held.at[yy * 4 + zz],
            send_sem=sum_send.at[p],
            recv_sem=core_recv.at[yy * 4 + zz],
            device_id=device(CORE),
            device_id_type=MESH_ID,
        )

    def from_core(slot):
        return pltpu.make_async_remote_copy(
            src_ref=pool.at[0],
            dst_ref=held.at[slot],
            send_sem=sum_send.at[0],
            recv_sem=core_recv.at[slot],
            device_id=device(CORE),
            device_id_type=MESH_ID,
        )

    def to_across(turn, zz):
        return pltpu.make_async_remote_copy(
            src_ref=pool.at[2 + turn],
            dst_ref=held.at[8 + zz],
            send_sem=sum_send.at[2 + turn],
            recv_sem=y_recv.at[zz],
            device_id=device(ACROSS),
            device_id_type=MESH_ID,
        )

    def to_line(kind, turn, zz, last):
        return pltpu.make_async_remote_copy(
            src_ref=pool.at[4 + turn],
            dst_ref=pool.at[7] if last else held.at[12 + zz],
            send_sem=sum_send.at[4 + turn],
            recv_sem=z_recv.at[4 if last else zz],
            device_id=device(kind),
            device_id_type=MESH_ID,
        )

    def summed(*refs):
        total = refs[0].astype(single)
        for value in refs[1:]:
            total = total + value.astype(single)
        return total.astype(bfloat)

    def back_block(step, p, target):
        local = pl.multiple_of(p * capacity, 32)
        pick = picks[step * 4 + p]
        for n in range(width // CHUNK):
            part = pl.ds(n * CHUNK, CHUNK)
            grads = jnp.concatenate(
                [work[j, pl.ds(local, capacity), part] for j in range(local_exp)], axis=0
            )
            pool[target, :, part] = contract_rows(pick, grads).astype(bfloat)

    def line_sum(step):
        zz = line_order(z, step)
        turn = step % 2
        core_slot = y * 4 + zz
        to_across(turn, zz).wait_recv()
        rising = zz > z

        def finish(comes):
            @pl.when(comes)
            def _():
                to_line(CORE, turn, zz, False).wait_recv()
                pool[4 + turn] = summed(
                    pool[4 + turn], held[core_slot], held[8 + zz], held[12 + zz]
                )

            @pl.when(jnp.logical_not(comes))
            def _():
                pool[4 + turn] = summed(pool[4 + turn], held[core_slot], held[8 + zz])

        @pl.when(rising)
        def _():
            finish(z > 0)
            to_line(UP, turn, zz, False).start()

        @pl.when(jnp.logical_not(rising))
        def _():
            finish(z < 3)

            @pl.when(zz == z - 1)
            def _():
                to_line(DOWN, turn, zz, True).start()

            @pl.when(zz < z - 1)
            def _():
                to_line(DOWN, turn, zz, False).start()

    def backward_group(turn_step, carry):
        step = 3 - turn_step
        zz = line_order(z, step)
        turn = step % 2
        base = pl.multiple_of(step * group_rows, 128)
        for j in range(local_exp):
            for n in range(hidden_units // HALF):
                part = pl.ds(n * HALF, HALF)
                grad_hidden = (
                    contract_last(rows_grad[j, pl.ds(base, group_rows), :], w_down[j, part, :])
                    .astype(bfloat)
                    .astype(single)
                )
                slope_gate[j, pl.ds(base, group_rows), part] = (
                    grad_hidden * slope_gate[j, pl.ds(base, group_rows), part].astype(single)
                ).astype(bfloat)
                slope_up[j, pl.ds(base, group_rows), part] = (
                    grad_hidden * slope_up[j, pl.ds(base, group_rows), part].astype(single)
                ).astype(bfloat)
            for n in range(width // CHUNK):
                part = pl.ds(n * CHUNK, CHUNK)
                work[j, :, part] = (
                    contract_last(slope_gate[j, pl.ds(base, group_rows), :], w_gate[j, part, :])
                    + contract_last(slope_up[j, pl.ds(base, group_rows), :], w_up[j, part, :])
                ).astype(bfloat)
        for p, member_p in ((0, 1), (1, 3)):

            @pl.when(turn_step > 0)
            def _():
                to_core(p, zz).wait_send()

            back_block(step, member_p, p)
            to_core(p, zz).start()

        @pl.when(turn_step > 1)
        def _():
            to_across(turn, zz).wait_send()
            to_line(CORE, turn, zz, False).wait_send()

        back_block(step, 2, 2 + turn)
        other = (1 - y) * 4 + zz
        from_core(other).wait_recv()
        pool[2 + turn] = summed(pool[2 + turn], held[other])
        to_across(turn, zz).start()
        back_block(step, 0, 4 + turn)
        from_core(y * 4 + zz).wait_recv()

        @pl.when(jnp.logical_and(turn_step > 0, turn_step < 3))
        def _():
            line_sum(step + 1)

        return carry

    lax.fori_loop(0, 4, backward_group, 0)

    def stores(j):
        return (
            pltpu.make_async_copy(w_gate.at[j], grad_gate_ref.at[j], load_sem.at[3 * j]),
            pltpu.make_async_copy(w_up.at[j], grad_up_ref.at[j], load_sem.at[3 * j + 1]),
            pltpu.make_async_copy(w_down.at[j], grad_down_ref.at[j], load_sem.at[3 * j + 2]),
        )

    def weight_grads(j):
        @pl.loop(0, width // CHUNK)
        def _(n):
            part = pl.ds(pl.multiple_of(n * CHUNK, CHUNK), CHUNK)
            w_gate[j, part, :] = contract_rows(rows_in[j, :, part], slope_gate[j]).astype(bfloat)
            w_up[j, part, :] = contract_rows(rows_in[j, :, part], slope_up[j]).astype(bfloat)
            w_down[j, :, part] = contract_rows(hidden_e[j], rows_grad[j, :, part]).astype(bfloat)

        for copy in stores(j):
            copy.start()

    weight_grads(0)
    line_sum(1)
    weight_grads(1)
    to_across(0, z).wait_recv()
    pool[4] = summed(pool[4], held[y * 4 + z], held[8 + z])

    @pl.when(z > 0)
    def _():
        to_line(CORE, 0, z, False).wait_recv()
        pool[4] = summed(pool[4], held[12 + z])

    @pl.when(z < 3)
    def _():
        to_line(CORE, 0, z, True).wait_recv()
        pool[4] = summed(pool[4], pool[7])

    result = pltpu.make_async_copy(pool.at[4], back_ref, local_sem)
    result.start()
    for j in range(local_exp):
        for copy in stores(j):
            copy.wait()
    for p in range(2):
        to_core(p, z).wait_send()
        to_across(p, z).wait_send()
    to_line(CORE, 1, z, False).wait_send()
    result.wait()


def experts_on_owner(hidden, final_all, routes_all, router_rows, w_gate, w_up, w_down, capacity):
    blocks = final_all.shape[0]
    tokens_block, width = hidden.shape
    local_exp, _, units = w_gate.shape
    bfloat = jnp.bfloat16
    single = jnp.float32
    rows = blocks * capacity
    anywhere = pl.BlockSpec(memory_space=pl.ANY)
    vmem = pl.BlockSpec(memory_space=pltpu.VMEM)
    dma = pltpu.SemaphoreType.DMA
    return pl.pallas_call(
        experts_kernel,
        out_shape=(
            jax.ShapeDtypeStruct((tokens_block, width), bfloat),
            jax.ShapeDtypeStruct((blocks, tokens_block, width), bfloat),
            jax.ShapeDtypeStruct((blocks, 8, tokens_block), single),
            jax.ShapeDtypeStruct(w_gate.shape, bfloat),
            jax.ShapeDtypeStruct(w_up.shape, bfloat),
            jax.ShapeDtypeStruct(w_down.shape, bfloat),
        ),
        in_specs=[anywhere, anywhere, vmem, vmem, anywhere, anywhere, anywhere],
        out_specs=(anywhere, anywhere, vmem, anywhere, anywhere, anywhere),
        scratch_shapes=[
            pltpu.VMEM((blocks, tokens_block, width), bfloat),
            pltpu.VMEM(w_gate.shape, bfloat),
            pltpu.VMEM(w_up.shape, bfloat),
            pltpu.VMEM(w_down.shape, bfloat),
            pltpu.VMEM((local_exp, rows, width), bfloat),
            pltpu.VMEM((local_exp, rows, width), bfloat),
            pltpu.VMEM((local_exp, rows, units), bfloat),
            pltpu.VMEM((local_exp, rows, units), bfloat),
            pltpu.VMEM((local_exp, rows, units), bfloat),
            pltpu.VMEM((blocks, local_exp * capacity, tokens_block), bfloat),
            pltpu.VMEM((4, local_exp * capacity, 128), single),
            pltpu.VMEM((local_exp, 4 * capacity, width), bfloat),
            pltpu.VMEM((8, tokens_block, width), bfloat),
            pltpu.VMEM((tokens_block, tokens_block), bfloat),
            dma((4, blocks)),
            dma((blocks,)),
            dma,
            dma((6,)),
            dma((4,)),
            dma((6,)),
            dma((8,)),
            dma((4,)),
            dma((5,)),
            pltpu.SemaphoreType.REGULAR((4,)),
        ],
        compiler_params=pltpu.CompilerParams(
            collective_id=1, has_side_effects=True, vmem_limit_bytes=63 * 2**20
        ),
        name="experts",
    )(hidden, final_all, routes_all, router_rows, w_gate, w_up, w_down)


def on_device(
    tokens,
    lengths,
    routes,
    gain_attn,
    w_query,
    key_weight,
    value_weight,
    w_out,
    gain_ffn,
    w_router,
    w_gate,
    w_up,
    w_down,
    cotangent,
):
    query_groups = tokens.shape[0]
    sequence_per_device = tokens.shape[1]
    ctx_count = lax.axis_size("context")
    exp_count = lax.axis_size("expert")
    local_exp = w_gate.shape[0]
    experts = local_exp * ctx_count * exp_count
    capacity = sequence_per_device * TOP * 3 // (2 * experts)
    sequence_total = sequence_per_device * ctx_count
    group_ratio = QUERY_HEADS // KEY_VALUE_HEADS
    scale = HEAD_SIZE ** (-0.5)
    bfloat = jnp.bfloat16
    single = jnp.float32
    small = jnp.concatenate([w_router, gain_attn[:, None], gain_ffn[:, None]], axis=1)
    early = jnp.concatenate([w_query, key_weight, value_weight, small], axis=1)
    early = lax.all_gather(early, EVERY, axis=0, tiled=True)
    out_w = lax.all_gather(w_out, EVERY, axis=0, tiled=True)
    query_w = early[:, : w_query.shape[1]]
    key_w = early[:, w_query.shape[1] : w_query.shape[1] + key_weight.shape[1]]
    value_w = early[:, w_query.shape[1] + key_weight.shape[1] : -small.shape[1]]
    router_w = early[:, -small.shape[1] : -2]
    gain_one = early[:, -2]
    gain_two = early[:, -1]
    gain_one = gain_one.astype(single)
    gain_two = gain_two.astype(single)
    positions = lax.axis_index("context") * sequence_per_device + jnp.arange(
        sequence_per_device, dtype=jnp.int32
    )
    key_pos = jnp.arange(sequence_total, dtype=jnp.int32)
    valid = (positions[None, :] < lengths[:, None]).astype(single)[..., None]
    cosine_table, sine_table = rotation_tables(positions)
    inputs = tokens.astype(single)
    inverse_one = lax.rsqrt(jnp.mean(inputs * inputs, axis=-1, keepdims=True) + epsilon)
    normed_one = inputs * inverse_one
    hidden_one = (normed_one * gain_one).astype(bfloat)
    query_lin = jnp.einsum("gsd,de->gse", hidden_one, query_w, preferred_element_type=single)
    key_linear = jnp.einsum("gsd,de->gse", hidden_one, key_w, preferred_element_type=single)
    value_lower = jnp.einsum(
        "gsd,de->gse", hidden_one, value_w, preferred_element_type=single
    ).astype(bfloat)
    query_rotated = (
        apply_rotation(
            query_lin.reshape(query_groups, sequence_per_device, QUERY_HEADS, HEAD_SIZE),
            cosine_table,
            sine_table,
        )
        .astype(bfloat)
        .reshape(query_groups, sequence_per_device, QUERY_HEADS * HEAD_SIZE)
    )
    key_rotated = (
        apply_rotation(
            key_linear.reshape(query_groups, sequence_per_device, KEY_VALUE_HEADS, HEAD_SIZE),
            cosine_table,
            sine_table,
        )
        .astype(bfloat)
        .reshape(query_groups, sequence_per_device, KEY_VALUE_HEADS * HEAD_SIZE)
    )
    gathered_keys, gathered_values = (
        lax.all_gather(key_rotated, "context", axis=1, tiled=True),
        lax.all_gather(value_lower, "context", axis=1, tiled=True),
    )

    def attn_scores(slot_index):
        query_per_head = query_rotated[slot_index].reshape(
            sequence_per_device, KEY_VALUE_HEADS, group_ratio, HEAD_SIZE
        )
        key_per_head = gathered_keys[slot_index].reshape(sequence_total, KEY_VALUE_HEADS, HEAD_SIZE)
        scores = scale * jnp.einsum(
            "skrd,tkd->krst", query_per_head, key_per_head, preferred_element_type=single
        )
        allowed = (key_pos[None, :] <= positions[:, None]) & (
            key_pos[None, :] < lengths[slot_index]
        )
        return (jnp.where(allowed, scores, floor_score), allowed, query_per_head, key_per_head)

    slot_index = 0
    scores, allowed, query_per_head, key_per_head = attn_scores(slot_index)
    peak = jnp.max(scores, axis=-1, keepdims=True)
    raised = jnp.exp(scores - peak)
    total = jnp.sum(raised, axis=-1, keepdims=True)
    probs = raised / total
    value_per_head = gathered_values[slot_index].reshape(sequence_total, KEY_VALUE_HEADS, HEAD_SIZE)
    mixed_g = jnp.einsum(
        "krst,tkd->skrd", probs.astype(bfloat), value_per_head, preferred_element_type=single
    )
    mixed_list = [mixed_g.reshape(sequence_per_device, QUERY_HEADS * HEAD_SIZE)]
    lse_list = [peak + jnp.log(total)]
    mixed_low = jnp.stack(mixed_list).astype(bfloat)
    resid = inputs + jnp.einsum("gse,ed->gsd", mixed_low, out_w, preferred_element_type=single)
    inverse_two = lax.rsqrt(jnp.mean(resid * resid, axis=-1, keepdims=True) + epsilon)
    normed_two = resid * inverse_two
    hidden_two = (normed_two * gain_two).astype(bfloat)
    logits = jnp.einsum("gsd,de->gse", hidden_two, router_w, preferred_element_type=single)
    matches = routes[..., None] == jnp.arange(experts, dtype=jnp.int32)
    chosen = jnp.sum(jnp.where(matches, logits[:, :, None, :], 0.0), axis=-1)
    gates = jax.nn.softmax(chosen, axis=-1)
    final_low = (cotangent.astype(single) * valid).astype(bfloat)
    final_all = lax.all_gather(final_low[0], GROUP, axis=0, tiled=False)
    routes_all = lax.all_gather(routes[0].T, GROUP, axis=0, tiled=False)
    grad_hidden, combined, scores, grad_w_gate, grad_w_up, grad_w_down = experts_on_owner(
        hidden_two[0], final_all, routes_all, router_w.T, w_gate, w_up, w_down, capacity
    )
    combined = lax.psum_scatter(combined, GROUP, scatter_dimension=0, tiled=False)
    scores = scores[:, :local_exp]
    scores = lax.all_to_all(scores, GROUP, split_axis=0, concat_axis=0, tiled=True)
    scores = scores.reshape(experts, sequence_per_device)
    block_out = (valid * (resid + combined.astype(single)[None])).astype(bfloat)
    grad_final = cotangent.astype(single) * valid
    grad_gates = jnp.sum(jnp.where(matches, scores.T[None, :, None, :], 0.0), axis=-1)
    gate_mean = jnp.sum(gates * grad_gates, axis=-1, keepdims=True)
    grad_chosen = gates * (grad_gates - gate_mean)
    grad_logits = jnp.sum(jnp.where(matches, grad_chosen[..., None], 0.0), axis=2).astype(bfloat)
    grad_w_router = jnp.einsum(
        "gsd,gse->de", hidden_two, grad_logits, preferred_element_type=single
    )
    grad_hidden_two = grad_hidden.astype(single)[None]
    grad_hidden_two = grad_hidden_two + jnp.einsum(
        "gse,de->gsd", grad_logits, router_w, preferred_element_type=single
    )
    grad_gain_ffn = jnp.sum(grad_hidden_two * normed_two, axis=(0, 1))
    grad_resid = norm_back(grad_hidden_two * gain_two, normed_two, inverse_two) + grad_final
    grad_attn = grad_resid.astype(bfloat)
    grad_w_out = jnp.einsum("gse,gsd->ed", mixed_low, grad_attn, preferred_element_type=single)
    mixed_gradient = jnp.einsum(
        "gsd,ed->gse", grad_attn, out_w, preferred_element_type=single
    ).astype(bfloat)
    slot_index = 0
    scores, allowed, query_per_head, key_per_head = attn_scores(slot_index)
    probs = jnp.where(allowed, jnp.exp(scores - lse_list[slot_index]), 0.0)
    value_per_head = gathered_values[slot_index].reshape(sequence_total, KEY_VALUE_HEADS, HEAD_SIZE)
    head_gradient = mixed_gradient[slot_index].reshape(
        sequence_per_device, KEY_VALUE_HEADS, group_ratio, HEAD_SIZE
    )
    grad_probs = jnp.einsum(
        "skrd,tkd->krst", head_gradient, value_per_head, preferred_element_type=single
    )
    row_delta = jnp.sum(probs * grad_probs, axis=-1, keepdims=True)
    grad_scores = (probs * (grad_probs - row_delta)).astype(bfloat)
    grad_queries = [
        (
            scale
            * jnp.einsum("krst,tkd->skrd", grad_scores, key_per_head, preferred_element_type=single)
        ).reshape(sequence_per_device, QUERY_HEADS, HEAD_SIZE)
    ]
    grad_keys = [
        (
            scale
            * jnp.einsum(
                "krst,skrd->tkd", grad_scores, query_per_head, preferred_element_type=single
            )
        ).reshape(sequence_total, KEY_VALUE_HEADS * HEAD_SIZE)
    ]
    grad_values = [
        jnp.einsum(
            "krst,skrd->tkd", probs.astype(bfloat), head_gradient, preferred_element_type=single
        ).reshape(sequence_total, KEY_VALUE_HEADS * HEAD_SIZE)
    ]
    key_gradient_rows, value_grad = (
        lax.psum_scatter(
            jnp.stack(grad_keys).astype(jnp.bfloat16), "context", scatter_dimension=1, tiled=True
        ).astype(jnp.float32),
        lax.psum_scatter(
            jnp.stack(grad_values).astype(jnp.bfloat16), "context", scatter_dimension=1, tiled=True
        ).astype(jnp.float32),
    )
    grad_query_lin = (
        inverse_rotation(jnp.stack(grad_queries), cosine_table, sine_table)
        .astype(bfloat)
        .reshape(query_groups, sequence_per_device, QUERY_HEADS * HEAD_SIZE)
    )
    grad_key_lin = (
        inverse_rotation(
            key_gradient_rows.reshape(
                query_groups, sequence_per_device, KEY_VALUE_HEADS, HEAD_SIZE
            ),
            cosine_table,
            sine_table,
        )
        .astype(bfloat)
        .reshape(query_groups, sequence_per_device, KEY_VALUE_HEADS * HEAD_SIZE)
    )
    grad_value_low = value_grad.astype(bfloat)
    grad_w_query = jnp.einsum(
        "gsd,gse->de", hidden_one, grad_query_lin, preferred_element_type=single
    )
    grad_w_key = jnp.einsum("gsd,gse->de", hidden_one, grad_key_lin, preferred_element_type=single)
    grad_w_value = jnp.einsum(
        "gsd,gse->de", hidden_one, grad_value_low, preferred_element_type=single
    )
    grad_hidden_one = jnp.einsum(
        "gse,de->gsd", grad_query_lin, query_w, preferred_element_type=single
    )
    grad_hidden_one = grad_hidden_one + jnp.einsum(
        "gse,de->gsd", grad_key_lin, key_w, preferred_element_type=single
    )
    grad_hidden_one = grad_hidden_one + jnp.einsum(
        "gse,de->gsd", grad_value_low, value_w, preferred_element_type=single
    )
    grad_gain_attn = jnp.sum(grad_hidden_one * normed_one, axis=(0, 1))
    grad_tokens = norm_back(grad_hidden_one * gain_one, normed_one, inverse_one) + grad_resid
    late = jnp.concatenate(
        [
            grad_w_query,
            grad_w_key,
            grad_w_value,
            grad_w_router,
            grad_gain_attn[:, None],
            grad_gain_ffn[:, None],
        ],
        axis=1,
    ).astype(bfloat)
    late = lax.psum_scatter(late, EVERY, scatter_dimension=0, tiled=True).astype(single)
    out_grad = lax.psum_scatter(
        grad_w_out.astype(bfloat), EVERY, scatter_dimension=0, tiled=True
    ).astype(single)
    width = grad_w_query.shape[1]
    narrow = grad_w_key.shape[1]
    shard_grads = (
        late[:, -2],
        late[:, :width],
        late[:, width : width + narrow],
        late[:, width + narrow : width + 2 * narrow],
        out_grad,
        late[:, -1],
        late[:, width + 2 * narrow : -2],
    )
    expert_sums = (
        lax.psum_scatter(
            grad_w_gate.astype(jnp.bfloat16), "dp", scatter_dimension=1, tiled=True
        ).astype(jnp.float32),
        lax.psum_scatter(
            grad_w_up.astype(jnp.bfloat16), "dp", scatter_dimension=1, tiled=True
        ).astype(jnp.float32),
        lax.psum_scatter(
            grad_w_down.astype(jnp.bfloat16), "dp", scatter_dimension=1, tiled=True
        ).astype(jnp.float32),
    )
    return (
        block_out,
        grad_tokens,
        shard_grads[0],
        shard_grads[1],
        shard_grads[2],
        shard_grads[3],
        shard_grads[4],
        shard_grads[5],
        shard_grads[6],
        expert_sums[0],
        expert_sums[1],
        expert_sums[2],
    )


def solution(mesh):
    in_specs = (
        P(("dp", "expert"), "context", None),
        P(("dp", "expert")),
        P(("dp", "expert"), "context", None),
        P(("dp", "context", "expert")),
        P(("dp", "context", "expert"), None),
        P(("dp", "context", "expert"), None),
        P(("dp", "context", "expert"), None),
        P(("dp", "context", "expert"), None),
        P(("dp", "context", "expert")),
        P(("dp", "context", "expert"), None),
        P(("context", "expert"), None, None),
        P(("context", "expert"), None, None),
        P(("context", "expert"), None, None),
        P(("dp", "expert"), "context", None),
    )
    out_specs = (
        P(("dp", "expert"), "context", None),
        P(("dp", "expert"), "context", None),
        P(("dp", "context", "expert")),
        P(("dp", "context", "expert"), None),
        P(("dp", "context", "expert"), None),
        P(("dp", "context", "expert"), None),
        P(("dp", "context", "expert"), None),
        P(("dp", "context", "expert")),
        P(("dp", "context", "expert"), None),
        P(("context", "expert"), "dp", None),
        P(("context", "expert"), "dp", None),
        P(("context", "expert"), "dp", None),
    )
    return jax.shard_map(
        on_device, mesh=mesh, in_specs=in_specs, out_specs=out_specs, check_vma=False
    )
```

```python
import math

import jax
import jax.numpy as jnp
from jax import lax
from jax.experimental import pallas as pl
from jax.experimental.pallas import tpu as pltpu
from jax.sharding import PartitionSpec as P

MODEL_WIDTH = 1536
QUERY_HEADS = 24
KEY_VALUE_HEADS = 8
HEAD_SIZE = 64
TOP = 8


epsilon = 1e-05
floor_score = -1e30


def rotation_tables(positions):
    half_size = HEAD_SIZE // 2
    exponent = jnp.arange(half_size, dtype=jnp.int32).astype(jnp.float32) * (2.0 / HEAD_SIZE)
    frequency = jnp.exp(-math.log(10000.0) * exponent)
    angles = positions.astype(jnp.float32)[:, None] * frequency[None, :]
    return (jnp.cos(angles)[:, None, :], jnp.sin(angles)[:, None, :])


def apply_rotation(values, cosine_table, sine_table):
    half_size = values.shape[-1] // 2
    first = values[..., :half_size]
    second = values[..., half_size:]
    return jnp.concatenate(
        [first * cosine_table - second * sine_table, second * cosine_table + first * sine_table],
        axis=-1,
    )


def inverse_rotation(gradient, cosine_table, sine_table):
    half_size = gradient.shape[-1] // 2
    first = gradient[..., :half_size]
    second = gradient[..., half_size:]
    return jnp.concatenate(
        [first * cosine_table + second * sine_table, second * cosine_table - first * sine_table],
        axis=-1,
    )


def norm_back(gradient, normed, inverse):
    return inverse * (gradient - normed * jnp.mean(gradient * normed, axis=-1, keepdims=True))


GROUP = ("context", "expert")
EVERY = ("dp", "context", "expert")


MESH_ID = pl.DeviceIdType.MESH
CHUNK = 512
HALF = 256
UP, DOWN, ACROSS, CORE, DP = 0, 1, 2, 3, 4


def contract_rows(left, right):
    return lax.dot_general(left, right, (((0,), (0,)), ((), ())), preferred_element_type=jnp.float32)


def contract_last(left, right):
    return lax.dot_general(left, right, (((1,), (1,)), ((), ())), preferred_element_type=jnp.float32)


def matmul(left, right):
    return jnp.dot(left, right, preferred_element_type=jnp.float32)


def line_order(z, step):
    half = z // 2
    inner = z + half * (3 - 2 * z)
    base = step + inner * (1 - 2 * step) * (1 - step // 2)
    return base + half * (3 - 2 * base)


def place():
    ctx = lax.axis_index("context")
    z = lax.axis_index("expert")
    y = ctx // 2
    c = ctx % 2
    inner = z + (z // 2) * (3 - 2 * z)

    def device(kind):
        if kind == UP:
            return {"context": ctx, "expert": z + 1}
        if kind == DOWN:
            return {"context": ctx, "expert": z - 1}
        if kind == ACROSS:
            return {"context": (1 - y) * 2 + c, "expert": z}
        if kind == CORE:
            return {"context": y * 2 + 1 - c, "expert": z}
        return {"dp": 1 - lax.axis_index("dp")}

    def per_side(action, more=()):
        @pl.when(z < 3)
        def _():
            action(UP)

        @pl.when(z > 0)
        def _():
            action(DOWN)

        for kind in (ACROSS, CORE, *more):
            action(kind)

    return y, c, z, inner, device, per_side


def block_id(yy, cc, zz):
    return (yy * 2 + cc) * 4 + zz


def greet(per_side, device, count, more=()):
    barrier = pltpu.get_barrier_semaphore()
    per_side(
        lambda kind: pl.semaphore_signal(
            barrier, inc=1, device_id=device(kind), device_id_type=MESH_ID
        ),
        more,
    )
    pl.semaphore_wait(barrier, count)


def gather_kernel(
    query_ref,
    key_ref,
    value_ref,
    small_ref,
    out_ref,
    early_ref,
    late_ref,
    early,
    late,
    local_sem,
    early_send,
    early_core,
    early_recv,
    late_send,
    late_dp,
    late_recv,
):
    y, c, z, inner, device, per_side = place()
    d = lax.axis_index("dp")
    mine = d * 16 + block_id(y, c, z)
    loads = []
    at = 0
    for index, ref in enumerate((query_ref, key_ref, value_ref, small_ref)):
        size = ref.shape[1]
        loads.append(
            pltpu.make_async_copy(ref, early.at[mine, :, pl.ds(at, size)], local_sem.at[index])
        )
        at += size
    loads.append(pltpu.make_async_copy(out_ref, late.at[mine], local_sem.at[4]))
    for copy in loads:
        copy.start()
    greet(per_side, device, 4 + inner, (DP,))
    for copy in loads:
        copy.wait()

    def early_copy(kind, slot, sem):
        return pltpu.make_async_remote_copy(
            src_ref=early.at[slot],
            dst_ref=early.at[slot],
            send_sem=sem,
            recv_sem=early_recv.at[slot],
            device_id=device(kind),
            device_id_type=MESH_ID,
        )

    def early_own(kind, block):
        return early_copy(kind, d * 16 + block, early_send.at[kind, block])

    def early_other(block):
        return early_copy(CORE, (1 - d) * 16 + block, early_core.at[block])

    def late_copy(kind, slot, sem):
        return pltpu.make_async_remote_copy(
            src_ref=late.at[slot],
            dst_ref=late.at[slot],
            send_sem=sem,
            recv_sem=late_recv.at[slot],
            device_id=device(kind),
            device_id_type=MESH_ID,
        )

    def late_own(kind, plane, block):
        slot = plane * 16 + block
        return late_copy(kind, slot, late_send.at[kind, slot])

    def along(kind, zz):
        if kind == UP:
            return jnp.logical_and(z < 3, zz <= z)
        return jnp.logical_and(z > 0, zz >= z)

    def fan(zz, act):
        block = block_id(y, c, zz)
        for kind in (UP, DOWN):

            @pl.when(along(kind, zz))
            def _():
                act(early_own(kind, block))
                act(late_own(kind, d, block))

        for kind in (ACROSS, CORE):
            act(early_own(kind, block))
            act(late_own(kind, d, block))
        act(early_own(DP, block))

    def fan_other(zz, act):
        block = block_id(y, c, zz)
        for kind in (UP, DOWN):

            @pl.when(along(kind, zz))
            def _():
                act(late_own(kind, 1 - d, block))

        for kind in (ACROSS, CORE):
            act(late_own(kind, 1 - d, block))

    def fan_across(zz, act):
        block = block_id(1 - y, c, zz)
        act(early_own(CORE, block))
        act(early_own(DP, block))
        act(late_own(CORE, d, block))
        act(late_own(CORE, 1 - d, block))

    def fan_dp(zz, act):
        act(early_other(block_id(y, c, zz)))
        act(early_other(block_id(1 - y, c, zz)))

    start = lambda copy: copy.start()
    over_dp = late_copy(DP, mine, late_dp)
    over_dp.start()
    fan(z, start)

    def arrive(step, carry):
        @pl.when(step < 4)
        def _():
            zz = line_order(z, step)
            block = block_id(y, c, zz)

            @pl.when(step > 0)
            def _():
                early_own(ACROSS, block).wait_recv()
                late_own(ACROSS, d, block).wait_recv()
                fan(zz, start)

            late_own(ACROSS, 1 - d, block).wait_recv()
            fan_other(zz, start)

        @pl.when(jnp.logical_and(step > 0, step < 5))
        def _():
            zz = line_order(z, jnp.maximum(step - 1, 0))
            block = block_id(1 - y, c, zz)
            early_own(CORE, block).wait_recv()
            late_own(CORE, d, block).wait_recv()
            late_own(CORE, 1 - d, block).wait_recv()
            fan_across(zz, start)

        @pl.when(step > 1)
        def _():
            zz = line_order(z, jnp.maximum(step - 2, 0))
            early_other(block_id(y, c, zz)).wait_recv()
            early_other(block_id(1 - y, c, zz)).wait_recv()
            fan_dp(zz, start)

        return carry

    lax.fori_loop(0, 6, arrive, 0)

    def finish(zz, carry):
        for yy in range(2):
            block = block_id(yy, 1 - c, zz)
            early_own(CORE, block).wait_recv()
            early_other(block).wait_recv()
            late_own(CORE, d, block).wait_recv()
            late_own(CORE, 1 - d, block).wait_recv()
        return carry

    lax.fori_loop(0, 4, finish, 0)
    results = (
        pltpu.make_async_copy(early, early_ref, local_sem.at[0]),
        pltpu.make_async_copy(late, late_ref, local_sem.at[1]),
    )
    for copy in results:
        copy.start()
    end = lambda copy: copy.wait_send()
    over_dp.wait_send()

    def ends(zz, carry):
        fan(zz, end)
        fan_other(zz, end)
        fan_across(zz, end)
        fan_dp(zz, end)
        return carry

    lax.fori_loop(0, 4, ends, 0)
    for copy in results:
        copy.wait()


def gather_weights(query, key, value, small, out):
    bfloat = jnp.bfloat16
    dma = pltpu.SemaphoreType.DMA
    rows = query.shape[0]
    early_width = query.shape[1] + key.shape[1] + value.shape[1] + small.shape[1]
    anywhere = pl.BlockSpec(memory_space=pl.ANY)
    early = (32, rows, early_width)
    late = (32, rows, out.shape[1])
    return pl.pallas_call(
        gather_kernel,
        out_shape=(jax.ShapeDtypeStruct(early, bfloat), jax.ShapeDtypeStruct(late, bfloat)),
        in_specs=[anywhere] * 5,
        out_specs=(anywhere, anywhere),
        scratch_shapes=[
            pltpu.VMEM(early, bfloat),
            pltpu.VMEM(late, bfloat),
            dma((5,)),
            dma((5, 16)),
            dma((16,)),
            dma((32,)),
            dma((4, 32)),
            dma,
            dma((32,)),
        ],
        compiler_params=pltpu.CompilerParams(
            collective_id=0, has_side_effects=True, vmem_limit_bytes=40 * 2**20
        ),
        name="gather_weights",
    )(query, key, value, small, out)


def sums_kernel(
    proj_ref,
    small_ref,
    out_ref,
    gate_ref,
    up_ref,
    down_ref,
    sum_ref,
    gate_got,
    up_got,
    down_got,
    parts,
    core_got,
    y_got,
    z_got,
    dp_got,
    load_sem,
    swap_send,
    swap_recv,
    core_send,
    core_recv,
    y_send,
    y_recv,
    z_send,
    z_recv,
    dp_send,
    dp_recv,
):
    single = jnp.float32
    bfloat = jnp.bfloat16
    y, c, z, inner, device, per_side = place()
    d = lax.axis_index("dp")
    rows = proj_ref.shape[2]
    loads = []
    at = 0
    for index, ref in enumerate((proj_ref, small_ref, out_ref)):
        size = ref.shape[3]
        for plane in range(2):
            loads.append(
                pltpu.make_async_copy(
                    ref.at[plane],
                    parts.at[:, pl.ds(plane * rows, rows), pl.ds(at, size)],
                    load_sem.at[index * 2 + plane],
                )
            )
        at += size
    for copy in loads:
        copy.start()
    greet(per_side, device, 4 + inner, (DP,))

    swaps = []
    for index, (source, target) in enumerate(
        ((gate_ref, gate_got), (up_ref, up_got), (down_ref, down_got))
    ):
        half = target.shape[1]
        for j in range(target.shape[0]):
            swaps.append(
                pltpu.make_async_remote_copy(
                    src_ref=source.at[j, pl.ds(pl.multiple_of((1 - d) * half, 128), half), :],
                    dst_ref=target.at[j],
                    send_sem=swap_send.at[index * 2 + j],
                    recv_sem=swap_recv.at[index * 2 + j],
                    device_id=device(DP),
                    device_id_type=MESH_ID,
                )
            )
    for copy in swaps:
        copy.start()
    for copy in loads:
        copy.wait()

    def remote(kind, source, target, send_sem, recv_sem):
        return pltpu.make_async_remote_copy(
            src_ref=source,
            dst_ref=target,
            send_sem=send_sem,
            recv_sem=recv_sem,
            device_id=device(kind),
            device_id_type=MESH_ID,
        )

    def to_core(yy, zz):
        slot = yy * 4 + zz
        return remote(
            CORE, parts.at[block_id(yy, 1 - c, zz)], core_got.at[slot], core_send.at[slot], core_recv.at[slot]
        )

    def to_across(zz):
        return remote(ACROSS, parts.at[block_id(1 - y, c, zz)], y_got.at[zz], y_send.at[zz], y_recv.at[zz])

    def to_line(kind, zz, slot):
        return remote(kind, parts.at[block_id(y, c, zz)], z_got.at[slot], z_send.at[zz], z_recv.at[slot])

    def add(block, got):
        parts[block] = (parts[block].astype(single) + got.astype(single)).astype(bfloat)

    def core_sends(step, carry):
        zz = line_order(z, 3 - step)
        to_core(1 - y, zz).start()
        to_core(y, zz).start()
        return carry

    lax.fori_loop(0, 4, core_sends, 0)

    def line_sum(step):
        zz = line_order(z, step)
        block = block_id(y, c, zz)
        to_across(zz).wait_recv()
        add(block, y_got[zz])
        rising = zz > z
        comes = jnp.logical_or(jnp.logical_and(rising, z > 0), jnp.logical_and(zz < z, z < 3))

        @pl.when(comes)
        def _():
            to_line(CORE, zz, zz).wait_recv()
            add(block, z_got[zz])

        @pl.when(rising)
        def _():
            to_line(UP, zz, zz).start()

        @pl.when(zz == z - 1)
        def _():
            to_line(DOWN, zz, 4).start()

        @pl.when(zz < z - 1)
        def _():
            to_line(DOWN, zz, zz).start()

    def stage(turn, carry):
        @pl.when(turn < 4)
        def _():
            zz = line_order(z, 3 - jnp.minimum(turn, 3))
            to_core(1 - y, zz).wait_recv()
            add(block_id(1 - y, c, zz), core_got[(1 - y) * 4 + zz])
            to_across(zz).start()
            to_core(y, zz).wait_recv()
            add(block_id(y, c, zz), core_got[y * 4 + zz])

        @pl.when(jnp.logical_and(turn > 0, turn < 4))
        def _():
            line_sum(4 - jnp.maximum(turn, 1))

        return carry

    lax.fori_loop(0, 4, stage, 0)
    mine = block_id(y, c, z)
    to_across(z).wait_recv()
    add(mine, y_got[z])

    @pl.when(z > 0)
    def _():
        to_line(CORE, z, z).wait_recv()
        add(mine, z_got[z])

    @pl.when(z < 3)
    def _():
        to_line(CORE, z, 4).wait_recv()
        add(mine, z_got[4])

    there = pl.ds(pl.multiple_of((1 - d) * rows, 16), rows)
    here = pl.ds(pl.multiple_of(d * rows, 16), rows)
    last = remote(DP, parts.at[mine, there, :], dp_got, dp_send, dp_recv)
    last.start()
    last.wait_recv()
    sum_ref[...] = parts[mine, here, :].astype(single) + dp_got[...].astype(single)
    last.wait_send()
    for copy in swaps:
        copy.wait()

    def ends(zz, carry):
        to_core(y, zz).wait_send()
        to_core(1 - y, zz).wait_send()
        to_across(zz).wait_send()

        @pl.when(zz != z)
        def _():
            to_line(CORE, zz, zz).wait_send()

        return carry

    lax.fori_loop(0, 4, ends, 0)


def sum_gradients(proj, small, out, gate, up, down):
    bfloat = jnp.bfloat16
    dma = pltpu.SemaphoreType.DMA
    rows = proj.shape[0] // 32
    parts = [x.reshape(2, 16, rows, x.shape[1]) for x in (proj, small, out)]
    width = sum(x.shape[3] for x in parts)
    anywhere = pl.BlockSpec(memory_space=pl.ANY)
    halves = [(x.shape[0], x.shape[1] // 2, x.shape[2]) for x in (gate, up, down)]
    return pl.pallas_call(
        sums_kernel,
        out_shape=(
            jax.ShapeDtypeStruct((rows, width), jnp.float32),
            *(jax.ShapeDtypeStruct(shape, bfloat) for shape in halves),
        ),
        in_specs=[anywhere] * 6,
        out_specs=(pl.BlockSpec(memory_space=pltpu.VMEM), anywhere, anywhere, anywhere),
        scratch_shapes=[
            pltpu.VMEM((16, 2 * rows, width), bfloat),
            pltpu.VMEM((8, 2 * rows, width), bfloat),
            pltpu.VMEM((4, 2 * rows, width), bfloat),
            pltpu.VMEM((5, 2 * rows, width), bfloat),
            pltpu.VMEM((rows, width), bfloat),
            dma((6,)),
            dma((6,)),
            dma((6,)),
            dma((8,)),
            dma((8,)),
            dma((4,)),
            dma((4,)),
            dma((4,)),
            dma((5,)),
            dma,
            dma,
        ],
        compiler_params=pltpu.CompilerParams(
            collective_id=2, has_side_effects=True, vmem_limit_bytes=40 * 2**20
        ),
        name="sum_gradients",
    )(*parts, gate, up, down)


def experts_kernel(
    hidden_ref,
    final_ref,
    routes_ref,
    router_ref,
    gate_hbm,
    up_hbm,
    down_hbm,
    back_ref,
    part_ref,
    score_ref,
    grad_gate_ref,
    grad_up_ref,
    grad_down_ref,
    held,
    w_gate,
    w_up,
    w_down,
    rows_in,
    rows_grad,
    slope_gate,
    slope_up,
    hidden_e,
    picks,
    row_gates,
    work,
    pool,
    before,
    gather_send,
    gather_recv,
    local_sem,
    load_sem,
    part_sem,
    sum_send,
    core_recv,
    y_recv,
    z_recv,
    ready,
):
    single = jnp.float32
    bfloat = jnp.bfloat16
    tokens_block = hidden_ref.shape[0]
    width = hidden_ref.shape[1]
    experts = router_ref.shape[0]
    local_exp = w_gate.shape[0]
    hidden_units = w_gate.shape[2]
    capacity = picks.shape[1] // local_exp
    group_rows = 4 * capacity
    ctx = lax.axis_index("context")
    z = lax.axis_index("expert")
    y = ctx // 2
    c = ctx % 2
    inner = z + (z // 2) * (3 - 2 * z)

    def device(kind):
        if kind == UP:
            return {"context": ctx, "expert": z + 1}
        if kind == DOWN:
            return {"context": ctx, "expert": z - 1}
        if kind == ACROSS:
            return {"context": (1 - y) * 2 + c, "expert": z}
        return {"context": y * 2 + 1 - c, "expert": z}

    def block_id(yy, cc, zz):
        return (yy * 2 + cc) * 4 + zz

    def per_side(action):
        @pl.when(z < 3)
        def _():
            action(UP)

        @pl.when(z > 0)
        def _():
            action(DOWN)

        action(ACROSS)
        action(CORE)

    weights = (
        pltpu.make_async_copy(gate_hbm, w_gate, load_sem.at[0]),
        pltpu.make_async_copy(up_hbm, w_up, load_sem.at[1]),
        pltpu.make_async_copy(down_hbm, w_down, load_sem.at[2]),
    )
    mine = block_id(y, c, z)
    own = pltpu.make_async_copy(hidden_ref, held.at[mine], local_sem)
    own.start()
    for copy in weights:
        copy.start()

    barrier = pltpu.get_barrier_semaphore()
    per_side(
        lambda kind: pl.semaphore_signal(
            barrier, inc=1, device_id=device(kind), device_id_type=MESH_ID
        )
    )
    pl.semaphore_wait(barrier, 3 + inner)
    own.wait()

    def spread(kind, block):
        return pltpu.make_async_remote_copy(
            src_ref=held.at[block],
            dst_ref=held.at[block],
            send_sem=gather_send.at[kind, block],
            recv_sem=gather_recv.at[block],
            device_id=device(kind),
            device_id_type=MESH_ID,
        )

    def along(kind, zz):
        if kind == UP:
            return jnp.logical_and(z < 3, zz <= z)
        return jnp.logical_and(z > 0, zz >= z)

    def send_on(zz):
        block = block_id(y, c, zz)
        for kind in (UP, DOWN):

            @pl.when(along(kind, zz))
            def _():
                spread(kind, block).start()

        spread(ACROSS, block).start()
        spread(CORE, block).start()

    def forward(step):
        zz = line_order(z, step)
        spread(ACROSS, block_id(y, c, zz)).wait_recv()
        send_on(zz)

    send_on(z)
    row = lax.broadcasted_iota(jnp.int32, (tokens_block, tokens_block), 0)
    column = lax.broadcasted_iota(jnp.int32, (tokens_block, tokens_block), 1)
    before[...] = jnp.where(row < column, 1.0, 0.0).astype(bfloat)
    for copy in weights:
        copy.wait()
    first = (ctx * 4 + z) * local_exp

    def member(zz, p):
        yy = y + (p // 2) * (1 - 2 * y)
        cc = c + (p % 2) * (1 - 2 * c)
        return block_id(yy, cc, zz)

    def load_final(zz, p):
        return pltpu.make_async_copy(final_ref.at[member(zz, p)], pool.at[p], load_sem.at[p])

    def store_part(zz, p):
        return pltpu.make_async_copy(pool.at[4 + p], part_ref.at[member(zz, p)], part_sem.at[p])

    def forward_group(step, carry):
        zz = line_order(z, step)
        after = step + 1 + inner * jnp.minimum(step, 1)

        @pl.when(after < 4)
        def _():
            forward(after)

        @pl.when(jnp.logical_and(step == 0, inner == 1))
        def _():
            forward(2)

        @pl.loop(0, 4)
        def _(p):
            load_final(zz, p).start()

        spread(CORE, block_id(y, 1 - c, zz)).wait_recv()
        spread(CORE, block_id(1 - y, c, zz)).wait_recv()
        spread(CORE, block_id(1 - y, c, zz)).start()
        spread(CORE, block_id(1 - y, 1 - c, zz)).wait_recv()

        @pl.loop(0, 4)
        def _(p):
            block = member(zz, p)
            tokens_in = held[block]
            logits = contract_last(router_ref[...], tokens_in)
            expert_row = lax.broadcasted_iota(jnp.int32, (experts, tokens_block), 0)
            routed = jnp.zeros((experts, tokens_block), single)
            for k in range(routes_ref.shape[1]):
                routed = routed + jnp.where(routes_ref[block, k : k + 1, :] == expert_row, 1.0, 0.0)
            named = routed > 0.5
            peak = jnp.max(jnp.where(named, logits, floor_score), axis=0, keepdims=True)
            raised = jnp.where(named, jnp.exp(jnp.minimum(logits - peak, 0.0)), 0.0)
            gates = raised / jnp.sum(raised, axis=0, keepdims=True)
            eight = lax.broadcasted_iota(jnp.int32, (8, tokens_block), 0)
            masks = jnp.zeros((8, tokens_block), single)
            own_mask = []
            own_gate = []
            for j in range(local_exp):
                here = expert_row == first + j
                own_mask.append(jnp.sum(jnp.where(here, routed, 0.0), axis=0, keepdims=True))
                own_gate.append(jnp.sum(jnp.where(here, gates, 0.0), axis=0, keepdims=True))
                masks = masks + jnp.where(eight == j, own_mask[j], 0.0)
            rank = matmul(masks.astype(bfloat), before[...])
            slot = lax.broadcasted_iota(jnp.int32, (capacity, tokens_block), 0).astype(single)
            for j in range(local_exp):
                hit = jnp.logical_and(slot == rank[j : j + 1, :], own_mask[j] > 0.5)
                pick = jnp.where(hit, 1.0, 0.0)
                picks[step * 4 + p, pl.ds(j * capacity, capacity), :] = pick.astype(bfloat)
                gate_column = jnp.sum(pick * own_gate[j], axis=1, keepdims=True)
                row_gates[p, pl.ds(j * capacity, capacity), :] = jnp.broadcast_to(
                    gate_column, (capacity, 128)
                )
            at = pl.multiple_of(step * group_rows + p * capacity, 32)
            for n in range(width // CHUNK):
                part = pl.ds(n * CHUNK, CHUNK)
                got = matmul(picks[step * 4 + p], held[block, :, part]).astype(bfloat)
                for j in range(local_exp):
                    rows_in[j, pl.ds(at, capacity), part] = got[j * capacity : (j + 1) * capacity]

        base = pl.multiple_of(step * group_rows, 128)
        for j in range(local_exp):
            given = rows_in[j, pl.ds(base, group_rows), :]
            for n in range(hidden_units // HALF):
                part = pl.ds(n * HALF, HALF)
                gate_pre = matmul(given, w_gate[j, :, part])
                up_pre = matmul(given, w_up[j, :, part])
                sigmoid = 1.0 / (1.0 + jnp.exp(-gate_pre))
                silu = gate_pre * sigmoid
                hidden_e[j, pl.ds(base, group_rows), part] = (silu * up_pre).astype(bfloat)
                slope_gate[j, pl.ds(base, group_rows), part] = (
                    up_pre * sigmoid * (1.0 + gate_pre * (1.0 - sigmoid))
                ).astype(bfloat)
                slope_up[j, pl.ds(base, group_rows), part] = silu.astype(bfloat)
            for n in range(width // CHUNK):
                part = pl.ds(n * CHUNK, CHUNK)
                work[j, :, part] = matmul(
                    hidden_e[j, pl.ds(base, group_rows), :], w_down[j, :, part]
                ).astype(bfloat)

        @pl.loop(0, 4)
        def _(p):
            block = member(zz, p)
            at = pl.multiple_of(step * group_rows + p * capacity, 32)
            local = pl.multiple_of(p * capacity, 32)
            pick = picks[step * 4 + p]
            weight = row_gates[p][:, 0:1]
            weighted = (pick.astype(single) * weight).astype(bfloat)
            load_final(zz, p).wait()

            @pl.when(step > 0)
            def _():
                store_part(zz, p).wait()

            row_score = jnp.zeros((local_exp * capacity, 1), single)
            for n in range(width // CHUNK):
                part = pl.ds(n * CHUNK, CHUNK)
                out = jnp.concatenate(
                    [work[j, pl.ds(local, capacity), part] for j in range(local_exp)], axis=0
                )
                pool[4 + p, :, part] = contract_rows(weighted, out).astype(bfloat)
                final = matmul(pick, pool[p, :, part])
                row_score = row_score + jnp.sum(final * out.astype(single), axis=1, keepdims=True)
                graded = (final * weight).astype(bfloat)
                for j in range(local_exp):
                    rows_grad[j, pl.ds(at, capacity), part] = graded[j * capacity : (j + 1) * capacity]
            store_part(zz, p).start()
            spread_score = pick.astype(single) * row_score
            eight = lax.broadcasted_iota(jnp.int32, (8, tokens_block), 0)
            scores = jnp.zeros((8, tokens_block), single)
            for j in range(local_exp):
                total = jnp.sum(spread_score[j * capacity : (j + 1) * capacity], axis=0, keepdims=True)
                scores = scores + jnp.where(eight == j, total, 0.0)
            score_ref[block] = scores

        return carry

    lax.fori_loop(0, 4, forward_group, 0)

    @pl.loop(0, 4)
    def _(p):
        store_part(line_order(z, 3), p).wait()

    @pl.loop(0, 4)
    def _(zz):
        block = block_id(y, c, zz)
        for kind in (UP, DOWN):

            @pl.when(along(kind, zz))
            def _():
                spread(kind, block).wait_send()

        spread(ACROSS, block).wait_send()
        spread(CORE, block).wait_send()
        spread(CORE, block_id(1 - y, c, zz)).wait_send()

    opposite = {UP: DOWN, DOWN: UP, ACROSS: ACROSS, CORE: CORE}
    per_side(
        lambda kind: pl.semaphore_signal(
            ready.at[opposite[kind]], inc=1, device_id=device(kind), device_id_type=MESH_ID
        )
    )
    per_side(lambda kind: pl.semaphore_wait(ready.at[kind], 1))

    def to_core(p, zz):
        yy = y + p * (1 - 2 * y)
        return pltpu.make_async_remote_copy(
            src_ref=pool.at[p],
            dst_ref=held.at[yy * 4 + zz],
            send_sem=sum_send.at[p],
            recv_sem=core_recv.at[yy * 4 + zz],
            device_id=device(CORE),
            device_id_type=MESH_ID,
        )

    def from_core(slot):
        return pltpu.make_async_remote_copy(
            src_ref=pool.at[0],
            dst_ref=held.at[slot],
            send_sem=sum_send.at[0],
            recv_sem=core_recv.at[slot],
            device_id=device(CORE),
            device_id_type=MESH_ID,
        )

    def to_across(turn, zz):
        return pltpu.make_async_remote_copy(
            src_ref=pool.at[2 + turn],
            dst_ref=held.at[8 + zz],
            send_sem=sum_send.at[2 + turn],
            recv_sem=y_recv.at[zz],
            device_id=device(ACROSS),
            device_id_type=MESH_ID,
        )

    def to_line(kind, turn, zz, last):
        return pltpu.make_async_remote_copy(
            src_ref=pool.at[4 + turn],
            dst_ref=pool.at[7] if last else held.at[12 + zz],
            send_sem=sum_send.at[4 + turn],
            recv_sem=z_recv.at[4 if last else zz],
            device_id=device(kind),
            device_id_type=MESH_ID,
        )

    def summed(*refs):
        total = refs[0].astype(single)
        for value in refs[1:]:
            total = total + value.astype(single)
        return total.astype(bfloat)

    def back_block(step, p, target):
        local = pl.multiple_of(p * capacity, 32)
        pick = picks[step * 4 + p]
        for n in range(width // CHUNK):
            part = pl.ds(n * CHUNK, CHUNK)
            grads = jnp.concatenate(
                [work[j, pl.ds(local, capacity), part] for j in range(local_exp)], axis=0
            )
            pool[target, :, part] = contract_rows(pick, grads).astype(bfloat)

    def line_sum(step):
        zz = line_order(z, step)
        turn = step % 2
        core_slot = y * 4 + zz
        to_across(turn, zz).wait_recv()
        rising = zz > z

        def finish(comes):
            @pl.when(comes)
            def _():
                to_line(CORE, turn, zz, False).wait_recv()
                pool[4 + turn] = summed(
                    pool[4 + turn], held[core_slot], held[8 + zz], held[12 + zz]
                )

            @pl.when(jnp.logical_not(comes))
            def _():
                pool[4 + turn] = summed(pool[4 + turn], held[core_slot], held[8 + zz])

        @pl.when(rising)
        def _():
            finish(z > 0)
            to_line(UP, turn, zz, False).start()

        @pl.when(jnp.logical_not(rising))
        def _():
            finish(z < 3)

            @pl.when(zz == z - 1)
            def _():
                to_line(DOWN, turn, zz, True).start()

            @pl.when(zz < z - 1)
            def _():
                to_line(DOWN, turn, zz, False).start()

    def backward_group(turn_step, carry):
        step = 3 - turn_step
        zz = line_order(z, step)
        turn = step % 2
        base = pl.multiple_of(step * group_rows, 128)
        for j in range(local_exp):
            for n in range(hidden_units // HALF):
                part = pl.ds(n * HALF, HALF)
                grad_hidden = (
                    contract_last(rows_grad[j, pl.ds(base, group_rows), :], w_down[j, part, :])
                    .astype(bfloat)
                    .astype(single)
                )
                slope_gate[j, pl.ds(base, group_rows), part] = (
                    grad_hidden * slope_gate[j, pl.ds(base, group_rows), part].astype(single)
                ).astype(bfloat)
                slope_up[j, pl.ds(base, group_rows), part] = (
                    grad_hidden * slope_up[j, pl.ds(base, group_rows), part].astype(single)
                ).astype(bfloat)
            for n in range(width // CHUNK):
                part = pl.ds(n * CHUNK, CHUNK)
                work[j, :, part] = (
                    contract_last(slope_gate[j, pl.ds(base, group_rows), :], w_gate[j, part, :])
                    + contract_last(slope_up[j, pl.ds(base, group_rows), :], w_up[j, part, :])
                ).astype(bfloat)
        for p, member_p in ((0, 1), (1, 3)):

            @pl.when(turn_step > 0)
            def _():
                to_core(p, zz).wait_send()

            back_block(step, member_p, p)
            to_core(p, zz).start()

        @pl.when(turn_step > 1)
        def _():
            to_across(turn, zz).wait_send()
            to_line(CORE, turn, zz, False).wait_send()

        back_block(step, 2, 2 + turn)
        other = (1 - y) * 4 + zz
        from_core(other).wait_recv()
        pool[2 + turn] = summed(pool[2 + turn], held[other])
        to_across(turn, zz).start()
        back_block(step, 0, 4 + turn)
        from_core(y * 4 + zz).wait_recv()

        @pl.when(jnp.logical_and(turn_step > 0, turn_step < 3))
        def _():
            line_sum(step + 1)

        return carry

    lax.fori_loop(0, 4, backward_group, 0)

    def stores(j):
        return (
            pltpu.make_async_copy(w_gate.at[j], grad_gate_ref.at[j], load_sem.at[3 * j]),
            pltpu.make_async_copy(w_up.at[j], grad_up_ref.at[j], load_sem.at[3 * j + 1]),
            pltpu.make_async_copy(w_down.at[j], grad_down_ref.at[j], load_sem.at[3 * j + 2]),
        )

    def weight_grads(j):
        @pl.loop(0, width // CHUNK)
        def _(n):
            part = pl.ds(pl.multiple_of(n * CHUNK, CHUNK), CHUNK)
            w_gate[j, part, :] = contract_rows(rows_in[j, :, part], slope_gate[j]).astype(bfloat)
            w_up[j, part, :] = contract_rows(rows_in[j, :, part], slope_up[j]).astype(bfloat)
            w_down[j, :, part] = contract_rows(hidden_e[j], rows_grad[j, :, part]).astype(bfloat)

        for copy in stores(j):
            copy.start()

    weight_grads(0)
    line_sum(1)
    weight_grads(1)
    to_across(0, z).wait_recv()
    pool[4] = summed(pool[4], held[y * 4 + z], held[8 + z])

    @pl.when(z > 0)
    def _():
        to_line(CORE, 0, z, False).wait_recv()
        pool[4] = summed(pool[4], held[12 + z])

    @pl.when(z < 3)
    def _():
        to_line(CORE, 0, z, True).wait_recv()
        pool[4] = summed(pool[4], pool[7])

    result = pltpu.make_async_copy(pool.at[4], back_ref, local_sem)
    result.start()
    for j in range(local_exp):
        for copy in stores(j):
            copy.wait()
    for p in range(2):
        to_core(p, z).wait_send()
        to_across(p, z).wait_send()
    to_line(CORE, 1, z, False).wait_send()
    result.wait()


def experts_on_owner(hidden, final_all, routes_all, router_rows, w_gate, w_up, w_down, capacity):
    blocks = final_all.shape[0]
    tokens_block, width = hidden.shape
    local_exp, _, units = w_gate.shape
    bfloat = jnp.bfloat16
    single = jnp.float32
    rows = blocks * capacity
    anywhere = pl.BlockSpec(memory_space=pl.ANY)
    vmem = pl.BlockSpec(memory_space=pltpu.VMEM)
    dma = pltpu.SemaphoreType.DMA
    return pl.pallas_call(
        experts_kernel,
        out_shape=(
            jax.ShapeDtypeStruct((tokens_block, width), bfloat),
            jax.ShapeDtypeStruct((blocks, tokens_block, width), bfloat),
            jax.ShapeDtypeStruct((blocks, 8, tokens_block), single),
            jax.ShapeDtypeStruct(w_gate.shape, bfloat),
            jax.ShapeDtypeStruct(w_up.shape, bfloat),
            jax.ShapeDtypeStruct(w_down.shape, bfloat),
        ),
        in_specs=[anywhere, anywhere, vmem, vmem, anywhere, anywhere, anywhere],
        out_specs=(anywhere, anywhere, vmem, anywhere, anywhere, anywhere),
        scratch_shapes=[
            pltpu.VMEM((blocks, tokens_block, width), bfloat),
            pltpu.VMEM(w_gate.shape, bfloat),
            pltpu.VMEM(w_up.shape, bfloat),
            pltpu.VMEM(w_down.shape, bfloat),
            pltpu.VMEM((local_exp, rows, width), bfloat),
            pltpu.VMEM((local_exp, rows, width), bfloat),
            pltpu.VMEM((local_exp, rows, units), bfloat),
            pltpu.VMEM((local_exp, rows, units), bfloat),
            pltpu.VMEM((local_exp, rows, units), bfloat),
            pltpu.VMEM((blocks, local_exp * capacity, tokens_block), bfloat),
            pltpu.VMEM((4, local_exp * capacity, 128), single),
            pltpu.VMEM((local_exp, 4 * capacity, width), bfloat),
            pltpu.VMEM((8, tokens_block, width), bfloat),
            pltpu.VMEM((tokens_block, tokens_block), bfloat),
            dma((4, blocks)),
            dma((blocks,)),
            dma,
            dma((6,)),
            dma((4,)),
            dma((6,)),
            dma((8,)),
            dma((4,)),
            dma((5,)),
            pltpu.SemaphoreType.REGULAR((4,)),
        ],
        compiler_params=pltpu.CompilerParams(
            collective_id=1, has_side_effects=True, vmem_limit_bytes=63 * 2**20
        ),
        name="experts",
    )(hidden, final_all, routes_all, router_rows, w_gate, w_up, w_down)


def on_device(
    tokens,
    lengths,
    routes,
    gain_attn,
    w_query,
    key_weight,
    value_weight,
    w_out,
    gain_ffn,
    w_router,
    w_gate,
    w_up,
    w_down,
    cotangent,
):
    query_groups = tokens.shape[0]
    sequence_per_device = tokens.shape[1]
    ctx_count = lax.axis_size("context")
    exp_count = lax.axis_size("expert")
    local_exp = w_gate.shape[0]
    experts = local_exp * ctx_count * exp_count
    capacity = sequence_per_device * TOP * 3 // (2 * experts)
    sequence_total = sequence_per_device * ctx_count
    group_ratio = QUERY_HEADS // KEY_VALUE_HEADS
    scale = HEAD_SIZE ** (-0.5)
    bfloat = jnp.bfloat16
    single = jnp.float32
    proj_width = w_query.shape[1] + key_weight.shape[1] + value_weight.shape[1]
    own_rows = w_query.shape[0]
    small = jnp.concatenate(
        [
            w_router,
            gain_attn[:, None],
            gain_ffn[:, None],
            jnp.zeros((own_rows, 64 - experts - 2), bfloat),
        ],
        axis=1,
    )
    if lax.axis_size("dp") == 2:
        packed = routes.reshape(-1, 64).astype(bfloat)
        packed = jnp.pad(packed, ((0, own_rows - packed.shape[0]), (0, 0)))
        early, late = gather_weights(
            w_query, key_weight, value_weight, jnp.concatenate([small, packed], axis=1), w_out
        )
        routes_all = lax.dynamic_slice(
            early,
            (lax.axis_index("dp") * 16, 0, proj_width + 64),
            (16, sequence_per_device * TOP // 64, 64),
        )
        routes_all = routes_all.astype(jnp.int32).reshape(16, sequence_per_device, TOP)
        routes_all = routes_all.swapaxes(1, 2)
        early = early.reshape(-1, early.shape[2])
        out_w = late.reshape(-1, late.shape[2])
    else:
        early = jnp.concatenate([w_query, key_weight, value_weight, small], axis=1)
        early = lax.all_gather(early, EVERY, axis=0, tiled=True)
        out_w = lax.all_gather(w_out, EVERY, axis=0, tiled=True)
        routes_all = lax.all_gather(routes[0].T, GROUP, axis=0, tiled=False)
    proj_w = early[:, :proj_width]
    router_w = early[:, proj_width : proj_width + experts]
    gain_one = early[:, proj_width + experts]
    gain_two = early[:, proj_width + experts + 1]
    gain_one = gain_one.astype(single)
    gain_two = gain_two.astype(single)
    positions = lax.axis_index("context") * sequence_per_device + jnp.arange(
        sequence_per_device, dtype=jnp.int32
    )
    key_pos = jnp.arange(sequence_total, dtype=jnp.int32)
    valid = (positions[None, :] < lengths[:, None]).astype(single)[..., None]
    cosine_table, sine_table = rotation_tables(positions)
    inputs = tokens.astype(single)
    inverse_one = lax.rsqrt(jnp.mean(inputs * inputs, axis=-1, keepdims=True) + epsilon)
    normed_one = inputs * inverse_one
    hidden_one = (normed_one * gain_one).astype(bfloat)
    projected = jnp.einsum("gsd,de->gse", hidden_one, proj_w, preferred_element_type=single)
    query_lin = projected[..., : w_query.shape[1]]
    key_linear = projected[..., w_query.shape[1] : w_query.shape[1] + key_weight.shape[1]]
    value_lower = projected[..., -value_weight.shape[1] :].astype(bfloat)
    query_rotated = (
        apply_rotation(
            query_lin.reshape(query_groups, sequence_per_device, QUERY_HEADS, HEAD_SIZE),
            cosine_table,
            sine_table,
        )
        .astype(bfloat)
        .reshape(query_groups, sequence_per_device, QUERY_HEADS * HEAD_SIZE)
    )
    key_rotated = (
        apply_rotation(
            key_linear.reshape(query_groups, sequence_per_device, KEY_VALUE_HEADS, HEAD_SIZE),
            cosine_table,
            sine_table,
        )
        .astype(bfloat)
        .reshape(query_groups, sequence_per_device, KEY_VALUE_HEADS * HEAD_SIZE)
    )
    gathered_keys, gathered_values = (
        lax.all_gather(key_rotated, "context", axis=1, tiled=True),
        lax.all_gather(value_lower, "context", axis=1, tiled=True),
    )

    final_low = (cotangent.astype(single) * valid).astype(bfloat)
    final_low, gathered_keys, gathered_values = lax.optimization_barrier(
        (final_low, gathered_keys, gathered_values)
    )
    final_all = lax.all_gather(final_low[0], GROUP, axis=0, tiled=False)

    def attn_scores(slot_index):
        query_per_head = query_rotated[slot_index].reshape(
            sequence_per_device, KEY_VALUE_HEADS, group_ratio, HEAD_SIZE
        )
        key_per_head = gathered_keys[slot_index].reshape(sequence_total, KEY_VALUE_HEADS, HEAD_SIZE)
        scores = scale * jnp.einsum(
            "skrd,tkd->krst", query_per_head, key_per_head, preferred_element_type=single
        )
        allowed = (key_pos[None, :] <= positions[:, None]) & (
            key_pos[None, :] < lengths[slot_index]
        )
        return (jnp.where(allowed, scores, floor_score), allowed, query_per_head, key_per_head)

    slot_index = 0
    scores, allowed, query_per_head, key_per_head = attn_scores(slot_index)
    peak = jnp.max(scores, axis=-1, keepdims=True)
    raised = jnp.exp(scores - peak)
    total = jnp.sum(raised, axis=-1, keepdims=True)
    probs = raised / total
    value_per_head = gathered_values[slot_index].reshape(sequence_total, KEY_VALUE_HEADS, HEAD_SIZE)
    mixed_g = jnp.einsum(
        "krst,tkd->skrd", probs.astype(bfloat), value_per_head, preferred_element_type=single
    )
    mixed_list = [mixed_g.reshape(sequence_per_device, QUERY_HEADS * HEAD_SIZE)]
    lse_list = [peak + jnp.log(total)]
    mixed_low = jnp.stack(mixed_list).astype(bfloat)
    resid = inputs + jnp.einsum("gse,ed->gsd", mixed_low, out_w, preferred_element_type=single)
    inverse_two = lax.rsqrt(jnp.mean(resid * resid, axis=-1, keepdims=True) + epsilon)
    normed_two = resid * inverse_two
    hidden_two = (normed_two * gain_two).astype(bfloat)
    logits = jnp.einsum("gsd,de->gse", hidden_two, router_w, preferred_element_type=single)
    matches = routes[..., None] == jnp.arange(experts, dtype=jnp.int32)
    chosen = jnp.sum(jnp.where(matches, logits[:, :, None, :], 0.0), axis=-1)
    gates = jax.nn.softmax(chosen, axis=-1)
    grad_hidden, combined, scores, grad_w_gate, grad_w_up, grad_w_down = experts_on_owner(
        hidden_two[0], final_all, routes_all, router_w.T, w_gate, w_up, w_down, capacity
    )
    combined = lax.psum_scatter(combined, GROUP, scatter_dimension=0, tiled=False)
    scores = scores[:, :local_exp]
    scores = lax.all_to_all(scores, GROUP, split_axis=0, concat_axis=0, tiled=True)
    scores = scores.reshape(experts, sequence_per_device)
    grad_final = cotangent.astype(single) * valid
    grad_gates = jnp.sum(jnp.where(matches, scores.T[None, :, None, :], 0.0), axis=-1)
    gate_mean = jnp.sum(gates * grad_gates, axis=-1, keepdims=True)
    grad_chosen = gates * (grad_gates - gate_mean)
    grad_logits = jnp.sum(jnp.where(matches, grad_chosen[..., None], 0.0), axis=2).astype(bfloat)
    grad_w_router = jnp.einsum(
        "gsd,gse->de", hidden_two, grad_logits, preferred_element_type=single
    )
    grad_hidden_two = grad_hidden.astype(single)[None]
    grad_hidden_two = grad_hidden_two + jnp.einsum(
        "gse,de->gsd", grad_logits, router_w, preferred_element_type=single
    )
    grad_gain_ffn = jnp.sum(grad_hidden_two * normed_two, axis=(0, 1))
    grad_resid = norm_back(grad_hidden_two * gain_two, normed_two, inverse_two) + grad_final
    grad_attn = grad_resid.astype(bfloat)
    grad_w_out = jnp.einsum("gse,gsd->ed", mixed_low, grad_attn, preferred_element_type=single)
    mixed_gradient = jnp.einsum(
        "gsd,ed->gse", grad_attn, out_w, preferred_element_type=single
    ).astype(bfloat)
    slot_index = 0
    scores, allowed, query_per_head, key_per_head = attn_scores(slot_index)
    probs = jnp.where(allowed, jnp.exp(scores - lse_list[slot_index]), 0.0)
    value_per_head = gathered_values[slot_index].reshape(sequence_total, KEY_VALUE_HEADS, HEAD_SIZE)
    head_gradient = mixed_gradient[slot_index].reshape(
        sequence_per_device, KEY_VALUE_HEADS, group_ratio, HEAD_SIZE
    )
    grad_probs = jnp.einsum(
        "skrd,tkd->krst", head_gradient, value_per_head, preferred_element_type=single
    )
    row_delta = jnp.sum(probs * grad_probs, axis=-1, keepdims=True)
    grad_scores = (probs * (grad_probs - row_delta)).astype(bfloat)
    grad_queries = [
        (
            scale
            * jnp.einsum("krst,tkd->skrd", grad_scores, key_per_head, preferred_element_type=single)
        ).reshape(sequence_per_device, QUERY_HEADS, HEAD_SIZE)
    ]
    grad_keys = [
        (
            scale
            * jnp.einsum(
                "krst,skrd->tkd", grad_scores, query_per_head, preferred_element_type=single
            )
        ).reshape(sequence_total, KEY_VALUE_HEADS * HEAD_SIZE)
    ]
    grad_values = [
        jnp.einsum(
            "krst,skrd->tkd", probs.astype(bfloat), head_gradient, preferred_element_type=single
        ).reshape(sequence_total, KEY_VALUE_HEADS * HEAD_SIZE)
    ]
    key_gradient_rows, value_grad = (
        lax.psum_scatter(
            jnp.stack(grad_keys).astype(jnp.bfloat16), "context", scatter_dimension=1, tiled=True
        ).astype(jnp.float32),
        lax.psum_scatter(
            jnp.stack(grad_values).astype(jnp.bfloat16), "context", scatter_dimension=1, tiled=True
        ).astype(jnp.float32),
    )
    grad_query_lin = (
        inverse_rotation(jnp.stack(grad_queries), cosine_table, sine_table)
        .astype(bfloat)
        .reshape(query_groups, sequence_per_device, QUERY_HEADS * HEAD_SIZE)
    )
    grad_key_lin = (
        inverse_rotation(
            key_gradient_rows.reshape(
                query_groups, sequence_per_device, KEY_VALUE_HEADS, HEAD_SIZE
            ),
            cosine_table,
            sine_table,
        )
        .astype(bfloat)
        .reshape(query_groups, sequence_per_device, KEY_VALUE_HEADS * HEAD_SIZE)
    )
    grad_value_low = value_grad.astype(bfloat)
    grad_proj = jnp.concatenate([grad_query_lin, grad_key_lin, grad_value_low], axis=-1)
    grad_proj_w = jnp.einsum("gsd,gse->de", hidden_one, grad_proj, preferred_element_type=single)
    grad_hidden_one = jnp.einsum("gse,de->gsd", grad_proj, proj_w, preferred_element_type=single)
    grad_gain_attn = jnp.sum(grad_hidden_one * normed_one, axis=(0, 1))
    grad_tokens = norm_back(grad_hidden_one * gain_one, normed_one, inverse_one) + grad_resid
    grad_proj_w = grad_proj_w.astype(bfloat)
    grad_out_w = grad_w_out.astype(bfloat)
    combined, grad_proj_w = lax.optimization_barrier((combined, grad_proj_w))
    block_out = (valid * (resid + combined.astype(single)[None])).astype(bfloat)
    grad_small = jnp.concatenate(
        [
            grad_w_router,
            grad_gain_attn[:, None],
            grad_gain_ffn[:, None],
            jnp.zeros((MODEL_WIDTH, 128 - experts - 2), single),
        ],
        axis=1,
    ).astype(bfloat)
    if lax.axis_size("dp") == 2:
        summed, *got = sum_gradients(
            grad_proj_w, grad_small, grad_out_w, grad_w_gate, grad_w_up, grad_w_down
        )

        def both(whole, other):
            half = whole.shape[1] // 2
            own = lax.dynamic_slice_in_dim(whole, lax.axis_index("dp") * half, half, axis=1)
            return own.astype(single) + other.astype(single)

        expert_sums = tuple(
            both(whole, other)
            for whole, other in zip((grad_w_gate, grad_w_up, grad_w_down), got)
        )
    else:
        summed = lax.psum_scatter(
            jnp.concatenate([grad_proj_w, grad_small, grad_out_w], axis=1),
            EVERY,
            scatter_dimension=0,
            tiled=True,
        ).astype(single)
        expert_sums = tuple(
            lax.psum_scatter(x, "dp", scatter_dimension=1, tiled=True).astype(single)
            for x in (grad_w_gate, grad_w_up, grad_w_down)
        )
    ends = (w_query.shape[1], proj_width - value_weight.shape[1], proj_width)
    shard_grads = (
        summed[:, proj_width + experts],
        summed[:, : ends[0]],
        summed[:, ends[0] : ends[1]],
        summed[:, ends[1] : ends[2]],
        summed[:, proj_width + 128 :],
        summed[:, proj_width + experts + 1],
        summed[:, proj_width : proj_width + experts],
    )
    return (
        block_out,
        grad_tokens,
        shard_grads[0],
        shard_grads[1],
        shard_grads[2],
        shard_grads[3],
        shard_grads[4],
        shard_grads[5],
        shard_grads[6],
        expert_sums[0],
        expert_sums[1],
        expert_sums[2],
    )


def solution(mesh):
    in_specs = (
        P(("dp", "expert"), "context", None),
        P(("dp", "expert")),
        P(("dp", "expert"), "context", None),
        P(("dp", "context", "expert")),
        P(("dp", "context", "expert"), None),
        P(("dp", "context", "expert"), None),
        P(("dp", "context", "expert"), None),
        P(("dp", "context", "expert"), None),
        P(("dp", "context", "expert")),
        P(("dp", "context", "expert"), None),
        P(("context", "expert"), None, None),
        P(("context", "expert"), None, None),
        P(("context", "expert"), None, None),
        P(("dp", "expert"), "context", None),
    )
    out_specs = (
        P(("dp", "expert"), "context", None),
        P(("dp", "expert"), "context", None),
        P(("dp", "context", "expert")),
        P(("dp", "context", "expert"), None),
        P(("dp", "context", "expert"), None),
        P(("dp", "context", "expert"), None),
        P(("dp", "context", "expert"), None),
        P(("dp", "context", "expert")),
        P(("dp", "context", "expert"), None),
        P(("context", "expert"), "dp", None),
        P(("context", "expert"), "dp", None),
        P(("context", "expert"), "dp", None),
    )
    return jax.shard_map(
        on_device, mesh=mesh, in_specs=in_specs, out_specs=out_specs, check_vma=False
    )
```

```python
import functools
import math

import jax
import jax.numpy as jnp
from jax import lax
from jax.experimental import pallas as pl
from jax.experimental.pallas import tpu as pltpu
from jax.sharding import PartitionSpec as P

MODEL_WIDTH = 1536
HEAD_SIZE = 64
TOP = 8
epsilon = 1e-05
floor_score = -1e30


def rotation_tables(positions):
    half_size = HEAD_SIZE // 2
    exponent = jnp.arange(half_size, dtype=jnp.int32).astype(jnp.float32) * (2.0 / HEAD_SIZE)
    frequency = jnp.exp(-math.log(10000.0) * exponent)
    angles = frequency[:, None] * positions.astype(jnp.float32)[None, :]
    return (jnp.cos(angles), jnp.sin(angles))


def apply_rotation(values, cosine, sine):
    split = values.reshape(-1, 2, HEAD_SIZE // 2, values.shape[1])
    first = split[:, 0]
    second = split[:, 1]
    turned = jnp.stack([first * cosine - second * sine, second * cosine + first * sine], axis=1)
    return turned.reshape(values.shape)


def inverse_rotation(gradient, cosine, sine):
    return apply_rotation(gradient, cosine, -sine)


def norm_back(gradient, normed, inverse):
    return inverse * (gradient - normed * jnp.mean(gradient * normed, axis=-1, keepdims=True))


GROUP = ("context", "expert")
EVERY = ("dp", "context", "expert")


MESH_ID = pl.DeviceIdType.MESH
CHUNK = 512
HALF = 256
UP, DOWN, ACROSS, CORE, DP = 0, 1, 2, 3, 4


def contract_rows(left, right):
    return lax.dot_general(left, right, (((0,), (0,)), ((), ())), preferred_element_type=jnp.float32)


def contract_last(left, right):
    return lax.dot_general(left, right, (((1,), (1,)), ((), ())), preferred_element_type=jnp.float32)


def matmul(left, right):
    return jnp.dot(left, right, preferred_element_type=jnp.float32)


def line_order(z, step):
    half = z // 2
    inner = z + half * (3 - 2 * z)
    base = step + inner * (1 - 2 * step) * (1 - step // 2)
    return base + half * (3 - 2 * base)


def place():
    ctx = lax.axis_index("context")
    z = lax.axis_index("expert")
    y = ctx // 2
    c = ctx % 2
    inner = z + (z // 2) * (3 - 2 * z)

    def device(kind):
        if kind == UP:
            return {"context": ctx, "expert": z + 1}
        if kind == DOWN:
            return {"context": ctx, "expert": z - 1}
        if kind == ACROSS:
            return {"context": (1 - y) * 2 + c, "expert": z}
        if kind == CORE:
            return {"context": y * 2 + 1 - c, "expert": z}
        return {"dp": 1 - lax.axis_index("dp")}

    def per_side(action, more=()):
        @pl.when(z < 3)
        def _():
            action(UP)

        @pl.when(z > 0)
        def _():
            action(DOWN)

        for kind in (ACROSS, CORE, *more):
            action(kind)

    return y, c, z, inner, device, per_side


def block_id(yy, cc, zz):
    return (yy * 2 + cc) * 4 + zz


def greet(per_side, device, count, more=()):
    barrier = pltpu.get_barrier_semaphore()
    per_side(
        lambda kind: pl.semaphore_signal(
            barrier, inc=1, device_id=device(kind), device_id_type=MESH_ID
        ),
        more,
    )
    pl.semaphore_wait(barrier, count)


def swap_copies(sources, targets, j, device, send_sem, recv_sem):
    d = lax.axis_index("dp")
    copies = []
    for index, (source, target) in enumerate(zip(sources, targets)):
        half = target.shape[0]
        copies.append(
            pltpu.make_async_remote_copy(
                src_ref=source.at[j, pl.ds(pl.multiple_of((1 - d) * half, 128), half), :],
                dst_ref=target,
                send_sem=send_sem.at[index],
                recv_sem=recv_sem.at[index],
                device_id=device(DP),
                device_id_type=MESH_ID,
            )
        )
    return copies


def gather_kernel(
    query_ref,
    key_ref,
    value_ref,
    small_ref,
    out_ref,
    early_ref,
    late_ref,
    early,
    late,
    local_sem,
    early_send,
    early_core,
    early_recv,
    late_send,
    late_dp,
    late_recv,
):
    y, c, z, inner, device, per_side = place()
    d = lax.axis_index("dp")
    mine = d * 16 + block_id(y, c, z)
    loads = []
    at = 0
    for index, ref in enumerate((query_ref, key_ref, value_ref, small_ref)):
        size = ref.shape[1]
        loads.append(
            pltpu.make_async_copy(ref, early.at[mine, :, pl.ds(at, size)], local_sem.at[index])
        )
        at += size
    loads.append(pltpu.make_async_copy(out_ref, late.at[mine], local_sem.at[4]))
    for copy in loads:
        copy.start()
    greet(per_side, device, 4 + inner, (DP,))
    for copy in loads:
        copy.wait()

    def early_copy(kind, slot, sem):
        return pltpu.make_async_remote_copy(
            src_ref=early.at[slot],
            dst_ref=early.at[slot],
            send_sem=sem,
            recv_sem=early_recv.at[slot],
            device_id=device(kind),
            device_id_type=MESH_ID,
        )

    def early_own(kind, block):
        return early_copy(kind, d * 16 + block, early_send.at[kind, block])

    def early_other(block):
        return early_copy(CORE, (1 - d) * 16 + block, early_core.at[block])

    def late_copy(kind, slot, sem):
        return pltpu.make_async_remote_copy(
            src_ref=late.at[slot],
            dst_ref=late.at[slot],
            send_sem=sem,
            recv_sem=late_recv.at[slot],
            device_id=device(kind),
            device_id_type=MESH_ID,
        )

    def late_own(kind, plane, block):
        slot = plane * 16 + block
        return late_copy(kind, slot, late_send.at[kind, slot])

    def along(kind, zz):
        if kind == UP:
            return jnp.logical_and(z < 3, zz <= z)
        return jnp.logical_and(z > 0, zz >= z)

    def fan(zz, act):
        block = block_id(y, c, zz)
        for kind in (UP, DOWN):

            @pl.when(along(kind, zz))
            def _():
                act(early_own(kind, block))
                act(late_own(kind, d, block))

        for kind in (ACROSS, CORE):
            act(early_own(kind, block))
            act(late_own(kind, d, block))
        act(early_own(DP, block))

    def fan_other(zz, act):
        block = block_id(y, c, zz)
        for kind in (UP, DOWN):

            @pl.when(along(kind, zz))
            def _():
                act(late_own(kind, 1 - d, block))

        for kind in (ACROSS, CORE):
            act(late_own(kind, 1 - d, block))

    def fan_across(zz, act):
        block = block_id(1 - y, c, zz)
        act(early_own(CORE, block))
        act(early_own(DP, block))
        act(late_own(CORE, d, block))
        act(late_own(CORE, 1 - d, block))

    def fan_dp(zz, act):
        act(early_other(block_id(y, c, zz)))
        act(early_other(block_id(1 - y, c, zz)))

    start = lambda copy: copy.start()
    over_dp = late_copy(DP, mine, late_dp)
    over_dp.start()
    fan(z, start)

    def arrive(step, carry):
        @pl.when(step < 4)
        def _():
            zz = line_order(z, step)
            block = block_id(y, c, zz)

            @pl.when(step > 0)
            def _():
                early_own(ACROSS, block).wait_recv()
                late_own(ACROSS, d, block).wait_recv()
                fan(zz, start)

            late_own(ACROSS, 1 - d, block).wait_recv()
            fan_other(zz, start)

        @pl.when(jnp.logical_and(step > 0, step < 5))
        def _():
            zz = line_order(z, jnp.maximum(step - 1, 0))
            block = block_id(1 - y, c, zz)
            early_own(CORE, block).wait_recv()
            late_own(CORE, d, block).wait_recv()
            late_own(CORE, 1 - d, block).wait_recv()
            fan_across(zz, start)

        @pl.when(step > 1)
        def _():
            zz = line_order(z, jnp.maximum(step - 2, 0))
            early_other(block_id(y, c, zz)).wait_recv()
            early_other(block_id(1 - y, c, zz)).wait_recv()
            fan_dp(zz, start)

        return carry

    lax.fori_loop(0, 6, arrive, 0)

    def finish(zz, carry):
        for yy in range(2):
            block = block_id(yy, 1 - c, zz)
            early_own(CORE, block).wait_recv()
            early_other(block).wait_recv()
            late_own(CORE, d, block).wait_recv()
            late_own(CORE, 1 - d, block).wait_recv()
        return carry

    lax.fori_loop(0, 4, finish, 0)
    results = (
        pltpu.make_async_copy(early, early_ref, local_sem.at[0]),
        pltpu.make_async_copy(late, late_ref, local_sem.at[1]),
    )
    for copy in results:
        copy.start()
    end = lambda copy: copy.wait_send()
    over_dp.wait_send()

    def ends(zz, carry):
        fan(zz, end)
        fan_other(zz, end)
        fan_across(zz, end)
        fan_dp(zz, end)
        return carry

    lax.fori_loop(0, 4, ends, 0)
    for copy in results:
        copy.wait()


def gather_weights(query, key, value, small, out):
    bfloat = jnp.bfloat16
    dma = pltpu.SemaphoreType.DMA
    rows = query.shape[0]
    early_width = query.shape[1] + key.shape[1] + value.shape[1] + small.shape[1]
    anywhere = pl.BlockSpec(memory_space=pl.ANY)
    early = (32, rows, early_width)
    late = (32, rows, out.shape[1])
    return pl.pallas_call(
        gather_kernel,
        out_shape=(jax.ShapeDtypeStruct(early, bfloat), jax.ShapeDtypeStruct(late, bfloat)),
        in_specs=[anywhere] * 5,
        out_specs=(anywhere, anywhere),
        scratch_shapes=[
            pltpu.VMEM(early, bfloat),
            pltpu.VMEM(late, bfloat),
            dma((5,)),
            dma((5, 16)),
            dma((16,)),
            dma((32,)),
            dma((4, 32)),
            dma,
            dma((32,)),
        ],
        compiler_params=pltpu.CompilerParams(
            collective_id=0, has_side_effects=True, vmem_limit_bytes=40 * 2**20
        ),
        name="gather_weights",
    )(query, key, value, small, out)


def sums_kernel(
    proj_ref,
    small_ref,
    out_ref,
    gate_ref,
    up_ref,
    down_ref,
    sum_ref,
    gate_got,
    up_got,
    down_got,
    parts,
    core_got,
    y_got,
    z_got,
    dp_got,
    load_sem,
    swap_send,
    swap_recv,
    core_send,
    core_recv,
    y_send,
    y_recv,
    z_send,
    z_recv,
    dp_send,
    dp_recv,
):
    single = jnp.float32
    bfloat = jnp.bfloat16
    y, c, z, inner, device, per_side = place()
    d = lax.axis_index("dp")
    rows = proj_ref.shape[2]
    loads = []
    at = 0
    for index, ref in enumerate((proj_ref, small_ref, out_ref)):
        size = ref.shape[3]
        for plane in range(2):
            loads.append(
                pltpu.make_async_copy(
                    ref.at[plane],
                    parts.at[:, pl.ds(plane * rows, rows), pl.ds(at, size)],
                    load_sem.at[index * 2 + plane],
                )
            )
        at += size
    for copy in loads:
        copy.start()
    greet(per_side, device, 4 + inner, (DP,))

    swaps = swap_copies(
        (gate_ref, up_ref, down_ref), (gate_got, up_got, down_got), 1, device, swap_send, swap_recv
    )
    for copy in swaps:
        copy.start()
    for copy in loads:
        copy.wait()

    def remote(kind, source, target, send_sem, recv_sem):
        return pltpu.make_async_remote_copy(
            src_ref=source,
            dst_ref=target,
            send_sem=send_sem,
            recv_sem=recv_sem,
            device_id=device(kind),
            device_id_type=MESH_ID,
        )

    def to_core(yy, zz):
        slot = yy * 4 + zz
        return remote(
            CORE, parts.at[block_id(yy, 1 - c, zz)], core_got.at[slot], core_send.at[slot], core_recv.at[slot]
        )

    def to_across(zz):
        return remote(ACROSS, parts.at[block_id(1 - y, c, zz)], y_got.at[zz], y_send.at[zz], y_recv.at[zz])

    def to_line(kind, zz, slot):
        return remote(kind, parts.at[block_id(y, c, zz)], z_got.at[slot], z_send.at[zz], z_recv.at[slot])

    def add(block, got):
        parts[block] = (parts[block].astype(single) + got.astype(single)).astype(bfloat)

    def core_sends(step, carry):
        zz = line_order(z, 3 - step)
        to_core(1 - y, zz).start()
        to_core(y, zz).start()
        return carry

    lax.fori_loop(0, 4, core_sends, 0)

    def line_sum(step):
        zz = line_order(z, step)
        block = block_id(y, c, zz)
        to_across(zz).wait_recv()
        add(block, y_got[zz])
        rising = zz > z
        comes = jnp.logical_or(jnp.logical_and(rising, z > 0), jnp.logical_and(zz < z, z < 3))

        @pl.when(comes)
        def _():
            to_line(CORE, zz, zz).wait_recv()
            add(block, z_got[zz])

        @pl.when(rising)
        def _():
            to_line(UP, zz, zz).start()

        @pl.when(zz == z - 1)
        def _():
            to_line(DOWN, zz, 4).start()

        @pl.when(zz < z - 1)
        def _():
            to_line(DOWN, zz, zz).start()

    def stage(turn, carry):
        @pl.when(turn < 4)
        def _():
            zz = line_order(z, 3 - jnp.minimum(turn, 3))
            to_core(1 - y, zz).wait_recv()
            add(block_id(1 - y, c, zz), core_got[(1 - y) * 4 + zz])
            to_across(zz).start()
            to_core(y, zz).wait_recv()
            add(block_id(y, c, zz), core_got[y * 4 + zz])

        @pl.when(jnp.logical_and(turn > 0, turn < 4))
        def _():
            line_sum(4 - jnp.maximum(turn, 1))

        return carry

    lax.fori_loop(0, 4, stage, 0)
    mine = block_id(y, c, z)
    to_across(z).wait_recv()
    add(mine, y_got[z])

    @pl.when(z > 0)
    def _():
        to_line(CORE, z, z).wait_recv()
        add(mine, z_got[z])

    @pl.when(z < 3)
    def _():
        to_line(CORE, z, 4).wait_recv()
        add(mine, z_got[4])

    there = pl.ds(pl.multiple_of((1 - d) * rows, 16), rows)
    here = pl.ds(pl.multiple_of(d * rows, 16), rows)
    last = remote(DP, parts.at[mine, there, :], dp_got, dp_send, dp_recv)
    last.start()
    last.wait_recv()
    sum_ref[...] = parts[mine, here, :].astype(single) + dp_got[...].astype(single)
    last.wait_send()
    for copy in swaps:
        copy.wait()

    def ends(zz, carry):
        to_core(y, zz).wait_send()
        to_core(1 - y, zz).wait_send()
        to_across(zz).wait_send()

        @pl.when(zz != z)
        def _():
            to_line(CORE, zz, zz).wait_send()

        return carry

    lax.fori_loop(0, 4, ends, 0)


def sum_gradients(proj, small, out, gate, up, down):
    bfloat = jnp.bfloat16
    dma = pltpu.SemaphoreType.DMA
    rows = proj.shape[0] // 32
    parts = [x.reshape(2, 16, rows, x.shape[1]) for x in (proj, small, out)]
    width = sum(x.shape[3] for x in parts)
    anywhere = pl.BlockSpec(memory_space=pl.ANY)
    halves = [(x.shape[1] // 2, x.shape[2]) for x in (gate, up, down)]
    return pl.pallas_call(
        sums_kernel,
        out_shape=(
            jax.ShapeDtypeStruct((rows, width), jnp.float32),
            *(jax.ShapeDtypeStruct(shape, bfloat) for shape in halves),
        ),
        in_specs=[anywhere] * 6,
        out_specs=(pl.BlockSpec(memory_space=pltpu.VMEM), anywhere, anywhere, anywhere),
        scratch_shapes=[
            pltpu.VMEM((16, 2 * rows, width), bfloat),
            pltpu.VMEM((8, 2 * rows, width), bfloat),
            pltpu.VMEM((4, 2 * rows, width), bfloat),
            pltpu.VMEM((5, 2 * rows, width), bfloat),
            pltpu.VMEM((rows, width), bfloat),
            dma((6,)),
            dma((6,)),
            dma((6,)),
            dma((8,)),
            dma((8,)),
            dma((4,)),
            dma((4,)),
            dma((4,)),
            dma((5,)),
            dma,
            dma,
        ],
        compiler_params=pltpu.CompilerParams(
            collective_id=2, has_side_effects=True, vmem_limit_bytes=40 * 2**20
        ),
        name="sum_gradients",
    )(*parts, gate, up, down)


def fill_bias(length_ref, bias, ctx):
    blocks, keys, queries = bias.shape
    row = lax.broadcasted_iota(jnp.int32, (keys, queries), 0)
    column = lax.broadcasted_iota(jnp.int32, (keys, queries), 1) + ctx * queries
    for j in range(blocks):
        key = row + j * keys
        allowed = jnp.logical_and(key <= column, key < length_ref[0])
        bias[j] = jnp.where(allowed, 0.0, floor_score)


def head_probs(query, keys, bias):
    scores = [contract_rows(key, query) + bias[j] for j, key in enumerate(keys)]
    peak = jnp.max(scores[0], axis=0, keepdims=True)
    for score in scores[1:]:
        peak = jnp.maximum(peak, jnp.max(score, axis=0, keepdims=True))
    raised = [jnp.exp(score - peak) for score in scores]
    total = jnp.sum(raised[0], axis=0, keepdims=True)
    for value in raised[1:]:
        total = total + jnp.sum(value, axis=0, keepdims=True)
    inverse = 1.0 / total
    return [value * inverse for value in raised]


def attend_kernel(
    query_ref, own_ref, length_ref, mixed_ref, all_ref, pairs, bias, local_sem, send_sem, recv_sem
):
    bfloat = jnp.bfloat16
    y, c, _, _, device, _ = place()
    mine = y * 2 + c
    own = pltpu.make_async_copy(own_ref, pairs.at[mine], local_sem)
    own.start()
    barrier = pltpu.get_barrier_semaphore()
    for kind in (ACROSS, CORE):
        pl.semaphore_signal(barrier, inc=1, device_id=device(kind), device_id_type=MESH_ID)
    pl.semaphore_wait(barrier, 2)
    own.wait()

    def send(kind, slot, index):
        return pltpu.make_async_remote_copy(
            src_ref=pairs.at[slot],
            dst_ref=pairs.at[slot],
            send_sem=send_sem.at[index],
            recv_sem=recv_sem.at[slot],
            device_id=device(kind),
            device_id_type=MESH_ID,
        )

    across = send(ACROSS, mine, 0)
    core = send(CORE, mine, 1)
    onward = send(CORE, (1 - y) * 2 + c, 2)
    across.start()
    core.start()
    fill_bias(length_ref, bias, mine)
    send(ACROSS, (1 - y) * 2 + c, 0).wait_recv()
    onward.start()
    send(CORE, y * 2 + 1 - c, 1).wait_recv()
    send(CORE, (1 - y) * 2 + 1 - c, 2).wait_recv()
    result = pltpu.make_async_copy(pairs, all_ref, local_sem)
    result.start()
    blocks = pairs.shape[0]
    half = pairs.shape[1] // 2
    ratio = query_ref.shape[0] // half

    def group(g, carry):
        rows = pl.ds(pl.multiple_of(g * HEAD_SIZE, HEAD_SIZE), HEAD_SIZE)
        low = pl.ds(pl.multiple_of(half + g * HEAD_SIZE, HEAD_SIZE), HEAD_SIZE)
        keys = [pairs[j, rows, :] for j in range(blocks)]
        values = [pairs[j, low, :] for j in range(blocks)]
        for r in range(ratio):
            head = pl.ds(pl.multiple_of((g * ratio + r) * HEAD_SIZE, HEAD_SIZE), HEAD_SIZE)
            probs = head_probs(query_ref[head, :], keys, bias)
            total = matmul(values[0], probs[0].astype(bfloat))
            for j in range(1, blocks):
                total = total + matmul(values[j], probs[j].astype(bfloat))
            mixed_ref[head, :] = total.astype(bfloat)
        return carry

    lax.fori_loop(0, half // HEAD_SIZE, group, 0)
    for copy in (across, core, onward):
        copy.wait_send()
    result.wait()


def attend(query, own_pairs, lengths):
    bfloat = jnp.bfloat16
    dma = pltpu.SemaphoreType.DMA
    anywhere = pl.BlockSpec(memory_space=pl.ANY)
    vmem = pl.BlockSpec(memory_space=pltpu.VMEM)
    pairs = (4, *own_pairs.shape)
    keys = own_pairs.shape[1]
    return pl.pallas_call(
        attend_kernel,
        out_shape=(
            jax.ShapeDtypeStruct(query.shape, bfloat),
            jax.ShapeDtypeStruct(pairs, bfloat),
        ),
        in_specs=[vmem, anywhere, pl.BlockSpec(memory_space=pltpu.SMEM)],
        out_specs=(vmem, anywhere),
        scratch_shapes=[
            pltpu.VMEM(pairs, bfloat),
            pltpu.VMEM((4, keys, query.shape[1]), jnp.float32),
            dma,
            dma((3,)),
            dma((4,)),
        ],
        compiler_params=pltpu.CompilerParams(
            collective_id=3, has_side_effects=True, vmem_limit_bytes=40 * 2**20
        ),
        name="attend",
    )(query, own_pairs, lengths)


def attend_back_kernel(swap, *refs):
    query_ref, pairs_ref, grad_ref, length_ref, *refs = refs
    sources, refs = refs[:swap], refs[swap:]
    query_out, pairs_out, *refs = refs
    targets, refs = refs[:swap], refs[swap:]
    parts, core_got, y_got, bias, swap_send, swap_recv, core_send, core_recv, y_send, y_recv = refs
    bfloat = jnp.bfloat16
    single = jnp.float32
    y, c, _, _, device, _ = place()
    mine = y * 2 + c
    kinds = (ACROSS, CORE, DP) if swap else (ACROSS, CORE)
    barrier = pltpu.get_barrier_semaphore()
    for kind in kinds:
        pl.semaphore_signal(barrier, inc=1, device_id=device(kind), device_id_type=MESH_ID)
    pl.semaphore_wait(barrier, len(kinds))
    swaps = swap_copies(sources, targets, 0, device, swap_send, swap_recv)
    for copy in swaps:
        copy.start()
    fill_bias(length_ref, bias, mine)
    blocks = pairs_ref.shape[0]
    half = pairs_ref.shape[1] // 2
    ratio = query_ref.shape[0] // half
    groups = half // HEAD_SIZE
    turns = parts.shape[1]
    per_turn = groups // turns
    quarter = half // turns

    def to_core(yy, turn):
        return pltpu.make_async_remote_copy(
            src_ref=parts.at[yy * 2 + 1 - c, turn],
            dst_ref=core_got.at[turn, yy],
            send_sem=core_send.at[turn, yy],
            recv_sem=core_recv.at[turn, yy],
            device_id=device(CORE),
            device_id_type=MESH_ID,
        )

    def to_across(turn):
        return pltpu.make_async_remote_copy(
            src_ref=parts.at[(1 - y) * 2 + c, turn],
            dst_ref=y_got.at[turn],
            send_sem=y_send.at[turn],
            recv_sem=y_recv.at[turn],
            device_id=device(ACROSS),
            device_id_type=MESH_ID,
        )

    def core_stage(turn):
        to_core(1 - y, turn).start()
        to_core(y, turn).start()

    def across_stage(turn):
        to_core(1 - y, turn).wait_recv()
        slot = (1 - y) * 2 + c
        parts[slot, turn] = (
            parts[slot, turn].astype(single) + core_got[turn, 1 - y].astype(single)
        ).astype(bfloat)
        to_across(turn).start()

    def last_stage(turn):
        to_core(y, turn).wait_recv()
        to_across(turn).wait_recv()
        pairs_out[turn] = (
            parts[mine, turn].astype(single)
            + core_got[turn, y].astype(single)
            + y_got[turn].astype(single)
        )

    def group(g, carry):
        rows = pl.ds(pl.multiple_of(g * HEAD_SIZE, HEAD_SIZE), HEAD_SIZE)
        low = pl.ds(pl.multiple_of(half + g * HEAD_SIZE, HEAD_SIZE), HEAD_SIZE)
        keys = [pairs_ref[j, rows, :] for j in range(blocks)]
        values = [pairs_ref[j, low, :] for j in range(blocks)]
        grad_keys = [None] * blocks
        grad_values = [None] * blocks
        for r in range(ratio):
            head = pl.ds(pl.multiple_of((g * ratio + r) * HEAD_SIZE, HEAD_SIZE), HEAD_SIZE)
            query = query_ref[head, :]
            grad = grad_ref[head, :]
            probs = head_probs(query, keys, bias)
            grad_probs = [contract_rows(value, grad) for value in values]
            delta = jnp.sum(probs[0] * grad_probs[0], axis=0, keepdims=True)
            for j in range(1, blocks):
                delta = delta + jnp.sum(probs[j] * grad_probs[j], axis=0, keepdims=True)
            grad_query = None
            for j in range(blocks):
                low_probs = probs[j].astype(bfloat)
                grad_score = (probs[j] * (grad_probs[j] - delta)).astype(bfloat)
                terms = (
                    matmul(keys[j], grad_score),
                    contract_last(query, grad_score),
                    contract_last(grad, low_probs),
                )
                grad_query = terms[0] if j == 0 else grad_query + terms[0]
                grad_keys[j] = terms[1] if r == 0 else grad_keys[j] + terms[1]
                grad_values[j] = terms[2] if r == 0 else grad_values[j] + terms[2]
            query_out[head, :] = grad_query * HEAD_SIZE ** (-0.5)
        turn = g // per_turn
        at = pl.multiple_of((g % per_turn) * HEAD_SIZE, HEAD_SIZE)
        for j in range(blocks):
            parts[j, turn, pl.ds(at, HEAD_SIZE), :] = grad_keys[j].astype(bfloat)
            parts[j, turn, pl.ds(quarter + at, HEAD_SIZE), :] = grad_values[j].astype(bfloat)
        for index in range(turns - 1):

            @pl.when(g == (index + 1) * per_turn - 1)
            def _():
                core_stage(index)

            @pl.when(g == (index + 1) * per_turn)
            def _():
                across_stage(index)

        return carry

    lax.fori_loop(0, groups, group, 0)
    core_stage(turns - 1)
    across_stage(turns - 1)
    for turn in range(turns):
        last_stage(turn)
    for turn in range(turns):
        to_core(y, turn).wait_send()
        to_core(1 - y, turn).wait_send()
        to_across(turn).wait_send()
    for copy in swaps:
        copy.wait()


def attend_back(query, pairs, grad, lengths, expert_grads):
    bfloat = jnp.bfloat16
    single = jnp.float32
    dma = pltpu.SemaphoreType.DMA
    anywhere = pl.BlockSpec(memory_space=pl.ANY)
    vmem = pl.BlockSpec(memory_space=pltpu.VMEM)
    swap = len(expert_grads)
    blocks, rows, keys = pairs.shape
    turns = 2
    part = (turns, rows // turns, keys)
    halves = [(x.shape[1] // 2, x.shape[2]) for x in expert_grads]
    return pl.pallas_call(
        functools.partial(attend_back_kernel, swap),
        out_shape=(
            jax.ShapeDtypeStruct(query.shape, single),
            jax.ShapeDtypeStruct(part, single),
            *(jax.ShapeDtypeStruct(shape, bfloat) for shape in halves),
        ),
        in_specs=[vmem, vmem, vmem, pl.BlockSpec(memory_space=pltpu.SMEM)] + [anywhere] * swap,
        out_specs=(vmem, vmem, *([anywhere] * swap)),
        scratch_shapes=[
            pltpu.VMEM((blocks, *part), bfloat),
            pltpu.VMEM((turns, 2, *part[1:]), bfloat),
            pltpu.VMEM(part, bfloat),
            pltpu.VMEM((blocks, keys, query.shape[1]), single),
            dma((3,)),
            dma((3,)),
            dma((turns, 2)),
            dma((turns, 2)),
            dma((turns,)),
            dma((turns,)),
        ],
        compiler_params=pltpu.CompilerParams(
            collective_id=4, has_side_effects=True, vmem_limit_bytes=48 * 2**20
        ),
        name="attend_back",
    )(query, pairs, grad, lengths, *expert_grads)


def experts_kernel(
    hidden_ref,
    final_ref,
    routes_ref,
    router_ref,
    gate_hbm,
    up_hbm,
    down_hbm,
    back_ref,
    part_ref,
    score_ref,
    grad_gate_ref,
    grad_up_ref,
    grad_down_ref,
    held,
    w_gate,
    w_up,
    w_down,
    rows_in,
    rows_grad,
    slope_gate,
    slope_up,
    hidden_e,
    picks,
    row_gates,
    work,
    pool,
    before,
    gather_send,
    gather_recv,
    local_sem,
    load_sem,
    part_sem,
    sum_send,
    core_recv,
    y_recv,
    z_recv,
    ready,
):
    single = jnp.float32
    bfloat = jnp.bfloat16
    tokens_block = hidden_ref.shape[0]
    width = hidden_ref.shape[1]
    experts = router_ref.shape[0]
    local_exp = w_gate.shape[0]
    hidden_units = w_gate.shape[2]
    capacity = picks.shape[1] // local_exp
    group_rows = 4 * capacity
    ctx = lax.axis_index("context")
    z = lax.axis_index("expert")
    y = ctx // 2
    c = ctx % 2
    inner = z + (z // 2) * (3 - 2 * z)

    def device(kind):
        if kind == UP:
            return {"context": ctx, "expert": z + 1}
        if kind == DOWN:
            return {"context": ctx, "expert": z - 1}
        if kind == ACROSS:
            return {"context": (1 - y) * 2 + c, "expert": z}
        return {"context": y * 2 + 1 - c, "expert": z}

    def block_id(yy, cc, zz):
        return (yy * 2 + cc) * 4 + zz

    def per_side(action):
        @pl.when(z < 3)
        def _():
            action(UP)

        @pl.when(z > 0)
        def _():
            action(DOWN)

        action(ACROSS)
        action(CORE)

    weights = (
        pltpu.make_async_copy(gate_hbm, w_gate, load_sem.at[0]),
        pltpu.make_async_copy(up_hbm, w_up, load_sem.at[1]),
        pltpu.make_async_copy(down_hbm, w_down, load_sem.at[2]),
    )
    mine = block_id(y, c, z)
    own = pltpu.make_async_copy(hidden_ref, held.at[mine], local_sem)
    own.start()
    for copy in weights:
        copy.start()

    barrier = pltpu.get_barrier_semaphore()
    per_side(
        lambda kind: pl.semaphore_signal(
            barrier, inc=1, device_id=device(kind), device_id_type=MESH_ID
        )
    )
    pl.semaphore_wait(barrier, 3 + inner)
    own.wait()

    def spread(kind, block):
        return pltpu.make_async_remote_copy(
            src_ref=held.at[block],
            dst_ref=held.at[block],
            send_sem=gather_send.at[kind, block],
            recv_sem=gather_recv.at[block],
            device_id=device(kind),
            device_id_type=MESH_ID,
        )

    def along(kind, zz):
        if kind == UP:
            return jnp.logical_and(z < 3, zz <= z)
        return jnp.logical_and(z > 0, zz >= z)

    def send_on(zz):
        block = block_id(y, c, zz)
        for kind in (UP, DOWN):

            @pl.when(along(kind, zz))
            def _():
                spread(kind, block).start()

        spread(ACROSS, block).start()
        spread(CORE, block).start()

    def forward(step):
        zz = line_order(z, step)
        spread(ACROSS, block_id(y, c, zz)).wait_recv()
        send_on(zz)

    send_on(z)
    row = lax.broadcasted_iota(jnp.int32, (tokens_block, tokens_block), 0)
    column = lax.broadcasted_iota(jnp.int32, (tokens_block, tokens_block), 1)
    before[...] = jnp.where(row < column, 1.0, 0.0).astype(bfloat)
    for copy in weights:
        copy.wait()
    first = (ctx * 4 + z) * local_exp

    def member(zz, p):
        yy = y + (p // 2) * (1 - 2 * y)
        cc = c + (p % 2) * (1 - 2 * c)
        return block_id(yy, cc, zz)

    def load_final(zz, p):
        return pltpu.make_async_copy(final_ref.at[member(zz, p)], pool.at[p], load_sem.at[p])

    def store_part(zz, p):
        return pltpu.make_async_copy(pool.at[4 + p], part_ref.at[member(zz, p)], part_sem.at[p])

    def forward_group(step, carry):
        zz = line_order(z, step)
        after = step + 1 + inner * jnp.minimum(step, 1)

        @pl.when(after < 4)
        def _():
            forward(after)

        @pl.when(jnp.logical_and(step == 0, inner == 1))
        def _():
            forward(2)

        @pl.loop(0, 4)
        def _(p):
            load_final(zz, p).start()

        spread(CORE, block_id(y, 1 - c, zz)).wait_recv()
        spread(CORE, block_id(1 - y, c, zz)).wait_recv()
        spread(CORE, block_id(1 - y, c, zz)).start()
        spread(CORE, block_id(1 - y, 1 - c, zz)).wait_recv()

        @pl.loop(0, 4)
        def _(p):
            block = member(zz, p)
            tokens_in = held[block]
            logits = contract_last(router_ref[...], tokens_in)
            expert_row = lax.broadcasted_iota(jnp.int32, (experts, tokens_block), 0)
            routed = jnp.zeros((experts, tokens_block), single)
            for k in range(routes_ref.shape[1]):
                routed = routed + jnp.where(routes_ref[block, k : k + 1, :] == expert_row, 1.0, 0.0)
            named = routed > 0.5
            peak = jnp.max(jnp.where(named, logits, floor_score), axis=0, keepdims=True)
            raised = jnp.where(named, jnp.exp(jnp.minimum(logits - peak, 0.0)), 0.0)
            gates = raised / jnp.sum(raised, axis=0, keepdims=True)
            eight = lax.broadcasted_iota(jnp.int32, (8, tokens_block), 0)
            masks = jnp.zeros((8, tokens_block), single)
            own_mask = []
            own_gate = []
            for j in range(local_exp):
                here = expert_row == first + j
                own_mask.append(jnp.sum(jnp.where(here, routed, 0.0), axis=0, keepdims=True))
                own_gate.append(jnp.sum(jnp.where(here, gates, 0.0), axis=0, keepdims=True))
                masks = masks + jnp.where(eight == j, own_mask[j], 0.0)
            rank = matmul(masks.astype(bfloat), before[...])
            slot = lax.broadcasted_iota(jnp.int32, (capacity, tokens_block), 0).astype(single)
            for j in range(local_exp):
                hit = jnp.logical_and(slot == rank[j : j + 1, :], own_mask[j] > 0.5)
                pick = jnp.where(hit, 1.0, 0.0)
                picks[step * 4 + p, pl.ds(j * capacity, capacity), :] = pick.astype(bfloat)
                gate_column = jnp.sum(pick * own_gate[j], axis=1, keepdims=True)
                row_gates[p, pl.ds(j * capacity, capacity), :] = jnp.broadcast_to(
                    gate_column, (capacity, 128)
                )
            at = pl.multiple_of(step * group_rows + p * capacity, 32)
            for n in range(width // CHUNK):
                part = pl.ds(n * CHUNK, CHUNK)
                got = matmul(picks[step * 4 + p], held[block, :, part]).astype(bfloat)
                for j in range(local_exp):
                    rows_in[j, pl.ds(at, capacity), part] = got[j * capacity : (j + 1) * capacity]

        base = pl.multiple_of(step * group_rows, 128)
        for j in range(local_exp):
            given = rows_in[j, pl.ds(base, group_rows), :]
            for n in range(hidden_units // HALF):
                part = pl.ds(n * HALF, HALF)
                gate_pre = matmul(given, w_gate[j, :, part])
                up_pre = matmul(given, w_up[j, :, part])
                sigmoid = 1.0 / (1.0 + jnp.exp(-gate_pre))
                silu = gate_pre * sigmoid
                hidden_e[j, pl.ds(base, group_rows), part] = (silu * up_pre).astype(bfloat)
                slope_gate[j, pl.ds(base, group_rows), part] = (
                    up_pre * sigmoid * (1.0 + gate_pre * (1.0 - sigmoid))
                ).astype(bfloat)
                slope_up[j, pl.ds(base, group_rows), part] = silu.astype(bfloat)
            for n in range(width // CHUNK):
                part = pl.ds(n * CHUNK, CHUNK)
                work[j, :, part] = matmul(
                    hidden_e[j, pl.ds(base, group_rows), :], w_down[j, :, part]
                ).astype(bfloat)

        @pl.loop(0, 4)
        def _(p):
            block = member(zz, p)
            at = pl.multiple_of(step * group_rows + p * capacity, 32)
            local = pl.multiple_of(p * capacity, 32)
            pick = picks[step * 4 + p]
            weight = row_gates[p][:, 0:1]
            weighted = (pick.astype(single) * weight).astype(bfloat)
            load_final(zz, p).wait()

            @pl.when(step > 0)
            def _():
                store_part(zz, p).wait()

            row_score = jnp.zeros((local_exp * capacity, 1), single)
            for n in range(width // CHUNK):
                part = pl.ds(n * CHUNK, CHUNK)
                out = jnp.concatenate(
                    [work[j, pl.ds(local, capacity), part] for j in range(local_exp)], axis=0
                )
                pool[4 + p, :, part] = contract_rows(weighted, out).astype(bfloat)
                final = matmul(pick, pool[p, :, part])
                row_score = row_score + jnp.sum(final * out.astype(single), axis=1, keepdims=True)
                graded = (final * weight).astype(bfloat)
                for j in range(local_exp):
                    rows_grad[j, pl.ds(at, capacity), part] = graded[j * capacity : (j + 1) * capacity]
            store_part(zz, p).start()
            spread_score = pick.astype(single) * row_score
            eight = lax.broadcasted_iota(jnp.int32, (8, tokens_block), 0)
            scores = jnp.zeros((8, tokens_block), single)
            for j in range(local_exp):
                total = jnp.sum(spread_score[j * capacity : (j + 1) * capacity], axis=0, keepdims=True)
                scores = scores + jnp.where(eight == j, total, 0.0)
            score_ref[block] = scores

        return carry

    lax.fori_loop(0, 4, forward_group, 0)

    @pl.loop(0, 4)
    def _(p):
        store_part(line_order(z, 3), p).wait()

    @pl.loop(0, 4)
    def _(zz):
        block = block_id(y, c, zz)
        for kind in (UP, DOWN):

            @pl.when(along(kind, zz))
            def _():
                spread(kind, block).wait_send()

        spread(ACROSS, block).wait_send()
        spread(CORE, block).wait_send()
        spread(CORE, block_id(1 - y, c, zz)).wait_send()

    opposite = {UP: DOWN, DOWN: UP, ACROSS: ACROSS, CORE: CORE}
    per_side(
        lambda kind: pl.semaphore_signal(
            ready.at[opposite[kind]], inc=1, device_id=device(kind), device_id_type=MESH_ID
        )
    )
    per_side(lambda kind: pl.semaphore_wait(ready.at[kind], 1))

    def to_core(p, zz):
        yy = y + p * (1 - 2 * y)
        return pltpu.make_async_remote_copy(
            src_ref=pool.at[p],
            dst_ref=held.at[yy * 4 + zz],
            send_sem=sum_send.at[p],
            recv_sem=core_recv.at[yy * 4 + zz],
            device_id=device(CORE),
            device_id_type=MESH_ID,
        )

    def from_core(slot):
        return pltpu.make_async_remote_copy(
            src_ref=pool.at[0],
            dst_ref=held.at[slot],
            send_sem=sum_send.at[0],
            recv_sem=core_recv.at[slot],
            device_id=device(CORE),
            device_id_type=MESH_ID,
        )

    def to_across(turn, zz):
        return pltpu.make_async_remote_copy(
            src_ref=pool.at[2 + turn],
            dst_ref=held.at[8 + zz],
            send_sem=sum_send.at[2 + turn],
            recv_sem=y_recv.at[zz],
            device_id=device(ACROSS),
            device_id_type=MESH_ID,
        )

    def to_line(kind, turn, zz, last):
        return pltpu.make_async_remote_copy(
            src_ref=pool.at[4 + turn],
            dst_ref=pool.at[7] if last else held.at[12 + zz],
            send_sem=sum_send.at[4 + turn],
            recv_sem=z_recv.at[4 if last else zz],
            device_id=device(kind),
            device_id_type=MESH_ID,
        )

    def summed(*refs):
        total = refs[0].astype(single)
        for value in refs[1:]:
            total = total + value.astype(single)
        return total.astype(bfloat)

    def back_block(step, p, target):
        local = pl.multiple_of(p * capacity, 32)
        pick = picks[step * 4 + p]
        for n in range(width // CHUNK):
            part = pl.ds(n * CHUNK, CHUNK)
            grads = jnp.concatenate(
                [work[j, pl.ds(local, capacity), part] for j in range(local_exp)], axis=0
            )
            pool[target, :, part] = contract_rows(pick, grads).astype(bfloat)

    def line_sum(step):
        zz = line_order(z, step)
        turn = step % 2
        core_slot = y * 4 + zz
        to_across(turn, zz).wait_recv()
        rising = zz > z

        def finish(comes):
            @pl.when(comes)
            def _():
                to_line(CORE, turn, zz, False).wait_recv()
                pool[4 + turn] = summed(
                    pool[4 + turn], held[core_slot], held[8 + zz], held[12 + zz]
                )

            @pl.when(jnp.logical_not(comes))
            def _():
                pool[4 + turn] = summed(pool[4 + turn], held[core_slot], held[8 + zz])

        @pl.when(rising)
        def _():
            finish(z > 0)
            to_line(UP, turn, zz, False).start()

        @pl.when(jnp.logical_not(rising))
        def _():
            finish(z < 3)

            @pl.when(zz == z - 1)
            def _():
                to_line(DOWN, turn, zz, True).start()

            @pl.when(zz < z - 1)
            def _():
                to_line(DOWN, turn, zz, False).start()

    def backward_group(turn_step, carry):
        step = 3 - turn_step
        zz = line_order(z, step)
        turn = step % 2
        base = pl.multiple_of(step * group_rows, 128)
        for j in range(local_exp):
            for n in range(hidden_units // HALF):
                part = pl.ds(n * HALF, HALF)
                grad_hidden = (
                    contract_last(rows_grad[j, pl.ds(base, group_rows), :], w_down[j, part, :])
                    .astype(bfloat)
                    .astype(single)
                )
                slope_gate[j, pl.ds(base, group_rows), part] = (
                    grad_hidden * slope_gate[j, pl.ds(base, group_rows), part].astype(single)
                ).astype(bfloat)
                slope_up[j, pl.ds(base, group_rows), part] = (
                    grad_hidden * slope_up[j, pl.ds(base, group_rows), part].astype(single)
                ).astype(bfloat)
            for n in range(width // CHUNK):
                part = pl.ds(n * CHUNK, CHUNK)
                work[j, :, part] = (
                    contract_last(slope_gate[j, pl.ds(base, group_rows), :], w_gate[j, part, :])
                    + contract_last(slope_up[j, pl.ds(base, group_rows), :], w_up[j, part, :])
                ).astype(bfloat)
        for p, member_p in ((0, 1), (1, 3)):

            @pl.when(turn_step > 0)
            def _():
                to_core(p, zz).wait_send()

            back_block(step, member_p, p)
            to_core(p, zz).start()

        @pl.when(turn_step > 1)
        def _():
            to_across(turn, zz).wait_send()
            to_line(CORE, turn, zz, False).wait_send()

        back_block(step, 2, 2 + turn)
        other = (1 - y) * 4 + zz
        from_core(other).wait_recv()
        pool[2 + turn] = summed(pool[2 + turn], held[other])
        to_across(turn, zz).start()
        back_block(step, 0, 4 + turn)
        from_core(y * 4 + zz).wait_recv()

        @pl.when(jnp.logical_and(turn_step > 0, turn_step < 3))
        def _():
            line_sum(step + 1)

        return carry

    lax.fori_loop(0, 4, backward_group, 0)

    def stores(j):
        return (
            pltpu.make_async_copy(w_gate.at[j], grad_gate_ref.at[j], load_sem.at[3 * j]),
            pltpu.make_async_copy(w_up.at[j], grad_up_ref.at[j], load_sem.at[3 * j + 1]),
            pltpu.make_async_copy(w_down.at[j], grad_down_ref.at[j], load_sem.at[3 * j + 2]),
        )

    def weight_grads(j):
        @pl.loop(0, width // CHUNK)
        def _(n):
            part = pl.ds(pl.multiple_of(n * CHUNK, CHUNK), CHUNK)
            w_gate[j, part, :] = contract_rows(rows_in[j, :, part], slope_gate[j]).astype(bfloat)
            w_up[j, part, :] = contract_rows(rows_in[j, :, part], slope_up[j]).astype(bfloat)
            w_down[j, :, part] = contract_rows(hidden_e[j], rows_grad[j, :, part]).astype(bfloat)

        for copy in stores(j):
            copy.start()

    weight_grads(0)
    line_sum(1)
    weight_grads(1)
    to_across(0, z).wait_recv()
    pool[4] = summed(pool[4], held[y * 4 + z], held[8 + z])

    @pl.when(z > 0)
    def _():
        to_line(CORE, 0, z, False).wait_recv()
        pool[4] = summed(pool[4], held[12 + z])

    @pl.when(z < 3)
    def _():
        to_line(CORE, 0, z, True).wait_recv()
        pool[4] = summed(pool[4], pool[7])

    result = pltpu.make_async_copy(pool.at[4], back_ref, local_sem)
    result.start()
    for j in range(local_exp):
        for copy in stores(j):
            copy.wait()
    for p in range(2):
        to_core(p, z).wait_send()
        to_across(p, z).wait_send()
    to_line(CORE, 1, z, False).wait_send()
    result.wait()


def experts_on_owner(hidden, final_all, routes_all, router_rows, w_gate, w_up, w_down, capacity):
    blocks = final_all.shape[0]
    tokens_block, width = hidden.shape
    local_exp, _, units = w_gate.shape
    bfloat = jnp.bfloat16
    single = jnp.float32
    rows = blocks * capacity
    anywhere = pl.BlockSpec(memory_space=pl.ANY)
    vmem = pl.BlockSpec(memory_space=pltpu.VMEM)
    dma = pltpu.SemaphoreType.DMA
    return pl.pallas_call(
        experts_kernel,
        out_shape=(
            jax.ShapeDtypeStruct((tokens_block, width), bfloat),
            jax.ShapeDtypeStruct((blocks, tokens_block, width), bfloat),
            jax.ShapeDtypeStruct((blocks, 8, tokens_block), single),
            jax.ShapeDtypeStruct(w_gate.shape, bfloat),
            jax.ShapeDtypeStruct(w_up.shape, bfloat),
            jax.ShapeDtypeStruct(w_down.shape, bfloat),
        ),
        in_specs=[anywhere, anywhere, vmem, vmem, anywhere, anywhere, anywhere],
        out_specs=(anywhere, anywhere, vmem, anywhere, anywhere, anywhere),
        scratch_shapes=[
            pltpu.VMEM((blocks, tokens_block, width), bfloat),
            pltpu.VMEM(w_gate.shape, bfloat),
            pltpu.VMEM(w_up.shape, bfloat),
            pltpu.VMEM(w_down.shape, bfloat),
            pltpu.VMEM((local_exp, rows, width), bfloat),
            pltpu.VMEM((local_exp, rows, width), bfloat),
            pltpu.VMEM((local_exp, rows, units), bfloat),
            pltpu.VMEM((local_exp, rows, units), bfloat),
            pltpu.VMEM((local_exp, rows, units), bfloat),
            pltpu.VMEM((blocks, local_exp * capacity, tokens_block), bfloat),
            pltpu.VMEM((4, local_exp * capacity, 128), single),
            pltpu.VMEM((local_exp, 4 * capacity, width), bfloat),
            pltpu.VMEM((8, tokens_block, width), bfloat),
            pltpu.VMEM((tokens_block, tokens_block), bfloat),
            dma((4, blocks)),
            dma((blocks,)),
            dma,
            dma((6,)),
            dma((4,)),
            dma((6,)),
            dma((8,)),
            dma((4,)),
            dma((5,)),
            pltpu.SemaphoreType.REGULAR((4,)),
        ],
        compiler_params=pltpu.CompilerParams(
            collective_id=1, has_side_effects=True, vmem_limit_bytes=63 * 2**20
        ),
        name="experts",
    )(hidden, final_all, routes_all, router_rows, w_gate, w_up, w_down)


def on_device(
    tokens,
    lengths,
    routes,
    gain_attn,
    w_query,
    key_weight,
    value_weight,
    w_out,
    gain_ffn,
    w_router,
    w_gate,
    w_up,
    w_down,
    cotangent,
):
    tokens_own = tokens.shape[1]
    exp_count = lax.axis_size("expert")
    ctx_count = lax.axis_size("context")
    local_exp = w_gate.shape[0]
    experts = local_exp * ctx_count * exp_count
    capacity = tokens_own * TOP * 3 // (2 * experts)
    bfloat = jnp.bfloat16
    single = jnp.float32
    query_width = w_query.shape[1]
    key_width = key_weight.shape[1]
    proj_width = query_width + 2 * key_width
    own_rows = w_query.shape[0]
    pair = lax.axis_size("dp") == 2
    small = jnp.concatenate(
        [
            w_router,
            gain_attn[:, None],
            gain_ffn[:, None],
            jnp.zeros((own_rows, 64 - experts - 2), bfloat),
        ],
        axis=1,
    )
    if pair:
        packed = routes.reshape(-1, 64).astype(bfloat)
        packed = jnp.pad(packed, ((0, own_rows - packed.shape[0]), (0, 0)))
        early, late = gather_weights(
            w_query, key_weight, value_weight, jnp.concatenate([small, packed], axis=1), w_out
        )
        routes_all = lax.dynamic_slice(
            early,
            (lax.axis_index("dp") * 16, 0, proj_width + 64),
            (16, tokens_own * TOP // 64, 64),
        )
        routes_all = routes_all.astype(jnp.int32).reshape(16, tokens_own, TOP)
        routes_all = routes_all.swapaxes(1, 2)
        early = early.reshape(-1, early.shape[2])
        out_w = late.reshape(-1, late.shape[2])
    else:
        early = jnp.concatenate([w_query, key_weight, value_weight, small], axis=1)
        early = lax.all_gather(early, EVERY, axis=0, tiled=True)
        out_w = lax.all_gather(w_out, EVERY, axis=0, tiled=True)
        routes_all = lax.all_gather(routes[0].T, GROUP, axis=0, tiled=False)
    positions = lax.axis_index("context") * tokens_own + jnp.arange(tokens_own, dtype=jnp.int32)
    valid = (positions < lengths[0]).astype(single)[:, None]
    grad_final = cotangent[0].astype(single) * valid
    final_low, early = lax.optimization_barrier((grad_final.astype(bfloat), early))
    final_all = lax.all_gather(final_low, GROUP, axis=0, tiled=False)
    proj_w = early[:, :proj_width]
    router_w = early[:, proj_width : proj_width + experts]
    gain_one = early[:, proj_width + experts].astype(single)
    gain_two = early[:, proj_width + experts + 1].astype(single)
    cosine, sine = rotation_tables(positions)

    inputs = tokens[0].astype(single)
    inverse_one = lax.rsqrt(jnp.mean(inputs * inputs, axis=-1, keepdims=True) + epsilon)
    normed_one = inputs * inverse_one
    hidden_one = (normed_one * gain_one).astype(bfloat)
    projected = jnp.einsum("de,sd->es", proj_w, hidden_one, preferred_element_type=single)
    rotated = apply_rotation(projected[: query_width + key_width], cosine, sine).astype(bfloat)
    query = rotated[:query_width] * HEAD_SIZE ** (-0.5)
    own_pairs = jnp.concatenate(
        [rotated[query_width:], projected[query_width + key_width :].astype(bfloat)], axis=0
    )
    mixed, pairs = attend(query, own_pairs, lengths)
    resid = inputs + jnp.einsum("es,ed->sd", mixed, out_w, preferred_element_type=single)
    inverse_two = lax.rsqrt(jnp.mean(resid * resid, axis=-1, keepdims=True) + epsilon)
    normed_two = resid * inverse_two
    hidden_two = (normed_two * gain_two).astype(bfloat)

    grad_hidden, combined, scores, grad_w_gate, grad_w_up, grad_w_down = experts_on_owner(
        hidden_two, final_all, routes_all, router_w.T, w_gate, w_up, w_down, capacity
    )
    combined = lax.psum_scatter(combined, GROUP, scatter_dimension=0, tiled=False)
    scores = lax.all_to_all(scores[:, :local_exp], GROUP, split_axis=0, concat_axis=0, tiled=True)
    grad_gates = scores.reshape(experts, tokens_own).T

    routed = jnp.any(routes[0][:, :, None] == jnp.arange(experts, dtype=jnp.int32), axis=1)
    logits = jnp.einsum("sd,de->se", hidden_two, router_w, preferred_element_type=single)
    gates = jax.nn.softmax(jnp.where(routed, logits, floor_score), axis=-1)
    gates = jnp.where(routed, gates, 0.0)
    gate_mean = jnp.sum(gates * grad_gates, axis=-1, keepdims=True)
    grad_logits = (gates * (grad_gates - gate_mean)).astype(bfloat)
    grad_w_router = jnp.einsum("sd,se->de", hidden_two, grad_logits, preferred_element_type=single)
    grad_hidden_two = grad_hidden.astype(single) + jnp.einsum(
        "se,de->sd", grad_logits, router_w, preferred_element_type=single
    )
    grad_gain_ffn = jnp.sum(grad_hidden_two * normed_two, axis=0)
    grad_resid = norm_back(grad_hidden_two * gain_two, normed_two, inverse_two) + grad_final
    grad_attn = grad_resid.astype(bfloat)

    grad_out_w = jnp.einsum("es,sd->ed", mixed, grad_attn, preferred_element_type=single)
    grad_mixed = jnp.einsum("ed,sd->es", out_w, grad_attn, preferred_element_type=single)
    expert_grads = (grad_w_gate, grad_w_up, grad_w_down)
    grad_query, grad_pairs, *first_got = attend_back(
        query, pairs, grad_mixed.astype(bfloat), lengths, expert_grads if pair else ()
    )
    grad_pairs = grad_pairs.reshape(2, 2, key_width // 2, tokens_own)
    grad_key = grad_pairs[:, 0].reshape(key_width, tokens_own)
    grad_value = grad_pairs[:, 1].reshape(key_width, tokens_own)
    grad_proj = jnp.concatenate(
        [
            inverse_rotation(grad_query, cosine, sine),
            inverse_rotation(grad_key, cosine, sine),
            grad_value,
        ],
        axis=0,
    ).astype(bfloat)
    grad_proj_w = jnp.einsum("sd,es->de", hidden_one, grad_proj, preferred_element_type=single)
    grad_hidden_one = jnp.einsum("es,de->sd", grad_proj, proj_w, preferred_element_type=single)
    grad_gain_attn = jnp.sum(grad_hidden_one * normed_one, axis=0)
    grad_tokens = norm_back(grad_hidden_one * gain_one, normed_one, inverse_one) + grad_resid

    grad_small = jnp.concatenate(
        [
            grad_w_router,
            grad_gain_attn[:, None],
            grad_gain_ffn[:, None],
            jnp.zeros((MODEL_WIDTH, 128 - experts - 2), single),
        ],
        axis=1,
    ).astype(bfloat)
    grad_proj_w = grad_proj_w.astype(bfloat)
    grad_out_w = grad_out_w.astype(bfloat)
    if pair:
        summed, *last_got = sum_gradients(grad_proj_w, grad_small, grad_out_w, *expert_grads)

        def both(whole, *others):
            half = whole.shape[1] // 2
            own = lax.dynamic_slice_in_dim(whole, lax.axis_index("dp") * half, half, axis=1)
            return own.astype(single) + jnp.stack(others).astype(single)

        expert_sums = tuple(
            both(whole, *others) for whole, *others in zip(expert_grads, first_got, last_got)
        )
    else:
        summed = lax.psum_scatter(
            jnp.concatenate([grad_proj_w, grad_small, grad_out_w], axis=1),
            EVERY,
            scatter_dimension=0,
            tiled=True,
        ).astype(single)
        expert_sums = tuple(
            lax.psum_scatter(x, "dp", scatter_dimension=1, tiled=True).astype(single)
            for x in expert_grads
        )
    combined, summed = lax.optimization_barrier((combined, summed))
    block_out = (valid * (resid + combined.astype(single))).astype(bfloat)
    return (
        block_out[None],
        grad_tokens[None],
        summed[:, proj_width + experts],
        summed[:, :query_width],
        summed[:, query_width : query_width + key_width],
        summed[:, query_width + key_width : proj_width],
        summed[:, proj_width + 128 :],
        summed[:, proj_width + experts + 1],
        summed[:, proj_width : proj_width + experts],
        *expert_sums,
    )


def solution(mesh):
    in_specs = (
        P(("dp", "expert"), "context", None),
        P(("dp", "expert")),
        P(("dp", "expert"), "context", None),
        P(("dp", "context", "expert")),
        P(("dp", "context", "expert"), None),
        P(("dp", "context", "expert"), None),
        P(("dp", "context", "expert"), None),
        P(("dp", "context", "expert"), None),
        P(("dp", "context", "expert")),
        P(("dp", "context", "expert"), None),
        P(("context", "expert"), None, None),
        P(("context", "expert"), None, None),
        P(("context", "expert"), None, None),
        P(("dp", "expert"), "context", None),
    )
    out_specs = (
        P(("dp", "expert"), "context", None),
        P(("dp", "expert"), "context", None),
        P(("dp", "context", "expert")),
        P(("dp", "context", "expert"), None),
        P(("dp", "context", "expert"), None),
        P(("dp", "context", "expert"), None),
        P(("dp", "context", "expert"), None),
        P(("dp", "context", "expert")),
        P(("dp", "context", "expert"), None),
        P(("context", "expert"), "dp", None),
        P(("context", "expert"), "dp", None),
        P(("context", "expert"), "dp", None),
    )
    return jax.shard_map(
        on_device, mesh=mesh, in_specs=in_specs, out_specs=out_specs, check_vma=False
    )
```

```python
import functools
import math

import jax
import jax.numpy as jnp
from jax import lax
from jax.experimental import pallas as pl
from jax.experimental.pallas import tpu as pltpu
from jax.sharding import PartitionSpec as P

MODEL_WIDTH = 1536
HEAD_SIZE = 64
TOP = 8
epsilon = 1e-05
floor_score = -1e30


def rotation_tables(positions):
    half_size = HEAD_SIZE // 2
    exponent = jnp.arange(half_size, dtype=jnp.int32).astype(jnp.float32) * (2.0 / HEAD_SIZE)
    frequency = jnp.exp(-math.log(10000.0) * exponent)
    angles = frequency[:, None] * positions.astype(jnp.float32)[None, :]
    return (jnp.cos(angles), jnp.sin(angles))


def apply_rotation(values, cosine, sine):
    split = values.reshape(-1, 2, HEAD_SIZE // 2, values.shape[1])
    first = split[:, 0]
    second = split[:, 1]
    turned = jnp.stack([first * cosine - second * sine, second * cosine + first * sine], axis=1)
    return turned.reshape(values.shape)


def inverse_rotation(gradient, cosine, sine):
    return apply_rotation(gradient, cosine, -sine)


def norm_back(gradient, normed, inverse):
    return inverse * (gradient - normed * jnp.mean(gradient * normed, axis=-1, keepdims=True))


GROUP = ("context", "expert")
EVERY = ("dp", "context", "expert")


MESH_ID = pl.DeviceIdType.MESH
CHUNK = 512
HALF = 256
UP, DOWN, ACROSS, CORE, DP = 0, 1, 2, 3, 4


def contract_rows(left, right):
    return lax.dot_general(left, right, (((0,), (0,)), ((), ())), preferred_element_type=jnp.float32)


def contract_last(left, right):
    return lax.dot_general(left, right, (((1,), (1,)), ((), ())), preferred_element_type=jnp.float32)


def matmul(left, right):
    return jnp.dot(left, right, preferred_element_type=jnp.float32)


def line_order(z, step):
    half = z // 2
    inner = z + half * (3 - 2 * z)
    base = step + inner * (1 - 2 * step) * (1 - step // 2)
    return base + half * (3 - 2 * base)


def place():
    ctx = lax.axis_index("context")
    z = lax.axis_index("expert")
    y = ctx // 2
    c = ctx % 2
    inner = z + (z // 2) * (3 - 2 * z)

    def device(kind):
        if kind == UP:
            return {"context": ctx, "expert": z + 1}
        if kind == DOWN:
            return {"context": ctx, "expert": z - 1}
        if kind == ACROSS:
            return {"context": (1 - y) * 2 + c, "expert": z}
        if kind == CORE:
            return {"context": y * 2 + 1 - c, "expert": z}
        return {"dp": 1 - lax.axis_index("dp")}

    def per_side(action, more=()):
        @pl.when(z < 3)
        def _():
            action(UP)

        @pl.when(z > 0)
        def _():
            action(DOWN)

        for kind in (ACROSS, CORE, *more):
            action(kind)

    return y, c, z, inner, device, per_side


def block_id(yy, cc, zz):
    return (yy * 2 + cc) * 4 + zz


def greet(per_side, device, count, more=()):
    barrier = pltpu.get_barrier_semaphore()
    per_side(
        lambda kind: pl.semaphore_signal(
            barrier, inc=1, device_id=device(kind), device_id_type=MESH_ID
        ),
        more,
    )
    pl.semaphore_wait(barrier, count)


def swap_copies(pieces, device, send_sem, recv_sem):
    d = lax.axis_index("dp")
    copies = []
    for index, (source, j, target) in enumerate(pieces):
        half = target.shape[0]
        copies.append(
            pltpu.make_async_remote_copy(
                src_ref=source.at[j, pl.ds(pl.multiple_of((1 - d) * half, 128), half), :],
                dst_ref=target,
                send_sem=send_sem.at[index],
                recv_sem=recv_sem.at[index],
                device_id=device(DP),
                device_id_type=MESH_ID,
            )
        )
    return copies


def ring_sum(parts, core_got, y_got, z_got, dp_got, sems):
    single = jnp.float32
    core_send, core_recv, y_send, y_recv, z_send, z_recv, dp_send, dp_recv = sems
    y, c, z, _, device, _ = place()
    d = lax.axis_index("dp")
    rows = parts.shape[1] // 2
    mine = block_id(y, c, z)

    def remote(kind, source, target, send_sem, recv_sem):
        return pltpu.make_async_remote_copy(
            src_ref=source,
            dst_ref=target,
            send_sem=send_sem,
            recv_sem=recv_sem,
            device_id=device(kind),
            device_id_type=MESH_ID,
        )

    def to_core(yy, zz):
        slot = yy * 4 + zz
        return remote(
            CORE, parts.at[block_id(yy, 1 - c, zz)], core_got.at[slot], core_send.at[slot], core_recv.at[slot]
        )

    def to_across(zz):
        return remote(ACROSS, parts.at[block_id(1 - y, c, zz)], y_got.at[zz], y_send.at[zz], y_recv.at[zz])

    def to_line(kind, zz, slot):
        return remote(kind, parts.at[block_id(y, c, zz)], z_got.at[slot], z_send.at[zz], z_recv.at[slot])

    def add(block, got):
        parts[block] = (parts[block].astype(single) + got.astype(single)).astype(parts.dtype)

    def core_sends():
        @pl.loop(0, 4)
        def _(turn):
            zz = line_order(z, 3 - turn)
            to_core(1 - y, zz).start()
            to_core(y, zz).start()

    def across(step):
        zz = line_order(z, step)
        to_core(1 - y, zz).wait_recv()
        add(block_id(1 - y, c, zz), core_got[(1 - y) * 4 + zz])
        to_across(zz).start()
        to_core(y, zz).wait_recv()
        add(block_id(y, c, zz), core_got[y * 4 + zz])

    def line(step):
        zz = line_order(z, step)
        block = block_id(y, c, zz)
        to_across(zz).wait_recv()
        add(block, y_got[zz])
        rising = zz > z
        comes = jnp.logical_or(jnp.logical_and(rising, z > 0), jnp.logical_and(zz < z, z < 3))

        @pl.when(comes)
        def _():
            to_line(CORE, zz, zz).wait_recv()
            add(block, z_got[zz])

        @pl.when(rising)
        def _():
            to_line(UP, zz, zz).start()

        @pl.when(zz == z - 1)
        def _():
            to_line(DOWN, zz, 4).start()

        @pl.when(zz < z - 1)
        def _():
            to_line(DOWN, zz, zz).start()

    there = pl.ds(pl.multiple_of((1 - d) * rows, 16), rows)
    here = pl.ds(pl.multiple_of(d * rows, 16), rows)
    last = remote(DP, parts.at[mine, there, :], dp_got, dp_send, dp_recv)

    def over_dp():
        to_across(z).wait_recv()
        add(mine, y_got[z])

        @pl.when(z > 0)
        def _():
            to_line(CORE, z, z).wait_recv()
            add(mine, z_got[z])

        @pl.when(z < 3)
        def _():
            to_line(CORE, z, 4).wait_recv()
            add(mine, z_got[4])

        last.start()

    def finish(result):
        last.wait_recv()
        result[...] = parts[mine, here, :].astype(single) + dp_got[...].astype(single)
        last.wait_send()

        @pl.loop(0, 4)
        def _(zz):
            to_core(y, zz).wait_send()
            to_core(1 - y, zz).wait_send()
            to_across(zz).wait_send()

            @pl.when(zz != z)
            def _():
                to_line(CORE, zz, zz).wait_send()

    return core_sends, across, line, over_dp, finish


def ring_scratch(rows, width):
    bfloat = jnp.bfloat16
    dma = pltpu.SemaphoreType.DMA
    return [
        pltpu.VMEM((16, 2 * rows, width), bfloat),
        pltpu.VMEM((8, 2 * rows, width), bfloat),
        pltpu.VMEM((4, 2 * rows, width), bfloat),
        pltpu.VMEM((5, 2 * rows, width), bfloat),
        pltpu.VMEM((rows, width), bfloat),
        dma((8,)),
        dma((8,)),
        dma((4,)),
        dma((4,)),
        dma((4,)),
        dma((5,)),
        dma,
        dma,
    ]


def load_parts(refs, parts, sem):
    loads = []
    at = 0
    for index, ref in enumerate(refs):
        rows, size = ref.shape[2], ref.shape[3]
        for plane in range(2):
            loads.append(
                pltpu.make_async_copy(
                    ref.at[plane],
                    parts.at[:, pl.ds(plane * rows, rows), pl.ds(at, size)],
                    sem.at[index * 2 + plane],
                )
            )
        at += size
    return loads


def gather_kernel(
    query_ref,
    key_ref,
    value_ref,
    small_ref,
    out_ref,
    proj_all,
    small_all,
    out_all,
    whole,
    local_sem,
    send_sem,
    core_sem,
    recv_sem,
):
    y, c, z, inner, device, per_side = place()
    d = lax.axis_index("dp")
    mine = d * 16 + block_id(y, c, z)
    loads = []
    at = 0
    for index, ref in enumerate((query_ref, key_ref, value_ref, small_ref, out_ref)):
        size = ref.shape[1]
        loads.append(
            pltpu.make_async_copy(ref, whole.at[mine, :, pl.ds(at, size)], local_sem.at[index])
        )
        at += size
    for copy in loads:
        copy.start()
    greet(per_side, device, 4 + inner, (DP,))
    for copy in loads:
        copy.wait()

    def copy_of(kind, slot, sem):
        return pltpu.make_async_remote_copy(
            src_ref=whole.at[slot],
            dst_ref=whole.at[slot],
            send_sem=sem,
            recv_sem=recv_sem.at[slot],
            device_id=device(kind),
            device_id_type=MESH_ID,
        )

    def own(kind, block):
        return copy_of(kind, d * 16 + block, send_sem.at[kind, block])

    def other(block):
        return copy_of(CORE, (1 - d) * 16 + block, core_sem.at[block])

    def along(kind, zz):
        if kind == UP:
            return jnp.logical_and(z < 3, zz <= z)
        return jnp.logical_and(z > 0, zz >= z)

    def fan(zz, act):
        block = block_id(y, c, zz)
        for kind in (UP, DOWN):

            @pl.when(along(kind, zz))
            def _():
                act(own(kind, block))

        for kind in (ACROSS, DP, CORE):
            act(own(kind, block))

    def fan_across(zz, act):
        block = block_id(1 - y, c, zz)
        act(own(DP, block))
        act(own(CORE, block))

    def fan_dp(zz, act):
        act(other(block_id(y, c, zz)))
        act(other(block_id(1 - y, c, zz)))

    start = lambda copy: copy.start()
    fan(z, start)

    def arrive(step, carry):
        @pl.when(jnp.logical_and(step > 0, step < 4))
        def _():
            zz = line_order(z, jnp.minimum(step, 3))
            own(ACROSS, block_id(y, c, zz)).wait_recv()
            fan(zz, start)

        @pl.when(jnp.logical_and(step > 0, step < 5))
        def _():
            zz = line_order(z, jnp.maximum(step - 1, 0))
            own(CORE, block_id(1 - y, c, zz)).wait_recv()
            fan_across(zz, start)

        @pl.when(step > 1)
        def _():
            zz = line_order(z, jnp.maximum(step - 2, 0))
            other(block_id(y, c, zz)).wait_recv()
            other(block_id(1 - y, c, zz)).wait_recv()
            fan_dp(zz, start)

        return carry

    lax.fori_loop(0, 6, arrive, 0)

    def finish(zz, carry):
        for yy in range(2):
            block = block_id(yy, 1 - c, zz)
            own(CORE, block).wait_recv()
            other(block).wait_recv()
        return carry

    lax.fori_loop(0, 4, finish, 0)
    results = []
    at = 0
    for index, ref in enumerate((proj_all, small_all, out_all)):
        size = ref.shape[2]
        results.append(
            pltpu.make_async_copy(whole.at[:, :, pl.ds(at, size)], ref, local_sem.at[index])
        )
        at += size
    for copy in results:
        copy.start()
    end = lambda copy: copy.wait_send()

    def ends(zz, carry):
        fan(zz, end)
        fan_across(zz, end)
        fan_dp(zz, end)
        return carry

    lax.fori_loop(0, 4, ends, 0)
    for copy in results:
        copy.wait()


def gather_weights(query, key, value, small, out):
    bfloat = jnp.bfloat16
    dma = pltpu.SemaphoreType.DMA
    rows = query.shape[0]
    widths = (query.shape[1] + key.shape[1] + value.shape[1], small.shape[1], out.shape[1])
    anywhere = pl.BlockSpec(memory_space=pl.ANY)
    return pl.pallas_call(
        gather_kernel,
        out_shape=tuple(jax.ShapeDtypeStruct((32, rows, width), bfloat) for width in widths),
        in_specs=[anywhere] * 5,
        out_specs=(anywhere, anywhere, anywhere),
        scratch_shapes=[
            pltpu.VMEM((32, rows, sum(widths)), bfloat),
            dma((5,)),
            dma((5, 16)),
            dma((16,)),
            dma((32,)),
        ],
        compiler_params=pltpu.CompilerParams(
            collective_id=0, has_side_effects=True, vmem_limit_bytes=60 * 2**20
        ),
        name="gather_weights",
    )(query, key, value, small, out)


def ring_sum_dp_early(parts, core_got, dp_got, y_got, z_got, sems):
    single = jnp.float32
    core_send, core_recv, dp_send, dp_recv, y_send, y_recv, z_send, z_recv = sems
    y, c, z, _, device, _ = place()
    d = lax.axis_index("dp")
    rows = parts.shape[1] // 2
    mine = block_id(y, c, z)
    there = pl.ds(pl.multiple_of((1 - d) * rows, 16), rows)
    here = pl.ds(pl.multiple_of(d * rows, 16), rows)

    def remote(kind, source, target, send_sem, recv_sem):
        return pltpu.make_async_remote_copy(
            src_ref=source,
            dst_ref=target,
            send_sem=send_sem,
            recv_sem=recv_sem,
            device_id=device(kind),
            device_id_type=MESH_ID,
        )

    def to_core(yy, zz):
        slot = yy * 4 + zz
        return remote(
            CORE, parts.at[block_id(yy, 1 - c, zz)], core_got.at[slot], core_send.at[slot], core_recv.at[slot]
        )

    def to_dp(yy, zz):
        slot = yy * 4 + zz
        return remote(
            DP, parts.at[block_id(yy, c, zz), there, :], dp_got.at[slot], dp_send.at[slot], dp_recv.at[slot]
        )

    def to_across(zz):
        return remote(
            ACROSS, parts.at[block_id(1 - y, c, zz), here, :], y_got.at[zz], y_send.at[zz], y_recv.at[zz]
        )

    def to_line(kind, zz, slot):
        return remote(
            kind, parts.at[block_id(y, c, zz), here, :], z_got.at[slot], z_send.at[zz], z_recv.at[slot]
        )

    def add(block, got):
        parts[block, here, :] = (
            parts[block, here, :].astype(single) + got.astype(single)
        ).astype(parts.dtype)

    def core_sends():
        @pl.loop(0, 4)
        def _(turn):
            zz = line_order(z, 3 - turn)
            to_core(1 - y, zz).start()
            to_core(y, zz).start()

    def meet(step):
        zz = line_order(z, step)
        for yy in (1 - y, y):
            block = block_id(yy, c, zz)
            to_core(yy, zz).wait_recv()
            parts[block] = (
                parts[block].astype(single) + core_got[yy * 4 + zz].astype(single)
            ).astype(parts.dtype)
            to_dp(yy, zz).start()

    def across(step):
        zz = line_order(z, step)
        for yy in (1 - y, y):
            to_dp(yy, zz).wait_recv()
            add(block_id(yy, c, zz), dp_got[yy * 4 + zz])
        to_across(zz).start()

    def line(step):
        zz = line_order(z, step)
        block = block_id(y, c, zz)
        to_across(zz).wait_recv()
        add(block, y_got[zz])
        rising = zz > z
        comes = jnp.logical_or(jnp.logical_and(rising, z > 0), jnp.logical_and(zz < z, z < 3))

        @pl.when(comes)
        def _():
            to_line(CORE, zz, zz).wait_recv()
            add(block, z_got[zz])

        @pl.when(rising)
        def _():
            to_line(UP, zz, zz).start()

        @pl.when(zz == z - 1)
        def _():
            to_line(DOWN, zz, 4).start()

        @pl.when(zz < z - 1)
        def _():
            to_line(DOWN, zz, zz).start()

    def finish(result):
        to_across(z).wait_recv()
        result[...] = parts[mine, here, :].astype(single) + y_got[z].astype(single)

        @pl.when(z > 0)
        def _():
            to_line(CORE, z, z).wait_recv()
            result[...] += z_got[z].astype(single)

        @pl.when(z < 3)
        def _():
            to_line(CORE, z, 4).wait_recv()
            result[...] += z_got[4].astype(single)

        @pl.loop(0, 4)
        def _(zz):
            for yy in (y, 1 - y):
                to_core(yy, zz).wait_send()
                to_dp(yy, zz).wait_send()
            to_across(zz).wait_send()

            @pl.when(zz != z)
            def _():
                to_line(CORE, zz, zz).wait_send()

    return core_sends, meet, across, line, finish


def ring_scratch_dp_early(rows, width):
    bfloat = jnp.bfloat16
    dma = pltpu.SemaphoreType.DMA
    return [
        pltpu.VMEM((16, 2 * rows, width), bfloat),
        pltpu.VMEM((8, 2 * rows, width), bfloat),
        pltpu.VMEM((8, rows, width), bfloat),
        pltpu.VMEM((4, rows, width), bfloat),
        pltpu.VMEM((5, rows, width), bfloat),
        *[dma((n,)) for n in (8, 8, 8, 8, 4, 4, 4, 5)],
    ]


def sums_kernel(
    proj_ref, small_ref, out_ref, down_ref, sum_ref, out_sum, down_got, load_sem, swap_send, swap_recv, *rings
):
    _, _, _, inner, device, per_side = place()
    ring, out_ring = rings[:13], rings[13:]
    loads = load_parts((proj_ref, small_ref), ring[0], load_sem) + load_parts(
        (out_ref,), out_ring[0], load_sem.at[pl.ds(4, 2)]
    )
    for copy in loads:
        copy.start()
    greet(per_side, device, 4 + inner, (DP,))
    for copy in loads:
        copy.wait()
    core_sends, meet, across, line, finish = ring_sum_dp_early(*ring[:5], ring[5:])
    out_core, out_across, out_line, out_dp, out_finish = ring_sum(*out_ring[:5], out_ring[5:])
    core_sends()
    out_core()

    @pl.loop(0, 4)
    def _(turn):
        meet(3 - turn)
        out_across(3 - turn)

    swaps = swap_copies(((down_ref, 1, down_got),), device, swap_send, swap_recv)
    for copy in swaps:
        copy.start()

    @pl.loop(0, 4)
    def _(turn):
        across(3 - turn)

        @pl.when(turn < 3)
        def _():
            out_line(3 - jnp.minimum(turn, 2))

        @pl.when(turn > 0)
        def _():
            line(4 - jnp.maximum(turn, 1))

    out_dp()
    finish(sum_ref)
    out_finish(out_sum)
    for copy in swaps:
        copy.wait()


def by_device(x):
    return x.reshape(2, 16, x.shape[0] // 32, x.shape[1])


def sum_gradients(proj, small, out, down):
    dma = pltpu.SemaphoreType.DMA
    anywhere = pl.BlockSpec(memory_space=pl.ANY)
    vmem = pl.BlockSpec(memory_space=pltpu.VMEM)
    rows = proj.shape[0] // 32
    width = proj.shape[1] + small.shape[1]
    return pl.pallas_call(
        sums_kernel,
        out_shape=(
            jax.ShapeDtypeStruct((rows, width), jnp.float32),
            jax.ShapeDtypeStruct((rows, out.shape[1]), jnp.float32),
            jax.ShapeDtypeStruct((down.shape[1] // 2, down.shape[2]), down.dtype),
        ),
        in_specs=[anywhere] * 4,
        out_specs=(vmem, vmem, anywhere),
        scratch_shapes=[
            dma((6,)),
            dma((1,)),
            dma((1,)),
            *ring_scratch_dp_early(rows, width),
            *ring_scratch(rows, out.shape[1]),
        ],
        compiler_params=pltpu.CompilerParams(
            collective_id=2, has_side_effects=True, vmem_limit_bytes=56 * 2**20
        ),
        name="sum_gradients",
    )(by_device(proj), by_device(small), by_device(out), down)


def fill_bias(length_ref, bias, ctx):
    blocks, keys, queries = bias.shape
    row = lax.broadcasted_iota(jnp.int32, (keys, queries), 0)
    column = lax.broadcasted_iota(jnp.int32, (keys, queries), 1) + ctx * queries
    for j in range(blocks):
        key = row + j * keys
        allowed = jnp.logical_and(key <= column, key < length_ref[0])
        bias[j] = jnp.where(allowed, 0.0, floor_score)


def head_probs(query, keys, bias):
    scores = [contract_rows(key, query) + bias[j] for j, key in enumerate(keys)]
    peak = jnp.max(scores[0], axis=0, keepdims=True)
    for score in scores[1:]:
        peak = jnp.maximum(peak, jnp.max(score, axis=0, keepdims=True))
    raised = [jnp.exp(score - peak) for score in scores]
    total = jnp.sum(raised[0], axis=0, keepdims=True)
    for value in raised[1:]:
        total = total + jnp.sum(value, axis=0, keepdims=True)
    inverse = 1.0 / total
    return [value * inverse for value in raised]


def attend_kernel(
    query_ref, own_ref, length_ref, mixed_ref, all_ref, pairs, bias, local_sem, send_sem, recv_sem
):
    bfloat = jnp.bfloat16
    y, c, _, _, device, _ = place()
    mine = y * 2 + c
    own = pltpu.make_async_copy(own_ref, pairs.at[mine], local_sem)
    own.start()
    barrier = pltpu.get_barrier_semaphore()
    for kind in (ACROSS, CORE):
        pl.semaphore_signal(barrier, inc=1, device_id=device(kind), device_id_type=MESH_ID)
    pl.semaphore_wait(barrier, 2)
    own.wait()

    def send(kind, slot, index):
        return pltpu.make_async_remote_copy(
            src_ref=pairs.at[slot],
            dst_ref=pairs.at[slot],
            send_sem=send_sem.at[index],
            recv_sem=recv_sem.at[slot],
            device_id=device(kind),
            device_id_type=MESH_ID,
        )

    across = send(ACROSS, mine, 0)
    core = send(CORE, mine, 1)
    onward = send(CORE, (1 - y) * 2 + c, 2)
    across.start()
    core.start()
    fill_bias(length_ref, bias, mine)
    send(ACROSS, (1 - y) * 2 + c, 0).wait_recv()
    onward.start()
    send(CORE, y * 2 + 1 - c, 1).wait_recv()
    send(CORE, (1 - y) * 2 + 1 - c, 2).wait_recv()
    result = pltpu.make_async_copy(pairs, all_ref, local_sem)
    result.start()
    blocks = pairs.shape[0]
    half = pairs.shape[1] // 2
    ratio = query_ref.shape[0] // half

    def group(g, carry):
        rows = pl.ds(pl.multiple_of(g * HEAD_SIZE, HEAD_SIZE), HEAD_SIZE)
        low = pl.ds(pl.multiple_of(half + g * HEAD_SIZE, HEAD_SIZE), HEAD_SIZE)
        keys = [pairs[j, rows, :] for j in range(blocks)]
        values = [pairs[j, low, :] for j in range(blocks)]
        for r in range(ratio):
            head = pl.ds(pl.multiple_of((g * ratio + r) * HEAD_SIZE, HEAD_SIZE), HEAD_SIZE)
            probs = head_probs(query_ref[head, :], keys, bias)
            total = matmul(values[0], probs[0].astype(bfloat))
            for j in range(1, blocks):
                total = total + matmul(values[j], probs[j].astype(bfloat))
            mixed_ref[head, :] = total.astype(bfloat)
        return carry

    lax.fori_loop(0, half // HEAD_SIZE, group, 0)
    for copy in (across, core, onward):
        copy.wait_send()
    result.wait()


def attend(query, own_pairs, lengths):
    bfloat = jnp.bfloat16
    dma = pltpu.SemaphoreType.DMA
    anywhere = pl.BlockSpec(memory_space=pl.ANY)
    vmem = pl.BlockSpec(memory_space=pltpu.VMEM)
    pairs = (4, *own_pairs.shape)
    keys = own_pairs.shape[1]
    return pl.pallas_call(
        attend_kernel,
        out_shape=(
            jax.ShapeDtypeStruct(query.shape, bfloat),
            jax.ShapeDtypeStruct(pairs, bfloat),
        ),
        in_specs=[vmem, anywhere, pl.BlockSpec(memory_space=pltpu.SMEM)],
        out_specs=(vmem, anywhere),
        scratch_shapes=[
            pltpu.VMEM(pairs, bfloat),
            pltpu.VMEM((4, keys, query.shape[1]), jnp.float32),
            dma,
            dma((3,)),
            dma((4,)),
        ],
        compiler_params=pltpu.CompilerParams(
            collective_id=3, has_side_effects=True, vmem_limit_bytes=40 * 2**20
        ),
        name="attend",
    )(query, own_pairs, lengths)


def attend_back_kernel(swap, *refs):
    query_ref, pairs_ref, grad_ref, length_ref, *refs = refs
    if swap:
        gate_ref, up_ref, down_ref, *refs = refs
    query_out, pairs_out, *refs = refs
    if swap:
        down_got, gate_got, up_got, *refs = refs
    parts, core_got, y_got, bias, core_send, core_recv, y_send, y_recv, *refs = refs
    bfloat = jnp.bfloat16
    single = jnp.float32
    y, c, _, _, device, _ = place()
    mine = y * 2 + c
    kinds = (ACROSS, CORE, DP) if swap else (ACROSS, CORE)
    barrier = pltpu.get_barrier_semaphore()
    for kind in kinds:
        pl.semaphore_signal(barrier, inc=1, device_id=device(kind), device_id_type=MESH_ID)
    pl.semaphore_wait(barrier, len(kinds))
    swaps = []
    if swap:
        swap_send, swap_recv = refs
        swaps = swap_copies(
            ((down_ref, 0, down_got), (gate_ref, 1, gate_got), (up_ref, 1, up_got)),
            device,
            swap_send,
            swap_recv,
        )
        for copy in swaps:
            copy.start()
    fill_bias(length_ref, bias, mine)
    blocks = pairs_ref.shape[0]
    half = pairs_ref.shape[1] // 2
    ratio = query_ref.shape[0] // half
    groups = half // HEAD_SIZE
    turns = parts.shape[1]
    per_turn = groups // turns
    quarter = half // turns

    def to_core(yy, turn):
        return pltpu.make_async_remote_copy(
            src_ref=parts.at[yy * 2 + 1 - c, turn],
            dst_ref=core_got.at[turn, yy],
            send_sem=core_send.at[turn, yy],
            recv_sem=core_recv.at[turn, yy],
            device_id=device(CORE),
            device_id_type=MESH_ID,
        )

    def to_across(turn):
        return pltpu.make_async_remote_copy(
            src_ref=parts.at[(1 - y) * 2 + c, turn],
            dst_ref=y_got.at[turn],
            send_sem=y_send.at[turn],
            recv_sem=y_recv.at[turn],
            device_id=device(ACROSS),
            device_id_type=MESH_ID,
        )

    def core_stage(turn):
        to_core(1 - y, turn).start()
        to_core(y, turn).start()

    def across_stage(turn):
        to_core(1 - y, turn).wait_recv()
        slot = (1 - y) * 2 + c
        parts[slot, turn] = (
            parts[slot, turn].astype(single) + core_got[turn, 1 - y].astype(single)
        ).astype(bfloat)
        to_across(turn).start()

    def last_stage(turn):
        to_core(y, turn).wait_recv()
        to_across(turn).wait_recv()
        pairs_out[turn] = (
            parts[mine, turn].astype(single)
            + core_got[turn, y].astype(single)
            + y_got[turn].astype(single)
        )

    def group(g, carry):
        rows = pl.ds(pl.multiple_of(g * HEAD_SIZE, HEAD_SIZE), HEAD_SIZE)
        low = pl.ds(pl.multiple_of(half + g * HEAD_SIZE, HEAD_SIZE), HEAD_SIZE)
        keys = [pairs_ref[j, rows, :] for j in range(blocks)]
        values = [pairs_ref[j, low, :] for j in range(blocks)]
        grad_keys = [None] * blocks
        grad_values = [None] * blocks
        for r in range(ratio):
            head = pl.ds(pl.multiple_of((g * ratio + r) * HEAD_SIZE, HEAD_SIZE), HEAD_SIZE)
            query = query_ref[head, :]
            grad = grad_ref[head, :]
            probs = head_probs(query, keys, bias)
            grad_probs = [contract_rows(value, grad) for value in values]
            delta = jnp.sum(probs[0] * grad_probs[0], axis=0, keepdims=True)
            for j in range(1, blocks):
                delta = delta + jnp.sum(probs[j] * grad_probs[j], axis=0, keepdims=True)
            grad_query = None
            for j in range(blocks):
                low_probs = probs[j].astype(bfloat)
                grad_score = (probs[j] * (grad_probs[j] - delta)).astype(bfloat)
                terms = (
                    matmul(keys[j], grad_score),
                    contract_last(query, grad_score),
                    contract_last(grad, low_probs),
                )
                grad_query = terms[0] if j == 0 else grad_query + terms[0]
                grad_keys[j] = terms[1] if r == 0 else grad_keys[j] + terms[1]
                grad_values[j] = terms[2] if r == 0 else grad_values[j] + terms[2]
            query_out[head, :] = grad_query * HEAD_SIZE ** (-0.5)
        turn = g // per_turn
        at = pl.multiple_of((g % per_turn) * HEAD_SIZE, HEAD_SIZE)
        for j in range(blocks):
            parts[j, turn, pl.ds(at, HEAD_SIZE), :] = grad_keys[j].astype(bfloat)
            parts[j, turn, pl.ds(quarter + at, HEAD_SIZE), :] = grad_values[j].astype(bfloat)
        for index in range(turns - 1):

            @pl.when(g == (index + 1) * per_turn - 1)
            def _():
                core_stage(index)

            @pl.when(g == (index + 1) * per_turn)
            def _():
                across_stage(index)

        return carry

    lax.fori_loop(0, groups, group, 0)
    core_stage(turns - 1)
    across_stage(turns - 1)
    for turn in range(turns):
        last_stage(turn)
    for turn in range(turns):
        to_core(y, turn).wait_send()
        to_core(1 - y, turn).wait_send()
        to_across(turn).wait_send()
    for copy in swaps:
        copy.wait()


def attend_back(query, pairs, grad, lengths, expert_grads):
    bfloat = jnp.bfloat16
    single = jnp.float32
    dma = pltpu.SemaphoreType.DMA
    anywhere = pl.BlockSpec(memory_space=pl.ANY)
    vmem = pl.BlockSpec(memory_space=pltpu.VMEM)
    swap = bool(expert_grads)
    blocks, rows, keys = pairs.shape
    turns = 2
    part = (turns, rows // turns, keys)
    more_in, more_out, more_scratch, more_specs = [], [], [], []
    if swap:
        gate, up, down = expert_grads
        more_in = [gate, up, down]
        more_out = [
            jax.ShapeDtypeStruct((x.shape[1] // 2, x.shape[2]), bfloat) for x in (down, gate, up)
        ]
        more_specs = [anywhere] * 3
        more_scratch = [dma((3,)), dma((3,))]
    return pl.pallas_call(
        functools.partial(attend_back_kernel, swap),
        out_shape=(
            jax.ShapeDtypeStruct(query.shape, single),
            jax.ShapeDtypeStruct(part, single),
            *more_out,
        ),
        in_specs=[vmem, vmem, vmem, pl.BlockSpec(memory_space=pltpu.SMEM)] + [anywhere] * len(more_in),
        out_specs=(vmem, vmem, *more_specs),
        scratch_shapes=[
            pltpu.VMEM((blocks, *part), bfloat),
            pltpu.VMEM((turns, 2, *part[1:]), bfloat),
            pltpu.VMEM(part, bfloat),
            pltpu.VMEM((blocks, keys, query.shape[1]), single),
            dma((turns, 2)),
            dma((turns, 2)),
            dma((turns,)),
            dma((turns,)),
            *more_scratch,
        ],
        compiler_params=pltpu.CompilerParams(
            collective_id=4, has_side_effects=True, vmem_limit_bytes=48 * 2**20
        ),
        name="attend_back",
    )(query, pairs, grad, lengths, *more_in)


def experts_kernel(
    swap,
    hidden_ref,
    final_ref,
    routes_ref,
    router_ref,
    gate_hbm,
    up_hbm,
    down_hbm,
    back_ref,
    part_ref,
    score_got,
    grad_gate_ref,
    grad_up_ref,
    grad_down_ref,
    *refs,
):
    gate_got, up_got, *refs = refs if swap else (None, None, *refs)
    experts_steps(
        swap,
        hidden_ref,
        final_ref,
        routes_ref,
        router_ref,
        gate_hbm,
        up_hbm,
        down_hbm,
        back_ref,
        part_ref,
        score_got,
        grad_gate_ref,
        grad_up_ref,
        grad_down_ref,
        gate_got,
        up_got,
        *refs,
    )


def experts_steps(
    swap,
    hidden_ref,
    final_ref,
    routes_ref,
    router_ref,
    gate_hbm,
    up_hbm,
    down_hbm,
    back_ref,
    part_ref,
    score_got,
    grad_gate_ref,
    grad_up_ref,
    grad_down_ref,
    gate_got,
    up_got,
    held,
    w_gate,
    w_up,
    w_down,
    rows_in,
    rows_grad,
    slope_gate,
    slope_up,
    hidden_e,
    picks,
    row_gates,
    work,
    pool,
    before,
    gather_send,
    gather_recv,
    local_sem,
    load_sem,
    part_sem,
    sum_send,
    core_recv,
    y_recv,
    z_recv,
    ready,
    score_ref,
    score_send,
    score_recv,
    swap_send,
    swap_recv,
):
    single = jnp.float32
    bfloat = jnp.bfloat16
    tokens_block = hidden_ref.shape[0]
    width = hidden_ref.shape[1]
    experts = router_ref.shape[0]
    local_exp = w_gate.shape[0]
    hidden_units = w_gate.shape[2]
    capacity = picks.shape[1] // local_exp
    group_rows = 4 * capacity
    ctx = lax.axis_index("context")
    y, c, z, inner, device, per_side = place()

    weights = (
        pltpu.make_async_copy(gate_hbm, w_gate, load_sem.at[0]),
        pltpu.make_async_copy(up_hbm, w_up, load_sem.at[1]),
        pltpu.make_async_copy(down_hbm, w_down, load_sem.at[2]),
    )
    mine = block_id(y, c, z)
    own = pltpu.make_async_copy(hidden_ref, held.at[mine], local_sem)
    own.start()
    for copy in weights:
        copy.start()

    barrier = pltpu.get_barrier_semaphore()

    def member_device(block):
        return {"context": block // 4, "expert": block % 4}

    @pl.loop(1, 16)
    def _(shift):
        pl.semaphore_signal(
            barrier,
            inc=1,
            device_id=member_device((mine + shift) % 16),
            device_id_type=MESH_ID,
        )

    if swap:
        pl.semaphore_signal(barrier, inc=1, device_id=device(DP), device_id_type=MESH_ID)
    pl.semaphore_wait(barrier, 16 if swap else 15)
    own.wait()

    def spread(kind, block):
        return pltpu.make_async_remote_copy(
            src_ref=held.at[block],
            dst_ref=held.at[block],
            send_sem=gather_send.at[kind, block],
            recv_sem=gather_recv.at[block],
            device_id=device(kind),
            device_id_type=MESH_ID,
        )

    def along(kind, zz):
        if kind == UP:
            return jnp.logical_and(z < 3, zz <= z)
        return jnp.logical_and(z > 0, zz >= z)

    def send_on(zz):
        block = block_id(y, c, zz)
        for kind in (UP, DOWN):

            @pl.when(along(kind, zz))
            def _():
                spread(kind, block).start()

        spread(ACROSS, block).start()
        spread(CORE, block).start()

    def forward(step):
        zz = line_order(z, step)
        spread(ACROSS, block_id(y, c, zz)).wait_recv()
        send_on(zz)

    send_on(z)
    row = lax.broadcasted_iota(jnp.int32, (tokens_block, tokens_block), 0)
    column = lax.broadcasted_iota(jnp.int32, (tokens_block, tokens_block), 1)
    before[...] = jnp.where(row < column, 1.0, 0.0).astype(bfloat)
    for copy in weights:
        copy.wait()
    first = (ctx * 4 + z) * local_exp

    def member(zz, p):
        yy = y + (p // 2) * (1 - 2 * y)
        cc = c + (p % 2) * (1 - 2 * c)
        return block_id(yy, cc, zz)

    def load_final(zz, p):
        return pltpu.make_async_copy(final_ref.at[member(zz, p)], pool.at[p], load_sem.at[p])

    def store_part(zz, p):
        return pltpu.make_async_copy(pool.at[4 + p], part_ref.at[member(zz, p)], part_sem.at[p])

    def forward_group(step, carry):
        zz = line_order(z, step)
        after = step + 1 + inner * jnp.minimum(step, 1)

        @pl.when(after < 4)
        def _():
            forward(after)

        @pl.when(jnp.logical_and(step == 0, inner == 1))
        def _():
            forward(2)

        @pl.loop(0, 4)
        def _(p):
            load_final(zz, p).start()

        spread(CORE, block_id(y, 1 - c, zz)).wait_recv()
        spread(CORE, block_id(1 - y, c, zz)).wait_recv()
        spread(CORE, block_id(1 - y, c, zz)).start()
        spread(CORE, block_id(1 - y, 1 - c, zz)).wait_recv()

        @pl.loop(0, 4)
        def _(p):
            block = member(zz, p)
            tokens_in = held[block]
            logits = contract_last(router_ref[...], tokens_in)
            expert_row = lax.broadcasted_iota(jnp.int32, (experts, tokens_block), 0)
            routed = jnp.zeros((experts, tokens_block), single)
            for k in range(routes_ref.shape[1]):
                routed = routed + jnp.where(routes_ref[block, k : k + 1, :] == expert_row, 1.0, 0.0)
            named = routed > 0.5
            peak = jnp.max(jnp.where(named, logits, floor_score), axis=0, keepdims=True)
            raised = jnp.where(named, jnp.exp(jnp.minimum(logits - peak, 0.0)), 0.0)
            gates = raised / jnp.sum(raised, axis=0, keepdims=True)
            eight = lax.broadcasted_iota(jnp.int32, (8, tokens_block), 0)
            masks = jnp.zeros((8, tokens_block), single)
            own_mask = []
            own_gate = []
            for j in range(local_exp):
                here = expert_row == first + j
                own_mask.append(jnp.sum(jnp.where(here, routed, 0.0), axis=0, keepdims=True))
                own_gate.append(jnp.sum(jnp.where(here, gates, 0.0), axis=0, keepdims=True))
                masks = masks + jnp.where(eight == j, own_mask[j], 0.0)
            rank = matmul(masks.astype(bfloat), before[...])
            slot = lax.broadcasted_iota(jnp.int32, (capacity, tokens_block), 0).astype(single)
            for j in range(local_exp):
                hit = jnp.logical_and(slot == rank[j : j + 1, :], own_mask[j] > 0.5)
                pick = jnp.where(hit, 1.0, 0.0)
                picks[step * 4 + p, pl.ds(j * capacity, capacity), :] = pick.astype(bfloat)
                gate_column = jnp.sum(pick * own_gate[j], axis=1, keepdims=True)
                row_gates[p, pl.ds(j * capacity, capacity), :] = jnp.broadcast_to(
                    gate_column, (capacity, 128)
                )
            at = pl.multiple_of(step * group_rows + p * capacity, 32)
            for n in range(width // CHUNK):
                part = pl.ds(n * CHUNK, CHUNK)
                got = matmul(picks[step * 4 + p], held[block, :, part]).astype(bfloat)
                for j in range(local_exp):
                    rows_in[j, pl.ds(at, capacity), part] = got[j * capacity : (j + 1) * capacity]

        base = pl.multiple_of(step * group_rows, 128)
        for j in range(local_exp):
            given = rows_in[j, pl.ds(base, group_rows), :]
            for n in range(hidden_units // HALF):
                part = pl.ds(n * HALF, HALF)
                gate_pre = matmul(given, w_gate[j, :, part])
                up_pre = matmul(given, w_up[j, :, part])
                sigmoid = 1.0 / (1.0 + jnp.exp(-gate_pre))
                silu = gate_pre * sigmoid
                hidden_e[j, pl.ds(base, group_rows), part] = (silu * up_pre).astype(bfloat)
                slope_gate[j, pl.ds(base, group_rows), part] = (
                    up_pre * sigmoid * (1.0 + gate_pre * (1.0 - sigmoid))
                ).astype(bfloat)
                slope_up[j, pl.ds(base, group_rows), part] = silu.astype(bfloat)
            for n in range(width // CHUNK):
                part = pl.ds(n * CHUNK, CHUNK)
                work[j, :, part] = matmul(
                    hidden_e[j, pl.ds(base, group_rows), :], w_down[j, :, part]
                ).astype(bfloat)

        @pl.loop(0, 4)
        def _(p):
            block = member(zz, p)
            at = pl.multiple_of(step * group_rows + p * capacity, 32)
            local = pl.multiple_of(p * capacity, 32)
            pick = picks[step * 4 + p]
            weight = row_gates[p][:, 0:1]
            weighted = (pick.astype(single) * weight).astype(bfloat)
            load_final(zz, p).wait()

            @pl.when(step > 0)
            def _():
                store_part(zz, p).wait()

            row_score = jnp.zeros((local_exp * capacity, 1), single)
            for n in range(width // CHUNK):
                part = pl.ds(n * CHUNK, CHUNK)
                out = jnp.concatenate(
                    [work[j, pl.ds(local, capacity), part] for j in range(local_exp)], axis=0
                )
                pool[4 + p, :, part] = contract_rows(weighted, out).astype(bfloat)
                final = matmul(pick, pool[p, :, part])
                row_score = row_score + jnp.sum(final * out.astype(single), axis=1, keepdims=True)
                graded = (final * weight).astype(bfloat)
                for j in range(local_exp):
                    rows_grad[j, pl.ds(at, capacity), part] = graded[j * capacity : (j + 1) * capacity]
            store_part(zz, p).start()
            spread_score = pick.astype(single) * row_score
            eight = lax.broadcasted_iota(jnp.int32, (8, tokens_block), 0)
            scores = jnp.zeros((8, tokens_block), single)
            for j in range(local_exp):
                total = jnp.sum(spread_score[j * capacity : (j + 1) * capacity], axis=0, keepdims=True)
                scores = scores + jnp.where(eight == j, total, 0.0)
            score_ref[block] = scores

        return carry

    lax.fori_loop(0, 4, forward_group, 0)

    def score_copy(block, source):
        return pltpu.make_async_remote_copy(
            src_ref=score_ref.at[block],
            dst_ref=score_got.at[source],
            send_sem=score_send.at[block],
            recv_sem=score_recv.at[source],
            device_id=member_device(block),
            device_id_type=MESH_ID,
        )

    @pl.loop(1, 16)
    def _(shift):
        score_copy((mine + shift) % 16, mine).start()

    score_got[mine] = score_ref[mine]

    @pl.loop(0, 4)
    def _(p):
        store_part(line_order(z, 3), p).wait()

    @pl.loop(0, 4)
    def _(zz):
        block = block_id(y, c, zz)
        for kind in (UP, DOWN):

            @pl.when(along(kind, zz))
            def _():
                spread(kind, block).wait_send()

        spread(ACROSS, block).wait_send()
        spread(CORE, block).wait_send()
        spread(CORE, block_id(1 - y, c, zz)).wait_send()

    opposite = {UP: DOWN, DOWN: UP, ACROSS: ACROSS, CORE: CORE}
    per_side(
        lambda kind: pl.semaphore_signal(
            ready.at[opposite[kind]], inc=1, device_id=device(kind), device_id_type=MESH_ID
        )
    )
    per_side(lambda kind: pl.semaphore_wait(ready.at[kind], 1))

    def to_core(p, zz):
        yy = y + p * (1 - 2 * y)
        return pltpu.make_async_remote_copy(
            src_ref=pool.at[p],
            dst_ref=held.at[yy * 4 + zz],
            send_sem=sum_send.at[p],
            recv_sem=core_recv.at[yy * 4 + zz],
            device_id=device(CORE),
            device_id_type=MESH_ID,
        )

    def from_core(slot):
        return pltpu.make_async_remote_copy(
            src_ref=pool.at[0],
            dst_ref=held.at[slot],
            send_sem=sum_send.at[0],
            recv_sem=core_recv.at[slot],
            device_id=device(CORE),
            device_id_type=MESH_ID,
        )

    def to_across(turn, zz):
        return pltpu.make_async_remote_copy(
            src_ref=pool.at[2 + turn],
            dst_ref=held.at[8 + zz],
            send_sem=sum_send.at[2 + turn],
            recv_sem=y_recv.at[zz],
            device_id=device(ACROSS),
            device_id_type=MESH_ID,
        )

    def to_line(kind, turn, zz, last):
        return pltpu.make_async_remote_copy(
            src_ref=pool.at[4 + turn],
            dst_ref=pool.at[7] if last else held.at[12 + zz],
            send_sem=sum_send.at[4 + turn],
            recv_sem=z_recv.at[4 if last else zz],
            device_id=device(kind),
            device_id_type=MESH_ID,
        )

    def summed(*refs):
        total = refs[0].astype(single)
        for value in refs[1:]:
            total = total + value.astype(single)
        return total.astype(bfloat)

    def back_block(step, p, target):
        local = pl.multiple_of(p * capacity, 32)
        pick = picks[step * 4 + p]
        for n in range(width // CHUNK):
            part = pl.ds(n * CHUNK, CHUNK)
            grads = jnp.concatenate(
                [work[j, pl.ds(local, capacity), part] for j in range(local_exp)], axis=0
            )
            pool[target, :, part] = contract_rows(pick, grads).astype(bfloat)

    def line_sum(step):
        zz = line_order(z, step)
        turn = step % 2
        core_slot = y * 4 + zz
        to_across(turn, zz).wait_recv()
        rising = zz > z

        def finish(comes):
            @pl.when(comes)
            def _():
                to_line(CORE, turn, zz, False).wait_recv()
                pool[4 + turn] = summed(
                    pool[4 + turn], held[core_slot], held[8 + zz], held[12 + zz]
                )

            @pl.when(jnp.logical_not(comes))
            def _():
                pool[4 + turn] = summed(pool[4 + turn], held[core_slot], held[8 + zz])

        @pl.when(rising)
        def _():
            finish(z > 0)
            to_line(UP, turn, zz, False).start()

        @pl.when(jnp.logical_not(rising))
        def _():
            finish(z < 3)

            @pl.when(zz == z - 1)
            def _():
                to_line(DOWN, turn, zz, True).start()

            @pl.when(zz < z - 1)
            def _():
                to_line(DOWN, turn, zz, False).start()

    def backward_group(turn_step, carry):
        step = 3 - turn_step
        zz = line_order(z, step)
        turn = step % 2
        base = pl.multiple_of(step * group_rows, 128)
        for j in range(local_exp):
            for n in range(hidden_units // HALF):
                part = pl.ds(n * HALF, HALF)
                grad_hidden = (
                    contract_last(rows_grad[j, pl.ds(base, group_rows), :], w_down[j, part, :])
                    .astype(bfloat)
                    .astype(single)
                )
                slope_gate[j, pl.ds(base, group_rows), part] = (
                    grad_hidden * slope_gate[j, pl.ds(base, group_rows), part].astype(single)
                ).astype(bfloat)
                slope_up[j, pl.ds(base, group_rows), part] = (
                    grad_hidden * slope_up[j, pl.ds(base, group_rows), part].astype(single)
                ).astype(bfloat)
            for n in range(width // CHUNK):
                part = pl.ds(n * CHUNK, CHUNK)
                work[j, :, part] = (
                    contract_last(slope_gate[j, pl.ds(base, group_rows), :], w_gate[j, part, :])
                    + contract_last(slope_up[j, pl.ds(base, group_rows), :], w_up[j, part, :])
                ).astype(bfloat)
        for p, member_p in ((0, 1), (1, 3)):

            @pl.when(turn_step > 0)
            def _():
                to_core(p, zz).wait_send()

            back_block(step, member_p, p)
            to_core(p, zz).start()

        @pl.when(turn_step > 1)
        def _():
            to_across(turn, zz).wait_send()
            to_line(CORE, turn, zz, False).wait_send()

        back_block(step, 2, 2 + turn)
        other = (1 - y) * 4 + zz
        from_core(other).wait_recv()
        pool[2 + turn] = summed(pool[2 + turn], held[other])
        to_across(turn, zz).start()
        back_block(step, 0, 4 + turn)
        from_core(y * 4 + zz).wait_recv()

        @pl.when(jnp.logical_and(turn_step > 0, turn_step < 3))
        def _():
            line_sum(step + 1)

        return carry

    lax.fori_loop(0, 4, backward_group, 0)

    def stores(j):
        return (
            pltpu.make_async_copy(w_gate.at[j], grad_gate_ref.at[j], load_sem.at[3 * j]),
            pltpu.make_async_copy(w_up.at[j], grad_up_ref.at[j], load_sem.at[3 * j + 1]),
            pltpu.make_async_copy(w_down.at[j], grad_down_ref.at[j], load_sem.at[3 * j + 2]),
        )

    def weight_grads(j):
        @pl.loop(0, width // CHUNK)
        def _(n):
            part = pl.ds(pl.multiple_of(n * CHUNK, CHUNK), CHUNK)
            w_gate[j, part, :] = contract_rows(rows_in[j, :, part], slope_gate[j]).astype(bfloat)
            w_up[j, part, :] = contract_rows(rows_in[j, :, part], slope_up[j]).astype(bfloat)
            w_down[j, :, part] = contract_rows(hidden_e[j], rows_grad[j, :, part]).astype(bfloat)

        for copy in stores(j):
            copy.start()

    weight_grads(0)
    swaps = []
    if swap:
        swaps = swap_copies(
            ((w_gate, 0, gate_got), (w_up, 0, up_got)), device, swap_send, swap_recv
        )
        for copy in swaps:
            copy.start()
    line_sum(1)
    weight_grads(1)
    to_across(0, z).wait_recv()
    pool[4] = summed(pool[4], held[y * 4 + z], held[8 + z])

    @pl.when(z > 0)
    def _():
        to_line(CORE, 0, z, False).wait_recv()
        pool[4] = summed(pool[4], held[12 + z])

    @pl.when(z < 3)
    def _():
        to_line(CORE, 0, z, True).wait_recv()
        pool[4] = summed(pool[4], pool[7])

    result = pltpu.make_async_copy(pool.at[4], back_ref, local_sem)
    result.start()
    for j in range(local_exp):
        for copy in stores(j):
            copy.wait()
    for p in range(2):
        to_core(p, z).wait_send()
        to_across(p, z).wait_send()
    to_line(CORE, 1, z, False).wait_send()

    @pl.loop(1, 16)
    def _(shift):
        other = (mine + shift) % 16
        score_copy(other, mine).wait_send()
        score_copy(other, other).wait_recv()

    for copy in swaps:
        copy.wait()
    result.wait()


def experts_on_owner(
    hidden, final_all, routes_all, router_rows, w_gate, w_up, w_down, capacity, swap
):
    blocks = final_all.shape[0]
    tokens_block, width = hidden.shape
    local_exp, _, units = w_gate.shape
    bfloat = jnp.bfloat16
    single = jnp.float32
    rows = blocks * capacity
    anywhere = pl.BlockSpec(memory_space=pl.ANY)
    vmem = pl.BlockSpec(memory_space=pltpu.VMEM)
    dma = pltpu.SemaphoreType.DMA
    return pl.pallas_call(
        functools.partial(experts_kernel, swap),
        out_shape=(
            jax.ShapeDtypeStruct((tokens_block, width), bfloat),
            jax.ShapeDtypeStruct((blocks, tokens_block, width), bfloat),
            jax.ShapeDtypeStruct((blocks, 8, tokens_block), single),
            jax.ShapeDtypeStruct(w_gate.shape, bfloat),
            jax.ShapeDtypeStruct(w_up.shape, bfloat),
            jax.ShapeDtypeStruct(w_down.shape, bfloat),
            *([jax.ShapeDtypeStruct((width // 2, units), bfloat)] * (2 if swap else 0)),
        ),
        in_specs=[anywhere, anywhere, vmem, vmem, anywhere, anywhere, anywhere],
        out_specs=(anywhere, anywhere, vmem, *([anywhere] * (5 if swap else 3))),
        scratch_shapes=[
            pltpu.VMEM((blocks, tokens_block, width), bfloat),
            pltpu.VMEM(w_gate.shape, bfloat),
            pltpu.VMEM(w_up.shape, bfloat),
            pltpu.VMEM(w_down.shape, bfloat),
            pltpu.VMEM((local_exp, rows, width), bfloat),
            pltpu.VMEM((local_exp, rows, width), bfloat),
            pltpu.VMEM((local_exp, rows, units), bfloat),
            pltpu.VMEM((local_exp, rows, units), bfloat),
            pltpu.VMEM((local_exp, rows, units), bfloat),
            pltpu.VMEM((blocks, local_exp * capacity, tokens_block), bfloat),
            pltpu.VMEM((4, local_exp * capacity, 128), single),
            pltpu.VMEM((local_exp, 4 * capacity, width), bfloat),
            pltpu.VMEM((8, tokens_block, width), bfloat),
            pltpu.VMEM((tokens_block, tokens_block), bfloat),
            dma((4, blocks)),
            dma((blocks,)),
            dma,
            dma((6,)),
            dma((4,)),
            dma((6,)),
            dma((8,)),
            dma((4,)),
            dma((5,)),
            pltpu.SemaphoreType.REGULAR((4,)),
            pltpu.VMEM((blocks, 8, tokens_block), single),
            dma((16,)),
            dma((16,)),
            dma((2,)),
            dma((2,)),
        ],
        compiler_params=pltpu.CompilerParams(
            collective_id=1, has_side_effects=True, vmem_limit_bytes=63 * 2**20
        ),
        name="experts",
    )(hidden, final_all, routes_all, router_rows, w_gate, w_up, w_down)


def on_device(
    tokens,
    lengths,
    routes,
    gain_attn,
    w_query,
    key_weight,
    value_weight,
    w_out,
    gain_ffn,
    w_router,
    w_gate,
    w_up,
    w_down,
    cotangent,
):
    tokens_own = tokens.shape[1]
    exp_count = lax.axis_size("expert")
    ctx_count = lax.axis_size("context")
    local_exp = w_gate.shape[0]
    experts = local_exp * ctx_count * exp_count
    capacity = tokens_own * TOP * 3 // (2 * experts)
    bfloat = jnp.bfloat16
    single = jnp.float32
    query_width = w_query.shape[1]
    key_width = key_weight.shape[1]
    proj_width = query_width + 2 * key_width
    own_rows = w_query.shape[0]
    pair = lax.axis_size("dp") == 2
    small = jnp.concatenate(
        [
            w_router,
            gain_attn[:, None],
            gain_ffn[:, None],
            jnp.zeros((own_rows, 64 - experts - 2), bfloat),
        ],
        axis=1,
    )
    if pair:
        packed = routes[0].T.reshape(-1, 64).astype(bfloat)
        packed = jnp.pad(packed, ((0, own_rows - packed.shape[0]), (0, 0)))
        early, small_all, late = gather_weights(
            w_query, key_weight, value_weight, jnp.concatenate([small, packed], axis=1), w_out
        )
        routes_all = lax.dynamic_slice(
            small_all, (lax.axis_index("dp") * 16, 0, 64), (16, tokens_own * TOP // 64, 64)
        )
        routes_all = routes_all.astype(jnp.int32).reshape(16, TOP, tokens_own)
        proj_w = early.reshape(-1, proj_width)
        small_all = small_all.reshape(-1, small_all.shape[2])
        out_w = late.reshape(-1, late.shape[2])
    else:
        proj_w = jnp.concatenate([w_query, key_weight, value_weight], axis=1)
        proj_w = lax.all_gather(proj_w, EVERY, axis=0, tiled=True)
        small_all = lax.all_gather(small, EVERY, axis=0, tiled=True)
        out_w = lax.all_gather(w_out, EVERY, axis=0, tiled=True)
        routes_all = lax.all_gather(routes[0].T, GROUP, axis=0, tiled=False)
    positions = lax.axis_index("context") * tokens_own + jnp.arange(tokens_own, dtype=jnp.int32)
    valid = (positions < lengths[0]).astype(single)[:, None]
    grad_final = cotangent[0].astype(single) * valid
    final_all = lax.all_gather(grad_final.astype(bfloat), GROUP, axis=0, tiled=False)
    router_w = small_all[:, :experts]
    gain_one = small_all[:, experts].astype(single)
    gain_two = small_all[:, experts + 1].astype(single)
    cosine, sine = rotation_tables(positions)

    inputs = tokens[0].astype(single)
    inverse_one = lax.rsqrt(jnp.mean(inputs * inputs, axis=-1, keepdims=True) + epsilon)
    normed_one = inputs * inverse_one
    hidden_one = (normed_one * gain_one).astype(bfloat)
    projected = jnp.einsum("de,sd->es", proj_w, hidden_one, preferred_element_type=single)
    rotated = apply_rotation(projected[: query_width + key_width], cosine, sine).astype(bfloat)
    query = rotated[:query_width] * HEAD_SIZE ** (-0.5)
    own_pairs = jnp.concatenate(
        [rotated[query_width:], projected[query_width + key_width :].astype(bfloat)], axis=0
    )
    mixed, pairs = attend(query, own_pairs, lengths)
    resid = inputs + jnp.einsum("es,ed->sd", mixed, out_w, preferred_element_type=single)
    inverse_two = lax.rsqrt(jnp.mean(resid * resid, axis=-1, keepdims=True) + epsilon)
    normed_two = resid * inverse_two
    hidden_two = (normed_two * gain_two).astype(bfloat)

    grad_hidden, combined, scores, *expert_grads = experts_on_owner(
        hidden_two, final_all, routes_all, router_w.T, w_gate, w_up, w_down, capacity, pair
    )
    expert_grads, got = expert_grads[:3], expert_grads[3:]
    combined = lax.psum_scatter(combined, GROUP, scatter_dimension=0, tiled=False)
    scores = scores[:, :local_exp]
    grad_gates = scores.reshape(experts, tokens_own).T

    routed = jnp.any(routes[0][:, :, None] == jnp.arange(experts, dtype=jnp.int32), axis=1)
    logits = jnp.einsum("sd,de->se", hidden_two, router_w, preferred_element_type=single)
    gates = jax.nn.softmax(jnp.where(routed, logits, floor_score), axis=-1)
    gates = jnp.where(routed, gates, 0.0)
    gate_mean = jnp.sum(gates * grad_gates, axis=-1, keepdims=True)
    grad_logits = (gates * (grad_gates - gate_mean)).astype(bfloat)
    grad_w_router = jnp.einsum("sd,se->de", hidden_two, grad_logits, preferred_element_type=single)
    grad_hidden_two = grad_hidden.astype(single) + jnp.einsum(
        "se,de->sd", grad_logits, router_w, preferred_element_type=single
    )
    grad_gain_ffn = jnp.sum(grad_hidden_two * normed_two, axis=0)
    grad_resid = norm_back(grad_hidden_two * gain_two, normed_two, inverse_two) + grad_final
    grad_attn = grad_resid.astype(bfloat)

    grad_out_w = jnp.einsum("es,sd->ed", mixed, grad_attn, preferred_element_type=single)
    grad_mixed = jnp.einsum("ed,sd->es", out_w, grad_attn, preferred_element_type=single)
    grad_out_w = grad_out_w.astype(bfloat)
    grad_query, grad_pairs, *more = attend_back(
        query,
        pairs,
        grad_mixed.astype(bfloat),
        lengths,
        expert_grads if pair else (),
    )
    grad_pairs = grad_pairs.reshape(2, 2, key_width // 2, tokens_own)
    grad_key = grad_pairs[:, 0].reshape(key_width, tokens_own)
    grad_value = grad_pairs[:, 1].reshape(key_width, tokens_own)
    grad_proj = jnp.concatenate(
        [
            inverse_rotation(grad_query, cosine, sine),
            inverse_rotation(grad_key, cosine, sine),
            grad_value,
        ],
        axis=0,
    ).astype(bfloat)
    grad_proj_w = jnp.einsum("sd,es->de", hidden_one, grad_proj, preferred_element_type=single)
    grad_hidden_one = jnp.einsum("es,de->sd", grad_proj, proj_w, preferred_element_type=single)
    grad_gain_attn = jnp.sum(grad_hidden_one * normed_one, axis=0)
    grad_tokens = norm_back(grad_hidden_one * gain_one, normed_one, inverse_one) + grad_resid

    grad_small = jnp.concatenate(
        [
            grad_w_router,
            grad_gain_attn[:, None],
            grad_gain_ffn[:, None],
            jnp.zeros((MODEL_WIDTH, 128 - experts - 2), single),
        ],
        axis=1,
    ).astype(bfloat)
    grad_proj_w = grad_proj_w.astype(bfloat)
    if pair:
        down_first, gate_last, up_last = more
        summed, out_sum, down_last = sum_gradients(
            grad_proj_w, grad_small, grad_out_w, expert_grads[2]
        )

        def both(whole, *others):
            half = whole.shape[1] // 2
            own = lax.dynamic_slice_in_dim(whole, lax.axis_index("dp") * half, half, axis=1)
            return own.astype(single) + jnp.stack(others).astype(single)

        expert_sums = tuple(
            both(whole, *others)
            for whole, *others in zip(
                expert_grads, (*got, down_first), (gate_last, up_last, down_last)
            )
        )
    else:
        summed = lax.psum_scatter(
            jnp.concatenate([grad_proj_w, grad_small, grad_out_w], axis=1),
            EVERY,
            scatter_dimension=0,
            tiled=True,
        ).astype(single)
        out_sum = summed[:, proj_width + 128 :]
        expert_sums = tuple(
            lax.psum_scatter(x, "dp", scatter_dimension=1, tiled=True).astype(single)
            for x in expert_grads
        )
    combined, summed = lax.optimization_barrier((combined, summed))
    block_out = (valid * (resid + combined.astype(single))).astype(bfloat)
    return (
        block_out[None],
        grad_tokens[None],
        summed[:, proj_width + experts],
        summed[:, :query_width],
        summed[:, query_width : query_width + key_width],
        summed[:, query_width + key_width : proj_width],
        out_sum,
        summed[:, proj_width + experts + 1],
        summed[:, proj_width : proj_width + experts],
        *expert_sums,
    )


def solution(mesh):
    in_specs = (
        P(("dp", "expert"), "context", None),
        P(("dp", "expert")),
        P(("dp", "expert"), "context", None),
        P(("dp", "context", "expert")),
        P(("dp", "context", "expert"), None),
        P(("dp", "context", "expert"), None),
        P(("dp", "context", "expert"), None),
        P(("dp", "context", "expert"), None),
        P(("dp", "context", "expert")),
        P(("dp", "context", "expert"), None),
        P(("context", "expert"), None, None),
        P(("context", "expert"), None, None),
        P(("context", "expert"), None, None),
        P(("dp", "expert"), "context", None),
    )
    out_specs = (
        P(("dp", "expert"), "context", None),
        P(("dp", "expert"), "context", None),
        P(("dp", "context", "expert")),
        P(("dp", "context", "expert"), None),
        P(("dp", "context", "expert"), None),
        P(("dp", "context", "expert"), None),
        P(("dp", "context", "expert"), None),
        P(("dp", "context", "expert")),
        P(("dp", "context", "expert"), None),
        P(("context", "expert"), "dp", None),
        P(("context", "expert"), "dp", None),
        P(("context", "expert"), "dp", None),
    )
    return jax.shard_map(
        on_device, mesh=mesh, in_specs=in_specs, out_specs=out_specs, check_vma=False
    )
```

```python
import functools
import math

import jax
import jax.numpy as jnp
from jax import lax
from jax.experimental import pallas as pl
from jax.experimental.pallas import tpu as pltpu
from jax.sharding import PartitionSpec as P

MODEL_WIDTH = 1536
HEAD_SIZE = 64
TOP = 8
epsilon = 1e-05
floor_score = -1e30


def rotation_tables(positions):
    half_size = HEAD_SIZE // 2
    exponent = jnp.arange(half_size, dtype=jnp.int32).astype(jnp.float32) * (2.0 / HEAD_SIZE)
    frequency = jnp.exp(-math.log(10000.0) * exponent)
    angles = frequency[:, None] * positions.astype(jnp.float32)[None, :]
    return (jnp.cos(angles), jnp.sin(angles))


def apply_rotation(values, cosine, sine):
    split = values.reshape(-1, 2, HEAD_SIZE // 2, values.shape[1])
    first = split[:, 0]
    second = split[:, 1]
    turned = jnp.stack([first * cosine - second * sine, second * cosine + first * sine], axis=1)
    return turned.reshape(values.shape)


def inverse_rotation(gradient, cosine, sine):
    return apply_rotation(gradient, cosine, -sine)


def norm_back(gradient, normed, inverse):
    return inverse * (gradient - normed * jnp.mean(gradient * normed, axis=-1, keepdims=True))


GROUP = ("context", "expert")
EVERY = ("dp", "context", "expert")


MESH_ID = pl.DeviceIdType.MESH
CHUNK = 512
HALF = 256
UP, DOWN, ACROSS, CORE, DP = 0, 1, 2, 3, 4


def contract_rows(left, right):
    return lax.dot_general(left, right, (((0,), (0,)), ((), ())), preferred_element_type=jnp.float32)


def contract_last(left, right):
    return lax.dot_general(left, right, (((1,), (1,)), ((), ())), preferred_element_type=jnp.float32)


def matmul(left, right):
    return jnp.dot(left, right, preferred_element_type=jnp.float32)


def line_order(z, step):
    half = z // 2
    inner = z + half * (3 - 2 * z)
    base = step + inner * (1 - 2 * step) * (1 - step // 2)
    return base + half * (3 - 2 * base)


def place():
    ctx = lax.axis_index("context")
    z = lax.axis_index("expert")
    y = ctx // 2
    c = ctx % 2
    inner = z + (z // 2) * (3 - 2 * z)

    def device(kind):
        if kind == UP:
            return {"context": ctx, "expert": z + 1}
        if kind == DOWN:
            return {"context": ctx, "expert": z - 1}
        if kind == ACROSS:
            return {"context": (1 - y) * 2 + c, "expert": z}
        if kind == CORE:
            return {"context": y * 2 + 1 - c, "expert": z}
        return {"dp": 1 - lax.axis_index("dp")}

    def per_side(action, more=()):
        @pl.when(z < 3)
        def _():
            action(UP)

        @pl.when(z > 0)
        def _():
            action(DOWN)

        for kind in (ACROSS, CORE, *more):
            action(kind)

    return y, c, z, inner, device, per_side


def block_id(yy, cc, zz):
    return (yy * 2 + cc) * 4 + zz


def greet(per_side, device, count, more=()):
    barrier = pltpu.get_barrier_semaphore()
    per_side(
        lambda kind: pl.semaphore_signal(
            barrier, inc=1, device_id=device(kind), device_id_type=MESH_ID
        ),
        more,
    )
    pl.semaphore_wait(barrier, count)


def swap_copies(pieces, device, send_sem, recv_sem):
    d = lax.axis_index("dp")
    copies = []
    for index, (source, j, target) in enumerate(pieces):
        half = target.shape[0]
        copies.append(
            pltpu.make_async_remote_copy(
                src_ref=source.at[j, pl.ds(pl.multiple_of((1 - d) * half, 128), half), :],
                dst_ref=target,
                send_sem=send_sem.at[index],
                recv_sem=recv_sem.at[index],
                device_id=device(DP),
                device_id_type=MESH_ID,
            )
        )
    return copies


def ring_sum(parts, core_got, y_got, z_got, dp_got, sems):
    single = jnp.float32
    core_send, core_recv, y_send, y_recv, z_send, z_recv, dp_send, dp_recv = sems
    y, c, z, _, device, _ = place()
    d = lax.axis_index("dp")
    rows = parts.shape[1] // 2
    mine = block_id(y, c, z)

    def remote(kind, source, target, send_sem, recv_sem):
        return pltpu.make_async_remote_copy(
            src_ref=source,
            dst_ref=target,
            send_sem=send_sem,
            recv_sem=recv_sem,
            device_id=device(kind),
            device_id_type=MESH_ID,
        )

    def to_core(yy, zz):
        slot = yy * 4 + zz
        return remote(
            CORE, parts.at[block_id(yy, 1 - c, zz)], core_got.at[slot], core_send.at[slot], core_recv.at[slot]
        )

    def to_across(zz):
        return remote(ACROSS, parts.at[block_id(1 - y, c, zz)], y_got.at[zz], y_send.at[zz], y_recv.at[zz])

    def to_line(kind, zz, slot):
        return remote(kind, parts.at[block_id(y, c, zz)], z_got.at[slot], z_send.at[zz], z_recv.at[slot])

    def add(block, got):
        parts[block] = (parts[block].astype(single) + got.astype(single)).astype(parts.dtype)

    def core_sends():
        @pl.loop(0, 4)
        def _(turn):
            zz = line_order(z, 3 - turn)
            to_core(1 - y, zz).start()
            to_core(y, zz).start()

    def across(step):
        zz = line_order(z, step)
        to_core(1 - y, zz).wait_recv()
        add(block_id(1 - y, c, zz), core_got[(1 - y) * 4 + zz])
        to_across(zz).start()
        to_core(y, zz).wait_recv()
        add(block_id(y, c, zz), core_got[y * 4 + zz])

    def line(step):
        zz = line_order(z, step)
        block = block_id(y, c, zz)
        to_across(zz).wait_recv()
        add(block, y_got[zz])
        rising = zz > z
        comes = jnp.logical_or(jnp.logical_and(rising, z > 0), jnp.logical_and(zz < z, z < 3))

        @pl.when(comes)
        def _():
            to_line(CORE, zz, zz).wait_recv()
            add(block, z_got[zz])

        @pl.when(rising)
        def _():
            to_line(UP, zz, zz).start()

        @pl.when(zz == z - 1)
        def _():
            to_line(DOWN, zz, 4).start()

        @pl.when(zz < z - 1)
        def _():
            to_line(DOWN, zz, zz).start()

    there = pl.ds(pl.multiple_of((1 - d) * rows, 16), rows)
    here = pl.ds(pl.multiple_of(d * rows, 16), rows)
    last = remote(DP, parts.at[mine, there, :], dp_got, dp_send, dp_recv)

    def over_dp():
        to_across(z).wait_recv()
        add(mine, y_got[z])

        @pl.when(z > 0)
        def _():
            to_line(CORE, z, z).wait_recv()
            add(mine, z_got[z])

        @pl.when(z < 3)
        def _():
            to_line(CORE, z, 4).wait_recv()
            add(mine, z_got[4])

        last.start()

    def finish(result):
        last.wait_recv()
        result[...] = parts[mine, here, :].astype(single) + dp_got[...].astype(single)
        last.wait_send()

        @pl.loop(0, 4)
        def _(zz):
            to_core(y, zz).wait_send()
            to_core(1 - y, zz).wait_send()
            to_across(zz).wait_send()

            @pl.when(zz != z)
            def _():
                to_line(CORE, zz, zz).wait_send()

    return core_sends, across, line, over_dp, finish


def ring_scratch(rows, width):
    bfloat = jnp.bfloat16
    dma = pltpu.SemaphoreType.DMA
    return [
        pltpu.VMEM((16, 2 * rows, width), bfloat),
        pltpu.VMEM((8, 2 * rows, width), bfloat),
        pltpu.VMEM((4, 2 * rows, width), bfloat),
        pltpu.VMEM((5, 2 * rows, width), bfloat),
        pltpu.VMEM((rows, width), bfloat),
        dma((8,)),
        dma((8,)),
        dma((4,)),
        dma((4,)),
        dma((4,)),
        dma((5,)),
        dma,
        dma,
    ]


def load_parts(refs, parts, sem):
    loads = []
    at = 0
    for index, ref in enumerate(refs):
        rows, size = ref.shape[2], ref.shape[3]
        for plane in range(2):
            loads.append(
                pltpu.make_async_copy(
                    ref.at[plane],
                    parts.at[:, pl.ds(plane * rows, rows), pl.ds(at, size)],
                    sem.at[index * 2 + plane],
                )
            )
        at += size
    return loads


def gather_kernel(
    query_ref,
    key_ref,
    value_ref,
    small_ref,
    out_ref,
    proj_all,
    small_all,
    out_all,
    whole,
    local_sem,
    send_sem,
    core_sem,
    recv_sem,
):
    y, c, z, inner, device, per_side = place()
    d = lax.axis_index("dp")
    mine = d * 16 + block_id(y, c, z)
    loads = []
    at = 0
    for index, ref in enumerate((query_ref, key_ref, value_ref, small_ref, out_ref)):
        size = ref.shape[1]
        loads.append(
            pltpu.make_async_copy(ref, whole.at[mine, :, pl.ds(at, size)], local_sem.at[index])
        )
        at += size
    for copy in loads:
        copy.start()
    greet(per_side, device, 4 + inner, (DP,))
    for copy in loads:
        copy.wait()

    def copy_of(kind, slot, sem):
        return pltpu.make_async_remote_copy(
            src_ref=whole.at[slot],
            dst_ref=whole.at[slot],
            send_sem=sem,
            recv_sem=recv_sem.at[slot],
            device_id=device(kind),
            device_id_type=MESH_ID,
        )

    def own(kind, block):
        return copy_of(kind, d * 16 + block, send_sem.at[kind, block])

    def other(block):
        return copy_of(CORE, (1 - d) * 16 + block, core_sem.at[block])

    def along(kind, zz):
        if kind == UP:
            return jnp.logical_and(z < 3, zz <= z)
        return jnp.logical_and(z > 0, zz >= z)

    def fan(zz, act):
        block = block_id(y, c, zz)
        for kind in (UP, DOWN):

            @pl.when(along(kind, zz))
            def _():
                act(own(kind, block))

        for kind in (ACROSS, DP, CORE):
            act(own(kind, block))

    def fan_across(zz, act):
        block = block_id(1 - y, c, zz)
        act(own(DP, block))
        act(own(CORE, block))

    def fan_dp(zz, act):
        act(other(block_id(y, c, zz)))
        act(other(block_id(1 - y, c, zz)))

    start = lambda copy: copy.start()
    fan(z, start)

    def arrive(step, carry):
        @pl.when(jnp.logical_and(step > 0, step < 4))
        def _():
            zz = line_order(z, jnp.minimum(step, 3))
            own(ACROSS, block_id(y, c, zz)).wait_recv()
            fan(zz, start)

        @pl.when(jnp.logical_and(step > 0, step < 5))
        def _():
            zz = line_order(z, jnp.maximum(step - 1, 0))
            own(CORE, block_id(1 - y, c, zz)).wait_recv()
            fan_across(zz, start)

        @pl.when(step > 1)
        def _():
            zz = line_order(z, jnp.maximum(step - 2, 0))
            other(block_id(y, c, zz)).wait_recv()
            other(block_id(1 - y, c, zz)).wait_recv()
            fan_dp(zz, start)

        return carry

    lax.fori_loop(0, 6, arrive, 0)

    def finish(zz, carry):
        for yy in range(2):
            block = block_id(yy, 1 - c, zz)
            own(CORE, block).wait_recv()
            other(block).wait_recv()
        return carry

    lax.fori_loop(0, 4, finish, 0)
    results = []
    at = 0
    for index, ref in enumerate((proj_all, small_all, out_all)):
        size = ref.shape[2]
        results.append(
            pltpu.make_async_copy(whole.at[:, :, pl.ds(at, size)], ref, local_sem.at[index])
        )
        at += size
    for copy in results:
        copy.start()
    end = lambda copy: copy.wait_send()

    def ends(zz, carry):
        fan(zz, end)
        fan_across(zz, end)
        fan_dp(zz, end)
        return carry

    lax.fori_loop(0, 4, ends, 0)
    for copy in results:
        copy.wait()


def gather_weights(query, key, value, small, out):
    bfloat = jnp.bfloat16
    dma = pltpu.SemaphoreType.DMA
    rows = query.shape[0]
    widths = (query.shape[1] + key.shape[1] + value.shape[1], small.shape[1], out.shape[1])
    anywhere = pl.BlockSpec(memory_space=pl.ANY)
    return pl.pallas_call(
        gather_kernel,
        out_shape=tuple(jax.ShapeDtypeStruct((32, rows, width), bfloat) for width in widths),
        in_specs=[anywhere] * 5,
        out_specs=(anywhere, anywhere, anywhere),
        scratch_shapes=[
            pltpu.VMEM((32, rows, sum(widths)), bfloat),
            dma((5,)),
            dma((5, 16)),
            dma((16,)),
            dma((32,)),
        ],
        compiler_params=pltpu.CompilerParams(
            collective_id=0, has_side_effects=True, vmem_limit_bytes=60 * 2**20
        ),
        name="gather_weights",
    )(query, key, value, small, out)


def ring_sum_dp_early(parts, core_got, dp_got, y_got, z_got, sems):
    single = jnp.float32
    core_send, core_recv, dp_send, dp_recv, y_send, y_recv, z_send, z_recv = sems
    y, c, z, _, device, _ = place()
    d = lax.axis_index("dp")
    rows = parts.shape[1] // 2
    mine = block_id(y, c, z)
    there = pl.ds(pl.multiple_of((1 - d) * rows, 16), rows)
    here = pl.ds(pl.multiple_of(d * rows, 16), rows)

    def remote(kind, source, target, send_sem, recv_sem):
        return pltpu.make_async_remote_copy(
            src_ref=source,
            dst_ref=target,
            send_sem=send_sem,
            recv_sem=recv_sem,
            device_id=device(kind),
            device_id_type=MESH_ID,
        )

    def to_core(yy, zz):
        slot = yy * 4 + zz
        return remote(
            CORE, parts.at[block_id(yy, 1 - c, zz)], core_got.at[slot], core_send.at[slot], core_recv.at[slot]
        )

    def to_dp(yy, zz):
        slot = yy * 4 + zz
        return remote(
            DP, parts.at[block_id(yy, c, zz), there, :], dp_got.at[slot], dp_send.at[slot], dp_recv.at[slot]
        )

    def to_across(zz):
        return remote(
            ACROSS, parts.at[block_id(1 - y, c, zz), here, :], y_got.at[zz], y_send.at[zz], y_recv.at[zz]
        )

    def to_line(kind, zz, slot):
        return remote(
            kind, parts.at[block_id(y, c, zz), here, :], z_got.at[slot], z_send.at[zz], z_recv.at[slot]
        )

    def add(block, got):
        parts[block, here, :] = (
            parts[block, here, :].astype(single) + got.astype(single)
        ).astype(parts.dtype)

    def core_sends():
        @pl.loop(0, 4)
        def _(turn):
            zz = line_order(z, 3 - turn)
            to_core(1 - y, zz).start()
            to_core(y, zz).start()

    def meet(step):
        zz = line_order(z, step)
        for yy in (1 - y, y):
            block = block_id(yy, c, zz)
            to_core(yy, zz).wait_recv()
            parts[block] = (
                parts[block].astype(single) + core_got[yy * 4 + zz].astype(single)
            ).astype(parts.dtype)
            to_dp(yy, zz).start()

    def across(step):
        zz = line_order(z, step)
        for yy in (1 - y, y):
            to_dp(yy, zz).wait_recv()
            add(block_id(yy, c, zz), dp_got[yy * 4 + zz])
        to_across(zz).start()

    def line(step):
        zz = line_order(z, step)
        block = block_id(y, c, zz)
        to_across(zz).wait_recv()
        add(block, y_got[zz])
        rising = zz > z
        comes = jnp.logical_or(jnp.logical_and(rising, z > 0), jnp.logical_and(zz < z, z < 3))

        @pl.when(comes)
        def _():
            to_line(CORE, zz, zz).wait_recv()
            add(block, z_got[zz])

        @pl.when(rising)
        def _():
            to_line(UP, zz, zz).start()

        @pl.when(zz == z - 1)
        def _():
            to_line(DOWN, zz, 4).start()

        @pl.when(zz < z - 1)
        def _():
            to_line(DOWN, zz, zz).start()

    def finish(result):
        to_across(z).wait_recv()
        result[...] = parts[mine, here, :].astype(single) + y_got[z].astype(single)

        @pl.when(z > 0)
        def _():
            to_line(CORE, z, z).wait_recv()
            result[...] += z_got[z].astype(single)

        @pl.when(z < 3)
        def _():
            to_line(CORE, z, 4).wait_recv()
            result[...] += z_got[4].astype(single)

        @pl.loop(0, 4)
        def _(zz):
            for yy in (y, 1 - y):
                to_core(yy, zz).wait_send()
                to_dp(yy, zz).wait_send()
            to_across(zz).wait_send()

            @pl.when(zz != z)
            def _():
                to_line(CORE, zz, zz).wait_send()

    return core_sends, meet, across, line, finish


def ring_scratch_dp_early(rows, width):
    bfloat = jnp.bfloat16
    dma = pltpu.SemaphoreType.DMA
    return [
        pltpu.VMEM((16, 2 * rows, width), bfloat),
        pltpu.VMEM((8, 2 * rows, width), bfloat),
        pltpu.VMEM((8, rows, width), bfloat),
        pltpu.VMEM((4, rows, width), bfloat),
        pltpu.VMEM((5, rows, width), bfloat),
        *[dma((n,)) for n in (8, 8, 8, 8, 4, 4, 4, 5)],
    ]


def sums_kernel(
    proj_ref, small_ref, out_ref, down_ref, sum_ref, out_sum, down_got, load_sem, swap_send, swap_recv, *rings
):
    _, _, _, inner, device, per_side = place()
    ring, out_ring = rings[:13], rings[13:]
    loads = load_parts((proj_ref, small_ref), ring[0], load_sem) + load_parts(
        (out_ref,), out_ring[0], load_sem.at[pl.ds(4, 2)]
    )
    for copy in loads:
        copy.start()
    greet(per_side, device, 4 + inner, (DP,))
    for copy in loads:
        copy.wait()
    core_sends, meet, across, line, finish = ring_sum_dp_early(*ring[:5], ring[5:])
    out_core, out_across, out_line, out_dp, out_finish = ring_sum(*out_ring[:5], out_ring[5:])
    core_sends()
    out_core()

    @pl.loop(0, 4)
    def _(turn):
        meet(3 - turn)
        out_across(3 - turn)

    swaps = swap_copies(((down_ref, 1, down_got),), device, swap_send, swap_recv)
    for copy in swaps:
        copy.start()

    @pl.loop(0, 4)
    def _(turn):
        across(3 - turn)

        @pl.when(turn < 3)
        def _():
            out_line(3 - jnp.minimum(turn, 2))

        @pl.when(turn > 0)
        def _():
            line(4 - jnp.maximum(turn, 1))

    out_dp()
    finish(sum_ref)
    out_finish(out_sum)
    for copy in swaps:
        copy.wait()


def by_device(x):
    return x.reshape(2, 16, x.shape[0] // 32, x.shape[1])


def sum_gradients(proj, small, out, down):
    dma = pltpu.SemaphoreType.DMA
    anywhere = pl.BlockSpec(memory_space=pl.ANY)
    vmem = pl.BlockSpec(memory_space=pltpu.VMEM)
    rows = proj.shape[0] // 32
    width = proj.shape[1] + small.shape[1]
    return pl.pallas_call(
        sums_kernel,
        out_shape=(
            jax.ShapeDtypeStruct((rows, width), jnp.float32),
            jax.ShapeDtypeStruct((rows, out.shape[1]), jnp.float32),
            jax.ShapeDtypeStruct((down.shape[1] // 2, down.shape[2]), down.dtype),
        ),
        in_specs=[anywhere] * 4,
        out_specs=(vmem, vmem, anywhere),
        scratch_shapes=[
            dma((6,)),
            dma((1,)),
            dma((1,)),
            *ring_scratch_dp_early(rows, width),
            *ring_scratch(rows, out.shape[1]),
        ],
        compiler_params=pltpu.CompilerParams(
            collective_id=2, has_side_effects=True, vmem_limit_bytes=56 * 2**20
        ),
        name="sum_gradients",
    )(by_device(proj), by_device(small), by_device(out), down)


def fill_bias(length_ref, bias, ctx):
    blocks, keys, queries = bias.shape
    row = lax.broadcasted_iota(jnp.int32, (keys, queries), 0)
    column = lax.broadcasted_iota(jnp.int32, (keys, queries), 1) + ctx * queries
    for j in range(blocks):
        key = row + j * keys
        allowed = jnp.logical_and(key <= column, key < length_ref[0])
        bias[j] = jnp.where(allowed, 0.0, floor_score)


def head_probs(query, keys, bias):
    scores = [contract_rows(key, query) + bias[j] for j, key in enumerate(keys)]
    peak = jnp.max(scores[0], axis=0, keepdims=True)
    for score in scores[1:]:
        peak = jnp.maximum(peak, jnp.max(score, axis=0, keepdims=True))
    raised = [jnp.exp(score - peak) for score in scores]
    total = jnp.sum(raised[0], axis=0, keepdims=True)
    for value in raised[1:]:
        total = total + jnp.sum(value, axis=0, keepdims=True)
    inverse = 1.0 / total
    return [value * inverse for value in raised]


def attend_kernel(
    query_ref, own_ref, length_ref, mixed_ref, all_ref, pairs, bias, local_sem, send_sem, recv_sem
):
    bfloat = jnp.bfloat16
    y, c, _, _, device, _ = place()
    mine = y * 2 + c
    own = pltpu.make_async_copy(own_ref, pairs.at[mine], local_sem)
    own.start()
    barrier = pltpu.get_barrier_semaphore()
    for kind in (ACROSS, CORE):
        pl.semaphore_signal(barrier, inc=1, device_id=device(kind), device_id_type=MESH_ID)
    pl.semaphore_wait(barrier, 2)
    own.wait()

    def send(kind, slot, index):
        return pltpu.make_async_remote_copy(
            src_ref=pairs.at[slot],
            dst_ref=pairs.at[slot],
            send_sem=send_sem.at[index],
            recv_sem=recv_sem.at[slot],
            device_id=device(kind),
            device_id_type=MESH_ID,
        )

    across = send(ACROSS, mine, 0)
    core = send(CORE, mine, 1)
    onward = send(CORE, (1 - y) * 2 + c, 2)
    across.start()
    core.start()
    fill_bias(length_ref, bias, mine)
    send(ACROSS, (1 - y) * 2 + c, 0).wait_recv()
    onward.start()
    send(CORE, y * 2 + 1 - c, 1).wait_recv()
    send(CORE, (1 - y) * 2 + 1 - c, 2).wait_recv()
    result = pltpu.make_async_copy(pairs, all_ref, local_sem)
    result.start()
    blocks = pairs.shape[0]
    half = pairs.shape[1] // 2
    ratio = query_ref.shape[0] // half

    def group(g, carry):
        rows = pl.ds(pl.multiple_of(g * HEAD_SIZE, HEAD_SIZE), HEAD_SIZE)
        low = pl.ds(pl.multiple_of(half + g * HEAD_SIZE, HEAD_SIZE), HEAD_SIZE)
        keys = [pairs[j, rows, :] for j in range(blocks)]
        values = [pairs[j, low, :] for j in range(blocks)]
        for r in range(ratio):
            head = pl.ds(pl.multiple_of((g * ratio + r) * HEAD_SIZE, HEAD_SIZE), HEAD_SIZE)
            probs = head_probs(query_ref[head, :], keys, bias)
            total = matmul(values[0], probs[0].astype(bfloat))
            for j in range(1, blocks):
                total = total + matmul(values[j], probs[j].astype(bfloat))
            mixed_ref[head, :] = total.astype(bfloat)
        return carry

    lax.fori_loop(0, half // HEAD_SIZE, group, 0)
    for copy in (across, core, onward):
        copy.wait_send()
    result.wait()


def attend(query, own_pairs, lengths):
    bfloat = jnp.bfloat16
    dma = pltpu.SemaphoreType.DMA
    anywhere = pl.BlockSpec(memory_space=pl.ANY)
    vmem = pl.BlockSpec(memory_space=pltpu.VMEM)
    pairs = (4, *own_pairs.shape)
    keys = own_pairs.shape[1]
    return pl.pallas_call(
        attend_kernel,
        out_shape=(
            jax.ShapeDtypeStruct(query.shape, bfloat),
            jax.ShapeDtypeStruct(pairs, bfloat),
        ),
        in_specs=[vmem, anywhere, pl.BlockSpec(memory_space=pltpu.SMEM)],
        out_specs=(vmem, anywhere),
        scratch_shapes=[
            pltpu.VMEM(pairs, bfloat),
            pltpu.VMEM((4, keys, query.shape[1]), jnp.float32),
            dma,
            dma((3,)),
            dma((4,)),
        ],
        compiler_params=pltpu.CompilerParams(
            collective_id=3, has_side_effects=True, vmem_limit_bytes=40 * 2**20
        ),
        name="attend",
    )(query, own_pairs, lengths)


def attend_back_kernel(swap, *refs):
    query_ref, pairs_ref, grad_ref, length_ref, *refs = refs
    if swap:
        gate_ref, up_ref, down_ref, *refs = refs
    query_out, pairs_out, *refs = refs
    if swap:
        down_got, gate_got, up_got, *refs = refs
    parts, core_got, y_got, bias, core_send, core_recv, y_send, y_recv, *refs = refs
    bfloat = jnp.bfloat16
    single = jnp.float32
    y, c, _, _, device, _ = place()
    mine = y * 2 + c
    kinds = (ACROSS, CORE, DP) if swap else (ACROSS, CORE)
    barrier = pltpu.get_barrier_semaphore()
    for kind in kinds:
        pl.semaphore_signal(barrier, inc=1, device_id=device(kind), device_id_type=MESH_ID)
    pl.semaphore_wait(barrier, len(kinds))
    swaps = []
    if swap:
        swap_send, swap_recv = refs
        swaps = swap_copies(
            ((down_ref, 0, down_got), (gate_ref, 1, gate_got), (up_ref, 1, up_got)),
            device,
            swap_send,
            swap_recv,
        )
        for copy in swaps:
            copy.start()
    fill_bias(length_ref, bias, mine)
    blocks = pairs_ref.shape[0]
    half = pairs_ref.shape[1] // 2
    ratio = query_ref.shape[0] // half
    groups = half // HEAD_SIZE
    turns = parts.shape[1]
    per_turn = groups // turns
    quarter = half // turns

    def to_core(yy, turn):
        return pltpu.make_async_remote_copy(
            src_ref=parts.at[yy * 2 + 1 - c, turn],
            dst_ref=core_got.at[turn, yy],
            send_sem=core_send.at[turn, yy],
            recv_sem=core_recv.at[turn, yy],
            device_id=device(CORE),
            device_id_type=MESH_ID,
        )

    def to_across(turn):
        return pltpu.make_async_remote_copy(
            src_ref=parts.at[(1 - y) * 2 + c, turn],
            dst_ref=y_got.at[turn],
            send_sem=y_send.at[turn],
            recv_sem=y_recv.at[turn],
            device_id=device(ACROSS),
            device_id_type=MESH_ID,
        )

    def core_stage(turn):
        to_core(1 - y, turn).start()
        to_core(y, turn).start()

    def across_stage(turn):
        to_core(1 - y, turn).wait_recv()
        slot = (1 - y) * 2 + c
        parts[slot, turn] = (
            parts[slot, turn].astype(single) + core_got[turn, 1 - y].astype(single)
        ).astype(bfloat)
        to_across(turn).start()

    def last_stage(turn):
        to_core(y, turn).wait_recv()
        to_across(turn).wait_recv()
        pairs_out[turn] = (
            parts[mine, turn].astype(single)
            + core_got[turn, y].astype(single)
            + y_got[turn].astype(single)
        )

    def group(g, carry):
        rows = pl.ds(pl.multiple_of(g * HEAD_SIZE, HEAD_SIZE), HEAD_SIZE)
        low = pl.ds(pl.multiple_of(half + g * HEAD_SIZE, HEAD_SIZE), HEAD_SIZE)
        keys = [pairs_ref[j, rows, :] for j in range(blocks)]
        values = [pairs_ref[j, low, :] for j in range(blocks)]
        grad_keys = [None] * blocks
        grad_values = [None] * blocks
        for r in range(ratio):
            head = pl.ds(pl.multiple_of((g * ratio + r) * HEAD_SIZE, HEAD_SIZE), HEAD_SIZE)
            query = query_ref[head, :]
            grad = grad_ref[head, :]
            probs = head_probs(query, keys, bias)
            grad_probs = [contract_rows(value, grad) for value in values]
            delta = jnp.sum(probs[0] * grad_probs[0], axis=0, keepdims=True)
            for j in range(1, blocks):
                delta = delta + jnp.sum(probs[j] * grad_probs[j], axis=0, keepdims=True)
            grad_query = None
            for j in range(blocks):
                low_probs = probs[j].astype(bfloat)
                grad_score = (probs[j] * (grad_probs[j] - delta)).astype(bfloat)
                terms = (
                    matmul(keys[j], grad_score),
                    contract_last(query, grad_score),
                    contract_last(grad, low_probs),
                )
                grad_query = terms[0] if j == 0 else grad_query + terms[0]
                grad_keys[j] = terms[1] if r == 0 else grad_keys[j] + terms[1]
                grad_values[j] = terms[2] if r == 0 else grad_values[j] + terms[2]
            query_out[head, :] = grad_query * HEAD_SIZE ** (-0.5)
        turn = g // per_turn
        at = pl.multiple_of((g % per_turn) * HEAD_SIZE, HEAD_SIZE)
        for j in range(blocks):
            parts[j, turn, pl.ds(at, HEAD_SIZE), :] = grad_keys[j].astype(bfloat)
            parts[j, turn, pl.ds(quarter + at, HEAD_SIZE), :] = grad_values[j].astype(bfloat)
        for index in range(turns - 1):

            @pl.when(g == (index + 1) * per_turn - 1)
            def _():
                core_stage(index)

            @pl.when(g == (index + 1) * per_turn)
            def _():
                across_stage(index)

        return carry

    lax.fori_loop(0, groups, group, 0)
    core_stage(turns - 1)
    across_stage(turns - 1)
    for turn in range(turns):
        last_stage(turn)
    for turn in range(turns):
        to_core(y, turn).wait_send()
        to_core(1 - y, turn).wait_send()
        to_across(turn).wait_send()
    for copy in swaps:
        copy.wait()


def attend_back(query, pairs, grad, lengths, expert_grads):
    bfloat = jnp.bfloat16
    single = jnp.float32
    dma = pltpu.SemaphoreType.DMA
    anywhere = pl.BlockSpec(memory_space=pl.ANY)
    vmem = pl.BlockSpec(memory_space=pltpu.VMEM)
    swap = bool(expert_grads)
    blocks, rows, keys = pairs.shape
    turns = 2
    part = (turns, rows // turns, keys)
    more_in, more_out, more_scratch, more_specs = [], [], [], []
    if swap:
        gate, up, down = expert_grads
        more_in = [gate, up, down]
        more_out = [
            jax.ShapeDtypeStruct((x.shape[1] // 2, x.shape[2]), bfloat) for x in (down, gate, up)
        ]
        more_specs = [anywhere] * 3
        more_scratch = [dma((3,)), dma((3,))]
    return pl.pallas_call(
        functools.partial(attend_back_kernel, swap),
        out_shape=(
            jax.ShapeDtypeStruct(query.shape, single),
            jax.ShapeDtypeStruct(part, single),
            *more_out,
        ),
        in_specs=[vmem, vmem, vmem, pl.BlockSpec(memory_space=pltpu.SMEM)] + [anywhere] * len(more_in),
        out_specs=(vmem, vmem, *more_specs),
        scratch_shapes=[
            pltpu.VMEM((blocks, *part), bfloat),
            pltpu.VMEM((turns, 2, *part[1:]), bfloat),
            pltpu.VMEM(part, bfloat),
            pltpu.VMEM((blocks, keys, query.shape[1]), single),
            dma((turns, 2)),
            dma((turns, 2)),
            dma((turns,)),
            dma((turns,)),
            *more_scratch,
        ],
        compiler_params=pltpu.CompilerParams(
            collective_id=4, has_side_effects=True, vmem_limit_bytes=48 * 2**20
        ),
        name="attend_back",
    )(query, pairs, grad, lengths, *more_in)


def experts_kernel(
    swap,
    hidden_ref,
    final_ref,
    routes_ref,
    router_ref,
    gate_hbm,
    up_hbm,
    down_hbm,
    back_ref,
    part_ref,
    score_got,
    grad_gate_ref,
    grad_up_ref,
    grad_down_ref,
    *refs,
):
    gate_got, up_got, *refs = refs if swap else (None, None, *refs)
    experts_steps(
        swap,
        hidden_ref,
        final_ref,
        routes_ref,
        router_ref,
        gate_hbm,
        up_hbm,
        down_hbm,
        back_ref,
        part_ref,
        score_got,
        grad_gate_ref,
        grad_up_ref,
        grad_down_ref,
        gate_got,
        up_got,
        *refs,
    )


def experts_steps(
    swap,
    hidden_ref,
    final_ref,
    routes_ref,
    router_ref,
    gate_hbm,
    up_hbm,
    down_hbm,
    back_ref,
    part_ref,
    score_got,
    grad_gate_ref,
    grad_up_ref,
    grad_down_ref,
    gate_got,
    up_got,
    held,
    w_gate,
    w_up,
    w_down,
    rows_in,
    rows_grad,
    slope_gate,
    slope_up,
    hidden_e,
    picks,
    row_gates,
    work,
    pool,
    before,
    gather_send,
    gather_recv,
    local_sem,
    load_sem,
    part_sem,
    sum_send,
    core_recv,
    y_recv,
    z_recv,
    ready,
    score_ref,
    score_send,
    score_recv,
    swap_send,
    swap_recv,
):
    single = jnp.float32
    bfloat = jnp.bfloat16
    tokens_block = hidden_ref.shape[0]
    width = hidden_ref.shape[1]
    experts = router_ref.shape[0]
    local_exp = w_gate.shape[0]
    hidden_units = w_gate.shape[2]
    capacity = picks.shape[1] // local_exp
    group_rows = 4 * capacity
    ctx = lax.axis_index("context")
    y, c, z, inner, device, per_side = place()

    weights = (
        pltpu.make_async_copy(gate_hbm, w_gate, load_sem.at[0]),
        pltpu.make_async_copy(up_hbm, w_up, load_sem.at[1]),
        pltpu.make_async_copy(down_hbm, w_down, load_sem.at[2]),
    )
    mine = block_id(y, c, z)
    own = pltpu.make_async_copy(hidden_ref, held.at[mine], local_sem)
    own.start()
    for copy in weights:
        copy.start()

    barrier = pltpu.get_barrier_semaphore()

    def member_device(block):
        return {"context": block // 4, "expert": block % 4}

    @pl.loop(1, 16)
    def _(shift):
        pl.semaphore_signal(
            barrier,
            inc=1,
            device_id=member_device((mine + shift) % 16),
            device_id_type=MESH_ID,
        )

    if swap:
        pl.semaphore_signal(barrier, inc=1, device_id=device(DP), device_id_type=MESH_ID)
    pl.semaphore_wait(barrier, 16 if swap else 15)
    own.wait()

    def spread(kind, block):
        return pltpu.make_async_remote_copy(
            src_ref=held.at[block],
            dst_ref=held.at[block],
            send_sem=gather_send.at[kind, block],
            recv_sem=gather_recv.at[block],
            device_id=device(kind),
            device_id_type=MESH_ID,
        )

    def along(kind, zz):
        if kind == UP:
            return jnp.logical_and(z < 3, zz <= z)
        return jnp.logical_and(z > 0, zz >= z)

    def send_on(zz):
        block = block_id(y, c, zz)
        for kind in (UP, DOWN):

            @pl.when(along(kind, zz))
            def _():
                spread(kind, block).start()

        spread(ACROSS, block).start()
        spread(CORE, block).start()

    def forward(step):
        zz = line_order(z, step)
        spread(ACROSS, block_id(y, c, zz)).wait_recv()
        send_on(zz)

    send_on(z)
    row = lax.broadcasted_iota(jnp.int32, (tokens_block, tokens_block), 0)
    column = lax.broadcasted_iota(jnp.int32, (tokens_block, tokens_block), 1)
    before[...] = jnp.where(row < column, 1.0, 0.0).astype(bfloat)
    for copy in weights:
        copy.wait()
    first = (ctx * 4 + z) * local_exp

    def member(zz, p):
        yy = y + (p // 2) * (1 - 2 * y)
        cc = c + (p % 2) * (1 - 2 * c)
        return block_id(yy, cc, zz)

    def load_final(zz, p):
        return pltpu.make_async_copy(final_ref.at[member(zz, p)], pool.at[p], load_sem.at[p])

    def store_part(zz, p):
        return pltpu.make_async_copy(
            pool.at[4 + p % 2], part_ref.at[member(zz, p)], part_sem.at[p % 2]
        )

    def forward_group(step, carry):
        zz = line_order(z, step)
        after = step + 1 + inner * jnp.minimum(step, 1)

        @pl.when(after < 4)
        def _():
            forward(after)

        @pl.when(jnp.logical_and(step == 0, inner == 1))
        def _():
            forward(2)

        @pl.loop(0, 4)
        def _(p):
            load_final(zz, p).start()

        spread(CORE, block_id(y, 1 - c, zz)).wait_recv()
        spread(CORE, block_id(1 - y, c, zz)).wait_recv()
        spread(CORE, block_id(1 - y, c, zz)).start()
        spread(CORE, block_id(1 - y, 1 - c, zz)).wait_recv()

        @pl.loop(0, 4)
        def _(p):
            block = member(zz, p)
            tokens_in = held[block]
            logits = contract_last(router_ref[...], tokens_in)
            expert_row = lax.broadcasted_iota(jnp.int32, (experts, tokens_block), 0)
            routed = jnp.zeros((experts, tokens_block), single)
            for k in range(routes_ref.shape[1]):
                routed = routed + jnp.where(routes_ref[block, k : k + 1, :] == expert_row, 1.0, 0.0)
            named = routed > 0.5
            peak = jnp.max(jnp.where(named, logits, floor_score), axis=0, keepdims=True)
            raised = jnp.where(named, jnp.exp(jnp.minimum(logits - peak, 0.0)), 0.0)
            gates = raised / jnp.sum(raised, axis=0, keepdims=True)
            eight = lax.broadcasted_iota(jnp.int32, (8, tokens_block), 0)
            masks = jnp.zeros((8, tokens_block), single)
            own_mask = []
            own_gate = []
            for j in range(local_exp):
                here = expert_row == first + j
                own_mask.append(jnp.sum(jnp.where(here, routed, 0.0), axis=0, keepdims=True))
                own_gate.append(jnp.sum(jnp.where(here, gates, 0.0), axis=0, keepdims=True))
                masks = masks + jnp.where(eight == j, own_mask[j], 0.0)
            rank = matmul(masks.astype(bfloat), before[...])
            slot = lax.broadcasted_iota(jnp.int32, (capacity, tokens_block), 0).astype(single)
            for j in range(local_exp):
                hit = jnp.logical_and(slot == rank[j : j + 1, :], own_mask[j] > 0.5)
                pick = jnp.where(hit, 1.0, 0.0)
                picks[step * 4 + p, pl.ds(j * capacity, capacity), :] = pick.astype(bfloat)
                gate_column = jnp.sum(pick * own_gate[j], axis=1, keepdims=True)
                row_gates[p, pl.ds(j * capacity, capacity), :] = jnp.broadcast_to(
                    gate_column, (capacity, 128)
                )
            at = pl.multiple_of(step * group_rows + p * capacity, 32)
            for n in range(width // CHUNK):
                part = pl.ds(n * CHUNK, CHUNK)
                got = matmul(picks[step * 4 + p], held[block, :, part]).astype(bfloat)
                for j in range(local_exp):
                    rows_in[j, pl.ds(at, capacity), part] = got[j * capacity : (j + 1) * capacity]

        base = pl.multiple_of(step * group_rows, 128)
        for j in range(local_exp):
            given = rows_in[j, pl.ds(base, group_rows), :]
            for n in range(hidden_units // HALF):
                part = pl.ds(n * HALF, HALF)
                gate_pre = matmul(given, w_gate[j, :, part])
                up_pre = matmul(given, w_up[j, :, part])
                sigmoid = 1.0 / (1.0 + jnp.exp(-gate_pre))
                silu = gate_pre * sigmoid
                hidden_e[j, pl.ds(base, group_rows), part] = (silu * up_pre).astype(bfloat)
                slope_gate[j, pl.ds(base, group_rows), part] = (
                    up_pre * sigmoid * (1.0 + gate_pre * (1.0 - sigmoid))
                ).astype(bfloat)
                slope_up[j, pl.ds(base, group_rows), part] = silu.astype(bfloat)
            for n in range(width // CHUNK):
                part = pl.ds(n * CHUNK, CHUNK)
                work[j, :, part] = matmul(
                    hidden_e[j, pl.ds(base, group_rows), :], w_down[j, :, part]
                ).astype(bfloat)

        @pl.loop(0, 4)
        def _(p):
            block = member(zz, p)
            at = pl.multiple_of(step * group_rows + p * capacity, 32)
            local = pl.multiple_of(p * capacity, 32)
            pick = picks[step * 4 + p]
            weight = row_gates[p][:, 0:1]
            weighted = (pick.astype(single) * weight).astype(bfloat)
            load_final(zz, p).wait()

            @pl.when(jnp.logical_or(step > 0, p > 1))
            def _():
                store_part(zz, p).wait()

            row_score = jnp.zeros((local_exp * capacity, 1), single)
            for n in range(width // CHUNK):
                part = pl.ds(n * CHUNK, CHUNK)
                out = jnp.concatenate(
                    [work[j, pl.ds(local, capacity), part] for j in range(local_exp)], axis=0
                )
                pool[4 + p % 2, :, part] = contract_rows(weighted, out).astype(bfloat)
                final = matmul(pick, pool[p, :, part])
                row_score = row_score + jnp.sum(final * out.astype(single), axis=1, keepdims=True)
                graded = (final * weight).astype(bfloat)
                for j in range(local_exp):
                    rows_grad[j, pl.ds(at, capacity), part] = graded[j * capacity : (j + 1) * capacity]
            store_part(zz, p).start()
            spread_score = pick.astype(single) * row_score
            eight = lax.broadcasted_iota(jnp.int32, (8, tokens_block), 0)
            scores = jnp.zeros((8, tokens_block), single)
            for j in range(local_exp):
                total = jnp.sum(spread_score[j * capacity : (j + 1) * capacity], axis=0, keepdims=True)
                scores = scores + jnp.where(eight == j, total, 0.0)
            score_ref[block] = scores

        return carry

    lax.fori_loop(0, 4, forward_group, 0)

    def score_copy(block, source):
        return pltpu.make_async_remote_copy(
            src_ref=score_ref.at[block],
            dst_ref=score_got.at[source],
            send_sem=score_send.at[block],
            recv_sem=score_recv.at[source],
            device_id=member_device(block),
            device_id_type=MESH_ID,
        )

    @pl.loop(1, 16)
    def _(shift):
        score_copy((mine + shift) % 16, mine).start()

    score_got[mine] = score_ref[mine]

    @pl.loop(2, 4)
    def _(p):
        store_part(line_order(z, 3), p).wait()

    @pl.loop(0, 4)
    def _(zz):
        block = block_id(y, c, zz)
        for kind in (UP, DOWN):

            @pl.when(along(kind, zz))
            def _():
                spread(kind, block).wait_send()

        spread(ACROSS, block).wait_send()
        spread(CORE, block).wait_send()
        spread(CORE, block_id(1 - y, c, zz)).wait_send()

    opposite = {UP: DOWN, DOWN: UP, ACROSS: ACROSS, CORE: CORE}
    per_side(
        lambda kind: pl.semaphore_signal(
            ready.at[opposite[kind]], inc=1, device_id=device(kind), device_id_type=MESH_ID
        )
    )

    def sum_copy(kind, source, target, send_index, recv_sem):
        return pltpu.make_async_remote_copy(
            src_ref=source,
            dst_ref=target,
            send_sem=sum_send.at[send_index],
            recv_sem=recv_sem,
            device_id=device(kind),
            device_id_type=MESH_ID,
        )

    def to_core(turn, p, zz):
        slot = (y + p * (1 - 2 * y)) * 4 + zz
        index = turn * 2 + p
        return sum_copy(CORE, pool.at[index], held.at[slot], index, core_recv.at[slot])

    def from_core(slot):
        return sum_copy(CORE, pool.at[0], held.at[slot], 0, core_recv.at[slot])

    def to_across(zz):
        return sum_copy(ACROSS, held.at[(1 - y) * 4 + zz], held.at[8 + zz], 4 + zz, y_recv.at[zz])

    def to_line(kind, zz, last):
        return sum_copy(
            kind,
            held.at[y * 4 + zz],
            pool.at[5] if last else held.at[12 + zz],
            8 + zz,
            z_recv.at[4 if last else zz],
        )

    def add_up(slot, *others):
        @pl.loop(0, tokens_block // 64)
        def _(r):
            rows = pl.ds(pl.multiple_of(r * 64, 64), 64)
            total = held[slot, rows, :].astype(single)
            for ref, index in others:
                total = total + ref[index, rows, :].astype(single)
            held[slot, rows, :] = total.astype(bfloat)

    def back_block(step, p, target, index, onto):
        local = pl.multiple_of(p * capacity, 32)
        pick = picks[step * 4 + p]
        for n in range(width // CHUNK):
            part = pl.ds(n * CHUNK, CHUNK)
            grads = jnp.concatenate(
                [work[j, pl.ds(local, capacity), part] for j in range(local_exp)], axis=0
            )
            block = contract_rows(pick, grads)
            if onto:
                block = block + target[index, :, part].astype(single)
            target[index, :, part] = block.astype(bfloat)

    def line_sum(step):
        zz = line_order(z, step)
        slot = y * 4 + zz
        to_across(zz).wait_recv()
        rising = zz > z
        comes = jnp.logical_or(jnp.logical_and(rising, z > 0), jnp.logical_and(zz < z, z < 3))

        @pl.when(comes)
        def _():
            to_line(CORE, zz, False).wait_recv()
            add_up(slot, (held, 8 + zz), (held, 12 + zz))

        @pl.when(jnp.logical_not(comes))
        def _():
            add_up(slot, (held, 8 + zz))

        @pl.when(rising)
        def _():
            to_line(UP, zz, False).start()

        @pl.when(zz == z - 1)
        def _():
            to_line(DOWN, zz, True).start()

        @pl.when(zz < z - 1)
        def _():
            to_line(DOWN, zz, False).start()

    def at_end(action):
        pl.when(inner == 0)(action)

    def at_middle(action):
        pl.when(inner == 1)(action)

    def backward_group(turn_step, carry):
        step = 3 - turn_step
        zz = line_order(z, step)
        turn = step % 2
        base = pl.multiple_of(step * group_rows, 128)
        for j in range(local_exp):
            for n in range(hidden_units // HALF):
                part = pl.ds(n * HALF, HALF)
                grad_hidden = (
                    contract_last(rows_grad[j, pl.ds(base, group_rows), :], w_down[j, part, :])
                    .astype(bfloat)
                    .astype(single)
                )
                slope_gate[j, pl.ds(base, group_rows), part] = (
                    grad_hidden * slope_gate[j, pl.ds(base, group_rows), part].astype(single)
                ).astype(bfloat)
                slope_up[j, pl.ds(base, group_rows), part] = (
                    grad_hidden * slope_up[j, pl.ds(base, group_rows), part].astype(single)
                ).astype(bfloat)
            for n in range(width // CHUNK):
                part = pl.ds(n * CHUNK, CHUNK)
                work[j, :, part] = (
                    contract_last(slope_gate[j, pl.ds(base, group_rows), :], w_gate[j, part, :])
                    + contract_last(slope_up[j, pl.ds(base, group_rows), :], w_up[j, part, :])
                ).astype(bfloat)

        @pl.when(turn_step == 0)
        def _():
            per_side(lambda kind: pl.semaphore_wait(ready.at[kind], 1))

        for p, member_p in ((1, 3), (0, 1)):

            @pl.when(turn_step > 1)
            def _():
                to_core(turn, p, zz).wait_send()

            back_block(step, member_p, pool, turn * 2 + p, False)
            to_core(turn, p, zz).start()

        other = (1 - y) * 4 + zz
        from_core(other).wait_recv()
        back_block(step, 2, held, other, True)
        to_across(zz).start()
        slot = y * 4 + zz
        from_core(slot).wait_recv()
        back_block(step, 0, held, slot, True)

        @pl.when(turn_step == 2)
        def _():
            at_end(lambda: line_sum(3))

        return carry

    lax.fori_loop(0, 4, backward_group, 0)
    at_middle(lambda: line_sum(3))
    at_end(lambda: line_sum(2))

    def stores(j):
        return (
            pltpu.make_async_copy(w_gate.at[j], grad_gate_ref.at[j], load_sem.at[3 * j]),
            pltpu.make_async_copy(w_up.at[j], grad_up_ref.at[j], load_sem.at[3 * j + 1]),
            pltpu.make_async_copy(w_down.at[j], grad_down_ref.at[j], load_sem.at[3 * j + 2]),
        )

    def weight_grads(j):
        @pl.loop(0, width // CHUNK)
        def _(n):
            part = pl.ds(pl.multiple_of(n * CHUNK, CHUNK), CHUNK)
            w_gate[j, part, :] = contract_rows(rows_in[j, :, part], slope_gate[j]).astype(bfloat)
            w_up[j, part, :] = contract_rows(rows_in[j, :, part], slope_up[j]).astype(bfloat)
            w_down[j, :, part] = contract_rows(hidden_e[j], rows_grad[j, :, part]).astype(bfloat)

        for copy in stores(j):
            copy.start()

    weight_grads(0)
    swaps = []
    if swap:
        swaps = swap_copies(
            ((w_gate, 0, gate_got), (w_up, 0, up_got)), device, swap_send, swap_recv
        )
        for copy in swaps:
            copy.start()
    weight_grads(1)
    at_middle(lambda: line_sum(2))
    line_sum(1)
    slot = y * 4 + z
    to_across(z).wait_recv()
    add_up(slot, (held, 8 + z))

    @pl.when(z > 0)
    def _():
        to_line(CORE, z, False).wait_recv()
        add_up(slot, (held, 12 + z))

    @pl.when(z < 3)
    def _():
        to_line(CORE, z, True).wait_recv()
        add_up(slot, (pool, 5))

    result = pltpu.make_async_copy(held.at[slot], back_ref, local_sem)
    result.start()
    for j in range(local_exp):
        for copy in stores(j):
            copy.wait()
    for turn in range(2):
        for p in range(2):
            to_core(turn, p, z).wait_send()

    @pl.loop(0, 4)
    def _(zz):
        to_across(zz).wait_send()

        @pl.when(zz != z)
        def _():
            to_line(CORE, zz, False).wait_send()

    @pl.loop(1, 16)
    def _(shift):
        other = (mine + shift) % 16
        score_copy(other, mine).wait_send()
        score_copy(other, other).wait_recv()

    for copy in swaps:
        copy.wait()
    result.wait()


def experts_on_owner(
    hidden, final_all, routes_all, router_rows, w_gate, w_up, w_down, capacity, swap
):
    blocks = final_all.shape[0]
    tokens_block, width = hidden.shape
    local_exp, _, units = w_gate.shape
    bfloat = jnp.bfloat16
    single = jnp.float32
    rows = blocks * capacity
    anywhere = pl.BlockSpec(memory_space=pl.ANY)
    vmem = pl.BlockSpec(memory_space=pltpu.VMEM)
    dma = pltpu.SemaphoreType.DMA
    return pl.pallas_call(
        functools.partial(experts_kernel, swap),
        out_shape=(
            jax.ShapeDtypeStruct((tokens_block, width), bfloat),
            jax.ShapeDtypeStruct((blocks, tokens_block, width), bfloat),
            jax.ShapeDtypeStruct((blocks, 8, tokens_block), single),
            jax.ShapeDtypeStruct(w_gate.shape, bfloat),
            jax.ShapeDtypeStruct(w_up.shape, bfloat),
            jax.ShapeDtypeStruct(w_down.shape, bfloat),
            *([jax.ShapeDtypeStruct((width // 2, units), bfloat)] * (2 if swap else 0)),
        ),
        in_specs=[anywhere, anywhere, vmem, vmem, anywhere, anywhere, anywhere],
        out_specs=(anywhere, anywhere, vmem, *([anywhere] * (5 if swap else 3))),
        scratch_shapes=[
            pltpu.VMEM((blocks, tokens_block, width), bfloat),
            pltpu.VMEM(w_gate.shape, bfloat),
            pltpu.VMEM(w_up.shape, bfloat),
            pltpu.VMEM(w_down.shape, bfloat),
            pltpu.VMEM((local_exp, rows, width), bfloat),
            pltpu.VMEM((local_exp, rows, width), bfloat),
            pltpu.VMEM((local_exp, rows, units), bfloat),
            pltpu.VMEM((local_exp, rows, units), bfloat),
            pltpu.VMEM((local_exp, rows, units), bfloat),
            pltpu.VMEM((blocks, local_exp * capacity, tokens_block), bfloat),
            pltpu.VMEM((4, local_exp * capacity, 128), single),
            pltpu.VMEM((local_exp, 4 * capacity, width), bfloat),
            pltpu.VMEM((6, tokens_block, width), bfloat),
            pltpu.VMEM((tokens_block, tokens_block), bfloat),
            dma((4, blocks)),
            dma((blocks,)),
            dma,
            dma((6,)),
            dma((2,)),
            dma((12,)),
            dma((8,)),
            dma((4,)),
            dma((5,)),
            pltpu.SemaphoreType.REGULAR((4,)),
            pltpu.VMEM((blocks, 8, tokens_block), single),
            dma((16,)),
            dma((16,)),
            dma((2,)),
            dma((2,)),
        ],
        compiler_params=pltpu.CompilerParams(
            collective_id=1, has_side_effects=True, vmem_limit_bytes=63 * 2**20
        ),
        name="experts",
    )(hidden, final_all, routes_all, router_rows, w_gate, w_up, w_down)


def on_device(
    tokens,
    lengths,
    routes,
    gain_attn,
    w_query,
    key_weight,
    value_weight,
    w_out,
    gain_ffn,
    w_router,
    w_gate,
    w_up,
    w_down,
    cotangent,
):
    tokens_own = tokens.shape[1]
    exp_count = lax.axis_size("expert")
    ctx_count = lax.axis_size("context")
    local_exp = w_gate.shape[0]
    experts = local_exp * ctx_count * exp_count
    capacity = tokens_own * TOP * 3 // (2 * experts)
    bfloat = jnp.bfloat16
    single = jnp.float32
    query_width = w_query.shape[1]
    key_width = key_weight.shape[1]
    proj_width = query_width + 2 * key_width
    own_rows = w_query.shape[0]
    pair = lax.axis_size("dp") == 2
    small = jnp.concatenate(
        [
            w_router,
            gain_attn[:, None],
            gain_ffn[:, None],
            jnp.zeros((own_rows, 64 - experts - 2), bfloat),
        ],
        axis=1,
    )
    if pair:
        packed = routes[0].T.reshape(-1, 64).astype(bfloat)
        packed = jnp.pad(packed, ((0, own_rows - packed.shape[0]), (0, 0)))
        early, small_all, late = gather_weights(
            w_query, key_weight, value_weight, jnp.concatenate([small, packed], axis=1), w_out
        )
        routes_all = lax.dynamic_slice(
            small_all, (lax.axis_index("dp") * 16, 0, 64), (16, tokens_own * TOP // 64, 64)
        )
        routes_all = routes_all.astype(jnp.int32).reshape(16, TOP, tokens_own)
        proj_w = early.reshape(-1, proj_width)
        small_all = small_all.reshape(-1, small_all.shape[2])
        out_w = late.reshape(-1, late.shape[2])
    else:
        proj_w = jnp.concatenate([w_query, key_weight, value_weight], axis=1)
        proj_w = lax.all_gather(proj_w, EVERY, axis=0, tiled=True)
        small_all = lax.all_gather(small, EVERY, axis=0, tiled=True)
        out_w = lax.all_gather(w_out, EVERY, axis=0, tiled=True)
        routes_all = lax.all_gather(routes[0].T, GROUP, axis=0, tiled=False)
    positions = lax.axis_index("context") * tokens_own + jnp.arange(tokens_own, dtype=jnp.int32)
    valid = (positions < lengths[0]).astype(single)[:, None]
    grad_final = cotangent[0].astype(single) * valid
    final_all = lax.all_gather(grad_final.astype(bfloat), GROUP, axis=0, tiled=False)
    router_w = small_all[:, :experts]
    gain_one = small_all[:, experts].astype(single)
    gain_two = small_all[:, experts + 1].astype(single)
    cosine, sine = rotation_tables(positions)

    inputs = tokens[0].astype(single)
    inverse_one = lax.rsqrt(jnp.mean(inputs * inputs, axis=-1, keepdims=True) + epsilon)
    normed_one = inputs * inverse_one
    hidden_one = (normed_one * gain_one).astype(bfloat)
    projected = jnp.einsum("de,sd->es", proj_w, hidden_one, preferred_element_type=single)
    rotated = apply_rotation(projected[: query_width + key_width], cosine, sine).astype(bfloat)
    query = rotated[:query_width] * HEAD_SIZE ** (-0.5)
    own_pairs = jnp.concatenate(
        [rotated[query_width:], projected[query_width + key_width :].astype(bfloat)], axis=0
    )
    mixed, pairs = attend(query, own_pairs, lengths)
    resid = inputs + jnp.einsum("es,ed->sd", mixed, out_w, preferred_element_type=single)
    inverse_two = lax.rsqrt(jnp.mean(resid * resid, axis=-1, keepdims=True) + epsilon)
    normed_two = resid * inverse_two
    hidden_two = (normed_two * gain_two).astype(bfloat)

    grad_hidden, combined, scores, *expert_grads = experts_on_owner(
        hidden_two, final_all, routes_all, router_w.T, w_gate, w_up, w_down, capacity, pair
    )
    expert_grads, got = expert_grads[:3], expert_grads[3:]
    combined = lax.psum_scatter(combined, GROUP, scatter_dimension=0, tiled=False)
    scores = scores[:, :local_exp]
    grad_gates = scores.reshape(experts, tokens_own).T

    routed = jnp.any(routes[0][:, :, None] == jnp.arange(experts, dtype=jnp.int32), axis=1)
    logits = jnp.einsum("sd,de->se", hidden_two, router_w, preferred_element_type=single)
    gates = jax.nn.softmax(jnp.where(routed, logits, floor_score), axis=-1)
    gates = jnp.where(routed, gates, 0.0)
    gate_mean = jnp.sum(gates * grad_gates, axis=-1, keepdims=True)
    grad_logits = (gates * (grad_gates - gate_mean)).astype(bfloat)
    grad_w_router = jnp.einsum("sd,se->de", hidden_two, grad_logits, preferred_element_type=single)
    grad_hidden_two = grad_hidden.astype(single) + jnp.einsum(
        "se,de->sd", grad_logits, router_w, preferred_element_type=single
    )
    grad_gain_ffn = jnp.sum(grad_hidden_two * normed_two, axis=0)
    grad_resid = norm_back(grad_hidden_two * gain_two, normed_two, inverse_two) + grad_final
    grad_attn = grad_resid.astype(bfloat)

    grad_out_w = jnp.einsum("es,sd->ed", mixed, grad_attn, preferred_element_type=single)
    grad_mixed = jnp.einsum("ed,sd->es", out_w, grad_attn, preferred_element_type=single)
    grad_out_w = grad_out_w.astype(bfloat)
    grad_query, grad_pairs, *more = attend_back(
        query,
        pairs,
        grad_mixed.astype(bfloat),
        lengths,
        expert_grads if pair else (),
    )
    grad_pairs = grad_pairs.reshape(2, 2, key_width // 2, tokens_own)
    grad_key = grad_pairs[:, 0].reshape(key_width, tokens_own)
    grad_value = grad_pairs[:, 1].reshape(key_width, tokens_own)
    grad_proj = jnp.concatenate(
        [
            inverse_rotation(grad_query, cosine, sine),
            inverse_rotation(grad_key, cosine, sine),
            grad_value,
        ],
        axis=0,
    ).astype(bfloat)
    grad_proj_w = jnp.einsum("sd,es->de", hidden_one, grad_proj, preferred_element_type=single)
    grad_hidden_one = jnp.einsum("es,de->sd", grad_proj, proj_w, preferred_element_type=single)
    grad_gain_attn = jnp.sum(grad_hidden_one * normed_one, axis=0)
    grad_tokens = norm_back(grad_hidden_one * gain_one, normed_one, inverse_one) + grad_resid

    grad_small = jnp.concatenate(
        [
            grad_w_router,
            grad_gain_attn[:, None],
            grad_gain_ffn[:, None],
            jnp.zeros((MODEL_WIDTH, 128 - experts - 2), single),
        ],
        axis=1,
    ).astype(bfloat)
    grad_proj_w = grad_proj_w.astype(bfloat)
    if pair:
        down_first, gate_last, up_last = more
        summed, out_sum, down_last = sum_gradients(
            grad_proj_w, grad_small, grad_out_w, expert_grads[2]
        )

        def both(whole, *others):
            half = whole.shape[1] // 2
            own = lax.dynamic_slice_in_dim(whole, lax.axis_index("dp") * half, half, axis=1)
            return own.astype(single) + jnp.stack(others).astype(single)

        expert_sums = tuple(
            both(whole, *others)
            for whole, *others in zip(
                expert_grads, (*got, down_first), (gate_last, up_last, down_last)
            )
        )
    else:
        summed = lax.psum_scatter(
            jnp.concatenate([grad_proj_w, grad_small, grad_out_w], axis=1),
            EVERY,
            scatter_dimension=0,
            tiled=True,
        ).astype(single)
        out_sum = summed[:, proj_width + 128 :]
        expert_sums = tuple(
            lax.psum_scatter(x, "dp", scatter_dimension=1, tiled=True).astype(single)
            for x in expert_grads
        )
    combined, summed = lax.optimization_barrier((combined, summed))
    block_out = (valid * (resid + combined.astype(single))).astype(bfloat)
    return (
        block_out[None],
        grad_tokens[None],
        summed[:, proj_width + experts],
        summed[:, :query_width],
        summed[:, query_width : query_width + key_width],
        summed[:, query_width + key_width : proj_width],
        out_sum,
        summed[:, proj_width + experts + 1],
        summed[:, proj_width : proj_width + experts],
        *expert_sums,
    )


def solution(mesh):
    in_specs = (
        P(("dp", "expert"), "context", None),
        P(("dp", "expert")),
        P(("dp", "expert"), "context", None),
        P(("dp", "context", "expert")),
        P(("dp", "context", "expert"), None),
        P(("dp", "context", "expert"), None),
        P(("dp", "context", "expert"), None),
        P(("dp", "context", "expert"), None),
        P(("dp", "context", "expert")),
        P(("dp", "context", "expert"), None),
        P(("context", "expert"), None, None),
        P(("context", "expert"), None, None),
        P(("context", "expert"), None, None),
        P(("dp", "expert"), "context", None),
    )
    out_specs = (
        P(("dp", "expert"), "context", None),
        P(("dp", "expert"), "context", None),
        P(("dp", "context", "expert")),
        P(("dp", "context", "expert"), None),
        P(("dp", "context", "expert"), None),
        P(("dp", "context", "expert"), None),
        P(("dp", "context", "expert"), None),
        P(("dp", "context", "expert")),
        P(("dp", "context", "expert"), None),
        P(("context", "expert"), "dp", None),
        P(("context", "expert"), "dp", None),
        P(("context", "expert"), "dp", None),
    )
    return jax.shard_map(
        on_device, mesh=mesh, in_specs=in_specs, out_specs=out_specs, check_vma=False
    )
```

```python
import functools
import math

import jax
import jax.numpy as jnp
from jax import lax
from jax.experimental import pallas as pl
from jax.experimental.pallas import tpu as pltpu
from jax.sharding import PartitionSpec as P

MODEL_WIDTH = 1536
HEAD_SIZE = 64
TOP = 8
epsilon = 1e-05
floor_score = -1e30


def rotation_tables(positions):
    half_size = HEAD_SIZE // 2
    exponent = jnp.arange(half_size, dtype=jnp.int32).astype(jnp.float32) * (2.0 / HEAD_SIZE)
    frequency = jnp.exp(-math.log(10000.0) * exponent)
    angles = frequency[:, None] * positions.astype(jnp.float32)[None, :]
    return (jnp.cos(angles), jnp.sin(angles))


def apply_rotation(values, cosine, sine):
    split = values.reshape(-1, 2, HEAD_SIZE // 2, values.shape[1])
    first = split[:, 0]
    second = split[:, 1]
    turned = jnp.stack([first * cosine - second * sine, second * cosine + first * sine], axis=1)
    return turned.reshape(values.shape)


def inverse_rotation(gradient, cosine, sine):
    return apply_rotation(gradient, cosine, -sine)


def norm_back(gradient, normed, inverse):
    return inverse * (gradient - normed * jnp.mean(gradient * normed, axis=-1, keepdims=True))


GROUP = ("context", "expert")
EVERY = ("dp", "context", "expert")


MESH_ID = pl.DeviceIdType.MESH
CHUNK = 512
HALF = 256
UP, DOWN, ACROSS, CORE, DP = 0, 1, 2, 3, 4


def contract_rows(left, right):
    return lax.dot_general(left, right, (((0,), (0,)), ((), ())), preferred_element_type=jnp.float32)


def contract_last(left, right):
    return lax.dot_general(left, right, (((1,), (1,)), ((), ())), preferred_element_type=jnp.float32)


def matmul(left, right):
    return jnp.dot(left, right, preferred_element_type=jnp.float32)


def line_order(z, step):
    half = z // 2
    inner = z + half * (3 - 2 * z)
    base = step + inner * (1 - 2 * step) * (1 - step // 2)
    return base + half * (3 - 2 * base)


def place():
    ctx = lax.axis_index("context")
    z = lax.axis_index("expert")
    y = ctx // 2
    c = ctx % 2
    inner = z + (z // 2) * (3 - 2 * z)

    def device(kind):
        if kind == UP:
            return {"context": ctx, "expert": z + 1}
        if kind == DOWN:
            return {"context": ctx, "expert": z - 1}
        if kind == ACROSS:
            return {"context": (1 - y) * 2 + c, "expert": z}
        if kind == CORE:
            return {"context": y * 2 + 1 - c, "expert": z}
        return {"dp": 1 - lax.axis_index("dp")}

    def per_side(action, more=()):
        @pl.when(z < 3)
        def _():
            action(UP)

        @pl.when(z > 0)
        def _():
            action(DOWN)

        for kind in (ACROSS, CORE, *more):
            action(kind)

    return y, c, z, inner, device, per_side


def block_id(yy, cc, zz):
    return (yy * 2 + cc) * 4 + zz


def greet(per_side, device, count, more=()):
    barrier = pltpu.get_barrier_semaphore()
    per_side(
        lambda kind: pl.semaphore_signal(
            barrier, inc=1, device_id=device(kind), device_id_type=MESH_ID
        ),
        more,
    )
    pl.semaphore_wait(barrier, count)


def swap_copies(pieces, device, send_sem, recv_sem):
    d = lax.axis_index("dp")
    copies = []
    for index, (source, j, target) in enumerate(pieces):
        half = target.shape[0]
        copies.append(
            pltpu.make_async_remote_copy(
                src_ref=source.at[j, pl.ds(pl.multiple_of((1 - d) * half, 128), half), :],
                dst_ref=target,
                send_sem=send_sem.at[index],
                recv_sem=recv_sem.at[index],
                device_id=device(DP),
                device_id_type=MESH_ID,
            )
        )
    return copies


def ring_sum(parts, core_got, y_got, z_got, dp_got, sems):
    single = jnp.float32
    core_send, core_recv, y_send, y_recv, z_send, z_recv, dp_send, dp_recv = sems
    y, c, z, _, device, _ = place()
    d = lax.axis_index("dp")
    rows = parts.shape[1] // 2
    mine = block_id(y, c, z)

    def remote(kind, source, target, send_sem, recv_sem):
        return pltpu.make_async_remote_copy(
            src_ref=source,
            dst_ref=target,
            send_sem=send_sem,
            recv_sem=recv_sem,
            device_id=device(kind),
            device_id_type=MESH_ID,
        )

    def to_core(yy, zz):
        slot = yy * 4 + zz
        return remote(
            CORE, parts.at[block_id(yy, 1 - c, zz)], core_got.at[slot], core_send.at[slot], core_recv.at[slot]
        )

    def to_across(zz):
        return remote(ACROSS, parts.at[block_id(1 - y, c, zz)], y_got.at[zz], y_send.at[zz], y_recv.at[zz])

    def to_line(kind, zz, slot):
        return remote(kind, parts.at[block_id(y, c, zz)], z_got.at[slot], z_send.at[zz], z_recv.at[slot])

    def add(block, got):
        parts[block] = (parts[block].astype(single) + got.astype(single)).astype(parts.dtype)

    def core_sends():
        @pl.loop(0, 4)
        def _(turn):
            zz = line_order(z, 3 - turn)
            to_core(1 - y, zz).start()
            to_core(y, zz).start()

    def across(step):
        zz = line_order(z, step)
        to_core(1 - y, zz).wait_recv()
        add(block_id(1 - y, c, zz), core_got[(1 - y) * 4 + zz])
        to_across(zz).start()
        to_core(y, zz).wait_recv()
        add(block_id(y, c, zz), core_got[y * 4 + zz])

    def line(step):
        zz = line_order(z, step)
        block = block_id(y, c, zz)
        to_across(zz).wait_recv()
        add(block, y_got[zz])
        rising = zz > z
        comes = jnp.logical_or(jnp.logical_and(rising, z > 0), jnp.logical_and(zz < z, z < 3))

        @pl.when(comes)
        def _():
            to_line(CORE, zz, zz).wait_recv()
            add(block, z_got[zz])

        @pl.when(rising)
        def _():
            to_line(UP, zz, zz).start()

        @pl.when(zz == z - 1)
        def _():
            to_line(DOWN, zz, 4).start()

        @pl.when(zz < z - 1)
        def _():
            to_line(DOWN, zz, zz).start()

    there = pl.ds(pl.multiple_of((1 - d) * rows, 16), rows)
    here = pl.ds(pl.multiple_of(d * rows, 16), rows)
    last = remote(DP, parts.at[mine, there, :], dp_got, dp_send, dp_recv)

    def over_dp():
        to_across(z).wait_recv()
        add(mine, y_got[z])

        @pl.when(z > 0)
        def _():
            to_line(CORE, z, z).wait_recv()
            add(mine, z_got[z])

        @pl.when(z < 3)
        def _():
            to_line(CORE, z, 4).wait_recv()
            add(mine, z_got[4])

        last.start()

    def finish(result):
        last.wait_recv()
        result[...] = parts[mine, here, :].astype(single) + dp_got[...].astype(single)
        last.wait_send()

        @pl.loop(0, 4)
        def _(zz):
            to_core(y, zz).wait_send()
            to_core(1 - y, zz).wait_send()
            to_across(zz).wait_send()

            @pl.when(zz != z)
            def _():
                to_line(CORE, zz, zz).wait_send()

    return core_sends, across, line, over_dp, finish


def ring_scratch(rows, width):
    bfloat = jnp.bfloat16
    dma = pltpu.SemaphoreType.DMA
    return [
        pltpu.VMEM((16, 2 * rows, width), bfloat),
        pltpu.VMEM((8, 2 * rows, width), bfloat),
        pltpu.VMEM((4, 2 * rows, width), bfloat),
        pltpu.VMEM((5, 2 * rows, width), bfloat),
        pltpu.VMEM((rows, width), bfloat),
        dma((8,)),
        dma((8,)),
        dma((4,)),
        dma((4,)),
        dma((4,)),
        dma((5,)),
        dma,
        dma,
    ]


def load_parts(refs, parts, sem):
    loads = []
    at = 0
    for index, ref in enumerate(refs):
        rows, size = ref.shape[2], ref.shape[3]
        for plane in range(2):
            loads.append(
                pltpu.make_async_copy(
                    ref.at[plane],
                    parts.at[:, pl.ds(plane * rows, rows), pl.ds(at, size)],
                    sem.at[index * 2 + plane],
                )
            )
        at += size
    return loads


def spread_rows(whole, send_sem, core_sem, recv_sem):
    y, c, z, _, device, _ = place()
    d = lax.axis_index("dp")

    def copy_of(kind, slot, sem):
        return pltpu.make_async_remote_copy(
            src_ref=whole.at[slot],
            dst_ref=whole.at[slot],
            send_sem=sem,
            recv_sem=recv_sem.at[slot],
            device_id=device(kind),
            device_id_type=MESH_ID,
        )

    def own(kind, block):
        return copy_of(kind, d * 16 + block, send_sem.at[kind, block])

    def other(block):
        return copy_of(CORE, (1 - d) * 16 + block, core_sem.at[block])

    def along(kind, zz):
        if kind == UP:
            return jnp.logical_and(z < 3, zz <= z)
        return jnp.logical_and(z > 0, zz >= z)

    def fan(zz, act):
        block = block_id(y, c, zz)
        for kind in (UP, DOWN):

            @pl.when(along(kind, zz))
            def _():
                act(own(kind, block))

        for kind in (ACROSS, DP, CORE):
            act(own(kind, block))

    def fan_across(zz, act):
        block = block_id(1 - y, c, zz)
        act(own(DP, block))
        act(own(CORE, block))

    def fan_dp(zz, act):
        act(other(block_id(y, c, zz)))
        act(other(block_id(1 - y, c, zz)))

    start = lambda copy: copy.start()
    end = lambda copy: copy.wait_send()

    def begin():
        fan(z, start)

    def arrive(step):
        @pl.when(step < 4)
        def _():
            zz = line_order(z, jnp.minimum(step, 3))
            own(ACROSS, block_id(y, c, zz)).wait_recv()
            fan(zz, start)

        @pl.when(step < 5)
        def _():
            zz = line_order(z, jnp.minimum(step - 1, 3))
            own(CORE, block_id(1 - y, c, zz)).wait_recv()
            fan_across(zz, start)

        @pl.when(step > 1)
        def _():
            zz = line_order(z, jnp.maximum(step - 2, 0))
            other(block_id(y, c, zz)).wait_recv()
            other(block_id(1 - y, c, zz)).wait_recv()
            fan_dp(zz, start)

    def finish():
        @pl.loop(0, 4)
        def _(zz):
            for yy in range(2):
                block = block_id(yy, 1 - c, zz)
                own(CORE, block).wait_recv()
                other(block).wait_recv()

    def ends():
        @pl.loop(0, 4)
        def _(zz):
            fan(zz, end)
            fan_across(zz, end)
            fan_dp(zz, end)

    return begin, arrive, finish, ends


def spread_scratch(rows, width):
    dma = pltpu.SemaphoreType.DMA
    return [pltpu.VMEM((32, rows, width), jnp.bfloat16), dma((5, 16)), dma((16,)), dma((32,))]


def gather_kernel(
    query_ref,
    key_ref,
    value_ref,
    small_ref,
    out_ref,
    proj_all,
    small_all,
    out_all,
    local_sem,
    whole,
    *sems,
):
    y, c, z, inner, device, per_side = place()
    mine = lax.axis_index("dp") * 16 + block_id(y, c, z)
    loads = []
    at = 0
    for index, ref in enumerate((query_ref, key_ref, value_ref, small_ref, out_ref)):
        size = ref.shape[1]
        loads.append(
            pltpu.make_async_copy(ref, whole.at[mine, :, pl.ds(at, size)], local_sem.at[index])
        )
        at += size
    for copy in loads:
        copy.start()
    greet(per_side, device, 4 + inner, (DP,))
    for copy in loads:
        copy.wait()
    begin, arrive, finish, ends = spread_rows(whole, *sems)
    begin()

    @pl.loop(1, 6)
    def _(step):
        arrive(step)

    finish()
    results = []
    at = 0
    for index, ref in enumerate((proj_all, small_all, out_all)):
        size = ref.shape[2]
        results.append(
            pltpu.make_async_copy(whole.at[:, :, pl.ds(at, size)], ref, local_sem.at[index])
        )
        at += size
    for copy in results:
        copy.start()
    ends()
    for copy in results:
        copy.wait()


def gather_weights(query, key, value, small, out):
    rows = query.shape[0]
    widths = (query.shape[1] + key.shape[1] + value.shape[1], small.shape[1], out.shape[1])
    anywhere = pl.BlockSpec(memory_space=pl.ANY)
    return pl.pallas_call(
        gather_kernel,
        out_shape=tuple(
            jax.ShapeDtypeStruct((32, rows, width), jnp.bfloat16) for width in widths
        ),
        in_specs=[anywhere] * 5,
        out_specs=(anywhere, anywhere, anywhere),
        scratch_shapes=[pltpu.SemaphoreType.DMA((5,)), *spread_scratch(rows, sum(widths))],
        compiler_params=pltpu.CompilerParams(
            collective_id=0, has_side_effects=True, vmem_limit_bytes=60 * 2**20
        ),
        name="gather_weights",
    )(query, key, value, small, out)


def ring_sum_dp_early(parts, core_got, dp_got, y_got, z_got, sems):
    single = jnp.float32
    core_send, core_recv, dp_send, dp_recv, y_send, y_recv, z_send, z_recv = sems
    y, c, z, _, device, _ = place()
    d = lax.axis_index("dp")
    rows = parts.shape[1] // 2
    mine = block_id(y, c, z)
    there = pl.ds(pl.multiple_of((1 - d) * rows, 16), rows)
    here = pl.ds(pl.multiple_of(d * rows, 16), rows)

    def remote(kind, source, target, send_sem, recv_sem):
        return pltpu.make_async_remote_copy(
            src_ref=source,
            dst_ref=target,
            send_sem=send_sem,
            recv_sem=recv_sem,
            device_id=device(kind),
            device_id_type=MESH_ID,
        )

    def to_core(yy, zz):
        slot = yy * 4 + zz
        return remote(
            CORE, parts.at[block_id(yy, 1 - c, zz)], core_got.at[slot], core_send.at[slot], core_recv.at[slot]
        )

    def to_dp(yy, zz):
        slot = yy * 4 + zz
        return remote(
            DP, parts.at[block_id(yy, c, zz), there, :], dp_got.at[slot], dp_send.at[slot], dp_recv.at[slot]
        )

    def to_across(zz):
        return remote(
            ACROSS, parts.at[block_id(1 - y, c, zz), here, :], y_got.at[zz], y_send.at[zz], y_recv.at[zz]
        )

    def to_line(kind, zz, slot):
        return remote(
            kind, parts.at[block_id(y, c, zz), here, :], z_got.at[slot], z_send.at[zz], z_recv.at[slot]
        )

    def add(block, got):
        parts[block, here, :] = (
            parts[block, here, :].astype(single) + got.astype(single)
        ).astype(parts.dtype)

    def core_sends():
        @pl.loop(0, 4)
        def _(turn):
            zz = line_order(z, 3 - turn)
            to_core(1 - y, zz).start()
            to_core(y, zz).start()

    def meet(step):
        zz = line_order(z, step)
        for yy in (1 - y, y):
            block = block_id(yy, c, zz)
            to_core(yy, zz).wait_recv()
            parts[block] = (
                parts[block].astype(single) + core_got[yy * 4 + zz].astype(single)
            ).astype(parts.dtype)
            to_dp(yy, zz).start()

    def across(step):
        zz = line_order(z, step)
        for yy in (1 - y, y):
            to_dp(yy, zz).wait_recv()
            add(block_id(yy, c, zz), dp_got[yy * 4 + zz])
        to_across(zz).start()

    def line(step):
        zz = line_order(z, step)
        block = block_id(y, c, zz)
        to_across(zz).wait_recv()
        add(block, y_got[zz])
        rising = zz > z
        comes = jnp.logical_or(jnp.logical_and(rising, z > 0), jnp.logical_and(zz < z, z < 3))

        @pl.when(comes)
        def _():
            to_line(CORE, zz, zz).wait_recv()
            add(block, z_got[zz])

        @pl.when(rising)
        def _():
            to_line(UP, zz, zz).start()

        @pl.when(zz == z - 1)
        def _():
            to_line(DOWN, zz, 4).start()

        @pl.when(zz < z - 1)
        def _():
            to_line(DOWN, zz, zz).start()

    def finish(result):
        to_across(z).wait_recv()
        result[...] = parts[mine, here, :].astype(single) + y_got[z].astype(single)

        @pl.when(z > 0)
        def _():
            to_line(CORE, z, z).wait_recv()
            result[...] += z_got[z].astype(single)

        @pl.when(z < 3)
        def _():
            to_line(CORE, z, 4).wait_recv()
            result[...] += z_got[4].astype(single)

        @pl.loop(0, 4)
        def _(zz):
            for yy in (y, 1 - y):
                to_core(yy, zz).wait_send()
                to_dp(yy, zz).wait_send()
            to_across(zz).wait_send()

            @pl.when(zz != z)
            def _():
                to_line(CORE, zz, zz).wait_send()

    return core_sends, meet, across, line, finish


def ring_scratch_dp_early(rows, width):
    bfloat = jnp.bfloat16
    dma = pltpu.SemaphoreType.DMA
    return [
        pltpu.VMEM((16, 2 * rows, width), bfloat),
        pltpu.VMEM((8, 2 * rows, width), bfloat),
        pltpu.VMEM((8, rows, width), bfloat),
        pltpu.VMEM((4, rows, width), bfloat),
        pltpu.VMEM((5, rows, width), bfloat),
        *[dma((n,)) for n in (8, 8, 8, 8, 4, 4, 4, 5)],
    ]


def sums_kernel(
    proj_ref, small_ref, out_ref, sum_ref, out_sum, load_sem, *rings
):
    _, _, _, inner, device, per_side = place()
    ring, out_ring = rings[:13], rings[13:]
    loads = load_parts((proj_ref, small_ref), ring[0], load_sem) + load_parts(
        (out_ref,), out_ring[0], load_sem.at[pl.ds(4, 2)]
    )
    for copy in loads:
        copy.start()
    greet(per_side, device, 4 + inner, (DP,))
    for copy in loads:
        copy.wait()
    core_sends, meet, across, line, finish = ring_sum_dp_early(*ring[:5], ring[5:])
    out_core, out_across, out_line, out_dp, out_finish = ring_sum(*out_ring[:5], out_ring[5:])
    core_sends()
    out_core()

    @pl.loop(0, 4)
    def _(turn):
        meet(3 - turn)
        out_across(3 - turn)

    @pl.loop(0, 4)
    def _(turn):
        across(3 - turn)

        @pl.when(turn < 3)
        def _():
            out_line(3 - jnp.minimum(turn, 2))

        @pl.when(turn > 0)
        def _():
            line(4 - jnp.maximum(turn, 1))

    out_dp()
    finish(sum_ref)
    out_finish(out_sum)


def by_device(x):
    return x.reshape(2, 16, x.shape[0] // 32, x.shape[1])


def sum_gradients(proj, small, out):
    dma = pltpu.SemaphoreType.DMA
    anywhere = pl.BlockSpec(memory_space=pl.ANY)
    vmem = pl.BlockSpec(memory_space=pltpu.VMEM)
    rows = proj.shape[0] // 32
    width = proj.shape[1] + small.shape[1]
    return pl.pallas_call(
        sums_kernel,
        out_shape=(
            jax.ShapeDtypeStruct((rows, width), jnp.float32),
            jax.ShapeDtypeStruct((rows, out.shape[1]), jnp.float32),
        ),
        in_specs=[anywhere] * 3,
        out_specs=(vmem, vmem),
        scratch_shapes=[
            dma((6,)),
            *ring_scratch_dp_early(rows, width),
            *ring_scratch(rows, out.shape[1]),
        ],
        compiler_params=pltpu.CompilerParams(
            collective_id=2, has_side_effects=True, vmem_limit_bytes=56 * 2**20
        ),
        cost_estimate=pl.CostEstimate(flops=1 << 20, bytes_accessed=1 << 16, transcendentals=0),
        name="sum_gradients",
    )(by_device(proj), by_device(small), by_device(out))


def fill_bias(length_ref, bias, ctx):
    blocks, keys, queries = bias.shape
    row = lax.broadcasted_iota(jnp.int32, (keys, queries), 0)
    column = lax.broadcasted_iota(jnp.int32, (keys, queries), 1) + ctx * queries
    for j in range(blocks):
        key = row + j * keys
        allowed = jnp.logical_and(key <= column, key < length_ref[0])
        bias[j] = jnp.where(allowed, 0.0, floor_score)


def head_probs(query, keys, bias):
    scores = [contract_rows(key, query) + bias[j] for j, key in enumerate(keys)]
    peak = jnp.max(scores[0], axis=0, keepdims=True)
    for score in scores[1:]:
        peak = jnp.maximum(peak, jnp.max(score, axis=0, keepdims=True))
    raised = [jnp.exp(score - peak) for score in scores]
    total = jnp.sum(raised[0], axis=0, keepdims=True)
    for value in raised[1:]:
        total = total + jnp.sum(value, axis=0, keepdims=True)
    inverse = 1.0 / total
    return [value * inverse for value in raised]


def attend_kernel(
    query_ref,
    own_ref,
    length_ref,
    mixed_ref,
    all_ref,
    pairs,
    bias,
    first,
    stats,
    local_sem,
    send_sem,
    recv_sem,
):
    bfloat = jnp.bfloat16
    y, c, _, _, device, _ = place()
    mine = y * 2 + c
    own = pltpu.make_async_copy(own_ref, pairs.at[mine], local_sem)
    own.start()
    barrier = pltpu.get_barrier_semaphore()
    for kind in (ACROSS, CORE):
        pl.semaphore_signal(barrier, inc=1, device_id=device(kind), device_id_type=MESH_ID)
    pl.semaphore_wait(barrier, 2)
    own.wait()

    def send(kind, slot, index):
        return pltpu.make_async_remote_copy(
            src_ref=pairs.at[slot],
            dst_ref=pairs.at[slot],
            send_sem=send_sem.at[index],
            recv_sem=recv_sem.at[slot],
            device_id=device(kind),
            device_id_type=MESH_ID,
        )

    far = (1 - y) * 2 + c
    across = send(ACROSS, mine, 0)
    core = send(CORE, mine, 1)
    onward = send(CORE, far, 2)
    across.start()
    core.start()
    fill_bias(length_ref, bias, mine)
    half = pairs.shape[1] // 2
    ratio = query_ref.shape[0] // half
    groups = half // HEAD_SIZE

    def pass_over(blocks, g, merge):
        rows = pl.ds(pl.multiple_of(g * HEAD_SIZE, HEAD_SIZE), HEAD_SIZE)
        low = pl.ds(pl.multiple_of(half + g * HEAD_SIZE, HEAD_SIZE), HEAD_SIZE)
        keys = [pairs[j, rows, :] for j in blocks]
        values = [pairs[j, low, :] for j in blocks]
        for r in range(ratio):
            h = g * ratio + r
            head = pl.ds(pl.multiple_of(h * HEAD_SIZE, HEAD_SIZE), HEAD_SIZE)
            query = query_ref[head, :]
            scores = [contract_rows(key, query) + bias[j] for key, j in zip(keys, blocks)]
            peak = jnp.maximum(
                jnp.max(scores[0], axis=0, keepdims=True), jnp.max(scores[1], axis=0, keepdims=True)
            )
            if merge:
                before = stats[h, 0:1, :]
                peak = jnp.maximum(peak, before)
            raised = [jnp.exp(score - peak) for score in scores]
            total = jnp.sum(raised[0] + raised[1], axis=0, keepdims=True)
            sums = matmul(values[0], raised[0].astype(bfloat)) + matmul(
                values[1], raised[1].astype(bfloat)
            )
            if merge:
                shrink = jnp.exp(before - peak)
                total = total + stats[h, 1:2, :] * shrink
                mixed_ref[head, :] = ((sums + first[head, :] * shrink) / total).astype(bfloat)
            else:
                first[head, :] = sums
                stats[h, 0:1, :] = peak
                stats[h, 1:2, :] = total

    send(CORE, y * 2 + 1 - c, 1).wait_recv()

    @pl.loop(0, groups)
    def _(g):
        pass_over((mine, y * 2 + 1 - c), g, False)

    send(ACROSS, far, 0).wait_recv()
    onward.start()
    send(CORE, (1 - y) * 2 + 1 - c, 2).wait_recv()
    result = pltpu.make_async_copy(pairs, all_ref, local_sem)
    result.start()

    @pl.loop(0, groups)
    def _(g):
        pass_over((far, (1 - y) * 2 + 1 - c), g, True)

    for copy in (across, core, onward):
        copy.wait_send()
    result.wait()


def attend(query, own_pairs, lengths):
    bfloat = jnp.bfloat16
    single = jnp.float32
    dma = pltpu.SemaphoreType.DMA
    anywhere = pl.BlockSpec(memory_space=pl.ANY)
    vmem = pl.BlockSpec(memory_space=pltpu.VMEM)
    pairs = (4, *own_pairs.shape)
    keys = own_pairs.shape[1]
    return pl.pallas_call(
        attend_kernel,
        out_shape=(
            jax.ShapeDtypeStruct(query.shape, bfloat),
            jax.ShapeDtypeStruct(pairs, bfloat),
        ),
        in_specs=[vmem, anywhere, pl.BlockSpec(memory_space=pltpu.SMEM)],
        out_specs=(vmem, anywhere),
        scratch_shapes=[
            pltpu.VMEM(pairs, bfloat),
            pltpu.VMEM((4, keys, query.shape[1]), single),
            pltpu.VMEM(query.shape, single),
            pltpu.VMEM((query.shape[0] // HEAD_SIZE, 8, query.shape[1]), single),
            dma,
            dma((3,)),
            dma((4,)),
        ],
        compiler_params=pltpu.CompilerParams(
            collective_id=3, has_side_effects=True, vmem_limit_bytes=48 * 2**20
        ),
        name="attend",
    )(query, own_pairs, lengths)


def turn_back(gradient, cosine, sine):
    first, second = gradient[: HEAD_SIZE // 2], gradient[HEAD_SIZE // 2 :]
    return jnp.concatenate(
        [first * cosine + second * sine, second * cosine - first * sine], axis=0
    ).astype(jnp.bfloat16)


def attend_back_kernel(
    query_ref,
    pairs_ref,
    grad_ref,
    length_ref,
    cosine_ref,
    sine_ref,
    proj_out,
    parts,
    core_got,
    y_got,
    bias,
    core_send,
    core_recv,
    y_send,
    y_recv,
):
    bfloat = jnp.bfloat16
    single = jnp.float32
    y, c, _, _, device, _ = place()
    mine = y * 2 + c
    barrier = pltpu.get_barrier_semaphore()
    for kind in (ACROSS, CORE):
        pl.semaphore_signal(barrier, inc=1, device_id=device(kind), device_id_type=MESH_ID)
    pl.semaphore_wait(barrier, 2)
    fill_bias(length_ref, bias, mine)
    blocks = pairs_ref.shape[0]
    half = pairs_ref.shape[1] // 2
    ratio = query_ref.shape[0] // half
    groups = half // HEAD_SIZE
    turns = parts.shape[1]
    per_turn = groups // turns
    quarter = half // turns

    def to_core(yy, turn):
        return pltpu.make_async_remote_copy(
            src_ref=parts.at[yy * 2 + 1 - c, turn],
            dst_ref=core_got.at[turn, yy],
            send_sem=core_send.at[turn, yy],
            recv_sem=core_recv.at[turn, yy],
            device_id=device(CORE),
            device_id_type=MESH_ID,
        )

    def to_across(turn):
        return pltpu.make_async_remote_copy(
            src_ref=parts.at[(1 - y) * 2 + c, turn],
            dst_ref=y_got.at[turn],
            send_sem=y_send.at[turn],
            recv_sem=y_recv.at[turn],
            device_id=device(ACROSS),
            device_id_type=MESH_ID,
        )

    def core_stage(turn):
        to_core(1 - y, turn).start()
        to_core(y, turn).start()

    def across_stage(turn):
        to_core(1 - y, turn).wait_recv()
        slot = (1 - y) * 2 + c
        parts[slot, turn] = (
            parts[slot, turn].astype(single) + core_got[turn, 1 - y].astype(single)
        ).astype(bfloat)
        to_across(turn).start()

    def last_stage(turn):
        to_core(y, turn).wait_recv()
        to_across(turn).wait_recv()
        total = (
            parts[mine, turn].astype(single)
            + core_got[turn, y].astype(single)
            + y_got[turn].astype(single)
        )
        at = query_ref.shape[0] + turn * quarter
        for h in range(per_turn):
            rows = slice(h * HEAD_SIZE, (h + 1) * HEAD_SIZE)
            proj_out[pl.ds(at + h * HEAD_SIZE, HEAD_SIZE), :] = turn_back(
                total[rows], cosine_ref[...], sine_ref[...]
            )
        proj_out[pl.ds(at + half, quarter), :] = total[quarter:].astype(bfloat)

    def group(g, carry):
        rows = pl.ds(pl.multiple_of(g * HEAD_SIZE, HEAD_SIZE), HEAD_SIZE)
        low = pl.ds(pl.multiple_of(half + g * HEAD_SIZE, HEAD_SIZE), HEAD_SIZE)
        keys = [pairs_ref[j, rows, :] for j in range(blocks)]
        values = [pairs_ref[j, low, :] for j in range(blocks)]
        grad_keys = [None] * blocks
        grad_values = [None] * blocks
        for r in range(ratio):
            head = pl.ds(pl.multiple_of((g * ratio + r) * HEAD_SIZE, HEAD_SIZE), HEAD_SIZE)
            query = query_ref[head, :]
            grad = grad_ref[head, :]
            probs = head_probs(query, keys, bias)
            grad_probs = [contract_rows(value, grad) for value in values]
            delta = jnp.sum(probs[0] * grad_probs[0], axis=0, keepdims=True)
            for j in range(1, blocks):
                delta = delta + jnp.sum(probs[j] * grad_probs[j], axis=0, keepdims=True)
            grad_query = None
            for j in range(blocks):
                low_probs = probs[j].astype(bfloat)
                grad_score = (probs[j] * (grad_probs[j] - delta)).astype(bfloat)
                terms = (
                    matmul(keys[j], grad_score),
                    contract_last(query, grad_score),
                    contract_last(grad, low_probs),
                )
                grad_query = terms[0] if j == 0 else grad_query + terms[0]
                grad_keys[j] = terms[1] if r == 0 else grad_keys[j] + terms[1]
                grad_values[j] = terms[2] if r == 0 else grad_values[j] + terms[2]
            proj_out[head, :] = turn_back(
                grad_query * HEAD_SIZE ** (-0.5), cosine_ref[...], sine_ref[...]
            )
        turn = g // per_turn
        at = pl.multiple_of((g % per_turn) * HEAD_SIZE, HEAD_SIZE)
        for j in range(blocks):
            parts[j, turn, pl.ds(at, HEAD_SIZE), :] = grad_keys[j].astype(bfloat)
            parts[j, turn, pl.ds(quarter + at, HEAD_SIZE), :] = grad_values[j].astype(bfloat)
        for index in range(turns - 1):

            @pl.when(g == (index + 1) * per_turn - 1)
            def _():
                core_stage(index)

            @pl.when(g == (index + 1) * per_turn)
            def _():
                across_stage(index)

        return carry

    lax.fori_loop(0, groups, group, 0)
    core_stage(turns - 1)
    across_stage(turns - 1)
    for turn in range(turns):
        last_stage(turn)
    for turn in range(turns):
        to_core(y, turn).wait_send()
        to_core(1 - y, turn).wait_send()
        to_across(turn).wait_send()


def attend_back(query, pairs, grad, lengths, cosine, sine):
    bfloat = jnp.bfloat16
    single = jnp.float32
    dma = pltpu.SemaphoreType.DMA
    anywhere = pl.BlockSpec(memory_space=pl.ANY)
    vmem = pl.BlockSpec(memory_space=pltpu.VMEM)
    blocks, rows, keys = pairs.shape
    turns = 2
    part = (turns, rows // turns, keys)
    return pl.pallas_call(
        attend_back_kernel,
        out_shape=jax.ShapeDtypeStruct((query.shape[0] + rows, query.shape[1]), bfloat),
        in_specs=[vmem, vmem, vmem, pl.BlockSpec(memory_space=pltpu.SMEM), vmem, vmem],
        out_specs=vmem,
        scratch_shapes=[
            pltpu.VMEM((blocks, *part), bfloat),
            pltpu.VMEM((turns, 2, *part[1:]), bfloat),
            pltpu.VMEM(part, bfloat),
            pltpu.VMEM((blocks, keys, query.shape[1]), single),
            dma((turns, 2)),
            dma((turns, 2)),
            dma((turns,)),
            dma((turns,)),
        ],
        compiler_params=pltpu.CompilerParams(
            collective_id=4, has_side_effects=True, vmem_limit_bytes=48 * 2**20
        ),
        cost_estimate=pl.CostEstimate(flops=1 << 20, bytes_accessed=1 << 16, transcendentals=0),
        name="attend_back",
    )(query, pairs, grad, lengths, cosine, sine)


def experts_kernel(
    swap,
    hidden_ref,
    final_ref,
    routes_ref,
    router_ref,
    gate_hbm,
    up_hbm,
    down_hbm,
    back_ref,
    part_ref,
    score_got,
    grad_gate_ref,
    grad_up_ref,
    grad_down_ref,
    *refs,
):
    if swap:
        gate_got, up_got, leaving, *refs = refs
        swap = (gate_got, up_got, leaving)
    experts_steps(
        swap,
        hidden_ref,
        final_ref,
        routes_ref,
        router_ref,
        gate_hbm,
        up_hbm,
        down_hbm,
        back_ref,
        part_ref,
        score_got,
        grad_gate_ref,
        grad_up_ref,
        grad_down_ref,
        *refs,
    )


def experts_steps(
    swap,
    hidden_ref,
    final_ref,
    routes_ref,
    router_ref,
    gate_hbm,
    up_hbm,
    down_hbm,
    back_ref,
    part_ref,
    score_got,
    grad_gate_ref,
    grad_up_ref,
    grad_down_ref,
    held,
    w_gate,
    w_up,
    w_down,
    rows_in,
    rows_grad,
    slope_gate,
    slope_up,
    hidden_e,
    picks,
    row_gates,
    work,
    pool,
    before,
    gather_send,
    gather_recv,
    local_sem,
    load_sem,
    part_sem,
    sum_send,
    core_recv,
    y_recv,
    z_recv,
    ready,
    score_ref,
    score_send,
    score_recv,
    swap_send,
    swap_recv,
):
    single = jnp.float32
    bfloat = jnp.bfloat16
    tokens_block = hidden_ref.shape[0]
    width = hidden_ref.shape[1]
    experts = router_ref.shape[0]
    local_exp = w_gate.shape[0]
    hidden_units = w_gate.shape[2]
    capacity = picks.shape[1] // local_exp
    group_rows = 4 * capacity
    ctx = lax.axis_index("context")
    y, c, z, inner, device, per_side = place()

    weights = (
        pltpu.make_async_copy(gate_hbm, w_gate, load_sem.at[0]),
        pltpu.make_async_copy(up_hbm, w_up, load_sem.at[1]),
        pltpu.make_async_copy(down_hbm, w_down, load_sem.at[2]),
    )
    mine = block_id(y, c, z)
    own = pltpu.make_async_copy(hidden_ref, held.at[mine], local_sem)
    own.start()
    for copy in weights:
        copy.start()

    barrier = pltpu.get_barrier_semaphore()

    def member_device(block):
        return {"context": block // 4, "expert": block % 4}

    @pl.loop(1, 16)
    def _(shift):
        pl.semaphore_signal(
            barrier,
            inc=1,
            device_id=member_device((mine + shift) % 16),
            device_id_type=MESH_ID,
        )

    if swap:
        pl.semaphore_signal(barrier, inc=1, device_id=device(DP), device_id_type=MESH_ID)
    pl.semaphore_wait(barrier, 16 if swap else 15)
    own.wait()

    def spread(kind, block):
        return pltpu.make_async_remote_copy(
            src_ref=held.at[block],
            dst_ref=held.at[block],
            send_sem=gather_send.at[kind, block],
            recv_sem=gather_recv.at[block],
            device_id=device(kind),
            device_id_type=MESH_ID,
        )

    def along(kind, zz):
        if kind == UP:
            return jnp.logical_and(z < 3, zz <= z)
        return jnp.logical_and(z > 0, zz >= z)

    def send_on(zz):
        block = block_id(y, c, zz)
        for kind in (UP, DOWN):

            @pl.when(along(kind, zz))
            def _():
                spread(kind, block).start()

        spread(ACROSS, block).start()
        spread(CORE, block).start()

    def forward(step):
        zz = line_order(z, step)
        spread(ACROSS, block_id(y, c, zz)).wait_recv()
        send_on(zz)

    send_on(z)
    row = lax.broadcasted_iota(jnp.int32, (tokens_block, tokens_block), 0)
    column = lax.broadcasted_iota(jnp.int32, (tokens_block, tokens_block), 1)
    before[...] = jnp.where(row < column, 1.0, 0.0).astype(bfloat)
    for copy in weights:
        copy.wait()
    first = (ctx * 4 + z) * local_exp

    def member(zz, p):
        yy = y + (p // 2) * (1 - 2 * y)
        cc = c + (p % 2) * (1 - 2 * c)
        return block_id(yy, cc, zz)

    def load_final(zz, p):
        return pltpu.make_async_copy(final_ref.at[member(zz, p)], pool.at[p], load_sem.at[p])

    def store_part(zz, p):
        return pltpu.make_async_copy(
            pool.at[4 + p % 2], part_ref.at[member(zz, p)], part_sem.at[p % 2]
        )

    def forward_group(step, carry):
        zz = line_order(z, step)
        after = step + 1 + inner * jnp.minimum(step, 1)

        @pl.when(after < 4)
        def _():
            forward(after)

        @pl.when(jnp.logical_and(step == 0, inner == 1))
        def _():
            forward(2)

        @pl.loop(0, 4)
        def _(p):
            load_final(zz, p).start()

        spread(CORE, block_id(y, 1 - c, zz)).wait_recv()
        spread(CORE, block_id(1 - y, c, zz)).wait_recv()
        spread(CORE, block_id(1 - y, c, zz)).start()
        spread(CORE, block_id(1 - y, 1 - c, zz)).wait_recv()

        @pl.loop(0, 4)
        def _(p):
            block = member(zz, p)
            tokens_in = held[block]
            logits = contract_last(router_ref[...], tokens_in)
            expert_row = lax.broadcasted_iota(jnp.int32, (experts, tokens_block), 0)
            routed = jnp.zeros((experts, tokens_block), single)
            for k in range(routes_ref.shape[1]):
                routed = routed + jnp.where(routes_ref[block, k : k + 1, :] == expert_row, 1.0, 0.0)
            named = routed > 0.5
            peak = jnp.max(jnp.where(named, logits, floor_score), axis=0, keepdims=True)
            raised = jnp.where(named, jnp.exp(jnp.minimum(logits - peak, 0.0)), 0.0)
            gates = raised / jnp.sum(raised, axis=0, keepdims=True)
            eight = lax.broadcasted_iota(jnp.int32, (8, tokens_block), 0)
            masks = jnp.zeros((8, tokens_block), single)
            own_mask = []
            own_gate = []
            for j in range(local_exp):
                here = expert_row == first + j
                own_mask.append(jnp.sum(jnp.where(here, routed, 0.0), axis=0, keepdims=True))
                own_gate.append(jnp.sum(jnp.where(here, gates, 0.0), axis=0, keepdims=True))
                masks = masks + jnp.where(eight == j, own_mask[j], 0.0)
            rank = matmul(masks.astype(bfloat), before[...])
            slot = lax.broadcasted_iota(jnp.int32, (capacity, tokens_block), 0).astype(single)
            for j in range(local_exp):
                hit = jnp.logical_and(slot == rank[j : j + 1, :], own_mask[j] > 0.5)
                pick = jnp.where(hit, 1.0, 0.0)
                picks[step * 4 + p, pl.ds(j * capacity, capacity), :] = pick.astype(bfloat)
                gate_column = jnp.sum(pick * own_gate[j], axis=1, keepdims=True)
                row_gates[p, pl.ds(j * capacity, capacity), :] = jnp.broadcast_to(
                    gate_column, (capacity, 128)
                )
            at = pl.multiple_of(step * group_rows + p * capacity, 32)
            for n in range(width // CHUNK):
                part = pl.ds(n * CHUNK, CHUNK)
                got = matmul(picks[step * 4 + p], held[block, :, part]).astype(bfloat)
                for j in range(local_exp):
                    rows_in[j, pl.ds(at, capacity), part] = got[j * capacity : (j + 1) * capacity]

        base = pl.multiple_of(step * group_rows, 128)
        for j in range(local_exp):
            given = rows_in[j, pl.ds(base, group_rows), :]
            for n in range(hidden_units // HALF):
                part = pl.ds(n * HALF, HALF)
                gate_pre = matmul(given, w_gate[j, :, part])
                up_pre = matmul(given, w_up[j, :, part])
                sigmoid = 1.0 / (1.0 + jnp.exp(-gate_pre))
                silu = gate_pre * sigmoid
                hidden_e[j, pl.ds(base, group_rows), part] = (silu * up_pre).astype(bfloat)
                slope_gate[j, pl.ds(base, group_rows), part] = (
                    up_pre * sigmoid * (1.0 + gate_pre * (1.0 - sigmoid))
                ).astype(bfloat)
                slope_up[j, pl.ds(base, group_rows), part] = silu.astype(bfloat)
            for n in range(width // CHUNK):
                part = pl.ds(n * CHUNK, CHUNK)
                work[j, :, part] = matmul(
                    hidden_e[j, pl.ds(base, group_rows), :], w_down[j, :, part]
                ).astype(bfloat)

        @pl.loop(0, 4)
        def _(p):
            block = member(zz, p)
            at = pl.multiple_of(step * group_rows + p * capacity, 32)
            local = pl.multiple_of(p * capacity, 32)
            pick = picks[step * 4 + p]
            weight = row_gates[p][:, 0:1]
            weighted = (pick.astype(single) * weight).astype(bfloat)
            load_final(zz, p).wait()

            @pl.when(jnp.logical_or(step > 0, p > 1))
            def _():
                store_part(zz, p).wait()

            row_score = jnp.zeros((local_exp * capacity, 1), single)
            for n in range(width // CHUNK):
                part = pl.ds(n * CHUNK, CHUNK)
                out = jnp.concatenate(
                    [work[j, pl.ds(local, capacity), part] for j in range(local_exp)], axis=0
                )
                pool[4 + p % 2, :, part] = contract_rows(weighted, out).astype(bfloat)
                final = matmul(pick, pool[p, :, part])
                row_score = row_score + jnp.sum(final * out.astype(single), axis=1, keepdims=True)
                graded = (final * weight).astype(bfloat)
                for j in range(local_exp):
                    rows_grad[j, pl.ds(at, capacity), part] = graded[j * capacity : (j + 1) * capacity]
            store_part(zz, p).start()
            spread_score = pick.astype(single) * row_score
            eight = lax.broadcasted_iota(jnp.int32, (8, tokens_block), 0)
            scores = jnp.zeros((8, tokens_block), single)
            for j in range(local_exp):
                total = jnp.sum(spread_score[j * capacity : (j + 1) * capacity], axis=0, keepdims=True)
                scores = scores + jnp.where(eight == j, total, 0.0)
            score_ref[block] = scores

        return carry

    lax.fori_loop(0, 4, forward_group, 0)

    def score_copy(block, source):
        return pltpu.make_async_remote_copy(
            src_ref=score_ref.at[block],
            dst_ref=score_got.at[source],
            send_sem=score_send.at[block],
            recv_sem=score_recv.at[source],
            device_id=member_device(block),
            device_id_type=MESH_ID,
        )

    @pl.loop(1, 16)
    def _(shift):
        score_copy((mine + shift) % 16, mine).start()

    score_got[mine] = score_ref[mine]

    @pl.loop(2, 4)
    def _(p):
        store_part(line_order(z, 3), p).wait()

    @pl.loop(0, 4)
    def _(zz):
        block = block_id(y, c, zz)
        for kind in (UP, DOWN):

            @pl.when(along(kind, zz))
            def _():
                spread(kind, block).wait_send()

        spread(ACROSS, block).wait_send()
        spread(CORE, block).wait_send()
        spread(CORE, block_id(1 - y, c, zz)).wait_send()

    opposite = {UP: DOWN, DOWN: UP, ACROSS: ACROSS, CORE: CORE}
    per_side(
        lambda kind: pl.semaphore_signal(
            ready.at[opposite[kind]], inc=1, device_id=device(kind), device_id_type=MESH_ID
        )
    )

    def sum_copy(kind, source, target, send_index, recv_sem):
        return pltpu.make_async_remote_copy(
            src_ref=source,
            dst_ref=target,
            send_sem=sum_send.at[send_index],
            recv_sem=recv_sem,
            device_id=device(kind),
            device_id_type=MESH_ID,
        )

    def to_core(turn, p, zz):
        slot = (y + p * (1 - 2 * y)) * 4 + zz
        index = turn * 2 + p
        return sum_copy(CORE, pool.at[index], held.at[slot], index, core_recv.at[slot])

    def from_core(slot):
        return sum_copy(CORE, pool.at[0], held.at[slot], 0, core_recv.at[slot])

    def to_across(zz):
        return sum_copy(ACROSS, held.at[(1 - y) * 4 + zz], held.at[8 + zz], 4 + zz, y_recv.at[zz])

    def to_line(kind, zz, last):
        return sum_copy(
            kind,
            held.at[y * 4 + zz],
            pool.at[5] if last else held.at[12 + zz],
            8 + zz,
            z_recv.at[4 if last else zz],
        )

    def add_up(slot, *others):
        @pl.loop(0, tokens_block // 64)
        def _(r):
            rows = pl.ds(pl.multiple_of(r * 64, 64), 64)
            total = held[slot, rows, :].astype(single)
            for ref, index in others:
                total = total + ref[index, rows, :].astype(single)
            held[slot, rows, :] = total.astype(bfloat)

    def back_block(step, p, target, index, onto):
        local = pl.multiple_of(p * capacity, 32)
        pick = picks[step * 4 + p]
        for n in range(width // CHUNK):
            part = pl.ds(n * CHUNK, CHUNK)
            grads = jnp.concatenate(
                [work[j, pl.ds(local, capacity), part] for j in range(local_exp)], axis=0
            )
            block = contract_rows(pick, grads)
            if onto:
                block = block + target[index, :, part].astype(single)
            target[index, :, part] = block.astype(bfloat)

    def line_sum(step):
        zz = line_order(z, step)
        slot = y * 4 + zz
        to_across(zz).wait_recv()
        rising = zz > z
        comes = jnp.logical_or(jnp.logical_and(rising, z > 0), jnp.logical_and(zz < z, z < 3))

        @pl.when(comes)
        def _():
            to_line(CORE, zz, False).wait_recv()
            add_up(slot, (held, 8 + zz), (held, 12 + zz))

        @pl.when(jnp.logical_not(comes))
        def _():
            add_up(slot, (held, 8 + zz))

        @pl.when(rising)
        def _():
            to_line(UP, zz, False).start()

        @pl.when(zz == z - 1)
        def _():
            to_line(DOWN, zz, True).start()

        @pl.when(zz < z - 1)
        def _():
            to_line(DOWN, zz, False).start()

    def at_end(action):
        pl.when(inner == 0)(action)

    def at_middle(action):
        pl.when(inner == 1)(action)

    def backward_group(turn_step, carry):
        step = 3 - turn_step
        zz = line_order(z, step)
        turn = step % 2
        base = pl.multiple_of(step * group_rows, 128)
        for j in range(local_exp):
            for n in range(hidden_units // HALF):
                part = pl.ds(n * HALF, HALF)
                grad_hidden = (
                    contract_last(rows_grad[j, pl.ds(base, group_rows), :], w_down[j, part, :])
                    .astype(bfloat)
                    .astype(single)
                )
                slope_gate[j, pl.ds(base, group_rows), part] = (
                    grad_hidden * slope_gate[j, pl.ds(base, group_rows), part].astype(single)
                ).astype(bfloat)
                slope_up[j, pl.ds(base, group_rows), part] = (
                    grad_hidden * slope_up[j, pl.ds(base, group_rows), part].astype(single)
                ).astype(bfloat)
            for n in range(width // CHUNK):
                part = pl.ds(n * CHUNK, CHUNK)
                work[j, :, part] = (
                    contract_last(slope_gate[j, pl.ds(base, group_rows), :], w_gate[j, part, :])
                    + contract_last(slope_up[j, pl.ds(base, group_rows), :], w_up[j, part, :])
                ).astype(bfloat)

        @pl.when(turn_step == 0)
        def _():
            per_side(lambda kind: pl.semaphore_wait(ready.at[kind], 1))

        for p, member_p in ((1, 3), (0, 1)):

            @pl.when(turn_step > 1)
            def _():
                to_core(turn, p, zz).wait_send()

            back_block(step, member_p, pool, turn * 2 + p, False)
            to_core(turn, p, zz).start()

        other = (1 - y) * 4 + zz
        from_core(other).wait_recv()
        back_block(step, 2, held, other, True)
        to_across(zz).start()
        slot = y * 4 + zz
        from_core(slot).wait_recv()
        back_block(step, 0, held, slot, True)

        @pl.when(turn_step == 2)
        def _():
            at_end(lambda: line_sum(3))

        return carry

    lax.fori_loop(0, 4, backward_group, 0)
    at_middle(lambda: line_sum(3))
    at_end(lambda: line_sum(2))

    def stores(j):
        pairs = ((w_gate, grad_gate_ref), (w_up, grad_up_ref), (w_down, grad_down_ref))
        if not swap:
            return [
                pltpu.make_async_copy(source.at[j], target.at[j], load_sem.at[3 * j + i])
                for i, (source, target) in enumerate(pairs)
            ]
        d = lax.axis_index("dp")
        copies = []
        for i, (source, target) in enumerate(pairs):
            size = target.shape[1]
            here = pl.ds(pl.multiple_of(d * size, 128), size)
            copies.append(
                pltpu.make_async_copy(source.at[j, here, :], target.at[j], load_sem.at[3 * j + i])
            )
        there = lambda size: pl.ds(pl.multiple_of((1 - d) * size, 128), size)
        low = w_down.shape[1] // 2
        leaving = [
            (
                w_down.at[j, there(low), pl.ds(n * hidden_units, hidden_units)],
                swap[2].at[2 + j, pl.ds(n * low, low), :],
            )
            for n in range(width // hidden_units)
        ]
        if j == 1:
            leaving += [
                (source.at[1, there(width // 2), :], swap[2].at[i])
                for i, source in enumerate((w_gate, w_up))
            ]
        for i, (source, target) in enumerate(leaving):
            copies.append(pltpu.make_async_copy(source, target, load_sem.at[6 + 3 * j + i]))
        return copies

    def weight_grads(j):
        @pl.loop(0, width // CHUNK)
        def _(n):
            part = pl.ds(pl.multiple_of(n * CHUNK, CHUNK), CHUNK)
            w_gate[j, part, :] = contract_rows(rows_in[j, :, part], slope_gate[j]).astype(bfloat)
            w_up[j, part, :] = contract_rows(rows_in[j, :, part], slope_up[j]).astype(bfloat)
            w_down[j, :, part] = contract_rows(hidden_e[j], rows_grad[j, :, part]).astype(bfloat)

        for copy in stores(j):
            copy.start()

    weight_grads(0)
    swaps = []
    if swap:
        swaps = swap_copies(
            ((w_gate, 0, swap[0]), (w_up, 0, swap[1])), device, swap_send, swap_recv
        )
        for copy in swaps:
            copy.start()
    weight_grads(1)
    at_middle(lambda: line_sum(2))
    line_sum(1)
    slot = y * 4 + z
    to_across(z).wait_recv()
    add_up(slot, (held, 8 + z))

    @pl.when(z > 0)
    def _():
        to_line(CORE, z, False).wait_recv()
        add_up(slot, (held, 12 + z))

    @pl.when(z < 3)
    def _():
        to_line(CORE, z, True).wait_recv()
        add_up(slot, (pool, 5))

    result = pltpu.make_async_copy(held.at[slot], back_ref, local_sem)
    result.start()
    for j in range(local_exp):
        for copy in stores(j):
            copy.wait()
    for turn in range(2):
        for p in range(2):
            to_core(turn, p, z).wait_send()

    @pl.loop(0, 4)
    def _(zz):
        to_across(zz).wait_send()

        @pl.when(zz != z)
        def _():
            to_line(CORE, zz, False).wait_send()

    @pl.loop(1, 16)
    def _(shift):
        other = (mine + shift) % 16
        score_copy(other, mine).wait_send()
        score_copy(other, other).wait_recv()

    for copy in swaps:
        copy.wait()
    result.wait()


def experts_on_owner(
    hidden, final_all, routes_all, router_rows, w_gate, w_up, w_down, capacity, swap
):
    blocks = final_all.shape[0]
    tokens_block, width = hidden.shape
    local_exp, _, units = w_gate.shape
    bfloat = jnp.bfloat16
    single = jnp.float32
    rows = blocks * capacity
    grads = [x.shape for x in (w_gate, w_up, w_down)]
    if swap:
        wide, low = (width // 2, units), (units // 2, width)
        grads = [(2, *wide), (2, *wide), (2, *low), wide, wide, (4, *wide)]
    anywhere = pl.BlockSpec(memory_space=pl.ANY)
    vmem = pl.BlockSpec(memory_space=pltpu.VMEM)
    dma = pltpu.SemaphoreType.DMA
    return pl.pallas_call(
        functools.partial(experts_kernel, swap),
        out_shape=(
            jax.ShapeDtypeStruct((tokens_block, width), bfloat),
            jax.ShapeDtypeStruct((blocks, tokens_block, width), bfloat),
            jax.ShapeDtypeStruct((blocks, 8, tokens_block), single),
            *(jax.ShapeDtypeStruct(shape, bfloat) for shape in grads),
        ),
        in_specs=[anywhere, anywhere, vmem, vmem, anywhere, anywhere, anywhere],
        out_specs=(anywhere, anywhere, vmem, *([anywhere] * len(grads))),
        scratch_shapes=[
            pltpu.VMEM((blocks, tokens_block, width), bfloat),
            pltpu.VMEM(w_gate.shape, bfloat),
            pltpu.VMEM(w_up.shape, bfloat),
            pltpu.VMEM(w_down.shape, bfloat),
            pltpu.VMEM((local_exp, rows, width), bfloat),
            pltpu.VMEM((local_exp, rows, width), bfloat),
            pltpu.VMEM((local_exp, rows, units), bfloat),
            pltpu.VMEM((local_exp, rows, units), bfloat),
            pltpu.VMEM((local_exp, rows, units), bfloat),
            pltpu.VMEM((blocks, local_exp * capacity, tokens_block), bfloat),
            pltpu.VMEM((4, local_exp * capacity, 128), single),
            pltpu.VMEM((local_exp, 4 * capacity, width), bfloat),
            pltpu.VMEM((6, tokens_block, width), bfloat),
            pltpu.VMEM((tokens_block, tokens_block), bfloat),
            dma((4, blocks)),
            dma((blocks,)),
            dma,
            dma((14,)),
            dma((2,)),
            dma((12,)),
            dma((8,)),
            dma((4,)),
            dma((5,)),
            pltpu.SemaphoreType.REGULAR((4,)),
            pltpu.VMEM((blocks, 8, tokens_block), single),
            dma((16,)),
            dma((16,)),
            dma((2,)),
            dma((2,)),
        ],
        compiler_params=pltpu.CompilerParams(
            collective_id=1, has_side_effects=True, vmem_limit_bytes=63 * 2**20
        ),
        name="experts",
    )(hidden, final_all, routes_all, router_rows, w_gate, w_up, w_down)


def on_device(
    tokens,
    lengths,
    routes,
    gain_attn,
    w_query,
    key_weight,
    value_weight,
    w_out,
    gain_ffn,
    w_router,
    w_gate,
    w_up,
    w_down,
    cotangent,
):
    tokens_own = tokens.shape[1]
    exp_count = lax.axis_size("expert")
    ctx_count = lax.axis_size("context")
    local_exp = w_gate.shape[0]
    experts = local_exp * ctx_count * exp_count
    capacity = tokens_own * TOP * 3 // (2 * experts)
    bfloat = jnp.bfloat16
    single = jnp.float32
    query_width = w_query.shape[1]
    key_width = key_weight.shape[1]
    proj_width = query_width + 2 * key_width
    own_rows = w_query.shape[0]
    pair = lax.axis_size("dp") == 2
    small = jnp.concatenate(
        [
            w_router,
            gain_attn[:, None],
            gain_ffn[:, None],
            jnp.zeros((own_rows, 64 - experts - 2), bfloat),
        ],
        axis=1,
    )
    if pair:
        packed = routes[0].T.reshape(-1, 64).astype(bfloat)
        packed = jnp.pad(packed, ((0, own_rows - packed.shape[0]), (0, 0)))
        early, small_all, out_w = gather_weights(
            w_query, key_weight, value_weight, jnp.concatenate([small, packed], axis=1), w_out
        )
        out_w = out_w.reshape(-1, out_w.shape[2])
        routes_all = lax.dynamic_slice(
            small_all, (lax.axis_index("dp") * 16, 0, 64), (16, tokens_own * TOP // 64, 64)
        )
        routes_all = routes_all.astype(jnp.int32).reshape(16, TOP, tokens_own)
        proj_w = early.reshape(-1, proj_width)
        small_all = small_all.reshape(-1, small_all.shape[2])
    else:
        proj_w = jnp.concatenate([w_query, key_weight, value_weight], axis=1)
        proj_w = lax.all_gather(proj_w, EVERY, axis=0, tiled=True)
        small_all = lax.all_gather(small, EVERY, axis=0, tiled=True)
        out_w = lax.all_gather(w_out, EVERY, axis=0, tiled=True)
        routes_all = lax.all_gather(routes[0].T, GROUP, axis=0, tiled=False)
    positions = lax.axis_index("context") * tokens_own + jnp.arange(tokens_own, dtype=jnp.int32)
    valid = (positions < lengths[0]).astype(single)[:, None]
    grad_final = cotangent[0].astype(single) * valid
    final_all = lax.all_gather(grad_final.astype(bfloat), GROUP, axis=0, tiled=False)
    router_w = small_all[:, :experts]
    gain_one = small_all[:, experts].astype(single)
    gain_two = small_all[:, experts + 1].astype(single)
    cosine, sine = rotation_tables(positions)

    inputs = tokens[0].astype(single)
    inverse_one = lax.rsqrt(jnp.mean(inputs * inputs, axis=-1, keepdims=True) + epsilon)
    normed_one = inputs * inverse_one
    hidden_one = (normed_one * gain_one).astype(bfloat)
    projected = jnp.einsum("de,sd->es", proj_w, hidden_one, preferred_element_type=single)
    rotated = apply_rotation(projected[: query_width + key_width], cosine, sine).astype(bfloat)
    query = rotated[:query_width] * HEAD_SIZE ** (-0.5)
    own_pairs = jnp.concatenate(
        [rotated[query_width:], projected[query_width + key_width :].astype(bfloat)], axis=0
    )
    mixed, pairs = attend(query, own_pairs, lengths)
    resid = inputs + jnp.einsum("es,ed->sd", mixed, out_w, preferred_element_type=single)
    inverse_two = lax.rsqrt(jnp.mean(resid * resid, axis=-1, keepdims=True) + epsilon)
    normed_two = resid * inverse_two
    hidden_two = (normed_two * gain_two).astype(bfloat)

    grad_hidden, combined, scores, *expert_grads = experts_on_owner(
        hidden_two, final_all, routes_all, router_w.T, w_gate, w_up, w_down, capacity, pair
    )
    expert_grads, got = expert_grads[:3], expert_grads[3:]
    combined = lax.psum_scatter(combined, GROUP, scatter_dimension=0, tiled=False)

    if pair:
        moved = lax.ppermute(got[2], "dp", ((0, 1), (1, 0)))
        low = w_down.shape[1] // 2
        others = (
            jnp.stack([got[0], moved[0]]),
            jnp.stack([got[1], moved[1]]),
            jnp.concatenate(
                [moved[2:, n * low : (n + 1) * low] for n in range(MODEL_WIDTH // w_down.shape[1])],
                axis=2,
            ),
        )
    scores = scores[:, :local_exp]
    grad_gates = scores.reshape(experts, tokens_own).T

    routed = jnp.any(routes[0][:, :, None] == jnp.arange(experts, dtype=jnp.int32), axis=1)
    logits = jnp.einsum("sd,de->se", hidden_two, router_w, preferred_element_type=single)
    gates = jax.nn.softmax(jnp.where(routed, logits, floor_score), axis=-1)
    gates = jnp.where(routed, gates, 0.0)
    gate_mean = jnp.sum(gates * grad_gates, axis=-1, keepdims=True)
    grad_logits = (gates * (grad_gates - gate_mean)).astype(bfloat)
    grad_w_router = jnp.einsum("sd,se->de", hidden_two, grad_logits, preferred_element_type=single)
    grad_hidden_two = grad_hidden.astype(single) + jnp.einsum(
        "se,de->sd", grad_logits, router_w, preferred_element_type=single
    )
    grad_gain_ffn = jnp.sum(grad_hidden_two * normed_two, axis=0)
    grad_resid = norm_back(grad_hidden_two * gain_two, normed_two, inverse_two) + grad_final
    grad_attn = grad_resid.astype(bfloat)

    grad_out_w = jnp.einsum("es,sd->ed", mixed, grad_attn, preferred_element_type=single)
    grad_mixed = jnp.einsum("ed,sd->es", out_w, grad_attn, preferred_element_type=single)
    grad_out_w = grad_out_w.astype(bfloat)
    grad_proj = attend_back(query, pairs, grad_mixed.astype(bfloat), lengths, cosine, sine)
    grad_proj_w = jnp.einsum("sd,es->de", hidden_one, grad_proj, preferred_element_type=single)
    grad_hidden_one = jnp.einsum("es,de->sd", grad_proj, proj_w, preferred_element_type=single)
    grad_gain_attn = jnp.sum(grad_hidden_one * normed_one, axis=0)
    grad_tokens = norm_back(grad_hidden_one * gain_one, normed_one, inverse_one) + grad_resid

    grad_small = jnp.concatenate(
        [
            grad_w_router,
            grad_gain_attn[:, None],
            grad_gain_ffn[:, None],
            jnp.zeros((MODEL_WIDTH, 128 - experts - 2), single),
        ],
        axis=1,
    ).astype(bfloat)
    grad_proj_w = grad_proj_w.astype(bfloat)
    if pair:
        expert_sums = tuple(
            own.astype(single) + other.astype(single)
            for own, other in zip(expert_grads, others)
        )
        grad_proj_w, grad_tokens, expert_sums = lax.optimization_barrier(
            (grad_proj_w, grad_tokens, expert_sums)
        )
        summed, out_sum = sum_gradients(grad_proj_w, grad_small, grad_out_w)
    else:
        summed = lax.psum_scatter(
            jnp.concatenate([grad_proj_w, grad_small, grad_out_w], axis=1),
            EVERY,
            scatter_dimension=0,
            tiled=True,
        ).astype(single)
        out_sum = summed[:, proj_width + 128 :]
        expert_sums = tuple(
            lax.psum_scatter(x, "dp", scatter_dimension=1, tiled=True).astype(single)
            for x in expert_grads
        )
    combined, summed = lax.optimization_barrier((combined, summed))
    block_out = (valid * (resid + combined.astype(single))).astype(bfloat)
    return (
        block_out[None],
        grad_tokens[None],
        summed[:, proj_width + experts],
        summed[:, :query_width],
        summed[:, query_width : query_width + key_width],
        summed[:, query_width + key_width : proj_width],
        out_sum,
        summed[:, proj_width + experts + 1],
        summed[:, proj_width : proj_width + experts],
        *expert_sums,
    )


def solution(mesh):
    in_specs = (
        P(("dp", "expert"), "context", None),
        P(("dp", "expert")),
        P(("dp", "expert"), "context", None),
        P(("dp", "context", "expert")),
        P(("dp", "context", "expert"), None),
        P(("dp", "context", "expert"), None),
        P(("dp", "context", "expert"), None),
        P(("dp", "context", "expert"), None),
        P(("dp", "context", "expert")),
        P(("dp", "context", "expert"), None),
        P(("context", "expert"), None, None),
        P(("context", "expert"), None, None),
        P(("context", "expert"), None, None),
        P(("dp", "expert"), "context", None),
    )
    out_specs = (
        P(("dp", "expert"), "context", None),
        P(("dp", "expert"), "context", None),
        P(("dp", "context", "expert")),
        P(("dp", "context", "expert"), None),
        P(("dp", "context", "expert"), None),
        P(("dp", "context", "expert"), None),
        P(("dp", "context", "expert"), None),
        P(("dp", "context", "expert")),
        P(("dp", "context", "expert"), None),
        P(("context", "expert"), "dp", None),
        P(("context", "expert"), "dp", None),
        P(("context", "expert"), "dp", None),
    )
    return jax.shard_map(
        on_device, mesh=mesh, in_specs=in_specs, out_specs=out_specs, check_vma=False
    )
```

```python
import functools
import math

import jax
import jax.numpy as jnp
from jax import lax
from jax.experimental import pallas as pl
from jax.experimental.pallas import tpu as pltpu
from jax.sharding import PartitionSpec as P

MODEL_WIDTH = 1536
HEAD_SIZE = 64
TOP = 8
epsilon = 1e-05
floor_score = -1e30


def rotation_tables(positions):
    half_size = HEAD_SIZE // 2
    exponent = jnp.arange(half_size, dtype=jnp.int32).astype(jnp.float32) * (2.0 / HEAD_SIZE)
    frequency = jnp.exp(-math.log(10000.0) * exponent)
    angles = frequency[:, None] * positions.astype(jnp.float32)[None, :]
    return (jnp.cos(angles), jnp.sin(angles))


def apply_rotation(values, cosine, sine):
    split = values.reshape(-1, 2, HEAD_SIZE // 2, values.shape[1])
    first = split[:, 0]
    second = split[:, 1]
    turned = jnp.stack([first * cosine - second * sine, second * cosine + first * sine], axis=1)
    return turned.reshape(values.shape)


def inverse_rotation(gradient, cosine, sine):
    return apply_rotation(gradient, cosine, -sine)


def norm_back(gradient, normed, inverse):
    return inverse * (gradient - normed * jnp.mean(gradient * normed, axis=-1, keepdims=True))


GROUP = ("context", "expert")
EVERY = ("dp", "context", "expert")


MESH_ID = pl.DeviceIdType.MESH
CHUNK = 512
HALF = 256
UP, DOWN, ACROSS, CORE, DP = 0, 1, 2, 3, 4


def contract_rows(left, right):
    return lax.dot_general(left, right, (((0,), (0,)), ((), ())), preferred_element_type=jnp.float32)


def contract_last(left, right):
    return lax.dot_general(left, right, (((1,), (1,)), ((), ())), preferred_element_type=jnp.float32)


def matmul(left, right):
    return jnp.dot(left, right, preferred_element_type=jnp.float32)


def line_order(z, step):
    half = z // 2
    inner = z + half * (3 - 2 * z)
    base = step + inner * (1 - 2 * step) * (1 - step // 2)
    return base + half * (3 - 2 * base)


def place():
    ctx = lax.axis_index("context")
    z = lax.axis_index("expert")
    y = ctx // 2
    c = ctx % 2
    inner = z + (z // 2) * (3 - 2 * z)

    def device(kind):
        if kind == UP:
            return {"context": ctx, "expert": z + 1}
        if kind == DOWN:
            return {"context": ctx, "expert": z - 1}
        if kind == ACROSS:
            return {"context": (1 - y) * 2 + c, "expert": z}
        if kind == CORE:
            return {"context": y * 2 + 1 - c, "expert": z}
        return {"dp": 1 - lax.axis_index("dp")}

    def per_side(action, more=()):
        @pl.when(z < 3)
        def _():
            action(UP)

        @pl.when(z > 0)
        def _():
            action(DOWN)

        for kind in (ACROSS, CORE, *more):
            action(kind)

    return y, c, z, inner, device, per_side


def block_id(yy, cc, zz):
    return (yy * 2 + cc) * 4 + zz


def greet(per_side, device, count, more=()):
    barrier = pltpu.get_barrier_semaphore()
    per_side(
        lambda kind: pl.semaphore_signal(
            barrier, inc=1, device_id=device(kind), device_id_type=MESH_ID
        ),
        more,
    )
    pl.semaphore_wait(barrier, count)


def swap_copies(pieces, device, send_sem, recv_sem):
    d = lax.axis_index("dp")
    copies = []
    for index, (source, j, target) in enumerate(pieces):
        half = target.shape[0]
        copies.append(
            pltpu.make_async_remote_copy(
                src_ref=source.at[j, pl.ds(pl.multiple_of((1 - d) * half, 128), half), :],
                dst_ref=target,
                send_sem=send_sem.at[index],
                recv_sem=recv_sem.at[index],
                device_id=device(DP),
                device_id_type=MESH_ID,
            )
        )
    return copies


def ring_sum(parts, core_got, y_got, z_got, dp_got, sems):
    single = jnp.float32
    core_send, core_recv, y_send, y_recv, z_send, z_recv, dp_send, dp_recv = sems
    y, c, z, _, device, _ = place()
    d = lax.axis_index("dp")
    rows = parts.shape[1] // 2
    mine = block_id(y, c, z)

    def remote(kind, source, target, send_sem, recv_sem):
        return pltpu.make_async_remote_copy(
            src_ref=source,
            dst_ref=target,
            send_sem=send_sem,
            recv_sem=recv_sem,
            device_id=device(kind),
            device_id_type=MESH_ID,
        )

    def to_core(yy, zz):
        slot = yy * 4 + zz
        return remote(
            CORE, parts.at[block_id(yy, 1 - c, zz)], core_got.at[slot], core_send.at[slot], core_recv.at[slot]
        )

    def to_across(zz):
        return remote(ACROSS, parts.at[block_id(1 - y, c, zz)], y_got.at[zz], y_send.at[zz], y_recv.at[zz])

    def to_line(kind, zz, slot):
        return remote(kind, parts.at[block_id(y, c, zz)], z_got.at[slot], z_send.at[zz], z_recv.at[slot])

    def add(block, got):
        parts[block] = (parts[block].astype(single) + got.astype(single)).astype(parts.dtype)

    def core_sends():
        @pl.loop(0, 4)
        def _(turn):
            zz = line_order(z, 3 - turn)
            to_core(1 - y, zz).start()
            to_core(y, zz).start()

    def across(step):
        zz = line_order(z, step)
        to_core(1 - y, zz).wait_recv()
        add(block_id(1 - y, c, zz), core_got[(1 - y) * 4 + zz])
        to_across(zz).start()
        to_core(y, zz).wait_recv()
        add(block_id(y, c, zz), core_got[y * 4 + zz])

    def line(step):
        zz = line_order(z, step)
        block = block_id(y, c, zz)
        to_across(zz).wait_recv()
        add(block, y_got[zz])
        rising = zz > z
        comes = jnp.logical_or(jnp.logical_and(rising, z > 0), jnp.logical_and(zz < z, z < 3))

        @pl.when(comes)
        def _():
            to_line(CORE, zz, zz).wait_recv()
            add(block, z_got[zz])

        @pl.when(rising)
        def _():
            to_line(UP, zz, zz).start()

        @pl.when(zz == z - 1)
        def _():
            to_line(DOWN, zz, 4).start()

        @pl.when(zz < z - 1)
        def _():
            to_line(DOWN, zz, zz).start()

    there = pl.ds(pl.multiple_of((1 - d) * rows, 16), rows)
    here = pl.ds(pl.multiple_of(d * rows, 16), rows)
    last = remote(DP, parts.at[mine, there, :], dp_got, dp_send, dp_recv)

    def over_dp():
        to_across(z).wait_recv()
        add(mine, y_got[z])

        @pl.when(z > 0)
        def _():
            to_line(CORE, z, z).wait_recv()
            add(mine, z_got[z])

        @pl.when(z < 3)
        def _():
            to_line(CORE, z, 4).wait_recv()
            add(mine, z_got[4])

        last.start()

    def finish(result):
        last.wait_recv()
        result[...] = parts[mine, here, :].astype(single) + dp_got[...].astype(single)
        last.wait_send()

        @pl.loop(0, 4)
        def _(zz):
            to_core(y, zz).wait_send()
            to_core(1 - y, zz).wait_send()
            to_across(zz).wait_send()

            @pl.when(zz != z)
            def _():
                to_line(CORE, zz, zz).wait_send()

    return core_sends, across, line, over_dp, finish


def ring_scratch(rows, width):
    bfloat = jnp.bfloat16
    dma = pltpu.SemaphoreType.DMA
    return [
        pltpu.VMEM((16, 2 * rows, width), bfloat),
        pltpu.VMEM((8, 2 * rows, width), bfloat),
        pltpu.VMEM((4, 2 * rows, width), bfloat),
        pltpu.VMEM((5, 2 * rows, width), bfloat),
        pltpu.VMEM((rows, width), bfloat),
        dma((8,)),
        dma((8,)),
        dma((4,)),
        dma((4,)),
        dma((4,)),
        dma((5,)),
        dma,
        dma,
    ]


def load_parts(refs, parts, sem):
    loads = []
    at = 0
    for index, ref in enumerate(refs):
        rows, size = ref.shape[2], ref.shape[3]
        for plane in range(2):
            loads.append(
                pltpu.make_async_copy(
                    ref.at[plane],
                    parts.at[:, pl.ds(plane * rows, rows), pl.ds(at, size)],
                    sem.at[index * 2 + plane],
                )
            )
        at += size
    return loads


def spread_rows(whole, send_sem, core_sem, recv_sem):
    y, c, z, _, device, _ = place()
    d = lax.axis_index("dp")

    def copy_of(kind, slot, sem):
        return pltpu.make_async_remote_copy(
            src_ref=whole.at[slot],
            dst_ref=whole.at[slot],
            send_sem=sem,
            recv_sem=recv_sem.at[slot],
            device_id=device(kind),
            device_id_type=MESH_ID,
        )

    def own(kind, block):
        return copy_of(kind, d * 16 + block, send_sem.at[kind, block])

    def other(block):
        return copy_of(CORE, (1 - d) * 16 + block, core_sem.at[block])

    def along(kind, zz):
        if kind == UP:
            return jnp.logical_and(z < 3, zz <= z)
        return jnp.logical_and(z > 0, zz >= z)

    def fan(zz, act):
        block = block_id(y, c, zz)
        for kind in (UP, DOWN):

            @pl.when(along(kind, zz))
            def _():
                act(own(kind, block))

        for kind in (ACROSS, DP, CORE):
            act(own(kind, block))

    def fan_across(zz, act):
        block = block_id(1 - y, c, zz)
        act(own(DP, block))
        act(own(CORE, block))

    def fan_dp(zz, act):
        act(other(block_id(y, c, zz)))
        act(other(block_id(1 - y, c, zz)))

    start = lambda copy: copy.start()
    end = lambda copy: copy.wait_send()

    def begin():
        fan(z, start)

    def arrive(step):
        @pl.when(step < 4)
        def _():
            zz = line_order(z, jnp.minimum(step, 3))
            own(ACROSS, block_id(y, c, zz)).wait_recv()
            fan(zz, start)

        @pl.when(step < 5)
        def _():
            zz = line_order(z, jnp.minimum(step - 1, 3))
            own(CORE, block_id(1 - y, c, zz)).wait_recv()
            fan_across(zz, start)

        @pl.when(step > 1)
        def _():
            zz = line_order(z, jnp.maximum(step - 2, 0))
            other(block_id(y, c, zz)).wait_recv()
            other(block_id(1 - y, c, zz)).wait_recv()
            fan_dp(zz, start)

    def finish():
        @pl.loop(0, 4)
        def _(zz):
            for yy in range(2):
                block = block_id(yy, 1 - c, zz)
                own(CORE, block).wait_recv()
                other(block).wait_recv()

    def ends():
        @pl.loop(0, 4)
        def _(zz):
            fan(zz, end)
            fan_across(zz, end)
            fan_dp(zz, end)

    return begin, arrive, finish, ends


def spread_scratch(rows, width):
    dma = pltpu.SemaphoreType.DMA
    return [pltpu.VMEM((32, rows, width), jnp.bfloat16), dma((5, 16)), dma((16,)), dma((32,))]


def gather_kernel(
    query_ref,
    key_ref,
    value_ref,
    small_ref,
    out_ref,
    proj_all,
    small_all,
    out_all,
    local_sem,
    whole,
    *sems,
):
    y, c, z, inner, device, per_side = place()
    mine = lax.axis_index("dp") * 16 + block_id(y, c, z)
    loads = []
    at = 0
    for index, ref in enumerate((query_ref, key_ref, value_ref, small_ref, out_ref)):
        size = ref.shape[1]
        loads.append(
            pltpu.make_async_copy(ref, whole.at[mine, :, pl.ds(at, size)], local_sem.at[index])
        )
        at += size
    for copy in loads:
        copy.start()
    greet(per_side, device, 4 + inner, (DP,))
    for copy in loads:
        copy.wait()
    begin, arrive, finish, ends = spread_rows(whole, *sems)
    begin()

    @pl.loop(1, 6)
    def _(step):
        arrive(step)

    finish()
    results = []
    at = 0
    for index, ref in enumerate((proj_all, small_all, out_all)):
        size = ref.shape[2]
        results.append(
            pltpu.make_async_copy(whole.at[:, :, pl.ds(at, size)], ref, local_sem.at[index])
        )
        at += size
    for copy in results:
        copy.start()
    ends()
    for copy in results:
        copy.wait()


def gather_weights(query, key, value, small, out):
    rows = query.shape[0]
    widths = (query.shape[1] + key.shape[1] + value.shape[1], small.shape[1], out.shape[1])
    anywhere = pl.BlockSpec(memory_space=pl.ANY)
    return pl.pallas_call(
        gather_kernel,
        out_shape=tuple(
            jax.ShapeDtypeStruct((32, rows, width), jnp.bfloat16) for width in widths
        ),
        in_specs=[anywhere] * 5,
        out_specs=(anywhere, anywhere, anywhere),
        scratch_shapes=[pltpu.SemaphoreType.DMA((5,)), *spread_scratch(rows, sum(widths))],
        compiler_params=pltpu.CompilerParams(
            collective_id=0, has_side_effects=True, vmem_limit_bytes=60 * 2**20
        ),
        name="gather_weights",
    )(query, key, value, small, out)


def ring_sum_dp_early(parts, core_got, dp_got, y_got, z_got, sems):
    single = jnp.float32
    core_send, core_recv, dp_send, dp_recv, y_send, y_recv, z_send, z_recv = sems
    y, c, z, _, device, _ = place()
    d = lax.axis_index("dp")
    rows = parts.shape[1] // 2
    mine = block_id(y, c, z)
    there = pl.ds(pl.multiple_of((1 - d) * rows, 16), rows)
    here = pl.ds(pl.multiple_of(d * rows, 16), rows)

    def remote(kind, source, target, send_sem, recv_sem):
        return pltpu.make_async_remote_copy(
            src_ref=source,
            dst_ref=target,
            send_sem=send_sem,
            recv_sem=recv_sem,
            device_id=device(kind),
            device_id_type=MESH_ID,
        )

    def to_core(yy, zz):
        slot = yy * 4 + zz
        return remote(
            CORE, parts.at[block_id(yy, 1 - c, zz)], core_got.at[slot], core_send.at[slot], core_recv.at[slot]
        )

    def to_dp(yy, zz):
        slot = yy * 4 + zz
        return remote(
            DP, parts.at[block_id(yy, c, zz), there, :], dp_got.at[slot], dp_send.at[slot], dp_recv.at[slot]
        )

    def to_across(zz):
        return remote(
            ACROSS, parts.at[block_id(1 - y, c, zz), here, :], y_got.at[zz], y_send.at[zz], y_recv.at[zz]
        )

    def to_line(kind, zz, slot):
        return remote(
            kind, parts.at[block_id(y, c, zz), here, :], z_got.at[slot], z_send.at[zz], z_recv.at[slot]
        )

    def add(block, got):
        parts[block, here, :] = (
            parts[block, here, :].astype(single) + got.astype(single)
        ).astype(parts.dtype)

    def core_sends():
        @pl.loop(0, 4)
        def _(turn):
            zz = line_order(z, 3 - turn)
            to_core(1 - y, zz).start()
            to_core(y, zz).start()

    def meet(step):
        zz = line_order(z, step)
        for yy in (1 - y, y):
            block = block_id(yy, c, zz)
            to_core(yy, zz).wait_recv()
            parts[block] = (
                parts[block].astype(single) + core_got[yy * 4 + zz].astype(single)
            ).astype(parts.dtype)
            to_dp(yy, zz).start()

    def across(step):
        zz = line_order(z, step)
        for yy in (1 - y, y):
            to_dp(yy, zz).wait_recv()
            add(block_id(yy, c, zz), dp_got[yy * 4 + zz])
        to_across(zz).start()

    def line(step):
        zz = line_order(z, step)
        block = block_id(y, c, zz)
        to_across(zz).wait_recv()
        add(block, y_got[zz])
        rising = zz > z
        comes = jnp.logical_or(jnp.logical_and(rising, z > 0), jnp.logical_and(zz < z, z < 3))

        @pl.when(comes)
        def _():
            to_line(CORE, zz, zz).wait_recv()
            add(block, z_got[zz])

        @pl.when(rising)
        def _():
            to_line(UP, zz, zz).start()

        @pl.when(zz == z - 1)
        def _():
            to_line(DOWN, zz, 4).start()

        @pl.when(zz < z - 1)
        def _():
            to_line(DOWN, zz, zz).start()

    def finish(results):
        spans = []
        at = 0
        for result in results:
            spans.append(pl.ds(at, result.shape[1]))
            at += result.shape[1]
        to_across(z).wait_recv()
        for result, span in zip(results, spans):
            result[...] = parts[mine, here, span].astype(single) + y_got[z, :, span].astype(single)

        @pl.when(z > 0)
        def _():
            to_line(CORE, z, z).wait_recv()
            for result, span in zip(results, spans):
                result[...] += z_got[z, :, span].astype(single)

        @pl.when(z < 3)
        def _():
            to_line(CORE, z, 4).wait_recv()
            for result, span in zip(results, spans):
                result[...] += z_got[4, :, span].astype(single)

        @pl.loop(0, 4)
        def _(zz):
            for yy in (y, 1 - y):
                to_core(yy, zz).wait_send()
                to_dp(yy, zz).wait_send()
            to_across(zz).wait_send()

            @pl.when(zz != z)
            def _():
                to_line(CORE, zz, zz).wait_send()

    return core_sends, meet, across, line, finish


def ring_scratch_dp_early(rows, width):
    bfloat = jnp.bfloat16
    dma = pltpu.SemaphoreType.DMA
    return [
        pltpu.VMEM((16, 2 * rows, width), bfloat),
        pltpu.VMEM((8, 2 * rows, width), bfloat),
        pltpu.VMEM((8, rows, width), bfloat),
        pltpu.VMEM((4, rows, width), bfloat),
        pltpu.VMEM((5, rows, width), bfloat),
        *[dma((n,)) for n in (8, 8, 8, 8, 4, 4, 4, 5)],
    ]


def sums_kernel(
    proj_ref, small_ref, out_ref, query_sum, key_sum, value_sum, small_sum, out_sum, load_sem, *rings
):
    _, _, _, inner, device, per_side = place()
    ring, out_ring = rings[:13], rings[13:]
    loads = load_parts((proj_ref, small_ref), ring[0], load_sem) + load_parts(
        (out_ref,), out_ring[0], load_sem.at[pl.ds(4, 2)]
    )
    for copy in loads:
        copy.start()
    greet(per_side, device, 4 + inner, (DP,))
    for copy in loads:
        copy.wait()
    core_sends, meet, across, line, finish = ring_sum_dp_early(*ring[:5], ring[5:])
    out_core, out_across, out_line, out_dp, out_finish = ring_sum(*out_ring[:5], out_ring[5:])
    core_sends()
    out_core()

    @pl.loop(0, 4)
    def _(turn):
        meet(3 - turn)
        out_across(3 - turn)

    @pl.loop(0, 4)
    def _(turn):
        across(3 - turn)

        @pl.when(turn < 3)
        def _():
            out_line(3 - jnp.minimum(turn, 2))

        @pl.when(turn > 0)
        def _():
            line(4 - jnp.maximum(turn, 1))

    out_dp()
    finish((query_sum, key_sum, value_sum, small_sum))
    out_finish(out_sum)


def by_device(x):
    return x.reshape(2, 16, x.shape[0] // 32, x.shape[1])


def sum_gradients(proj, small, out, widths):
    dma = pltpu.SemaphoreType.DMA
    anywhere = pl.BlockSpec(memory_space=pl.ANY)
    vmem = pl.BlockSpec(memory_space=pltpu.VMEM)
    rows = proj.shape[0] // 32
    width = proj.shape[1] + small.shape[1]
    return pl.pallas_call(
        sums_kernel,
        out_shape=(
            *(jax.ShapeDtypeStruct((rows, size), jnp.float32) for size in widths),
            jax.ShapeDtypeStruct((rows, small.shape[1]), jnp.float32),
            jax.ShapeDtypeStruct((rows, out.shape[1]), jnp.float32),
        ),
        in_specs=[anywhere] * 3,
        out_specs=(vmem,) * (2 + len(widths)),
        scratch_shapes=[
            dma((6,)),
            *ring_scratch_dp_early(rows, width),
            *ring_scratch(rows, out.shape[1]),
        ],
        compiler_params=pltpu.CompilerParams(
            collective_id=2, has_side_effects=True, vmem_limit_bytes=56 * 2**20
        ),
        cost_estimate=pl.CostEstimate(flops=1 << 20, bytes_accessed=1 << 16, transcendentals=0),
        name="sum_gradients",
    )(by_device(proj), by_device(small), by_device(out))


def fill_bias(length_ref, bias, ctx):
    blocks, keys, queries = bias.shape
    row = lax.broadcasted_iota(jnp.int32, (keys, queries), 0)
    column = lax.broadcasted_iota(jnp.int32, (keys, queries), 1) + ctx * queries
    for j in range(blocks):
        key = row + j * keys
        allowed = jnp.logical_and(key <= column, key < length_ref[0])
        bias[j] = jnp.where(allowed, 0.0, floor_score)


def head_probs(query, keys, bias):
    scores = [contract_rows(key, query) + bias[j] for j, key in enumerate(keys)]
    peak = jnp.max(scores[0], axis=0, keepdims=True)
    for score in scores[1:]:
        peak = jnp.maximum(peak, jnp.max(score, axis=0, keepdims=True))
    raised = [jnp.exp(score - peak) for score in scores]
    total = jnp.sum(raised[0], axis=0, keepdims=True)
    for value in raised[1:]:
        total = total + jnp.sum(value, axis=0, keepdims=True)
    inverse = 1.0 / total
    return [value * inverse for value in raised]


def attend_kernel(
    query_ref,
    own_ref,
    length_ref,
    mixed_ref,
    all_ref,
    pairs,
    bias,
    first,
    stats,
    local_sem,
    send_sem,
    recv_sem,
):
    bfloat = jnp.bfloat16
    y, c, _, _, device, _ = place()
    mine = y * 2 + c
    own = pltpu.make_async_copy(own_ref, pairs.at[mine], local_sem)
    own.start()
    barrier = pltpu.get_barrier_semaphore()
    for kind in (ACROSS, CORE):
        pl.semaphore_signal(barrier, inc=1, device_id=device(kind), device_id_type=MESH_ID)
    pl.semaphore_wait(barrier, 2)
    own.wait()

    def send(kind, slot, index):
        return pltpu.make_async_remote_copy(
            src_ref=pairs.at[slot],
            dst_ref=pairs.at[slot],
            send_sem=send_sem.at[index],
            recv_sem=recv_sem.at[slot],
            device_id=device(kind),
            device_id_type=MESH_ID,
        )

    far = (1 - y) * 2 + c
    across = send(ACROSS, mine, 0)
    core = send(CORE, mine, 1)
    onward = send(CORE, far, 2)
    across.start()
    core.start()
    fill_bias(length_ref, bias, mine)
    half = pairs.shape[1] // 2
    ratio = query_ref.shape[0] // half
    groups = half // HEAD_SIZE

    def pass_over(blocks, g, merge):
        rows = pl.ds(pl.multiple_of(g * HEAD_SIZE, HEAD_SIZE), HEAD_SIZE)
        low = pl.ds(pl.multiple_of(half + g * HEAD_SIZE, HEAD_SIZE), HEAD_SIZE)
        keys = [pairs[j, rows, :] for j in blocks]
        values = [pairs[j, low, :] for j in blocks]
        for r in range(ratio):
            h = g * ratio + r
            head = pl.ds(pl.multiple_of(h * HEAD_SIZE, HEAD_SIZE), HEAD_SIZE)
            query = query_ref[head, :]
            scores = [contract_rows(key, query) + bias[j] for key, j in zip(keys, blocks)]
            peak = jnp.maximum(
                jnp.max(scores[0], axis=0, keepdims=True), jnp.max(scores[1], axis=0, keepdims=True)
            )
            if merge:
                before = stats[h, 0:1, :]
                peak = jnp.maximum(peak, before)
            raised = [jnp.exp(score - peak) for score in scores]
            total = jnp.sum(raised[0] + raised[1], axis=0, keepdims=True)
            sums = matmul(values[0], raised[0].astype(bfloat)) + matmul(
                values[1], raised[1].astype(bfloat)
            )
            if merge:
                shrink = jnp.exp(before - peak)
                total = total + stats[h, 1:2, :] * shrink
                mixed_ref[head, :] = ((sums + first[head, :] * shrink) / total).astype(bfloat)
            else:
                first[head, :] = sums
                stats[h, 0:1, :] = peak
                stats[h, 1:2, :] = total

    send(CORE, y * 2 + 1 - c, 1).wait_recv()

    @pl.loop(0, groups)
    def _(g):
        pass_over((mine, y * 2 + 1 - c), g, False)

    send(ACROSS, far, 0).wait_recv()
    onward.start()
    send(CORE, (1 - y) * 2 + 1 - c, 2).wait_recv()
    result = pltpu.make_async_copy(pairs, all_ref, local_sem)
    result.start()

    @pl.loop(0, groups)
    def _(g):
        pass_over((far, (1 - y) * 2 + 1 - c), g, True)

    for copy in (across, core, onward):
        copy.wait_send()
    result.wait()


def attend(query, own_pairs, lengths):
    bfloat = jnp.bfloat16
    single = jnp.float32
    dma = pltpu.SemaphoreType.DMA
    anywhere = pl.BlockSpec(memory_space=pl.ANY)
    vmem = pl.BlockSpec(memory_space=pltpu.VMEM)
    pairs = (4, *own_pairs.shape)
    keys = own_pairs.shape[1]
    return pl.pallas_call(
        attend_kernel,
        out_shape=(
            jax.ShapeDtypeStruct(query.shape, bfloat),
            jax.ShapeDtypeStruct(pairs, bfloat),
        ),
        in_specs=[vmem, anywhere, pl.BlockSpec(memory_space=pltpu.SMEM)],
        out_specs=(vmem, anywhere),
        scratch_shapes=[
            pltpu.VMEM(pairs, bfloat),
            pltpu.VMEM((4, keys, query.shape[1]), single),
            pltpu.VMEM(query.shape, single),
            pltpu.VMEM((query.shape[0] // HEAD_SIZE, 8, query.shape[1]), single),
            dma,
            dma((3,)),
            dma((4,)),
        ],
        compiler_params=pltpu.CompilerParams(
            collective_id=3, has_side_effects=True, vmem_limit_bytes=48 * 2**20
        ),
        name="attend",
    )(query, own_pairs, lengths)


def turn_back(gradient, cosine, sine):
    first, second = gradient[: HEAD_SIZE // 2], gradient[HEAD_SIZE // 2 :]
    return jnp.concatenate(
        [first * cosine + second * sine, second * cosine - first * sine], axis=0
    ).astype(jnp.bfloat16)


def attend_back_kernel(
    query_ref,
    pairs_ref,
    grad_ref,
    length_ref,
    cosine_ref,
    sine_ref,
    proj_out,
    parts,
    core_got,
    y_got,
    bias,
    core_send,
    core_recv,
    y_send,
    y_recv,
):
    bfloat = jnp.bfloat16
    single = jnp.float32
    y, c, _, _, device, _ = place()
    mine = y * 2 + c
    barrier = pltpu.get_barrier_semaphore()
    for kind in (ACROSS, CORE):
        pl.semaphore_signal(barrier, inc=1, device_id=device(kind), device_id_type=MESH_ID)
    pl.semaphore_wait(barrier, 2)
    fill_bias(length_ref, bias, mine)
    blocks = pairs_ref.shape[0]
    half = pairs_ref.shape[1] // 2
    ratio = query_ref.shape[0] // half
    groups = half // HEAD_SIZE
    turns = parts.shape[1]
    per_turn = groups // turns
    quarter = half // turns

    def to_core(yy, turn):
        return pltpu.make_async_remote_copy(
            src_ref=parts.at[yy * 2 + 1 - c, turn],
            dst_ref=core_got.at[turn, yy],
            send_sem=core_send.at[turn, yy],
            recv_sem=core_recv.at[turn, yy],
            device_id=device(CORE),
            device_id_type=MESH_ID,
        )

    def to_across(turn):
        return pltpu.make_async_remote_copy(
            src_ref=parts.at[(1 - y) * 2 + c, turn],
            dst_ref=y_got.at[turn],
            send_sem=y_send.at[turn],
            recv_sem=y_recv.at[turn],
            device_id=device(ACROSS),
            device_id_type=MESH_ID,
        )

    def core_stage(turn):
        to_core(1 - y, turn).start()
        to_core(y, turn).start()

    def across_stage(turn):
        to_core(1 - y, turn).wait_recv()
        slot = (1 - y) * 2 + c
        parts[slot, turn] = (
            parts[slot, turn].astype(single) + core_got[turn, 1 - y].astype(single)
        ).astype(bfloat)
        to_across(turn).start()

    def last_stage(turn):
        to_core(y, turn).wait_recv()
        to_across(turn).wait_recv()
        total = (
            parts[mine, turn].astype(single)
            + core_got[turn, y].astype(single)
            + y_got[turn].astype(single)
        )
        at = query_ref.shape[0] + turn * quarter
        for h in range(per_turn):
            rows = slice(h * HEAD_SIZE, (h + 1) * HEAD_SIZE)
            proj_out[pl.ds(at + h * HEAD_SIZE, HEAD_SIZE), :] = turn_back(
                total[rows], cosine_ref[...], sine_ref[...]
            )
        proj_out[pl.ds(at + half, quarter), :] = total[quarter:].astype(bfloat)

    def group(g, carry):
        rows = pl.ds(pl.multiple_of(g * HEAD_SIZE, HEAD_SIZE), HEAD_SIZE)
        low = pl.ds(pl.multiple_of(half + g * HEAD_SIZE, HEAD_SIZE), HEAD_SIZE)
        keys = [pairs_ref[j, rows, :] for j in range(blocks)]
        values = [pairs_ref[j, low, :] for j in range(blocks)]
        grad_keys = [None] * blocks
        grad_values = [None] * blocks
        for r in range(ratio):
            head = pl.ds(pl.multiple_of((g * ratio + r) * HEAD_SIZE, HEAD_SIZE), HEAD_SIZE)
            query = query_ref[head, :]
            grad = grad_ref[head, :]
            probs = head_probs(query, keys, bias)
            grad_probs = [contract_rows(value, grad) for value in values]
            delta = jnp.sum(probs[0] * grad_probs[0], axis=0, keepdims=True)
            for j in range(1, blocks):
                delta = delta + jnp.sum(probs[j] * grad_probs[j], axis=0, keepdims=True)
            grad_query = None
            for j in range(blocks):
                low_probs = probs[j].astype(bfloat)
                grad_score = (probs[j] * (grad_probs[j] - delta)).astype(bfloat)
                terms = (
                    matmul(keys[j], grad_score),
                    contract_last(query, grad_score),
                    contract_last(grad, low_probs),
                )
                grad_query = terms[0] if j == 0 else grad_query + terms[0]
                grad_keys[j] = terms[1] if r == 0 else grad_keys[j] + terms[1]
                grad_values[j] = terms[2] if r == 0 else grad_values[j] + terms[2]
            proj_out[head, :] = turn_back(
                grad_query * HEAD_SIZE ** (-0.5), cosine_ref[...], sine_ref[...]
            )
        turn = g // per_turn
        at = pl.multiple_of((g % per_turn) * HEAD_SIZE, HEAD_SIZE)
        for j in range(blocks):
            parts[j, turn, pl.ds(at, HEAD_SIZE), :] = grad_keys[j].astype(bfloat)
            parts[j, turn, pl.ds(quarter + at, HEAD_SIZE), :] = grad_values[j].astype(bfloat)
        for index in range(turns - 1):

            @pl.when(g == (index + 1) * per_turn - 1)
            def _():
                core_stage(index)

            @pl.when(g == (index + 1) * per_turn)
            def _():
                across_stage(index)

        return carry

    lax.fori_loop(0, groups, group, 0)
    core_stage(turns - 1)
    across_stage(turns - 1)
    for turn in range(turns):
        last_stage(turn)
    for turn in range(turns):
        to_core(y, turn).wait_send()
        to_core(1 - y, turn).wait_send()
        to_across(turn).wait_send()


def attend_back(query, pairs, grad, lengths, cosine, sine):
    bfloat = jnp.bfloat16
    single = jnp.float32
    dma = pltpu.SemaphoreType.DMA
    anywhere = pl.BlockSpec(memory_space=pl.ANY)
    vmem = pl.BlockSpec(memory_space=pltpu.VMEM)
    blocks, rows, keys = pairs.shape
    turns = 4
    part = (turns, rows // turns, keys)
    return pl.pallas_call(
        attend_back_kernel,
        out_shape=jax.ShapeDtypeStruct((query.shape[0] + rows, query.shape[1]), bfloat),
        in_specs=[vmem, vmem, vmem, pl.BlockSpec(memory_space=pltpu.SMEM), vmem, vmem],
        out_specs=vmem,
        scratch_shapes=[
            pltpu.VMEM((blocks, *part), bfloat),
            pltpu.VMEM((turns, 2, *part[1:]), bfloat),
            pltpu.VMEM(part, bfloat),
            pltpu.VMEM((blocks, keys, query.shape[1]), single),
            dma((turns, 2)),
            dma((turns, 2)),
            dma((turns,)),
            dma((turns,)),
        ],
        compiler_params=pltpu.CompilerParams(
            collective_id=4, has_side_effects=True, vmem_limit_bytes=48 * 2**20
        ),
        cost_estimate=pl.CostEstimate(flops=1 << 20, bytes_accessed=1 << 16, transcendentals=0),
        name="attend_back",
    )(query, pairs, grad, lengths, cosine, sine)


def experts_kernel(
    swap,
    hidden_ref,
    final_ref,
    routes_ref,
    router_ref,
    gate_hbm,
    up_hbm,
    down_hbm,
    back_ref,
    part_ref,
    score_got,
    grad_gate_ref,
    grad_up_ref,
    grad_down_ref,
    *refs,
):
    if swap:
        gate_got, up_got, leaving, *refs = refs
        swap = (gate_got, up_got, leaving)
    experts_steps(
        swap,
        hidden_ref,
        final_ref,
        routes_ref,
        router_ref,
        gate_hbm,
        up_hbm,
        down_hbm,
        back_ref,
        part_ref,
        score_got,
        grad_gate_ref,
        grad_up_ref,
        grad_down_ref,
        *refs,
    )


def experts_steps(
    swap,
    hidden_ref,
    final_ref,
    routes_ref,
    router_ref,
    gate_hbm,
    up_hbm,
    down_hbm,
    back_ref,
    part_ref,
    score_got,
    grad_gate_ref,
    grad_up_ref,
    grad_down_ref,
    held,
    w_gate,
    w_up,
    w_down,
    rows_in,
    rows_grad,
    slope_gate,
    slope_up,
    hidden_e,
    picks,
    row_gates,
    work,
    pool,
    before,
    gather_send,
    gather_recv,
    local_sem,
    load_sem,
    part_sem,
    sum_send,
    core_recv,
    y_recv,
    z_recv,
    ready,
    score_ref,
    score_send,
    score_recv,
    swap_send,
    swap_recv,
):
    single = jnp.float32
    bfloat = jnp.bfloat16
    tokens_block = hidden_ref.shape[0]
    width = hidden_ref.shape[1]
    experts = router_ref.shape[0]
    local_exp = w_gate.shape[0]
    hidden_units = w_gate.shape[2]
    capacity = picks.shape[1] // local_exp
    group_rows = 4 * capacity
    ctx = lax.axis_index("context")
    y, c, z, inner, device, per_side = place()

    weights = (
        pltpu.make_async_copy(gate_hbm, w_gate, load_sem.at[0]),
        pltpu.make_async_copy(up_hbm, w_up, load_sem.at[1]),
        pltpu.make_async_copy(down_hbm, w_down, load_sem.at[2]),
    )
    mine = block_id(y, c, z)
    own = pltpu.make_async_copy(hidden_ref, held.at[mine], local_sem)
    own.start()
    for copy in weights:
        copy.start()

    barrier = pltpu.get_barrier_semaphore()

    def member_device(block):
        return {"context": block // 4, "expert": block % 4}

    @pl.loop(1, 16)
    def _(shift):
        pl.semaphore_signal(
            barrier,
            inc=1,
            device_id=member_device((mine + shift) % 16),
            device_id_type=MESH_ID,
        )

    if swap:
        pl.semaphore_signal(barrier, inc=1, device_id=device(DP), device_id_type=MESH_ID)
    pl.semaphore_wait(barrier, 16 if swap else 15)
    own.wait()

    def spread(kind, block):
        return pltpu.make_async_remote_copy(
            src_ref=held.at[block],
            dst_ref=held.at[block],
            send_sem=gather_send.at[kind, block],
            recv_sem=gather_recv.at[block],
            device_id=device(kind),
            device_id_type=MESH_ID,
        )

    def along(kind, zz):
        if kind == UP:
            return jnp.logical_and(z < 3, zz <= z)
        return jnp.logical_and(z > 0, zz >= z)

    def send_on(zz):
        block = block_id(y, c, zz)
        for kind in (UP, DOWN):

            @pl.when(along(kind, zz))
            def _():
                spread(kind, block).start()

        spread(ACROSS, block).start()
        spread(CORE, block).start()

    def forward(step):
        zz = line_order(z, step)
        spread(ACROSS, block_id(y, c, zz)).wait_recv()
        send_on(zz)

    send_on(z)
    row = lax.broadcasted_iota(jnp.int32, (tokens_block, tokens_block), 0)
    column = lax.broadcasted_iota(jnp.int32, (tokens_block, tokens_block), 1)
    before[...] = jnp.where(row < column, 1.0, 0.0).astype(bfloat)
    for copy in weights:
        copy.wait()
    first = (ctx * 4 + z) * local_exp

    def member(zz, p):
        yy = y + (p // 2) * (1 - 2 * y)
        cc = c + (p % 2) * (1 - 2 * c)
        return block_id(yy, cc, zz)

    def load_final(zz, p):
        return pltpu.make_async_copy(final_ref.at[member(zz, p)], pool.at[p], load_sem.at[p])

    def store_part(zz, p):
        return pltpu.make_async_copy(
            pool.at[4 + p % 2], part_ref.at[member(zz, p)], part_sem.at[p % 2]
        )

    def forward_group(step, carry):
        zz = line_order(z, step)
        after = step + 1 + inner * jnp.minimum(step, 1)

        @pl.when(after < 4)
        def _():
            forward(after)

        @pl.when(jnp.logical_and(step == 0, inner == 1))
        def _():
            forward(2)

        @pl.loop(0, 4)
        def _(p):
            load_final(zz, p).start()

        spread(CORE, block_id(y, 1 - c, zz)).wait_recv()
        spread(CORE, block_id(1 - y, c, zz)).wait_recv()
        spread(CORE, block_id(1 - y, c, zz)).start()
        spread(CORE, block_id(1 - y, 1 - c, zz)).wait_recv()

        @pl.loop(0, 4)
        def _(p):
            block = member(zz, p)
            tokens_in = held[block]
            logits = contract_last(router_ref[...], tokens_in)
            expert_row = lax.broadcasted_iota(jnp.int32, (experts, tokens_block), 0)
            routed = jnp.zeros((experts, tokens_block), single)
            for k in range(routes_ref.shape[1]):
                routed = routed + jnp.where(routes_ref[block, k : k + 1, :] == expert_row, 1.0, 0.0)
            named = routed > 0.5
            peak = jnp.max(jnp.where(named, logits, floor_score), axis=0, keepdims=True)
            raised = jnp.where(named, jnp.exp(jnp.minimum(logits - peak, 0.0)), 0.0)
            gates = raised / jnp.sum(raised, axis=0, keepdims=True)
            eight = lax.broadcasted_iota(jnp.int32, (8, tokens_block), 0)
            masks = jnp.zeros((8, tokens_block), single)
            own_mask = []
            own_gate = []
            for j in range(local_exp):
                here = expert_row == first + j
                own_mask.append(jnp.sum(jnp.where(here, routed, 0.0), axis=0, keepdims=True))
                own_gate.append(jnp.sum(jnp.where(here, gates, 0.0), axis=0, keepdims=True))
                masks = masks + jnp.where(eight == j, own_mask[j], 0.0)
            rank = matmul(masks.astype(bfloat), before[...])
            slot = lax.broadcasted_iota(jnp.int32, (capacity, tokens_block), 0).astype(single)
            for j in range(local_exp):
                hit = jnp.logical_and(slot == rank[j : j + 1, :], own_mask[j] > 0.5)
                pick = jnp.where(hit, 1.0, 0.0)
                picks[step * 4 + p, pl.ds(j * capacity, capacity), :] = pick.astype(bfloat)
                gate_column = jnp.sum(pick * own_gate[j], axis=1, keepdims=True)
                row_gates[p, pl.ds(j * capacity, capacity), :] = jnp.broadcast_to(
                    gate_column, (capacity, 128)
                )
            at = pl.multiple_of(step * group_rows + p * capacity, 32)
            for n in range(width // CHUNK):
                part = pl.ds(n * CHUNK, CHUNK)
                got = matmul(picks[step * 4 + p], held[block, :, part]).astype(bfloat)
                for j in range(local_exp):
                    rows_in[j, pl.ds(at, capacity), part] = got[j * capacity : (j + 1) * capacity]

        base = pl.multiple_of(step * group_rows, 128)
        for j in range(local_exp):
            given = rows_in[j, pl.ds(base, group_rows), :]
            for n in range(hidden_units // HALF):
                part = pl.ds(n * HALF, HALF)
                gate_pre = matmul(given, w_gate[j, :, part])
                up_pre = matmul(given, w_up[j, :, part])
                sigmoid = 1.0 / (1.0 + jnp.exp(-gate_pre))
                silu = gate_pre * sigmoid
                hidden_e[j, pl.ds(base, group_rows), part] = (silu * up_pre).astype(bfloat)
                slope_gate[j, pl.ds(base, group_rows), part] = (
                    up_pre * sigmoid * (1.0 + gate_pre * (1.0 - sigmoid))
                ).astype(bfloat)
                slope_up[j, pl.ds(base, group_rows), part] = silu.astype(bfloat)
            for n in range(width // CHUNK):
                part = pl.ds(n * CHUNK, CHUNK)
                work[j, :, part] = matmul(
                    hidden_e[j, pl.ds(base, group_rows), :], w_down[j, :, part]
                ).astype(bfloat)

        @pl.loop(0, 4)
        def _(p):
            block = member(zz, p)
            at = pl.multiple_of(step * group_rows + p * capacity, 32)
            local = pl.multiple_of(p * capacity, 32)
            pick = picks[step * 4 + p]
            weight = row_gates[p][:, 0:1]
            weighted = (pick.astype(single) * weight).astype(bfloat)
            load_final(zz, p).wait()

            @pl.when(jnp.logical_or(step > 0, p > 1))
            def _():
                store_part(zz, p).wait()

            row_score = jnp.zeros((local_exp * capacity, 1), single)
            for n in range(width // CHUNK):
                part = pl.ds(n * CHUNK, CHUNK)
                out = jnp.concatenate(
                    [work[j, pl.ds(local, capacity), part] for j in range(local_exp)], axis=0
                )
                pool[4 + p % 2, :, part] = contract_rows(weighted, out).astype(bfloat)
                final = matmul(pick, pool[p, :, part])
                row_score = row_score + jnp.sum(final * out.astype(single), axis=1, keepdims=True)
                graded = (final * weight).astype(bfloat)
                for j in range(local_exp):
                    rows_grad[j, pl.ds(at, capacity), part] = graded[j * capacity : (j + 1) * capacity]
            store_part(zz, p).start()
            spread_score = pick.astype(single) * row_score
            eight = lax.broadcasted_iota(jnp.int32, (8, tokens_block), 0)
            scores = jnp.zeros((8, tokens_block), single)
            for j in range(local_exp):
                total = jnp.sum(spread_score[j * capacity : (j + 1) * capacity], axis=0, keepdims=True)
                scores = scores + jnp.where(eight == j, total, 0.0)
            score_ref[block] = scores

        return carry

    lax.fori_loop(0, 4, forward_group, 0)

    def score_copy(block, source):
        return pltpu.make_async_remote_copy(
            src_ref=score_ref.at[block],
            dst_ref=score_got.at[source],
            send_sem=score_send.at[block],
            recv_sem=score_recv.at[source],
            device_id=member_device(block),
            device_id_type=MESH_ID,
        )

    @pl.loop(1, 16)
    def _(shift):
        score_copy((mine + shift) % 16, mine).start()

    score_got[mine] = score_ref[mine]

    @pl.loop(2, 4)
    def _(p):
        store_part(line_order(z, 3), p).wait()

    @pl.loop(0, 4)
    def _(zz):
        block = block_id(y, c, zz)
        for kind in (UP, DOWN):

            @pl.when(along(kind, zz))
            def _():
                spread(kind, block).wait_send()

        spread(ACROSS, block).wait_send()
        spread(CORE, block).wait_send()
        spread(CORE, block_id(1 - y, c, zz)).wait_send()

    opposite = {UP: DOWN, DOWN: UP, ACROSS: ACROSS, CORE: CORE}
    per_side(
        lambda kind: pl.semaphore_signal(
            ready.at[opposite[kind]], inc=1, device_id=device(kind), device_id_type=MESH_ID
        )
    )

    def sum_copy(kind, source, target, send_index, recv_sem):
        return pltpu.make_async_remote_copy(
            src_ref=source,
            dst_ref=target,
            send_sem=sum_send.at[send_index],
            recv_sem=recv_sem,
            device_id=device(kind),
            device_id_type=MESH_ID,
        )

    def to_core(turn, p, zz):
        slot = (y + p * (1 - 2 * y)) * 4 + zz
        index = turn * 2 + p
        return sum_copy(CORE, pool.at[index], held.at[slot], index, core_recv.at[slot])

    def from_core(slot):
        return sum_copy(CORE, pool.at[0], held.at[slot], 0, core_recv.at[slot])

    def to_across(zz):
        return sum_copy(ACROSS, held.at[(1 - y) * 4 + zz], held.at[8 + zz], 4 + zz, y_recv.at[zz])

    def to_line(kind, zz, last):
        return sum_copy(
            kind,
            held.at[y * 4 + zz],
            pool.at[5] if last else held.at[12 + zz],
            8 + zz,
            z_recv.at[4 if last else zz],
        )

    def add_up(slot, *others):
        @pl.loop(0, tokens_block // 64)
        def _(r):
            rows = pl.ds(pl.multiple_of(r * 64, 64), 64)
            total = held[slot, rows, :].astype(single)
            for ref, index in others:
                total = total + ref[index, rows, :].astype(single)
            held[slot, rows, :] = total.astype(bfloat)

    def back_block(step, p, target, index, onto):
        local = pl.multiple_of(p * capacity, 32)
        pick = picks[step * 4 + p]
        for n in range(width // CHUNK):
            part = pl.ds(n * CHUNK, CHUNK)
            grads = jnp.concatenate(
                [work[j, pl.ds(local, capacity), part] for j in range(local_exp)], axis=0
            )
            block = contract_rows(pick, grads)
            if onto:
                block = block + target[index, :, part].astype(single)
            target[index, :, part] = block.astype(bfloat)

    def line_sum(step):
        zz = line_order(z, step)
        slot = y * 4 + zz
        to_across(zz).wait_recv()
        rising = zz > z
        comes = jnp.logical_or(jnp.logical_and(rising, z > 0), jnp.logical_and(zz < z, z < 3))

        @pl.when(comes)
        def _():
            to_line(CORE, zz, False).wait_recv()
            add_up(slot, (held, 8 + zz), (held, 12 + zz))

        @pl.when(jnp.logical_not(comes))
        def _():
            add_up(slot, (held, 8 + zz))

        @pl.when(rising)
        def _():
            to_line(UP, zz, False).start()

        @pl.when(zz == z - 1)
        def _():
            to_line(DOWN, zz, True).start()

        @pl.when(zz < z - 1)
        def _():
            to_line(DOWN, zz, False).start()

    def at_end(action):
        pl.when(inner == 0)(action)

    def at_middle(action):
        pl.when(inner == 1)(action)

    def backward_group(turn_step, carry):
        step = 3 - turn_step
        zz = line_order(z, step)
        turn = step % 2
        base = pl.multiple_of(step * group_rows, 128)
        for j in range(local_exp):
            for n in range(hidden_units // HALF):
                part = pl.ds(n * HALF, HALF)
                grad_hidden = (
                    contract_last(rows_grad[j, pl.ds(base, group_rows), :], w_down[j, part, :])
                    .astype(bfloat)
                    .astype(single)
                )
                slope_gate[j, pl.ds(base, group_rows), part] = (
                    grad_hidden * slope_gate[j, pl.ds(base, group_rows), part].astype(single)
                ).astype(bfloat)
                slope_up[j, pl.ds(base, group_rows), part] = (
                    grad_hidden * slope_up[j, pl.ds(base, group_rows), part].astype(single)
                ).astype(bfloat)
            for n in range(width // CHUNK):
                part = pl.ds(n * CHUNK, CHUNK)
                work[j, :, part] = (
                    contract_last(slope_gate[j, pl.ds(base, group_rows), :], w_gate[j, part, :])
                    + contract_last(slope_up[j, pl.ds(base, group_rows), :], w_up[j, part, :])
                ).astype(bfloat)

        @pl.when(turn_step == 0)
        def _():
            per_side(lambda kind: pl.semaphore_wait(ready.at[kind], 1))

        for p, member_p in ((1, 3), (0, 1)):

            @pl.when(turn_step > 1)
            def _():
                to_core(turn, p, zz).wait_send()

            back_block(step, member_p, pool, turn * 2 + p, False)
            to_core(turn, p, zz).start()

        other = (1 - y) * 4 + zz
        from_core(other).wait_recv()
        back_block(step, 2, held, other, True)
        to_across(zz).start()
        slot = y * 4 + zz
        from_core(slot).wait_recv()
        back_block(step, 0, held, slot, True)

        @pl.when(turn_step == 2)
        def _():
            at_end(lambda: line_sum(3))

        return carry

    lax.fori_loop(0, 4, backward_group, 0)
    at_middle(lambda: line_sum(3))
    at_end(lambda: line_sum(2))

    def stores(j):
        pairs = ((w_gate, grad_gate_ref), (w_up, grad_up_ref), (w_down, grad_down_ref))
        if not swap:
            return [
                pltpu.make_async_copy(source.at[j], target.at[j], load_sem.at[3 * j + i])
                for i, (source, target) in enumerate(pairs)
            ]
        d = lax.axis_index("dp")
        copies = []
        for i, (source, target) in enumerate(pairs):
            size = target.shape[1]
            here = pl.ds(pl.multiple_of(d * size, 128), size)
            copies.append(
                pltpu.make_async_copy(source.at[j, here, :], target.at[j], load_sem.at[3 * j + i])
            )
        there = lambda size: pl.ds(pl.multiple_of((1 - d) * size, 128), size)
        low = w_down.shape[1] // 2
        leaving = [
            (
                w_down.at[j, there(low), pl.ds(n * hidden_units, hidden_units)],
                swap[2].at[2 + j, pl.ds(n * low, low), :],
            )
            for n in range(width // hidden_units)
        ]
        if j == 1:
            leaving += [
                (source.at[1, there(width // 2), :], swap[2].at[i])
                for i, source in enumerate((w_gate, w_up))
            ]
        for i, (source, target) in enumerate(leaving):
            copies.append(pltpu.make_async_copy(source, target, load_sem.at[6 + 3 * j + i]))
        return copies

    def weight_grads(j):
        @pl.loop(0, width // CHUNK)
        def _(n):
            part = pl.ds(pl.multiple_of(n * CHUNK, CHUNK), CHUNK)
            w_gate[j, part, :] = contract_rows(rows_in[j, :, part], slope_gate[j]).astype(bfloat)
            w_up[j, part, :] = contract_rows(rows_in[j, :, part], slope_up[j]).astype(bfloat)
            w_down[j, :, part] = contract_rows(hidden_e[j], rows_grad[j, :, part]).astype(bfloat)

        for copy in stores(j):
            copy.start()

    weight_grads(0)
    swaps = []
    if swap:
        swaps = swap_copies(
            ((w_gate, 0, swap[0]), (w_up, 0, swap[1])), device, swap_send, swap_recv
        )
        for copy in swaps:
            copy.start()
    weight_grads(1)
    at_middle(lambda: line_sum(2))
    line_sum(1)
    slot = y * 4 + z
    to_across(z).wait_recv()
    add_up(slot, (held, 8 + z))

    @pl.when(z > 0)
    def _():
        to_line(CORE, z, False).wait_recv()
        add_up(slot, (held, 12 + z))

    @pl.when(z < 3)
    def _():
        to_line(CORE, z, True).wait_recv()
        add_up(slot, (pool, 5))

    result = pltpu.make_async_copy(held.at[slot], back_ref, local_sem)
    result.start()
    for j in range(local_exp):
        for copy in stores(j):
            copy.wait()
    for turn in range(2):
        for p in range(2):
            to_core(turn, p, z).wait_send()

    @pl.loop(0, 4)
    def _(zz):
        to_across(zz).wait_send()

        @pl.when(zz != z)
        def _():
            to_line(CORE, zz, False).wait_send()

    @pl.loop(1, 16)
    def _(shift):
        other = (mine + shift) % 16
        score_copy(other, mine).wait_send()
        score_copy(other, other).wait_recv()

    for copy in swaps:
        copy.wait()
    result.wait()


def experts_on_owner(
    hidden, final_all, routes_all, router_rows, w_gate, w_up, w_down, capacity, swap
):
    blocks = final_all.shape[0]
    tokens_block, width = hidden.shape
    local_exp, _, units = w_gate.shape
    bfloat = jnp.bfloat16
    single = jnp.float32
    rows = blocks * capacity
    grads = [x.shape for x in (w_gate, w_up, w_down)]
    if swap:
        wide, low = (width // 2, units), (units // 2, width)
        grads = [(2, *wide), (2, *wide), (2, *low), wide, wide, (4, *wide)]
    anywhere = pl.BlockSpec(memory_space=pl.ANY)
    vmem = pl.BlockSpec(memory_space=pltpu.VMEM)
    dma = pltpu.SemaphoreType.DMA
    return pl.pallas_call(
        functools.partial(experts_kernel, swap),
        out_shape=(
            jax.ShapeDtypeStruct((tokens_block, width), bfloat),
            jax.ShapeDtypeStruct((blocks, tokens_block, width), bfloat),
            jax.ShapeDtypeStruct((blocks, 8, tokens_block), single),
            *(jax.ShapeDtypeStruct(shape, bfloat) for shape in grads),
        ),
        in_specs=[anywhere, anywhere, vmem, vmem, anywhere, anywhere, anywhere],
        out_specs=(anywhere, anywhere, vmem, *([anywhere] * len(grads))),
        scratch_shapes=[
            pltpu.VMEM((blocks, tokens_block, width), bfloat),
            pltpu.VMEM(w_gate.shape, bfloat),
            pltpu.VMEM(w_up.shape, bfloat),
            pltpu.VMEM(w_down.shape, bfloat),
            pltpu.VMEM((local_exp, rows, width), bfloat),
            pltpu.VMEM((local_exp, rows, width), bfloat),
            pltpu.VMEM((local_exp, rows, units), bfloat),
            pltpu.VMEM((local_exp, rows, units), bfloat),
            pltpu.VMEM((local_exp, rows, units), bfloat),
            pltpu.VMEM((blocks, local_exp * capacity, tokens_block), bfloat),
            pltpu.VMEM((4, local_exp * capacity, 128), single),
            pltpu.VMEM((local_exp, 4 * capacity, width), bfloat),
            pltpu.VMEM((6, tokens_block, width), bfloat),
            pltpu.VMEM((tokens_block, tokens_block), bfloat),
            dma((4, blocks)),
            dma((blocks,)),
            dma,
            dma((14,)),
            dma((2,)),
            dma((12,)),
            dma((8,)),
            dma((4,)),
            dma((5,)),
            pltpu.SemaphoreType.REGULAR((4,)),
            pltpu.VMEM((blocks, 8, tokens_block), single),
            dma((16,)),
            dma((16,)),
            dma((2,)),
            dma((2,)),
        ],
        compiler_params=pltpu.CompilerParams(
            collective_id=1, has_side_effects=True, vmem_limit_bytes=63 * 2**20
        ),
        name="experts",
    )(hidden, final_all, routes_all, router_rows, w_gate, w_up, w_down)


def on_device(
    tokens,
    lengths,
    routes,
    gain_attn,
    w_query,
    key_weight,
    value_weight,
    w_out,
    gain_ffn,
    w_router,
    w_gate,
    w_up,
    w_down,
    cotangent,
):
    tokens_own = tokens.shape[1]
    exp_count = lax.axis_size("expert")
    ctx_count = lax.axis_size("context")
    local_exp = w_gate.shape[0]
    experts = local_exp * ctx_count * exp_count
    capacity = tokens_own * TOP * 3 // (2 * experts)
    bfloat = jnp.bfloat16
    single = jnp.float32
    query_width = w_query.shape[1]
    key_width = key_weight.shape[1]
    proj_width = query_width + 2 * key_width
    own_rows = w_query.shape[0]
    pair = lax.axis_size("dp") == 2
    small = jnp.concatenate(
        [
            w_router,
            gain_attn[:, None],
            gain_ffn[:, None],
            jnp.zeros((own_rows, 64 - experts - 2), bfloat),
        ],
        axis=1,
    )
    if pair:
        packed = routes[0].T.reshape(-1, 64).astype(bfloat)
        packed = jnp.pad(packed, ((0, own_rows - packed.shape[0]), (0, 0)))
        early, small_all, out_w = gather_weights(
            w_query, key_weight, value_weight, jnp.concatenate([small, packed], axis=1), w_out
        )
        out_w = out_w.reshape(-1, out_w.shape[2])
        routes_all = lax.dynamic_slice(
            small_all, (lax.axis_index("dp") * 16, 0, 64), (16, tokens_own * TOP // 64, 64)
        )
        routes_all = routes_all.astype(jnp.int32).reshape(16, TOP, tokens_own)
        proj_w = early.reshape(-1, proj_width)
        small_all = small_all.reshape(-1, small_all.shape[2])
    else:
        proj_w = jnp.concatenate([w_query, key_weight, value_weight], axis=1)
        proj_w = lax.all_gather(proj_w, EVERY, axis=0, tiled=True)
        small_all = lax.all_gather(small, EVERY, axis=0, tiled=True)
        out_w = lax.all_gather(w_out, EVERY, axis=0, tiled=True)
        routes_all = lax.all_gather(routes[0].T, GROUP, axis=0, tiled=False)
    positions = lax.axis_index("context") * tokens_own + jnp.arange(tokens_own, dtype=jnp.int32)
    valid = (positions < lengths[0]).astype(single)[:, None]
    grad_final = cotangent[0].astype(single) * valid
    final_all = lax.all_gather(grad_final.astype(bfloat), GROUP, axis=0, tiled=False)
    router_w = small_all[:, :experts]
    gain_one = small_all[:, experts].astype(single)
    gain_two = small_all[:, experts + 1].astype(single)
    cosine, sine = rotation_tables(positions)

    inputs = tokens[0].astype(single)
    inverse_one = lax.rsqrt(jnp.mean(inputs * inputs, axis=-1, keepdims=True) + epsilon)
    normed_one = inputs * inverse_one
    hidden_one = lax.optimization_barrier((normed_one * gain_one).astype(bfloat))
    projected = jnp.einsum("de,sd->es", proj_w, hidden_one, preferred_element_type=single)
    rotated = apply_rotation(projected[: query_width + key_width], cosine, sine).astype(bfloat)
    query = rotated[:query_width] * HEAD_SIZE ** (-0.5)
    own_pairs = jnp.concatenate(
        [rotated[query_width:], projected[query_width + key_width :].astype(bfloat)], axis=0
    )
    mixed, pairs = attend(query, own_pairs, lengths)
    resid = inputs + jnp.einsum("es,ed->sd", mixed, out_w, preferred_element_type=single)
    inverse_two = lax.rsqrt(jnp.mean(resid * resid, axis=-1, keepdims=True) + epsilon)
    normed_two = resid * inverse_two
    hidden_two = (normed_two * gain_two).astype(bfloat)

    grad_hidden, combined, scores, *expert_grads = experts_on_owner(
        hidden_two, final_all, routes_all, router_w.T, w_gate, w_up, w_down, capacity, pair
    )
    expert_grads, got = expert_grads[:3], expert_grads[3:]
    combined = lax.psum_scatter(combined, GROUP, scatter_dimension=0, tiled=False)

    if pair:
        moved = lax.ppermute(got[2], "dp", ((0, 1), (1, 0)))
        low = w_down.shape[1] // 2
        others = (
            jnp.stack([got[0], moved[0]]),
            jnp.stack([got[1], moved[1]]),
            jnp.concatenate(
                [moved[2:, n * low : (n + 1) * low] for n in range(MODEL_WIDTH // w_down.shape[1])],
                axis=2,
            ),
        )
    scores = scores[:, :local_exp]
    grad_gates = scores.reshape(experts, tokens_own).T

    routed = jnp.any(routes[0][:, :, None] == jnp.arange(experts, dtype=jnp.int32), axis=1)
    logits = jnp.einsum("sd,de->se", hidden_two, router_w, preferred_element_type=single)
    gates = jax.nn.softmax(jnp.where(routed, logits, floor_score), axis=-1)
    gates = jnp.where(routed, gates, 0.0)
    gate_mean = jnp.sum(gates * grad_gates, axis=-1, keepdims=True)
    grad_logits = (gates * (grad_gates - gate_mean)).astype(bfloat)
    grad_w_router = jnp.einsum("sd,se->de", hidden_two, grad_logits, preferred_element_type=single)
    grad_hidden_two = grad_hidden.astype(single) + jnp.einsum(
        "se,de->sd", grad_logits, router_w, preferred_element_type=single
    )
    grad_gain_ffn = jnp.sum(grad_hidden_two * normed_two, axis=0)
    grad_resid = norm_back(grad_hidden_two * gain_two, normed_two, inverse_two) + grad_final
    grad_attn = lax.optimization_barrier(grad_resid.astype(bfloat))

    grad_out_w = jnp.einsum("es,sd->ed", mixed, grad_attn, preferred_element_type=single)
    grad_mixed = jnp.einsum("ed,sd->es", out_w, grad_attn, preferred_element_type=single)
    grad_out_w = grad_out_w.astype(bfloat)
    grad_proj = attend_back(query, pairs, grad_mixed.astype(bfloat), lengths, cosine, sine)
    grad_proj_w = jnp.einsum("sd,es->de", hidden_one, grad_proj, preferred_element_type=single)
    grad_hidden_one = jnp.einsum("es,de->sd", grad_proj, proj_w, preferred_element_type=single)
    grad_gain_attn = jnp.sum(grad_hidden_one * normed_one, axis=0)
    grad_tokens = norm_back(grad_hidden_one * gain_one, normed_one, inverse_one) + grad_resid

    grad_small = jnp.concatenate(
        [
            grad_w_router,
            grad_gain_attn[:, None],
            grad_gain_ffn[:, None],
            jnp.zeros((MODEL_WIDTH, 128 - experts - 2), single),
        ],
        axis=1,
    ).astype(bfloat)
    grad_proj_w = grad_proj_w.astype(bfloat)
    if pair:
        expert_sums = tuple(
            own.astype(single) + other.astype(single)
            for own, other in zip(expert_grads, others)
        )
        grad_proj_w, grad_tokens, expert_sums = lax.optimization_barrier(
            (grad_proj_w, grad_tokens, expert_sums)
        )
        *proj_sums, small_sum, out_sum = sum_gradients(
            grad_proj_w, grad_small, grad_out_w, (query_width, key_width, key_width)
        )
    else:
        summed = lax.psum_scatter(
            jnp.concatenate([grad_proj_w, grad_small, grad_out_w], axis=1),
            EVERY,
            scatter_dimension=0,
            tiled=True,
        ).astype(single)
        proj_sums = jnp.split(summed[:, :proj_width], (query_width, query_width + key_width), axis=1)
        small_sum = summed[:, proj_width : proj_width + 128]
        out_sum = summed[:, proj_width + 128 :]
        expert_sums = tuple(
            lax.psum_scatter(x, "dp", scatter_dimension=1, tiled=True).astype(single)
            for x in expert_grads
        )
    combined, small_sum = lax.optimization_barrier((combined, small_sum))
    block_out = (valid * (resid + combined.astype(single))).astype(bfloat)
    return (
        block_out[None],
        grad_tokens[None],
        small_sum[:, experts],
        *proj_sums,
        out_sum,
        small_sum[:, experts + 1],
        small_sum[:, :experts],
        *expert_sums,
    )


def solution(mesh):
    in_specs = (
        P(("dp", "expert"), "context", None),
        P(("dp", "expert")),
        P(("dp", "expert"), "context", None),
        P(("dp", "context", "expert")),
        P(("dp", "context", "expert"), None),
        P(("dp", "context", "expert"), None),
        P(("dp", "context", "expert"), None),
        P(("dp", "context", "expert"), None),
        P(("dp", "context", "expert")),
        P(("dp", "context", "expert"), None),
        P(("context", "expert"), None, None),
        P(("context", "expert"), None, None),
        P(("context", "expert"), None, None),
        P(("dp", "expert"), "context", None),
    )
    out_specs = (
        P(("dp", "expert"), "context", None),
        P(("dp", "expert"), "context", None),
        P(("dp", "context", "expert")),
        P(("dp", "context", "expert"), None),
        P(("dp", "context", "expert"), None),
        P(("dp", "context", "expert"), None),
        P(("dp", "context", "expert"), None),
        P(("dp", "context", "expert")),
        P(("dp", "context", "expert"), None),
        P(("context", "expert"), "dp", None),
        P(("context", "expert"), "dp", None),
        P(("context", "expert"), "dp", None),
    )
    return jax.shard_map(
        on_device, mesh=mesh, in_specs=in_specs, out_specs=out_specs, check_vma=False
    )
```

```python
import functools
import math

import jax
import jax.numpy as jnp
from jax import lax
from jax.experimental import pallas as pl
from jax.experimental.pallas import tpu as pltpu
from jax.sharding import PartitionSpec as P

MODEL_WIDTH = 1536
HEAD_SIZE = 64
TOP = 8
epsilon = 1e-05
floor_score = -1e30


def rotation_tables(positions):
    half_size = HEAD_SIZE // 2
    exponent = jnp.arange(half_size, dtype=jnp.int32).astype(jnp.float32) * (2.0 / HEAD_SIZE)
    frequency = jnp.exp(-math.log(10000.0) * exponent)
    angles = frequency[:, None] * positions.astype(jnp.float32)[None, :]
    return (jnp.cos(angles), jnp.sin(angles))


def apply_rotation(values, cosine, sine):
    split = values.reshape(-1, 2, HEAD_SIZE // 2, values.shape[1])
    first = split[:, 0]
    second = split[:, 1]
    turned = jnp.stack([first * cosine - second * sine, second * cosine + first * sine], axis=1)
    return turned.reshape(values.shape)


def inverse_rotation(gradient, cosine, sine):
    return apply_rotation(gradient, cosine, -sine)


def norm_back(gradient, normed, inverse):
    return inverse * (gradient - normed * jnp.mean(gradient * normed, axis=-1, keepdims=True))


GROUP = ("context", "expert")
EVERY = ("dp", "context", "expert")


MESH_ID = pl.DeviceIdType.MESH
CHUNK = 512
HALF = 256
UP, DOWN, ACROSS, CORE, DP = 0, 1, 2, 3, 4


def contract_rows(left, right):
    return lax.dot_general(left, right, (((0,), (0,)), ((), ())), preferred_element_type=jnp.float32)


def contract_last(left, right):
    return lax.dot_general(left, right, (((1,), (1,)), ((), ())), preferred_element_type=jnp.float32)


def matmul(left, right):
    return jnp.dot(left, right, preferred_element_type=jnp.float32)


def line_order(z, step):
    half = z // 2
    inner = z + half * (3 - 2 * z)
    base = step + inner * (1 - 2 * step) * (1 - step // 2)
    return base + half * (3 - 2 * base)


def place():
    ctx = lax.axis_index("context")
    z = lax.axis_index("expert")
    y = ctx // 2
    c = ctx % 2
    inner = z + (z // 2) * (3 - 2 * z)

    def device(kind):
        if kind == UP:
            return {"context": ctx, "expert": z + 1}
        if kind == DOWN:
            return {"context": ctx, "expert": z - 1}
        if kind == ACROSS:
            return {"context": (1 - y) * 2 + c, "expert": z}
        if kind == CORE:
            return {"context": y * 2 + 1 - c, "expert": z}
        return {"dp": 1 - lax.axis_index("dp")}

    def per_side(action, more=()):
        @pl.when(z < 3)
        def _():
            action(UP)

        @pl.when(z > 0)
        def _():
            action(DOWN)

        for kind in (ACROSS, CORE, *more):
            action(kind)

    return y, c, z, inner, device, per_side


def block_id(yy, cc, zz):
    return (yy * 2 + cc) * 4 + zz


def greet(per_side, device, count, more=()):
    barrier = pltpu.get_barrier_semaphore()
    per_side(
        lambda kind: pl.semaphore_signal(
            barrier, inc=1, device_id=device(kind), device_id_type=MESH_ID
        ),
        more,
    )
    pl.semaphore_wait(barrier, count)


def swap_copies(pieces, device, send_sem, recv_sem):
    d = lax.axis_index("dp")
    copies = []
    for index, (source, j, target) in enumerate(pieces):
        half = target.shape[0]
        copies.append(
            pltpu.make_async_remote_copy(
                src_ref=source.at[j, pl.ds(pl.multiple_of((1 - d) * half, 128), half), :],
                dst_ref=target,
                send_sem=send_sem.at[index],
                recv_sem=recv_sem.at[index],
                device_id=device(DP),
                device_id_type=MESH_ID,
            )
        )
    return copies


def ring_sum(parts, core_got, y_got, z_got, dp_got, sems):
    single = jnp.float32
    core_send, core_recv, y_send, y_recv, z_send, z_recv, dp_send, dp_recv = sems
    y, c, z, _, device, _ = place()
    d = lax.axis_index("dp")
    rows = parts.shape[1] // 2
    mine = block_id(y, c, z)

    def remote(kind, source, target, send_sem, recv_sem):
        return pltpu.make_async_remote_copy(
            src_ref=source,
            dst_ref=target,
            send_sem=send_sem,
            recv_sem=recv_sem,
            device_id=device(kind),
            device_id_type=MESH_ID,
        )

    def to_core(yy, zz):
        slot = yy * 4 + zz
        return remote(
            CORE, parts.at[block_id(yy, 1 - c, zz)], core_got.at[slot], core_send.at[slot], core_recv.at[slot]
        )

    def to_across(zz):
        return remote(ACROSS, parts.at[block_id(1 - y, c, zz)], y_got.at[zz], y_send.at[zz], y_recv.at[zz])

    def to_line(kind, zz, slot):
        return remote(kind, parts.at[block_id(y, c, zz)], z_got.at[slot], z_send.at[zz], z_recv.at[slot])

    def add(block, got):
        parts[block] = (parts[block].astype(single) + got.astype(single)).astype(parts.dtype)

    def core_sends():
        @pl.loop(0, 4)
        def _(turn):
            zz = line_order(z, 3 - turn)
            to_core(1 - y, zz).start()
            to_core(y, zz).start()

    def across(step):
        zz = line_order(z, step)
        to_core(1 - y, zz).wait_recv()
        add(block_id(1 - y, c, zz), core_got[(1 - y) * 4 + zz])
        to_across(zz).start()
        to_core(y, zz).wait_recv()
        add(block_id(y, c, zz), core_got[y * 4 + zz])

    def line(step):
        zz = line_order(z, step)
        block = block_id(y, c, zz)
        to_across(zz).wait_recv()
        add(block, y_got[zz])
        rising = zz > z
        comes = jnp.logical_or(jnp.logical_and(rising, z > 0), jnp.logical_and(zz < z, z < 3))

        @pl.when(comes)
        def _():
            to_line(CORE, zz, zz).wait_recv()
            add(block, z_got[zz])

        @pl.when(rising)
        def _():
            to_line(UP, zz, zz).start()

        @pl.when(zz == z - 1)
        def _():
            to_line(DOWN, zz, 4).start()

        @pl.when(zz < z - 1)
        def _():
            to_line(DOWN, zz, zz).start()

    there = pl.ds(pl.multiple_of((1 - d) * rows, 16), rows)
    here = pl.ds(pl.multiple_of(d * rows, 16), rows)
    last = remote(DP, parts.at[mine, there, :], dp_got, dp_send, dp_recv)

    def over_dp():
        to_across(z).wait_recv()
        add(mine, y_got[z])

        @pl.when(z > 0)
        def _():
            to_line(CORE, z, z).wait_recv()
            add(mine, z_got[z])

        @pl.when(z < 3)
        def _():
            to_line(CORE, z, 4).wait_recv()
            add(mine, z_got[4])

        last.start()

    def finish(result):
        last.wait_recv()
        result[...] = parts[mine, here, :].astype(single) + dp_got[...].astype(single)
        last.wait_send()

        @pl.loop(0, 4)
        def _(zz):
            to_core(y, zz).wait_send()
            to_core(1 - y, zz).wait_send()
            to_across(zz).wait_send()

            @pl.when(zz != z)
            def _():
                to_line(CORE, zz, zz).wait_send()

    return core_sends, across, line, over_dp, finish


def ring_scratch(rows, width):
    bfloat = jnp.bfloat16
    dma = pltpu.SemaphoreType.DMA
    return [
        pltpu.VMEM((16, 2 * rows, width), bfloat),
        pltpu.VMEM((8, 2 * rows, width), bfloat),
        pltpu.VMEM((4, 2 * rows, width), bfloat),
        pltpu.VMEM((5, 2 * rows, width), bfloat),
        pltpu.VMEM((rows, width), bfloat),
        dma((8,)),
        dma((8,)),
        dma((4,)),
        dma((4,)),
        dma((4,)),
        dma((5,)),
        dma,
        dma,
    ]


def load_parts(refs, parts, sem):
    loads = []
    at = 0
    for index, ref in enumerate(refs):
        rows, size = ref.shape[2], ref.shape[3]
        for plane in range(2):
            loads.append(
                pltpu.make_async_copy(
                    ref.at[plane],
                    parts.at[:, pl.ds(plane * rows, rows), pl.ds(at, size)],
                    sem.at[index * 2 + plane],
                )
            )
        at += size
    return loads


def spread_rows(whole, send_sem, core_sem, recv_sem):
    y, c, z, _, device, _ = place()
    d = lax.axis_index("dp")

    def copy_of(kind, slot, sem):
        return pltpu.make_async_remote_copy(
            src_ref=whole.at[slot],
            dst_ref=whole.at[slot],
            send_sem=sem,
            recv_sem=recv_sem.at[slot],
            device_id=device(kind),
            device_id_type=MESH_ID,
        )

    def own(kind, block):
        return copy_of(kind, d * 16 + block, send_sem.at[kind, block])

    def other(block):
        return copy_of(CORE, (1 - d) * 16 + block, core_sem.at[block])

    def along(kind, zz):
        if kind == UP:
            return jnp.logical_and(z < 3, zz <= z)
        return jnp.logical_and(z > 0, zz >= z)

    def fan(zz, act):
        block = block_id(y, c, zz)
        for kind in (UP, DOWN):

            @pl.when(along(kind, zz))
            def _():
                act(own(kind, block))

        for kind in (ACROSS, DP, CORE):
            act(own(kind, block))

    def fan_across(zz, act):
        block = block_id(1 - y, c, zz)
        act(own(DP, block))
        act(own(CORE, block))

    def fan_dp(zz, act):
        act(other(block_id(y, c, zz)))
        act(other(block_id(1 - y, c, zz)))

    start = lambda copy: copy.start()
    end = lambda copy: copy.wait_send()

    def begin():
        fan(z, start)

    def arrive(step):
        @pl.when(step < 4)
        def _():
            zz = line_order(z, jnp.minimum(step, 3))
            own(ACROSS, block_id(y, c, zz)).wait_recv()
            fan(zz, start)

        @pl.when(step < 5)
        def _():
            zz = line_order(z, jnp.minimum(step - 1, 3))
            own(CORE, block_id(1 - y, c, zz)).wait_recv()
            fan_across(zz, start)

        @pl.when(step > 1)
        def _():
            zz = line_order(z, jnp.maximum(step - 2, 0))
            other(block_id(y, c, zz)).wait_recv()
            other(block_id(1 - y, c, zz)).wait_recv()
            fan_dp(zz, start)

    def finish():
        @pl.loop(0, 4)
        def _(zz):
            for yy in range(2):
                block = block_id(yy, 1 - c, zz)
                own(CORE, block).wait_recv()
                other(block).wait_recv()

    def ends():
        @pl.loop(0, 4)
        def _(zz):
            fan(zz, end)
            fan_across(zz, end)
            fan_dp(zz, end)

    return begin, arrive, finish, ends


def spread_scratch(rows, width):
    dma = pltpu.SemaphoreType.DMA
    return [pltpu.VMEM((32, rows, width), jnp.bfloat16), dma((5, 16)), dma((16,)), dma((32,))]


def gather_kernel(
    query_ref,
    key_ref,
    value_ref,
    small_ref,
    out_ref,
    proj_all,
    small_all,
    out_all,
    local_sem,
    whole,
    *sems,
):
    y, c, z, inner, device, per_side = place()
    mine = lax.axis_index("dp") * 16 + block_id(y, c, z)
    loads = []
    at = 0
    for index, ref in enumerate((query_ref, key_ref, value_ref, small_ref, out_ref)):
        size = ref.shape[1]
        loads.append(
            pltpu.make_async_copy(ref, whole.at[mine, :, pl.ds(at, size)], local_sem.at[index])
        )
        at += size
    for copy in loads:
        copy.start()
    greet(per_side, device, 4 + inner, (DP,))
    for copy in loads:
        copy.wait()
    begin, arrive, finish, ends = spread_rows(whole, *sems)
    begin()

    @pl.loop(1, 6)
    def _(step):
        arrive(step)

    finish()
    results = []
    at = 0
    for index, ref in enumerate((proj_all, small_all, out_all)):
        size = ref.shape[2]
        results.append(
            pltpu.make_async_copy(whole.at[:, :, pl.ds(at, size)], ref, local_sem.at[index])
        )
        at += size
    for copy in results:
        copy.start()
    ends()
    for copy in results:
        copy.wait()


def gather_weights(query, key, value, small, out):
    rows = query.shape[0]
    widths = (query.shape[1] + key.shape[1] + value.shape[1], small.shape[1], out.shape[1])
    anywhere = pl.BlockSpec(memory_space=pl.ANY)
    return pl.pallas_call(
        gather_kernel,
        out_shape=tuple(
            jax.ShapeDtypeStruct((32, rows, width), jnp.bfloat16) for width in widths
        ),
        in_specs=[anywhere] * 5,
        out_specs=(anywhere, anywhere, anywhere),
        scratch_shapes=[pltpu.SemaphoreType.DMA((5,)), *spread_scratch(rows, sum(widths))],
        compiler_params=pltpu.CompilerParams(
            collective_id=0, has_side_effects=True, vmem_limit_bytes=60 * 2**20
        ),
        name="gather_weights",
    )(query, key, value, small, out)


def ring_sum_dp_early(parts, core_got, dp_got, y_got, z_got, sems):
    single = jnp.float32
    core_send, core_recv, dp_send, dp_recv, y_send, y_recv, z_send, z_recv = sems
    y, c, z, _, device, _ = place()
    d = lax.axis_index("dp")
    rows = parts.shape[1] // 2
    mine = block_id(y, c, z)
    there = pl.ds(pl.multiple_of((1 - d) * rows, 16), rows)
    here = pl.ds(pl.multiple_of(d * rows, 16), rows)

    def remote(kind, source, target, send_sem, recv_sem):
        return pltpu.make_async_remote_copy(
            src_ref=source,
            dst_ref=target,
            send_sem=send_sem,
            recv_sem=recv_sem,
            device_id=device(kind),
            device_id_type=MESH_ID,
        )

    def to_core(yy, zz):
        slot = yy * 4 + zz
        return remote(
            CORE, parts.at[block_id(yy, 1 - c, zz)], core_got.at[slot], core_send.at[slot], core_recv.at[slot]
        )

    def to_dp(yy, zz):
        slot = yy * 4 + zz
        return remote(
            DP, parts.at[block_id(yy, c, zz), there, :], dp_got.at[slot], dp_send.at[slot], dp_recv.at[slot]
        )

    def to_across(zz):
        return remote(
            ACROSS, parts.at[block_id(1 - y, c, zz), here, :], y_got.at[zz], y_send.at[zz], y_recv.at[zz]
        )

    def to_line(kind, zz, slot):
        return remote(
            kind, parts.at[block_id(y, c, zz), here, :], z_got.at[slot], z_send.at[zz], z_recv.at[slot]
        )

    def add(block, got):
        parts[block, here, :] = (
            parts[block, here, :].astype(single) + got.astype(single)
        ).astype(parts.dtype)

    def core_sends():
        @pl.loop(0, 4)
        def _(turn):
            zz = line_order(z, 3 - turn)
            to_core(1 - y, zz).start()
            to_core(y, zz).start()

    def meet(step):
        zz = line_order(z, step)
        for yy in (1 - y, y):
            block = block_id(yy, c, zz)
            to_core(yy, zz).wait_recv()
            parts[block] = (
                parts[block].astype(single) + core_got[yy * 4 + zz].astype(single)
            ).astype(parts.dtype)
            to_dp(yy, zz).start()

    def across(step):
        zz = line_order(z, step)
        for yy in (1 - y, y):
            to_dp(yy, zz).wait_recv()
            add(block_id(yy, c, zz), dp_got[yy * 4 + zz])
        to_across(zz).start()

    def line(step):
        zz = line_order(z, step)
        block = block_id(y, c, zz)
        to_across(zz).wait_recv()
        add(block, y_got[zz])
        rising = zz > z
        comes = jnp.logical_or(jnp.logical_and(rising, z > 0), jnp.logical_and(zz < z, z < 3))

        @pl.when(comes)
        def _():
            to_line(CORE, zz, zz).wait_recv()
            add(block, z_got[zz])

        @pl.when(rising)
        def _():
            to_line(UP, zz, zz).start()

        @pl.when(zz == z - 1)
        def _():
            to_line(DOWN, zz, 4).start()

        @pl.when(zz < z - 1)
        def _():
            to_line(DOWN, zz, zz).start()

    def finish(results):
        spans = []
        at = 0
        for result in results:
            spans.append(pl.ds(at, result.shape[1]))
            at += result.shape[1]
        to_across(z).wait_recv()
        for result, span in zip(results, spans):
            result[...] = parts[mine, here, span].astype(single) + y_got[z, :, span].astype(single)

        @pl.when(z > 0)
        def _():
            to_line(CORE, z, z).wait_recv()
            for result, span in zip(results, spans):
                result[...] += z_got[z, :, span].astype(single)

        @pl.when(z < 3)
        def _():
            to_line(CORE, z, 4).wait_recv()
            for result, span in zip(results, spans):
                result[...] += z_got[4, :, span].astype(single)

        @pl.loop(0, 4)
        def _(zz):
            for yy in (y, 1 - y):
                to_core(yy, zz).wait_send()
                to_dp(yy, zz).wait_send()
            to_across(zz).wait_send()

            @pl.when(zz != z)
            def _():
                to_line(CORE, zz, zz).wait_send()

    return core_sends, meet, across, line, finish


def ring_scratch_dp_early(rows, width):
    bfloat = jnp.bfloat16
    dma = pltpu.SemaphoreType.DMA
    return [
        pltpu.VMEM((16, 2 * rows, width), bfloat),
        pltpu.VMEM((8, 2 * rows, width), bfloat),
        pltpu.VMEM((8, rows, width), bfloat),
        pltpu.VMEM((4, rows, width), bfloat),
        pltpu.VMEM((5, rows, width), bfloat),
        *[dma((n,)) for n in (8, 8, 8, 8, 4, 4, 4, 5)],
    ]


def sums_kernel(
    proj_ref, small_ref, out_ref, query_sum, key_sum, value_sum, small_sum, out_sum, load_sem, *rings
):
    _, _, _, inner, device, per_side = place()
    ring, out_ring = rings[:13], rings[13:]
    loads = load_parts((proj_ref, small_ref), ring[0], load_sem) + load_parts(
        (out_ref,), out_ring[0], load_sem.at[pl.ds(4, 2)]
    )
    for copy in loads:
        copy.start()
    greet(per_side, device, 4 + inner, (DP,))
    for copy in loads:
        copy.wait()
    core_sends, meet, across, line, finish = ring_sum_dp_early(*ring[:5], ring[5:])
    out_core, out_across, out_line, out_dp, out_finish = ring_sum(*out_ring[:5], out_ring[5:])
    core_sends()
    out_core()

    @pl.loop(0, 4)
    def _(turn):
        meet(3 - turn)

    @pl.loop(0, 4)
    def _(turn):
        out_across(3 - turn)

    @pl.loop(0, 4)
    def _(turn):
        across(3 - turn)

        @pl.when(turn < 3)
        def _():
            out_line(3 - jnp.minimum(turn, 2))

        @pl.when(turn > 0)
        def _():
            line(4 - jnp.maximum(turn, 1))

    out_dp()
    finish((query_sum, key_sum, value_sum, small_sum))
    out_finish(out_sum)


def by_device(x):
    return x.reshape(2, 16, x.shape[0] // 32, x.shape[1])


def sum_gradients(proj, small, out, widths):
    dma = pltpu.SemaphoreType.DMA
    anywhere = pl.BlockSpec(memory_space=pl.ANY)
    vmem = pl.BlockSpec(memory_space=pltpu.VMEM)
    rows = proj.shape[0] // 32
    width = proj.shape[1] + small.shape[1]
    return pl.pallas_call(
        sums_kernel,
        out_shape=(
            *(jax.ShapeDtypeStruct((rows, size), jnp.float32) for size in widths),
            jax.ShapeDtypeStruct((rows, small.shape[1]), jnp.float32),
            jax.ShapeDtypeStruct((rows, out.shape[1]), jnp.float32),
        ),
        in_specs=[anywhere] * 3,
        out_specs=(vmem,) * (2 + len(widths)),
        scratch_shapes=[
            dma((6,)),
            *ring_scratch_dp_early(rows, width),
            *ring_scratch(rows, out.shape[1]),
        ],
        compiler_params=pltpu.CompilerParams(
            collective_id=2, has_side_effects=True, vmem_limit_bytes=56 * 2**20
        ),
        cost_estimate=pl.CostEstimate(flops=1 << 20, bytes_accessed=1 << 16, transcendentals=0),
        name="sum_gradients",
    )(by_device(proj), by_device(small), by_device(out))


def fill_bias(length_ref, bias, ctx):
    blocks, keys, queries = bias.shape
    row = lax.broadcasted_iota(jnp.int32, (keys, queries), 0)
    column = lax.broadcasted_iota(jnp.int32, (keys, queries), 1) + ctx * queries
    for j in range(blocks):
        key = row + j * keys
        allowed = jnp.logical_and(key <= column, key < length_ref[0])
        bias[j] = jnp.where(allowed, 0.0, floor_score)


def head_probs(query, keys, bias):
    scores = [contract_rows(key, query) + bias[j] for j, key in enumerate(keys)]
    peak = jnp.max(scores[0], axis=0, keepdims=True)
    for score in scores[1:]:
        peak = jnp.maximum(peak, jnp.max(score, axis=0, keepdims=True))
    raised = [jnp.exp(score - peak) for score in scores]
    total = jnp.sum(raised[0], axis=0, keepdims=True)
    for value in raised[1:]:
        total = total + jnp.sum(value, axis=0, keepdims=True)
    inverse = 1.0 / total
    return [value * inverse for value in raised]


def attend_kernel(
    query_ref,
    own_ref,
    length_ref,
    mixed_ref,
    all_ref,
    pairs,
    bias,
    first,
    stats,
    local_sem,
    send_sem,
    recv_sem,
):
    bfloat = jnp.bfloat16
    y, c, _, _, device, _ = place()
    mine = y * 2 + c
    own = pltpu.make_async_copy(own_ref, pairs.at[mine], local_sem)
    own.start()
    barrier = pltpu.get_barrier_semaphore()
    for kind in (ACROSS, CORE):
        pl.semaphore_signal(barrier, inc=1, device_id=device(kind), device_id_type=MESH_ID)
    pl.semaphore_wait(barrier, 2)
    own.wait()

    def send(kind, slot, index):
        return pltpu.make_async_remote_copy(
            src_ref=pairs.at[slot],
            dst_ref=pairs.at[slot],
            send_sem=send_sem.at[index],
            recv_sem=recv_sem.at[slot],
            device_id=device(kind),
            device_id_type=MESH_ID,
        )

    far = (1 - y) * 2 + c
    across = send(ACROSS, mine, 0)
    core = send(CORE, mine, 1)
    onward = send(CORE, far, 2)
    across.start()
    core.start()
    fill_bias(length_ref, bias, mine)
    half = pairs.shape[1] // 2
    ratio = query_ref.shape[0] // half
    groups = half // HEAD_SIZE

    def pass_over(blocks, g, merge):
        rows = pl.ds(pl.multiple_of(g * HEAD_SIZE, HEAD_SIZE), HEAD_SIZE)
        low = pl.ds(pl.multiple_of(half + g * HEAD_SIZE, HEAD_SIZE), HEAD_SIZE)
        keys = [pairs[j, rows, :] for j in blocks]
        values = [pairs[j, low, :] for j in blocks]
        for r in range(ratio):
            h = g * ratio + r
            head = pl.ds(pl.multiple_of(h * HEAD_SIZE, HEAD_SIZE), HEAD_SIZE)
            query = query_ref[head, :]
            scores = [contract_rows(key, query) + bias[j] for key, j in zip(keys, blocks)]
            peak = jnp.maximum(
                jnp.max(scores[0], axis=0, keepdims=True), jnp.max(scores[1], axis=0, keepdims=True)
            )
            if merge:
                before = stats[h, 0:1, :]
                peak = jnp.maximum(peak, before)
            raised = [jnp.exp(score - peak) for score in scores]
            total = jnp.sum(raised[0] + raised[1], axis=0, keepdims=True)
            sums = matmul(values[0], raised[0].astype(bfloat)) + matmul(
                values[1], raised[1].astype(bfloat)
            )
            if merge:
                shrink = jnp.exp(before - peak)
                total = total + stats[h, 1:2, :] * shrink
                mixed_ref[head, :] = ((sums + first[head, :] * shrink) / total).astype(bfloat)
            else:
                first[head, :] = sums
                stats[h, 0:1, :] = peak
                stats[h, 1:2, :] = total

    send(CORE, y * 2 + 1 - c, 1).wait_recv()

    @pl.loop(0, groups)
    def _(g):
        pass_over((mine, y * 2 + 1 - c), g, False)

    send(ACROSS, far, 0).wait_recv()
    onward.start()
    send(CORE, (1 - y) * 2 + 1 - c, 2).wait_recv()
    result = pltpu.make_async_copy(pairs, all_ref, local_sem)
    result.start()

    @pl.loop(0, groups)
    def _(g):
        pass_over((far, (1 - y) * 2 + 1 - c), g, True)

    for copy in (across, core, onward):
        copy.wait_send()
    result.wait()


def attend(query, own_pairs, lengths):
    bfloat = jnp.bfloat16
    single = jnp.float32
    dma = pltpu.SemaphoreType.DMA
    anywhere = pl.BlockSpec(memory_space=pl.ANY)
    vmem = pl.BlockSpec(memory_space=pltpu.VMEM)
    pairs = (4, *own_pairs.shape)
    keys = own_pairs.shape[1]
    return pl.pallas_call(
        attend_kernel,
        out_shape=(
            jax.ShapeDtypeStruct(query.shape, bfloat),
            jax.ShapeDtypeStruct(pairs, bfloat),
        ),
        in_specs=[vmem, anywhere, pl.BlockSpec(memory_space=pltpu.SMEM)],
        out_specs=(vmem, anywhere),
        scratch_shapes=[
            pltpu.VMEM(pairs, bfloat),
            pltpu.VMEM((4, keys, query.shape[1]), single),
            pltpu.VMEM(query.shape, single),
            pltpu.VMEM((query.shape[0] // HEAD_SIZE, 8, query.shape[1]), single),
            dma,
            dma((3,)),
            dma((4,)),
        ],
        compiler_params=pltpu.CompilerParams(
            collective_id=3, has_side_effects=True, vmem_limit_bytes=48 * 2**20
        ),
        name="attend",
    )(query, own_pairs, lengths)


def turn_back(gradient, cosine, sine):
    first, second = gradient[: HEAD_SIZE // 2], gradient[HEAD_SIZE // 2 :]
    return jnp.concatenate(
        [first * cosine + second * sine, second * cosine - first * sine], axis=0
    ).astype(jnp.bfloat16)


def attend_back_kernel(
    query_ref,
    pairs_ref,
    grad_ref,
    length_ref,
    cosine_ref,
    sine_ref,
    proj_out,
    parts,
    core_got,
    y_got,
    bias,
    core_send,
    core_recv,
    y_send,
    y_recv,
):
    bfloat = jnp.bfloat16
    single = jnp.float32
    y, c, _, _, device, _ = place()
    mine = y * 2 + c
    barrier = pltpu.get_barrier_semaphore()
    for kind in (ACROSS, CORE):
        pl.semaphore_signal(barrier, inc=1, device_id=device(kind), device_id_type=MESH_ID)
    pl.semaphore_wait(barrier, 2)
    fill_bias(length_ref, bias, mine)
    blocks = pairs_ref.shape[0]
    half = pairs_ref.shape[1] // 2
    ratio = query_ref.shape[0] // half
    groups = half // HEAD_SIZE
    turns = parts.shape[1]
    per_turn = groups // turns
    quarter = half // turns

    def to_core(yy, turn):
        return pltpu.make_async_remote_copy(
            src_ref=parts.at[yy * 2 + 1 - c, turn],
            dst_ref=core_got.at[turn, yy],
            send_sem=core_send.at[turn, yy],
            recv_sem=core_recv.at[turn, yy],
            device_id=device(CORE),
            device_id_type=MESH_ID,
        )

    def to_across(turn):
        return pltpu.make_async_remote_copy(
            src_ref=parts.at[(1 - y) * 2 + c, turn],
            dst_ref=y_got.at[turn],
            send_sem=y_send.at[turn],
            recv_sem=y_recv.at[turn],
            device_id=device(ACROSS),
            device_id_type=MESH_ID,
        )

    def core_stage(turn):
        to_core(1 - y, turn).start()
        to_core(y, turn).start()

    def across_stage(turn):
        to_core(1 - y, turn).wait_recv()
        slot = (1 - y) * 2 + c
        parts[slot, turn] = (
            parts[slot, turn].astype(single) + core_got[turn, 1 - y].astype(single)
        ).astype(bfloat)
        to_across(turn).start()

    def last_stage(turn):
        to_core(y, turn).wait_recv()
        to_across(turn).wait_recv()
        total = (
            parts[mine, turn].astype(single)
            + core_got[turn, y].astype(single)
            + y_got[turn].astype(single)
        )
        at = query_ref.shape[0] + turn * quarter
        for h in range(per_turn):
            rows = slice(h * HEAD_SIZE, (h + 1) * HEAD_SIZE)
            proj_out[pl.ds(at + h * HEAD_SIZE, HEAD_SIZE), :] = turn_back(
                total[rows], cosine_ref[...], sine_ref[...]
            )
        proj_out[pl.ds(at + half, quarter), :] = total[quarter:].astype(bfloat)

    def group(g, carry):
        rows = pl.ds(pl.multiple_of(g * HEAD_SIZE, HEAD_SIZE), HEAD_SIZE)
        low = pl.ds(pl.multiple_of(half + g * HEAD_SIZE, HEAD_SIZE), HEAD_SIZE)
        keys = [pairs_ref[j, rows, :] for j in range(blocks)]
        values = [pairs_ref[j, low, :] for j in range(blocks)]
        grad_keys = [None] * blocks
        grad_values = [None] * blocks
        for r in range(ratio):
            head = pl.ds(pl.multiple_of((g * ratio + r) * HEAD_SIZE, HEAD_SIZE), HEAD_SIZE)
            query = query_ref[head, :]
            grad = grad_ref[head, :]
            probs = head_probs(query, keys, bias)
            grad_probs = [contract_rows(value, grad) for value in values]
            delta = jnp.sum(probs[0] * grad_probs[0], axis=0, keepdims=True)
            for j in range(1, blocks):
                delta = delta + jnp.sum(probs[j] * grad_probs[j], axis=0, keepdims=True)
            grad_query = None
            for j in range(blocks):
                low_probs = probs[j].astype(bfloat)
                grad_score = (probs[j] * (grad_probs[j] - delta)).astype(bfloat)
                terms = (
                    matmul(keys[j], grad_score),
                    contract_last(query, grad_score),
                    contract_last(grad, low_probs),
                )
                grad_query = terms[0] if j == 0 else grad_query + terms[0]
                grad_keys[j] = terms[1] if r == 0 else grad_keys[j] + terms[1]
                grad_values[j] = terms[2] if r == 0 else grad_values[j] + terms[2]
            proj_out[head, :] = turn_back(
                grad_query * HEAD_SIZE ** (-0.5), cosine_ref[...], sine_ref[...]
            )
        turn = g // per_turn
        at = pl.multiple_of((g % per_turn) * HEAD_SIZE, HEAD_SIZE)
        for j in range(blocks):
            parts[j, turn, pl.ds(at, HEAD_SIZE), :] = grad_keys[j].astype(bfloat)
            parts[j, turn, pl.ds(quarter + at, HEAD_SIZE), :] = grad_values[j].astype(bfloat)
        for index in range(turns - 1):

            @pl.when(g == (index + 1) * per_turn - 1)
            def _():
                core_stage(index)

            @pl.when(g == (index + 1) * per_turn)
            def _():
                across_stage(index)

        return carry

    lax.fori_loop(0, groups, group, 0)
    core_stage(turns - 1)
    across_stage(turns - 1)
    for turn in range(turns):
        last_stage(turn)
    for turn in range(turns):
        to_core(y, turn).wait_send()
        to_core(1 - y, turn).wait_send()
        to_across(turn).wait_send()


def attend_back(query, pairs, grad, lengths, cosine, sine):
    bfloat = jnp.bfloat16
    single = jnp.float32
    dma = pltpu.SemaphoreType.DMA
    anywhere = pl.BlockSpec(memory_space=pl.ANY)
    vmem = pl.BlockSpec(memory_space=pltpu.VMEM)
    blocks, rows, keys = pairs.shape
    turns = 4
    part = (turns, rows // turns, keys)
    return pl.pallas_call(
        attend_back_kernel,
        out_shape=jax.ShapeDtypeStruct((query.shape[0] + rows, query.shape[1]), bfloat),
        in_specs=[vmem, vmem, vmem, pl.BlockSpec(memory_space=pltpu.SMEM), vmem, vmem],
        out_specs=vmem,
        scratch_shapes=[
            pltpu.VMEM((blocks, *part), bfloat),
            pltpu.VMEM((turns, 2, *part[1:]), bfloat),
            pltpu.VMEM(part, bfloat),
            pltpu.VMEM((blocks, keys, query.shape[1]), single),
            dma((turns, 2)),
            dma((turns, 2)),
            dma((turns,)),
            dma((turns,)),
        ],
        compiler_params=pltpu.CompilerParams(
            collective_id=4, has_side_effects=True, vmem_limit_bytes=48 * 2**20
        ),
        cost_estimate=pl.CostEstimate(flops=1 << 20, bytes_accessed=1 << 16, transcendentals=0),
        name="attend_back",
    )(query, pairs, grad, lengths, cosine, sine)


def experts_kernel(
    swap,
    hidden_ref,
    final_ref,
    routes_ref,
    router_ref,
    gate_hbm,
    up_hbm,
    down_hbm,
    back_ref,
    part_ref,
    score_got,
    grad_gate_ref,
    grad_up_ref,
    grad_down_ref,
    *refs,
):
    if swap:
        gate_got, up_got, leaving, *refs = refs
        swap = (gate_got, up_got, leaving)
    experts_steps(
        swap,
        hidden_ref,
        final_ref,
        routes_ref,
        router_ref,
        gate_hbm,
        up_hbm,
        down_hbm,
        back_ref,
        part_ref,
        score_got,
        grad_gate_ref,
        grad_up_ref,
        grad_down_ref,
        *refs,
    )


def experts_steps(
    swap,
    hidden_ref,
    final_ref,
    routes_ref,
    router_ref,
    gate_hbm,
    up_hbm,
    down_hbm,
    back_ref,
    part_ref,
    score_got,
    grad_gate_ref,
    grad_up_ref,
    grad_down_ref,
    held,
    w_gate,
    w_up,
    w_down,
    rows_in,
    rows_grad,
    slope_gate,
    slope_up,
    hidden_e,
    picks,
    row_gates,
    work,
    pool,
    before,
    gather_send,
    gather_recv,
    local_sem,
    load_sem,
    part_sem,
    sum_send,
    core_recv,
    y_recv,
    z_recv,
    ready,
    score_ref,
    score_send,
    score_recv,
    swap_send,
    swap_recv,
):
    single = jnp.float32
    bfloat = jnp.bfloat16
    tokens_block = hidden_ref.shape[0]
    width = hidden_ref.shape[1]
    experts = router_ref.shape[0]
    local_exp = w_gate.shape[0]
    hidden_units = w_gate.shape[2]
    capacity = picks.shape[1] // local_exp
    group_rows = 4 * capacity
    ctx = lax.axis_index("context")
    y, c, z, inner, device, per_side = place()

    weights = (
        pltpu.make_async_copy(gate_hbm, w_gate, load_sem.at[0]),
        pltpu.make_async_copy(up_hbm, w_up, load_sem.at[1]),
        pltpu.make_async_copy(down_hbm, w_down, load_sem.at[2]),
    )
    mine = block_id(y, c, z)
    own = pltpu.make_async_copy(hidden_ref, held.at[mine], local_sem)
    own.start()
    for copy in weights:
        copy.start()

    barrier = pltpu.get_barrier_semaphore()

    def member_device(block):
        return {"context": block // 4, "expert": block % 4}

    @pl.loop(1, 16)
    def _(shift):
        pl.semaphore_signal(
            barrier,
            inc=1,
            device_id=member_device((mine + shift) % 16),
            device_id_type=MESH_ID,
        )

    if swap:
        pl.semaphore_signal(barrier, inc=1, device_id=device(DP), device_id_type=MESH_ID)
    pl.semaphore_wait(barrier, 16 if swap else 15)
    own.wait()

    def spread(kind, block):
        return pltpu.make_async_remote_copy(
            src_ref=held.at[block],
            dst_ref=held.at[block],
            send_sem=gather_send.at[kind, block],
            recv_sem=gather_recv.at[block],
            device_id=device(kind),
            device_id_type=MESH_ID,
        )

    def along(kind, zz):
        if kind == UP:
            return jnp.logical_and(z < 3, zz <= z)
        return jnp.logical_and(z > 0, zz >= z)

    def send_on(zz):
        block = block_id(y, c, zz)
        for kind in (UP, DOWN):

            @pl.when(along(kind, zz))
            def _():
                spread(kind, block).start()

        spread(ACROSS, block).start()
        spread(CORE, block).start()

    def forward(step):
        zz = line_order(z, step)
        spread(ACROSS, block_id(y, c, zz)).wait_recv()
        send_on(zz)

    send_on(z)
    row = lax.broadcasted_iota(jnp.int32, (tokens_block, tokens_block), 0)
    column = lax.broadcasted_iota(jnp.int32, (tokens_block, tokens_block), 1)
    before[...] = jnp.where(row < column, 1.0, 0.0).astype(bfloat)
    for copy in weights:
        copy.wait()
    first = (ctx * 4 + z) * local_exp

    def member(zz, p):
        yy = y + (p // 2) * (1 - 2 * y)
        cc = c + (p % 2) * (1 - 2 * c)
        return block_id(yy, cc, zz)

    def load_final(zz, p):
        return pltpu.make_async_copy(final_ref.at[member(zz, p)], pool.at[p], load_sem.at[p])

    def store_part(zz, p):
        return pltpu.make_async_copy(
            pool.at[4 + p % 2], part_ref.at[member(zz, p)], part_sem.at[p % 2]
        )

    def forward_group(step, carry):
        zz = line_order(z, step)
        after = step + 1 + inner * jnp.minimum(step, 1)

        @pl.when(after < 4)
        def _():
            forward(after)

        @pl.when(jnp.logical_and(step == 0, inner == 1))
        def _():
            forward(2)

        @pl.loop(0, 4)
        def _(p):
            load_final(zz, p).start()

        spread(CORE, block_id(y, 1 - c, zz)).wait_recv()
        spread(CORE, block_id(1 - y, c, zz)).wait_recv()
        spread(CORE, block_id(1 - y, c, zz)).start()
        spread(CORE, block_id(1 - y, 1 - c, zz)).wait_recv()

        @pl.loop(0, 4)
        def _(p):
            block = member(zz, p)
            tokens_in = held[block]
            logits = contract_last(router_ref[...], tokens_in)
            expert_row = lax.broadcasted_iota(jnp.int32, (experts, tokens_block), 0)
            routed = jnp.zeros((experts, tokens_block), single)
            for k in range(routes_ref.shape[1]):
                routed = routed + jnp.where(routes_ref[block, k : k + 1, :] == expert_row, 1.0, 0.0)
            named = routed > 0.5
            peak = jnp.max(jnp.where(named, logits, floor_score), axis=0, keepdims=True)
            raised = jnp.where(named, jnp.exp(jnp.minimum(logits - peak, 0.0)), 0.0)
            gates = raised / jnp.sum(raised, axis=0, keepdims=True)
            eight = lax.broadcasted_iota(jnp.int32, (8, tokens_block), 0)
            masks = jnp.zeros((8, tokens_block), single)
            own_mask = []
            own_gate = []
            for j in range(local_exp):
                here = expert_row == first + j
                own_mask.append(jnp.sum(jnp.where(here, routed, 0.0), axis=0, keepdims=True))
                own_gate.append(jnp.sum(jnp.where(here, gates, 0.0), axis=0, keepdims=True))
                masks = masks + jnp.where(eight == j, own_mask[j], 0.0)
            rank = matmul(masks.astype(bfloat), before[...])
            slot = lax.broadcasted_iota(jnp.int32, (capacity, tokens_block), 0).astype(single)
            for j in range(local_exp):
                hit = jnp.logical_and(slot == rank[j : j + 1, :], own_mask[j] > 0.5)
                pick = jnp.where(hit, 1.0, 0.0)
                picks[step * 4 + p, pl.ds(j * capacity, capacity), :] = pick.astype(bfloat)
                gate_column = jnp.sum(pick * own_gate[j], axis=1, keepdims=True)
                row_gates[p, pl.ds(j * capacity, capacity), :] = jnp.broadcast_to(
                    gate_column, (capacity, 128)
                )
            at = pl.multiple_of(step * group_rows + p * capacity, 32)
            for n in range(width // CHUNK):
                part = pl.ds(n * CHUNK, CHUNK)
                got = matmul(picks[step * 4 + p], held[block, :, part]).astype(bfloat)
                for j in range(local_exp):
                    rows_in[j, pl.ds(at, capacity), part] = got[j * capacity : (j + 1) * capacity]

        base = pl.multiple_of(step * group_rows, 128)
        for j in range(local_exp):
            given = rows_in[j, pl.ds(base, group_rows), :]
            for n in range(hidden_units // HALF):
                part = pl.ds(n * HALF, HALF)
                gate_pre = matmul(given, w_gate[j, :, part])
                up_pre = matmul(given, w_up[j, :, part])
                sigmoid = 1.0 / (1.0 + jnp.exp(-gate_pre))
                silu = gate_pre * sigmoid
                hidden_e[j, pl.ds(base, group_rows), part] = (silu * up_pre).astype(bfloat)
                slope_gate[j, pl.ds(base, group_rows), part] = (
                    up_pre * sigmoid * (1.0 + gate_pre * (1.0 - sigmoid))
                ).astype(bfloat)
                slope_up[j, pl.ds(base, group_rows), part] = silu.astype(bfloat)
            for n in range(width // CHUNK):
                part = pl.ds(n * CHUNK, CHUNK)
                work[j, :, part] = matmul(
                    hidden_e[j, pl.ds(base, group_rows), :], w_down[j, :, part]
                ).astype(bfloat)

        @pl.loop(0, 4)
        def _(p):
            block = member(zz, p)
            at = pl.multiple_of(step * group_rows + p * capacity, 32)
            local = pl.multiple_of(p * capacity, 32)
            pick = picks[step * 4 + p]
            weight = row_gates[p][:, 0:1]
            weighted = (pick.astype(single) * weight).astype(bfloat)
            load_final(zz, p).wait()

            @pl.when(jnp.logical_or(step > 0, p > 1))
            def _():
                store_part(zz, p).wait()

            row_score = jnp.zeros((local_exp * capacity, 1), single)
            for n in range(width // CHUNK):
                part = pl.ds(n * CHUNK, CHUNK)
                out = jnp.concatenate(
                    [work[j, pl.ds(local, capacity), part] for j in range(local_exp)], axis=0
                )
                pool[4 + p % 2, :, part] = contract_rows(weighted, out).astype(bfloat)
                final = matmul(pick, pool[p, :, part])
                row_score = row_score + jnp.sum(final * out.astype(single), axis=1, keepdims=True)
                graded = (final * weight).astype(bfloat)
                for j in range(local_exp):
                    rows_grad[j, pl.ds(at, capacity), part] = graded[j * capacity : (j + 1) * capacity]
            store_part(zz, p).start()
            spread_score = pick.astype(single) * row_score
            eight = lax.broadcasted_iota(jnp.int32, (8, tokens_block), 0)
            scores = jnp.zeros((8, tokens_block), single)
            for j in range(local_exp):
                total = jnp.sum(spread_score[j * capacity : (j + 1) * capacity], axis=0, keepdims=True)
                scores = scores + jnp.where(eight == j, total, 0.0)
            score_ref[block] = scores

        return carry

    lax.fori_loop(0, 4, forward_group, 0)

    def score_copy(block, source):
        return pltpu.make_async_remote_copy(
            src_ref=score_ref.at[block],
            dst_ref=score_got.at[source],
            send_sem=score_send.at[block],
            recv_sem=score_recv.at[source],
            device_id=member_device(block),
            device_id_type=MESH_ID,
        )

    @pl.loop(1, 16)
    def _(shift):
        score_copy((mine + shift) % 16, mine).start()

    score_got[mine] = score_ref[mine]

    @pl.loop(2, 4)
    def _(p):
        store_part(line_order(z, 3), p).wait()

    @pl.loop(0, 4)
    def _(zz):
        block = block_id(y, c, zz)
        for kind in (UP, DOWN):

            @pl.when(along(kind, zz))
            def _():
                spread(kind, block).wait_send()

        spread(ACROSS, block).wait_send()
        spread(CORE, block).wait_send()
        spread(CORE, block_id(1 - y, c, zz)).wait_send()

    opposite = {UP: DOWN, DOWN: UP, ACROSS: ACROSS, CORE: CORE}
    per_side(
        lambda kind: pl.semaphore_signal(
            ready.at[opposite[kind]], inc=1, device_id=device(kind), device_id_type=MESH_ID
        )
    )

    def sum_copy(kind, source, target, send_index, recv_sem):
        return pltpu.make_async_remote_copy(
            src_ref=source,
            dst_ref=target,
            send_sem=sum_send.at[send_index],
            recv_sem=recv_sem,
            device_id=device(kind),
            device_id_type=MESH_ID,
        )

    def to_core(turn, p, zz):
        slot = (y + p * (1 - 2 * y)) * 4 + zz
        index = turn * 2 + p
        return sum_copy(CORE, pool.at[index], held.at[slot], index, core_recv.at[slot])

    def from_core(slot):
        return sum_copy(CORE, pool.at[0], held.at[slot], 0, core_recv.at[slot])

    def to_across(zz):
        return sum_copy(ACROSS, held.at[(1 - y) * 4 + zz], held.at[8 + zz], 4 + zz, y_recv.at[zz])

    def to_line(kind, zz, last):
        return sum_copy(
            kind,
            held.at[y * 4 + zz],
            pool.at[5] if last else held.at[12 + zz],
            8 + zz,
            z_recv.at[4 if last else zz],
        )

    def add_up(slot, *others):
        @pl.loop(0, tokens_block // 64)
        def _(r):
            rows = pl.ds(pl.multiple_of(r * 64, 64), 64)
            total = held[slot, rows, :].astype(single)
            for ref, index in others:
                total = total + ref[index, rows, :].astype(single)
            held[slot, rows, :] = total.astype(bfloat)

    def back_block(step, p, target, index, onto):
        local = pl.multiple_of(p * capacity, 32)
        pick = picks[step * 4 + p]
        for n in range(width // CHUNK):
            part = pl.ds(n * CHUNK, CHUNK)
            grads = jnp.concatenate(
                [work[j, pl.ds(local, capacity), part] for j in range(local_exp)], axis=0
            )
            block = contract_rows(pick, grads)
            if onto:
                block = block + target[index, :, part].astype(single)
            target[index, :, part] = block.astype(bfloat)

    def line_sum(step):
        zz = line_order(z, step)
        slot = y * 4 + zz
        to_across(zz).wait_recv()
        rising = zz > z
        comes = jnp.logical_or(jnp.logical_and(rising, z > 0), jnp.logical_and(zz < z, z < 3))

        @pl.when(comes)
        def _():
            to_line(CORE, zz, False).wait_recv()
            add_up(slot, (held, 8 + zz), (held, 12 + zz))

        @pl.when(jnp.logical_not(comes))
        def _():
            add_up(slot, (held, 8 + zz))

        @pl.when(rising)
        def _():
            to_line(UP, zz, False).start()

        @pl.when(zz == z - 1)
        def _():
            to_line(DOWN, zz, True).start()

        @pl.when(zz < z - 1)
        def _():
            to_line(DOWN, zz, False).start()

    def at_end(action):
        pl.when(inner == 0)(action)

    def at_middle(action):
        pl.when(inner == 1)(action)

    def backward_group(turn_step, carry):
        step = 3 - turn_step
        zz = line_order(z, step)
        turn = step % 2
        base = pl.multiple_of(step * group_rows, 128)
        for j in range(local_exp):
            for n in range(hidden_units // HALF):
                part = pl.ds(n * HALF, HALF)
                grad_hidden = (
                    contract_last(rows_grad[j, pl.ds(base, group_rows), :], w_down[j, part, :])
                    .astype(bfloat)
                    .astype(single)
                )
                slope_gate[j, pl.ds(base, group_rows), part] = (
                    grad_hidden * slope_gate[j, pl.ds(base, group_rows), part].astype(single)
                ).astype(bfloat)
                slope_up[j, pl.ds(base, group_rows), part] = (
                    grad_hidden * slope_up[j, pl.ds(base, group_rows), part].astype(single)
                ).astype(bfloat)
            for n in range(width // CHUNK):
                part = pl.ds(n * CHUNK, CHUNK)
                work[j, :, part] = (
                    contract_last(slope_gate[j, pl.ds(base, group_rows), :], w_gate[j, part, :])
                    + contract_last(slope_up[j, pl.ds(base, group_rows), :], w_up[j, part, :])
                ).astype(bfloat)

        @pl.when(turn_step == 0)
        def _():
            per_side(lambda kind: pl.semaphore_wait(ready.at[kind], 1))

        for p, member_p in ((1, 3), (0, 1)):

            @pl.when(turn_step > 1)
            def _():
                to_core(turn, p, zz).wait_send()

            back_block(step, member_p, pool, turn * 2 + p, False)
            to_core(turn, p, zz).start()

        other = (1 - y) * 4 + zz
        from_core(other).wait_recv()
        back_block(step, 2, held, other, True)
        to_across(zz).start()
        slot = y * 4 + zz
        from_core(slot).wait_recv()
        back_block(step, 0, held, slot, True)

        @pl.when(turn_step == 2)
        def _():
            at_end(lambda: line_sum(3))

        return carry

    lax.fori_loop(0, 4, backward_group, 0)
    at_middle(lambda: line_sum(3))
    at_end(lambda: line_sum(2))

    def stores(j):
        pairs = ((w_gate, grad_gate_ref), (w_up, grad_up_ref), (w_down, grad_down_ref))
        if not swap:
            return [
                pltpu.make_async_copy(source.at[j], target.at[j], load_sem.at[3 * j + i])
                for i, (source, target) in enumerate(pairs)
            ]
        d = lax.axis_index("dp")
        copies = []
        for i, (source, target) in enumerate(pairs):
            size = target.shape[1]
            here = pl.ds(pl.multiple_of(d * size, 128), size)
            copies.append(
                pltpu.make_async_copy(source.at[j, here, :], target.at[j], load_sem.at[3 * j + i])
            )
        there = lambda size: pl.ds(pl.multiple_of((1 - d) * size, 128), size)
        low = w_down.shape[1] // 2
        leaving = [
            (
                w_down.at[j, there(low), pl.ds(n * hidden_units, hidden_units)],
                swap[2].at[2 + j, pl.ds(n * low, low), :],
            )
            for n in range(width // hidden_units)
        ]
        if j == 1:
            leaving += [
                (source.at[1, there(width // 2), :], swap[2].at[i])
                for i, source in enumerate((w_gate, w_up))
            ]
        for i, (source, target) in enumerate(leaving):
            copies.append(pltpu.make_async_copy(source, target, load_sem.at[6 + 3 * j + i]))
        return copies

    def weight_grads(j):
        @pl.loop(0, width // CHUNK)
        def _(n):
            part = pl.ds(pl.multiple_of(n * CHUNK, CHUNK), CHUNK)
            w_gate[j, part, :] = contract_rows(rows_in[j, :, part], slope_gate[j]).astype(bfloat)
            w_up[j, part, :] = contract_rows(rows_in[j, :, part], slope_up[j]).astype(bfloat)
            w_down[j, :, part] = contract_rows(hidden_e[j], rows_grad[j, :, part]).astype(bfloat)

        for copy in stores(j):
            copy.start()

    weight_grads(0)
    swaps = []
    if swap:
        swaps = swap_copies(
            ((w_gate, 0, swap[0]), (w_up, 0, swap[1])), device, swap_send, swap_recv
        )
        for copy in swaps:
            copy.start()
    weight_grads(1)
    at_middle(lambda: line_sum(2))
    line_sum(1)
    slot = y * 4 + z
    to_across(z).wait_recv()
    add_up(slot, (held, 8 + z))

    @pl.when(z > 0)
    def _():
        to_line(CORE, z, False).wait_recv()
        add_up(slot, (held, 12 + z))

    @pl.when(z < 3)
    def _():
        to_line(CORE, z, True).wait_recv()
        add_up(slot, (pool, 5))

    result = pltpu.make_async_copy(held.at[slot], back_ref, local_sem)
    result.start()
    for j in range(local_exp):
        for copy in stores(j):
            copy.wait()
    for turn in range(2):
        for p in range(2):
            to_core(turn, p, z).wait_send()

    @pl.loop(0, 4)
    def _(zz):
        to_across(zz).wait_send()

        @pl.when(zz != z)
        def _():
            to_line(CORE, zz, False).wait_send()

    @pl.loop(1, 16)
    def _(shift):
        other = (mine + shift) % 16
        score_copy(other, mine).wait_send()
        score_copy(other, other).wait_recv()

    for copy in swaps:
        copy.wait()
    result.wait()


def experts_on_owner(
    hidden, final_all, routes_all, router_rows, w_gate, w_up, w_down, capacity, swap
):
    blocks = final_all.shape[0]
    tokens_block, width = hidden.shape
    local_exp, _, units = w_gate.shape
    bfloat = jnp.bfloat16
    single = jnp.float32
    rows = blocks * capacity
    grads = [x.shape for x in (w_gate, w_up, w_down)]
    if swap:
        wide, low = (width // 2, units), (units // 2, width)
        grads = [(2, *wide), (2, *wide), (2, *low), wide, wide, (4, *wide)]
    anywhere = pl.BlockSpec(memory_space=pl.ANY)
    vmem = pl.BlockSpec(memory_space=pltpu.VMEM)
    dma = pltpu.SemaphoreType.DMA
    return pl.pallas_call(
        functools.partial(experts_kernel, swap),
        out_shape=(
            jax.ShapeDtypeStruct((tokens_block, width), bfloat),
            jax.ShapeDtypeStruct((blocks, tokens_block, width), bfloat),
            jax.ShapeDtypeStruct((blocks, 8, tokens_block), single),
            *(jax.ShapeDtypeStruct(shape, bfloat) for shape in grads),
        ),
        in_specs=[anywhere, anywhere, vmem, vmem, anywhere, anywhere, anywhere],
        out_specs=(anywhere, anywhere, vmem, *([anywhere] * len(grads))),
        scratch_shapes=[
            pltpu.VMEM((blocks, tokens_block, width), bfloat),
            pltpu.VMEM(w_gate.shape, bfloat),
            pltpu.VMEM(w_up.shape, bfloat),
            pltpu.VMEM(w_down.shape, bfloat),
            pltpu.VMEM((local_exp, rows, width), bfloat),
            pltpu.VMEM((local_exp, rows, width), bfloat),
            pltpu.VMEM((local_exp, rows, units), bfloat),
            pltpu.VMEM((local_exp, rows, units), bfloat),
            pltpu.VMEM((local_exp, rows, units), bfloat),
            pltpu.VMEM((blocks, local_exp * capacity, tokens_block), bfloat),
            pltpu.VMEM((4, local_exp * capacity, 128), single),
            pltpu.VMEM((local_exp, 4 * capacity, width), bfloat),
            pltpu.VMEM((6, tokens_block, width), bfloat),
            pltpu.VMEM((tokens_block, tokens_block), bfloat),
            dma((4, blocks)),
            dma((blocks,)),
            dma,
            dma((14,)),
            dma((2,)),
            dma((12,)),
            dma((8,)),
            dma((4,)),
            dma((5,)),
            pltpu.SemaphoreType.REGULAR((4,)),
            pltpu.VMEM((blocks, 8, tokens_block), single),
            dma((16,)),
            dma((16,)),
            dma((2,)),
            dma((2,)),
        ],
        compiler_params=pltpu.CompilerParams(
            collective_id=1, has_side_effects=True, vmem_limit_bytes=63 * 2**20
        ),
        name="experts",
    )(hidden, final_all, routes_all, router_rows, w_gate, w_up, w_down)


def on_device(
    tokens,
    lengths,
    routes,
    gain_attn,
    w_query,
    key_weight,
    value_weight,
    w_out,
    gain_ffn,
    w_router,
    w_gate,
    w_up,
    w_down,
    cotangent,
):
    tokens_own = tokens.shape[1]
    exp_count = lax.axis_size("expert")
    ctx_count = lax.axis_size("context")
    local_exp = w_gate.shape[0]
    experts = local_exp * ctx_count * exp_count
    capacity = tokens_own * TOP * 3 // (2 * experts)
    bfloat = jnp.bfloat16
    single = jnp.float32
    query_width = w_query.shape[1]
    key_width = key_weight.shape[1]
    proj_width = query_width + 2 * key_width
    own_rows = w_query.shape[0]
    pair = lax.axis_size("dp") == 2
    small = jnp.concatenate(
        [
            w_router,
            gain_attn[:, None],
            gain_ffn[:, None],
            jnp.zeros((own_rows, 64 - experts - 2), bfloat),
        ],
        axis=1,
    )
    if pair:
        packed = routes[0].T.reshape(-1, 64).astype(bfloat)
        packed = jnp.pad(packed, ((0, own_rows - packed.shape[0]), (0, 0)))
        early, small_all, out_w = gather_weights(
            w_query, key_weight, value_weight, jnp.concatenate([small, packed], axis=1), w_out
        )
        out_w = out_w.reshape(-1, out_w.shape[2])
        routes_all = lax.dynamic_slice(
            small_all, (lax.axis_index("dp") * 16, 0, 64), (16, tokens_own * TOP // 64, 64)
        )
        routes_all = routes_all.astype(jnp.int32).reshape(16, TOP, tokens_own)
        proj_w = early.reshape(-1, proj_width)
        small_all = small_all.reshape(-1, small_all.shape[2])
    else:
        proj_w = jnp.concatenate([w_query, key_weight, value_weight], axis=1)
        proj_w = lax.all_gather(proj_w, EVERY, axis=0, tiled=True)
        small_all = lax.all_gather(small, EVERY, axis=0, tiled=True)
        out_w = lax.all_gather(w_out, EVERY, axis=0, tiled=True)
        routes_all = lax.all_gather(routes[0].T, GROUP, axis=0, tiled=False)
    positions = lax.axis_index("context") * tokens_own + jnp.arange(tokens_own, dtype=jnp.int32)
    valid = (positions < lengths[0]).astype(single)[:, None]
    grad_final = cotangent[0].astype(single) * valid
    final_all = lax.all_gather(grad_final.astype(bfloat), GROUP, axis=0, tiled=False)
    router_w = small_all[:, :experts]
    gain_one = small_all[:, experts].astype(single)
    gain_two = small_all[:, experts + 1].astype(single)
    cosine, sine = rotation_tables(positions)

    inputs = tokens[0].astype(single)
    inverse_one = lax.rsqrt(jnp.mean(inputs * inputs, axis=-1, keepdims=True) + epsilon)
    normed_one = inputs * inverse_one
    hidden_one = lax.optimization_barrier((normed_one * gain_one).astype(bfloat))
    projected = jnp.einsum("de,sd->es", proj_w, hidden_one, preferred_element_type=single)
    rotated = apply_rotation(projected[: query_width + key_width], cosine, sine).astype(bfloat)
    query = rotated[:query_width] * HEAD_SIZE ** (-0.5)
    own_pairs = jnp.concatenate(
        [rotated[query_width:], projected[query_width + key_width :].astype(bfloat)], axis=0
    )
    mixed, pairs = attend(query, own_pairs, lengths)
    resid = inputs + jnp.einsum("es,ed->sd", mixed, out_w, preferred_element_type=single)
    inverse_two = lax.rsqrt(jnp.mean(resid * resid, axis=-1, keepdims=True) + epsilon)
    normed_two = resid * inverse_two
    hidden_two = (normed_two * gain_two).astype(bfloat)

    grad_hidden, combined, scores, *expert_grads = experts_on_owner(
        hidden_two, final_all, routes_all, router_w.T, w_gate, w_up, w_down, capacity, pair
    )
    expert_grads, got = expert_grads[:3], expert_grads[3:]
    combined = lax.psum_scatter(combined, GROUP, scatter_dimension=0, tiled=False)

    if pair:
        moved = lax.ppermute(got[2], "dp", ((0, 1), (1, 0)))
        low = w_down.shape[1] // 2
        others = (
            jnp.stack([got[0], moved[0]]),
            jnp.stack([got[1], moved[1]]),
            jnp.concatenate(
                [moved[2:, n * low : (n + 1) * low] for n in range(MODEL_WIDTH // w_down.shape[1])],
                axis=2,
            ),
        )
    scores = scores[:, :local_exp]
    grad_gates = scores.reshape(experts, tokens_own).T

    routed = jnp.any(routes[0][:, :, None] == jnp.arange(experts, dtype=jnp.int32), axis=1)
    logits = jnp.einsum("sd,de->se", hidden_two, router_w, preferred_element_type=single)
    gates = jax.nn.softmax(jnp.where(routed, logits, floor_score), axis=-1)
    gates = jnp.where(routed, gates, 0.0)
    gate_mean = jnp.sum(gates * grad_gates, axis=-1, keepdims=True)
    grad_logits = (gates * (grad_gates - gate_mean)).astype(bfloat)
    grad_w_router = jnp.einsum("sd,se->de", hidden_two, grad_logits, preferred_element_type=single)
    grad_hidden_two = grad_hidden.astype(single) + jnp.einsum(
        "se,de->sd", grad_logits, router_w, preferred_element_type=single
    )
    grad_gain_ffn = jnp.sum(grad_hidden_two * normed_two, axis=0)
    grad_resid = norm_back(grad_hidden_two * gain_two, normed_two, inverse_two) + grad_final
    grad_attn = lax.optimization_barrier(grad_resid.astype(bfloat))

    grad_out_w = jnp.einsum("es,sd->ed", mixed, grad_attn, preferred_element_type=single)
    grad_mixed = jnp.einsum("ed,sd->es", out_w, grad_attn, preferred_element_type=single)
    grad_out_w = grad_out_w.astype(bfloat)
    grad_proj = attend_back(query, pairs, grad_mixed.astype(bfloat), lengths, cosine, sine)
    grad_proj_w = jnp.einsum("sd,es->de", hidden_one, grad_proj, preferred_element_type=single)
    grad_hidden_one = jnp.einsum("es,de->sd", grad_proj, proj_w, preferred_element_type=single)
    grad_gain_attn = jnp.sum(grad_hidden_one * normed_one, axis=0)
    grad_tokens = norm_back(grad_hidden_one * gain_one, normed_one, inverse_one) + grad_resid

    grad_small = jnp.concatenate(
        [
            grad_w_router,
            grad_gain_attn[:, None],
            grad_gain_ffn[:, None],
            jnp.zeros((MODEL_WIDTH, 128 - experts - 2), single),
        ],
        axis=1,
    ).astype(bfloat)
    grad_proj_w = grad_proj_w.astype(bfloat)
    if pair:
        expert_sums = tuple(
            own.astype(single) + other.astype(single)
            for own, other in zip(expert_grads, others)
        )
        grad_proj_w, grad_tokens, expert_sums = lax.optimization_barrier(
            (grad_proj_w, grad_tokens, expert_sums)
        )
        *proj_sums, small_sum, out_sum = sum_gradients(
            grad_proj_w, grad_small, grad_out_w, (query_width, key_width, key_width)
        )
    else:
        summed = lax.psum_scatter(
            jnp.concatenate([grad_proj_w, grad_small, grad_out_w], axis=1),
            EVERY,
            scatter_dimension=0,
            tiled=True,
        ).astype(single)
        proj_sums = jnp.split(summed[:, :proj_width], (query_width, query_width + key_width), axis=1)
        small_sum = summed[:, proj_width : proj_width + 128]
        out_sum = summed[:, proj_width + 128 :]
        expert_sums = tuple(
            lax.psum_scatter(x, "dp", scatter_dimension=1, tiled=True).astype(single)
            for x in expert_grads
        )
    combined, small_sum = lax.optimization_barrier((combined, small_sum))
    block_out = (valid * (resid + combined.astype(single))).astype(bfloat)
    return (
        block_out[None],
        grad_tokens[None],
        small_sum[:, experts],
        *proj_sums,
        out_sum,
        small_sum[:, experts + 1],
        small_sum[:, :experts],
        *expert_sums,
    )


def solution(mesh):
    in_specs = (
        P(("dp", "expert"), "context", None),
        P(("dp", "expert")),
        P(("dp", "expert"), "context", None),
        P(("dp", "context", "expert")),
        P(("dp", "context", "expert"), None),
        P(("dp", "context", "expert"), None),
        P(("dp", "context", "expert"), None),
        P(("dp", "context", "expert"), None),
        P(("dp", "context", "expert")),
        P(("dp", "context", "expert"), None),
        P(("context", "expert"), None, None),
        P(("context", "expert"), None, None),
        P(("context", "expert"), None, None),
        P(("dp", "expert"), "context", None),
    )
    out_specs = (
        P(("dp", "expert"), "context", None),
        P(("dp", "expert"), "context", None),
        P(("dp", "context", "expert")),
        P(("dp", "context", "expert"), None),
        P(("dp", "context", "expert"), None),
        P(("dp", "context", "expert"), None),
        P(("dp", "context", "expert"), None),
        P(("dp", "context", "expert")),
        P(("dp", "context", "expert"), None),
        P(("context", "expert"), "dp", None),
        P(("context", "expert"), "dp", None),
        P(("context", "expert"), "dp", None),
    )
    return jax.shard_map(
        on_device, mesh=mesh, in_specs=in_specs, out_specs=out_specs, check_vma=False
    )
```
